32 devices in a mesh: row: 2 (over x), col: 4 (over z), layer: 4 (over y, core).
Axes of the slice: x: 2, y: 2, z: 4, core: 2. Of those that a mesh axis runs over, the one named last changes fastest.
Arguments:
- sign_start: bfloat16 [32, 12, 128, 128], P(('row', 'col', 'layer')), as said below
- neighbors: int32 [32, 12], replicated, may hold values from 0 to 31, as said below
- atom_size: int32 [32], replicated, may hold values from 64 to 128
- basis_proj: bfloat16 [32, 6, 128], replicated, may hold values from -6 to 6
- pair_extent: int32 [32, 12], P(('row', 'col', 'layer')), may hold values from 3 to 6
- atom_x: int32 [32], replicated, may hold values from 6 to 9
- atom_y: int32 [32], replicated, may hold values from 6 to 9
- atom_z: int32 [32], replicated, may hold values from 62 to 65
Outputs:
- sign_next: bfloat16 [32, 12, 128, 128], P(('row', 'col', 'layer'))
- density: float32 [32, 64, 512], P('row', 'col', 'layer')
The draws below stay inside these ranges and needn't reach their ends.
Inputs may be any that keep to these rules, and one draw needn't show every extreme that they name: `neighbors`: atom a belongs to index a of row+col+layer. Row a lists 12 distinct atoms, a among them; b is in row a exactly when a is in row b; every listed atom lies on the same row and col indices as a or on one of the eight around them (with wrap), and exactly 3 entries of a row lie on each layer index. sign_start is symmetric: the block of atom b in row a is the transpose of the block of atom a in row b.
All inputs are finite; a program needn't handle non-finite values.
Results may differ from the reference program's by a relative error of at most 0.017.
Values may be sent and summed in bfloat16 or wider, within the bound.
No kernel may reach another device: no remote copies, remote signals or barrier semaphores. Data moves between devices by JAX's collectives and lax.ppermute only.
A program may use at most 64 MiB of HBM per device.

```python
import math
import jax
import jax.numpy as jnp
from jax import lax

BS = 128
W = 12
NS = 6
EXT = 6
DRIFT = 2
BX = 16
BY = 16
BZ = 128
BLOCKS = 32
N_ROW = 2
N_COL = 4
N_LAYER = 4


def neighbor_lists(key):
    atom_ids = jnp.arange(BLOCKS, dtype=jnp.int32)
    layer_pos = atom_ids % N_LAYER
    column = atom_ids // N_LAYER % N_COL
    rowpos = atom_ids // (N_LAYER * N_COL)

    def partner(step_row, step_col, is_even, layer_shift):
        direction = jnp.where(is_even, 1, -1)
        new_row = (rowpos + direction * step_row) % N_ROW
        new_col = (column + direction * step_col) % N_COL
        new_layer = (layer_pos + direction * layer_shift) % N_LAYER
        return (new_row * N_COL + new_col) * N_LAYER + new_layer

    def kind_rows(layer_shift, flipped):
        even_col = column % 2 == 0
        odd_col = column % 2 == 1
        even_row = rowpos % 2 == 0
        if flipped:
            even_col = column % 2 == 1
            odd_col = column % 2 == 0
            even_row = rowpos % 2 == 1
        return jnp.stack([partner(0, 1, even_col, layer_shift), partner(0, 1, odd_col, layer_shift), partner(1, 0, even_row, layer_shift), partner(1, 1, even_row, layer_shift), partner(1, -1, even_row, layer_shift)])
    subkeys = jax.random.split(key, 4)
    third_kinds = jax.random.permutation(subkeys[2], 5)
    same_layer = kind_rows(0, False)
    across = kind_rows(2, True)
    upper_shift = kind_rows(1, False)
    downward = kind_rows(3, False)
    entries = [atom_ids, partner(0, 0, rowpos >= 0, 2), same_layer[2], same_layer[0], across[2], across[0], upper_shift[third_kinds[0]], downward[third_kinds[0]], upper_shift[third_kinds[1]], downward[third_kinds[1]], upper_shift[third_kinds[2]], downward[third_kinds[2]]]
    listing = jnp.stack(entries, axis=1)
    orders = jax.vmap(lambda subkey: jax.random.permutation(subkey, W))(jax.random.split(subkeys[3], BLOCKS))
    return jnp.take_along_axis(listing, orders, axis=1).astype(jnp.int32)


def draw_neighbors(key, part):
    return neighbor_lists(key)


def draw_sign_start(key, part):
    listing = neighbor_lists(key)
    key = jax.random.fold_in(key, 7)
    atom_ids = jnp.arange(BLOCKS, dtype=jnp.int32)[:, None] + jnp.zeros_like(listing)
    lower_id = jnp.minimum(atom_ids, listing)
    upper_id = jnp.maximum(atom_ids, listing)
    pair_keys = jax.vmap(lambda index: jax.random.fold_in(key, index))((lower_id * BLOCKS + upper_id).reshape(-1))
    base_keys = jax.vmap(lambda subkey: jax.random.fold_in(subkey, 1))(pair_keys)
    site_keys = jax.vmap(lambda subkey: jax.random.fold_in(subkey, 2))(pair_keys)
    bases = jax.vmap(lambda subkey: jax.random.normal(subkey, (BS, BS), jnp.float32))(base_keys)
    onsites = jax.vmap(lambda subkey: jax.random.uniform(subkey, (BS,), jnp.float32, -0.6, 0.6))(site_keys)
    bases = bases.reshape(BLOCKS, W, BS, BS)
    onsites = onsites.reshape(BLOCKS, W, BS)
    scale = 1.0 / math.sqrt(W * BS)
    flipped = jnp.swapaxes(bases, 2, 3)
    is_self = atom_ids == listing
    is_lower = atom_ids > listing
    offdiag = jnp.where(is_lower[:, :, None, None], flipped, bases) * scale
    diagonal = 0.5 * (bases + flipped) * scale + onsites[:, :, :, None] * jnp.eye(BS, dtype=jnp.float32)
    return jnp.where(is_self[:, :, None, None], diagonal, offdiag).astype(jnp.bfloat16)


def set_ends(result, key, low, high):
    longest = result.shape.index(max(result.shape))
    spots = []
    for shift in (0, 1):
        where = [jax.random.randint(jax.random.fold_in(key, axis), (), 0, length) for axis, length in enumerate(result.shape)]
        where[longest] = (where[longest] + shift) % result.shape[longest]
        spots.append(tuple(where))
    return result.at[spots[0]].set(low).at[spots[1]].set(high)


def scatter_about(rng, shape, width, bound, held_as=jnp.bfloat16):
    return jnp.clip(width * jax.random.normal(rng, shape, jnp.float32), -bound, bound).astype(held_as)


def setup_inputs(seed: int = 0) -> dict:
    keys = jax.random.split(jax.random.key(seed), 9)
    sign_start = draw_sign_start(jax.random.fold_in(keys[8], 71), 0)
    neighbors = draw_neighbors(jax.random.fold_in(keys[8], 71), 0)
    atom_size = set_ends(jax.random.randint(keys[2], (BLOCKS,), BS // 2, BS + 1), jax.random.fold_in(keys[2], 1), BS // 2, BS).astype(jnp.int32)
    basis_proj = scatter_about(keys[3], (BLOCKS, NS, BS), 1.0, 6.0)
    pair_extent = set_ends(jax.random.randint(keys[4], (BLOCKS, W), max(2, EXT // 2), EXT + 1), jax.random.fold_in(keys[4], 1), max(2, EXT // 2), EXT).astype(jnp.int32)
    atom_x = set_ends(jax.random.randint(keys[5], (BLOCKS,), BX // 2 - DRIFT, BX // 2 + DRIFT), jax.random.fold_in(keys[5], 1), BX // 2 - DRIFT, (BX // 2 + DRIFT) - 1).astype(jnp.int32)
    atom_y = set_ends(jax.random.randint(keys[6], (BLOCKS,), BY // 2 - DRIFT, BY // 2 + DRIFT), jax.random.fold_in(keys[6], 1), BY // 2 - DRIFT, (BY // 2 + DRIFT) - 1).astype(jnp.int32)
    atom_z = set_ends(jax.random.randint(keys[7], (BLOCKS,), BZ // 2 - DRIFT, BZ // 2 + DRIFT), jax.random.fold_in(keys[7], 1), BZ // 2 - DRIFT, (BZ // 2 + DRIFT) - 1).astype(jnp.int32)
    return {"sign_start": sign_start, "neighbors": neighbors, "atom_size": atom_size, "basis_proj": basis_proj, "pair_extent": pair_extent, "atom_x": atom_x, "atom_y": atom_y, "atom_z": atom_z}


def kept_products(left, right, neighbors):
    atom_ids = jnp.arange(left.shape[0], dtype=jnp.int32)
    layer_ids = jnp.arange(N_LAYER, dtype=jnp.int32)

    def row_product(atom):
        listed = neighbors[atom]
        term_index_lists = jnp.take(neighbors, listed, axis=0)
        selector = (term_index_lists[:, None, :] == listed[None, :, None]).astype(jnp.float32)
        right_rows = jnp.take(right, listed, axis=0).astype(jnp.float32)
        selected_terms = jnp.einsum("vwu,vuab->vwab", selector, right_rows, precision=lax.Precision.HIGHEST)
        left_block_row = left[atom].astype(jnp.float32)
        block_products = jnp.einsum("rzd,rmdq->rmzq", left_block_row, selected_terms, precision=lax.Precision.HIGHEST)
        grouping = (listed[None, :] % N_LAYER == layer_ids[:, None]).astype(jnp.float32)
        layered = jnp.einsum("gv,vwac->gwac", grouping, block_products, precision=lax.Precision.HIGHEST)
        rounded = lax.optimization_barrier(layered.astype(jnp.bfloat16))
        return jnp.sum(rounded.astype(jnp.float32), axis=0)

    return lax.map(row_product, atom_ids)


def profile(coords, centers, extent, rates):
    offset = coords[None, :] - centers[:, None]
    inside = (jnp.abs(offset) <= extent[:, None]).astype(jnp.float32)
    return jnp.exp(-rates[:, :, :, None] * (offset * offset)[:, None, None, :]) * inside[:, None, None, :]


def collocate(coeffs, cent_x, cent_y, cent_z, extent, grid_x, grid_height, grid_z):
    shells_count = coeffs.shape[1]
    shells = jnp.arange(1, shells_count + 1).astype(jnp.float32)
    inverse = (shells_count / extent[:, None]) ** 2 / (shells[None, :] ** 2)
    rates = inverse[:, :, None] + inverse[:, None, :]
    along_x = profile(grid_x, cent_x, extent, rates)
    along_y = profile(grid_height, cent_y, extent, rates)
    along_z = profile(grid_z, cent_z, extent, rates) * coeffs[:, :, :, None]
    terms_count = coeffs.shape[0] * shells_count * shells_count
    outer_rows = (along_x[:, :, :, :, None] * along_y[:, :, :, None, :]).reshape(terms_count, -1)
    summed = jnp.einsum("kp,kz->pz", outer_rows, along_z.reshape(terms_count, -1), precision=lax.Precision.HIGHEST)
    return summed.reshape(grid_x.shape[0], grid_height.shape[0], grid_z.shape[0])


def reference(sign_start, neighbors, atom_size, basis_proj, pair_extent, atom_x, atom_y, atom_z):
    blocks = sign_start.shape[0]
    slots = sign_start.shape[1]
    block_size = sign_start.shape[2]
    lane_ids = jnp.arange(block_size, dtype=jnp.int32)
    size_mask = (lane_ids[None, :] < atom_size[:, None]).astype(jnp.float32)
    column_mask = jnp.take(size_mask, neighbors, axis=0)
    masked = (sign_start.astype(jnp.float32) * size_mask[:, None, :, None] * column_mask[:, :, None, :]).astype(jnp.bfloat16)
    square = kept_products(masked, masked, neighbors).astype(jnp.bfloat16)
    cubed = kept_products(square, masked, neighbors)
    sign_full = 1.5 * masked.astype(jnp.float32) - 0.5 * cubed
    sign_next = sign_full.astype(jnp.bfloat16)

    margin = DRIFT + EXT
    grid_x = jnp.arange(BX + 2 * margin).astype(jnp.float32) - margin
    grid_height = jnp.arange(BY + 2 * margin).astype(jnp.float32) - margin
    grid_z = jnp.arange(BZ + 2 * margin).astype(jnp.float32) - margin
    atom_ids = jnp.arange(blocks, dtype=jnp.int32)

    def per_atom(atom):
        listed = neighbors[atom]
        atom_row = atom // (N_COL * N_LAYER)
        atom_col = (atom // N_LAYER) % N_COL
        atom_lay = atom % N_LAYER
        pair_row = listed // (N_COL * N_LAYER)
        pair_col = (listed // N_LAYER) % N_COL
        pair_layer = listed % N_LAYER
        step_row = ((pair_row - atom_row + 1) % N_ROW - 1).astype(jnp.float32)
        step_col = ((pair_col - atom_col + 1) % N_COL - 1).astype(jnp.float32)
        step_lay = jnp.minimum((pair_layer - atom_lay + 1) % N_LAYER - 1, 1).astype(jnp.float32)
        own_mask = size_mask[atom]
        is_self = listed == atom
        dmat = 0.5 * (jnp.where(is_self[:, None, None], jnp.diag(own_mask)[None], 0.0) - sign_full[atom])
        own_basis = basis_proj[atom].astype(jnp.float32)
        pair_basis = jnp.take(basis_proj, listed, axis=0).astype(jnp.float32)
        halfway = jnp.einsum("sa,wab->wsb", own_basis, dmat, precision=lax.Precision.HIGHEST)
        coeffs = jnp.einsum("wsb,wtb->wst", halfway, pair_basis, precision=lax.Precision.HIGHEST)
        cent_x = 0.5 * (atom_x[atom].astype(jnp.float32) + jnp.take(atom_x, listed).astype(jnp.float32) + BX * step_row)
        cent_y = 0.5 * (atom_y[atom].astype(jnp.float32) + jnp.take(atom_y, listed).astype(jnp.float32) + BY * step_col)
        cent_z = 0.5 * (atom_z[atom].astype(jnp.float32) + jnp.take(atom_z, listed).astype(jnp.float32) + BZ * step_lay)
        extent = pair_extent[atom].astype(jnp.float32)
        return collocate(coeffs, cent_x, cent_y, cent_z, extent, grid_x, grid_height, grid_z)

    fields = lax.map(per_atom, atom_ids)
    grid = fields.reshape(N_ROW, N_COL, N_LAYER, BX + 2 * margin, BY + 2 * margin, BZ + 2 * margin)
    core_x = grid[:, :, :, margin:margin + BX]
    core_x = core_x.at[:, :, :, :margin].add(jnp.roll(grid[:, :, :, BX + margin:], 1, axis=0))
    core_x = core_x.at[:, :, :, BX - margin:].add(jnp.roll(grid[:, :, :, :margin], -1, axis=0))
    core_y = core_x[:, :, :, :, margin:margin + BY]
    core_y = core_y.at[:, :, :, :, :margin].add(jnp.roll(core_x[:, :, :, :, BY + margin:], 1, axis=1))
    core_y = core_y.at[:, :, :, :, BY - margin:].add(jnp.roll(core_x[:, :, :, :, :margin], -1, axis=1))
    core = core_y[:, :, :, :, :, margin:margin + BZ]
    core = core.at[:, :, :, :, :, :margin].add(jnp.roll(core_y[:, :, :, :, :, BZ + margin:], 1, axis=2))
    core = core.at[:, :, :, :, :, BZ - margin:].add(jnp.roll(core_y[:, :, :, :, :, :margin], -1, axis=2))
    density = core.transpose(0, 3, 1, 4, 2, 5).reshape(N_ROW * BX, N_COL * BY, N_LAYER * BZ)
    return sign_next, density
```

```python
import functools

import jax
import jax.numpy as jnp
from jax import lax
from jax.experimental import pallas as pl
from jax.experimental.pallas import tpu as pltpu
from jax.sharding import PartitionSpec as P

DRIFT = 2
BX = 16
BY = 16
BZ = 128
LANES = 128
VMEM = pl.BlockSpec(memory_space=pltpu.VMEM)
SMEM = pl.BlockSpec(memory_space=pltpu.SMEM)
ANY = pl.BlockSpec(memory_space=pl.ANY)


def from_offset(x, axis, step):
    count = lax.axis_size(axis)
    return lax.ppermute(x, axis, [((i + step) % count, i) for i in range(count)])


def from_layer(x, flip):
    count = lax.axis_size("layer")
    return lax.ppermute(x, "layer", [(i ^ flip, i) for i in range(count)])


def column_targets(n_row, row):
    same = [(0, 0), (0, 1), (0, 2)]
    if n_row == 2:
        return same + [(1, row), (1, row + 1)]
    return same + [(1, 0), (1, 1), (1, 2), (1, 3)]


def pick_kernel(n_row, n_col, n_lay, listed_ref, sign_ref, out_ref, sems):
    row = lax.axis_index("row")
    col = lax.axis_index("col")
    lay = lax.axis_index("layer")
    slots = sign_ref.shape[0]
    copies = []
    for i, (step_row, step_lay) in enumerate(column_targets(n_row, row)):
        target = (lax.rem(row + step_row, n_row) * n_col + col) * n_lay + lax.rem(lay + step_lay, n_lay)
        place = jnp.int32(0)
        for u in range(slots):
            place = jnp.where(listed_ref[u] == target, u, place)
        copy = pltpu.make_async_copy(sign_ref.at[place], out_ref.at[i], sems.at[i])
        copy.start()
        copies.append(copy)
    for copy in copies:
        copy.wait()


def step_kernel(offsets, lengths, pairs, n_pool, *refs):
    tab_ref, info_ref, basis_ref, spread_ref, sign_ref = refs[:5]
    piece_refs = refs[5 : 5 + len(offsets)]
    next_ref, coef_ref, pool, gram, own, square, sems = refs[5 + len(offsets) :]
    slots, size = sign_ref.shape[0], sign_ref.shape[1]
    copies = []
    for i, piece in enumerate(piece_refs):
        copy = pltpu.make_async_copy(piece, pool.at[pl.ds(offsets[i], lengths[i])], sems.at[i])
        copy.start()
        copies.append(copy)
    pool[n_pool] = jnp.zeros((size, size), pool.dtype)
    rows = lax.broadcasted_iota(jnp.int32, (size, size), 0)
    lanes = lax.broadcasted_iota(jnp.int32, (size, size), 1)
    own_size = info_ref[slots]
    self_slot = info_ref[slots + 1]
    for w in range(slots):
        kept = (rows < own_size) & (lanes < info_ref[w])
        block = jnp.where(kept, sign_ref[w].astype(jnp.float32), 0.0)
        own[:, w * size : (w + 1) * size] = block.astype(own.dtype)
    for copy in copies:
        copy.wait()

    def place(i, carry):
        p = pl.multiple_of(tab_ref[i] * size, size)
        q = pl.multiple_of(tab_ref[pairs + i] * size, size)
        block = pool[tab_ref[2 * pairs + i]]
        gram[pl.ds(p, size), pl.ds(q, size)] = block
        gram[pl.ds(q, size), pl.ds(p, size)] = block.T
        return carry

    lax.fori_loop(0, pairs, place, 0)
    wide = 2 * size
    wide_lanes = lax.broadcasted_iota(jnp.int32, (size, wide), 1)
    wide_rows = lax.broadcasted_iota(jnp.int32, (size, wide), 0)

    def column_kept(n):
        first = info_ref[2 * n]
        second = info_ref[2 * n + 1]
        return (wide_lanes < first) | ((wide_lanes >= size) & (wide_lanes < size + second))

    for n in range(slots // 2):
        part = jnp.dot(own[...], gram[:, n * wide : (n + 1) * wide], preferred_element_type=jnp.float32)
        square[:, n * wide : (n + 1) * wide] = jnp.where(column_kept(n), part, 0.0).astype(square.dtype)
    coef = jnp.zeros((basis_ref.shape[0], LANES), jnp.float32)
    for n in range(slots // 2):
        part = jnp.dot(square[...], gram[:, n * wide : (n + 1) * wide], preferred_element_type=jnp.float32)
        cube = jnp.where(column_kept(n), part, 0.0)
        full = 1.5 * own[:, n * wide : (n + 1) * wide].astype(jnp.float32) - 0.5 * cube
        next_ref[2 * n] = full[:, :size].astype(next_ref.dtype)
        next_ref[2 * n + 1] = full[:, size:].astype(next_ref.dtype)
        shift = (self_slot - 2 * n) * size
        is_self = (self_slot >= 2 * n) & (self_slot < 2 * n + 2)
        diag = (wide_lanes == wide_rows + shift) & (wide_rows < own_size) & is_self
        dmat = 0.5 * (jnp.where(diag, 1.0, 0.0) - full)
        high = dmat.astype(jnp.bfloat16)
        low = (dmat - high.astype(jnp.float32)).astype(jnp.bfloat16)
        half = jnp.dot(basis_ref[...], high, preferred_element_type=jnp.float32) + jnp.dot(
            basis_ref[...], low, preferred_element_type=jnp.float32
        )
        half_high = half.astype(jnp.bfloat16)
        half_low = (half - half_high.astype(jnp.float32)).astype(jnp.bfloat16)
        spread = spread_ref[n * wide : (n + 1) * wide]
        coef = coef + jnp.dot(half_high, spread, preferred_element_type=jnp.float32)
        coef = coef + jnp.dot(half_low, spread, preferred_element_type=jnp.float32)
    coef_ref[...] = coef[: coef_ref.shape[0]]


def profile_kernel(periods, lane_ref, sub_ref, plane_ref, line_ref):
    shells = plane_ref.shape[1]
    cells = plane_ref.shape[2]
    cell = lax.broadcasted_iota(jnp.int32, (cells, LANES), 0)
    grid_x = (cell // BY).astype(jnp.float32)
    grid_y = (cell % BY).astype(jnp.float32)
    grid_z = lax.broadcasted_iota(jnp.int32, (LANES, BZ), 1).astype(jnp.float32)

    def nearest(offset, period):
        return offset - period * jnp.floor(offset * (1.0 / period) + 0.5)

    for o in range(lane_ref.shape[0]):
        row = lane_ref[o]
        d_x = nearest(grid_x - row[0:1], periods[0])
        d_y = nearest(grid_y - row[1:2], periods[1])
        inside = (jnp.abs(d_x) <= row[3:4]) & (jnp.abs(d_y) <= row[3:4])
        squared = d_x * d_x + d_y * d_y
        sub = sub_ref[o]
        d_z = nearest(grid_z - sub[:, 2:3], periods[2])
        inside_z = jnp.abs(d_z) <= sub[:, 3:4]
        squared_z = d_z * d_z
        for s in range(shells):
            part = 1.0 / ((s + 1) * (s + 1))
            rate = row[5:6] * part + row[4:5]
            plane_ref[o, s] = jnp.where(inside, jnp.exp(-rate * squared), 0.0).astype(plane_ref.dtype)
            rate_z = sub[:, 5:6] * part + sub[:, 4:5]
            line_ref[o, s] = jnp.where(inside_z, jnp.exp(-rate_z * squared_z), 0.0).astype(line_ref.dtype)


def density_kernel(tiles, *refs):
    tile_refs = refs[:tiles]
    plane_ref, line_ref, out_ref, terms = refs[tiles:]
    shells = plane_ref.shape[1]
    for o in range(tiles):
        for s in range(shells):
            scaled = plane_ref[o, s].astype(jnp.float32) * tile_refs[o][s : s + 1, :]
            at = (o * shells + s) * LANES
            terms[:, at : at + LANES] = scaled.astype(terms.dtype)
    out_ref[...] = jnp.dot(terms[...], line_ref[...], preferred_element_type=jnp.float32)


def local(sign_start, neighbors, atom_size, basis_proj, pair_extent, atom_x, atom_y, atom_z):
    n_row = lax.axis_size("row")
    n_col = lax.axis_size("col")
    n_lay = lax.axis_size("layer")
    assert n_lay == 4 and n_col >= 4 and (n_row == 2 or n_row >= 4)
    row = lax.axis_index("row")
    col = lax.axis_index("col")
    lay = lax.axis_index("layer")
    atoms, slots = neighbors.shape
    size = sign_start.shape[2]
    shells = basis_proj.shape[1]
    me = (row * n_col + col) * n_lay + lay
    steps = [0, 1] if n_row == 2 else [0, 1, -1]
    count = len(steps)
    own = sign_start[0]
    listed = lax.dynamic_index_in_dim(neighbors, me, 0, keepdims=False)

    n_pick = len(column_targets(n_row, 0))
    picked = pl.pallas_call(
        functools.partial(pick_kernel, n_row, n_col, n_lay),
        out_shape=jax.ShapeDtypeStruct((n_pick, size, size), own.dtype),
        in_specs=[SMEM, ANY],
        out_specs=ANY,
        scratch_shapes=[pltpu.SemaphoreType.DMA((n_pick,))],
        name="pick_column_blocks",
    )(listed, own)
    half = slots // 2
    first, second = own[:half], own[half:]
    pieces = {}

    def give(name, di, flip, value, start, width):
        pieces[(name, di, flip)] = (value, start, width)

    a_parts, b_parts, up_parts, down_parts = {}, {}, {}, {}
    a_parts[0, 0], b_parts[0, 0] = first, second
    for di in range(1, count):
        a_parts[di, 0] = from_offset(first, "row", steps[di])
    b_parts[0, 2] = from_layer(second, 2)
    up_parts[0, 0] = from_offset(picked, "col", 1)
    down_parts[0, 0] = from_offset(picked, "col", -1)
    for di in range(count):
        a_parts[di, 2] = from_layer(a_parts[di, 0], 2)
    for di in range(1, count):
        for flip in (0, 2):
            b_parts[di, flip] = from_offset(b_parts[0, flip], "row", steps[di])
    for di in range(1, count):
        up_parts[di, 0] = from_offset(up_parts[0, 0], "row", steps[di])
    down_parts[0, 2] = from_layer(down_parts[0, 0], 2)
    for di in range(count):
        up_parts[di, 2] = from_layer(up_parts[di, 0], 2)
    for di in range(1, count):
        for flip in (0, 2):
            down_parts[di, flip] = from_offset(down_parts[0, flip], "row", steps[di])
    values, starts, widths = [], [], []

    def add(value, start):
        values.append(value)
        starts.append(start)
        widths.append(value.shape[0])

    column_base = count * 4 * slots
    for di in range(count):
        for flip in (0, 2):
            place = (di * 4 + flip) * slots
            mate = (di * 4 + flip + 1) * slots
            if di == 0 and flip == 0:
                add(own, place)
                add(from_layer(own, 1), mate)
            else:
                add(a_parts[di, flip], place)
                add(b_parts[di, flip], place + half)
                add(from_layer(a_parts[di, flip], 1), mate)
                add(from_layer(b_parts[di, flip], 1), mate + half)
            for side, parts in enumerate((up_parts, down_parts)):
                base = column_base + ((side * count + di) * 4 + flip) * n_pick
                add(parts[di, flip], base)
                add(from_layer(parts[di, flip], 1), base + n_pick)
    n_pool = column_base + 2 * count * 4 * n_pick

    atom_ids = jnp.arange(atoms, dtype=jnp.int32)
    l_row = listed // (n_lay * n_col)
    l_col = listed // n_lay % n_col
    l_lay = listed % n_lay
    step_row = (l_row - row) % n_row
    row_place = jnp.where(step_row == 0, 0, jnp.where(step_row == 1, 1, 2))
    step_col = (l_col - col) % n_col
    in_column = step_col == 0
    side = jnp.where(step_col == 1, 0, 1)
    line = row_place * 4 + (l_lay ^ lay)
    listings = jnp.take(neighbors, listed, axis=0)
    match = listings[:, None, :] == listed[None, :, None]
    present = jnp.any(match, axis=2)
    slot = jnp.sum(jnp.where(match, jnp.arange(slots, dtype=jnp.int32), 0), axis=2)
    d_row = (l_row[None, :] - l_row[:, None]) % n_row
    d_lay = (l_lay[None, :] - l_lay[:, None]) % n_lay
    if n_row == 2:
        lead = d_lay - l_row[:, None]
        across = jnp.where((lead >= 0) & (lead < 2), 3 + lead, -1)
    else:
        across = 3 + d_lay
    target = jnp.where(d_row == 0, jnp.where(d_lay < 3, d_lay, -1), jnp.where(d_row == 1, across, -1))
    beside = ~in_column[:, None] & (step_col[:, None] == step_col[None, :]) & (target >= 0)
    direct = present & (in_column[:, None] | beside)
    located = jnp.where(
        in_column[:, None],
        line[:, None] * slots + slot,
        column_base + (side[:, None] * count * 4 + line[:, None]) * n_pick + target,
    )
    upper = [(v, w) for v in range(slots) for w in range(v, slots)]
    pairs = len(upper)
    idx = jnp.arange(slots, dtype=jnp.int32)
    forward = direct
    backward = direct.T & ~direct
    from_p = jnp.where(backward, idx[None, :], idx[:, None])
    from_q = jnp.where(backward, idx[:, None], idx[None, :])
    source = jnp.where(forward, located, jnp.where(backward, located.T, n_pool))
    table = jnp.concatenate(
        [part[v, v:] for part in (from_p, from_q, source) for v in range(slots)]
    ).astype(jnp.int32)
    sizes = jnp.take(atom_size, listed)
    own_size = lax.dynamic_index_in_dim(atom_size, me, 0, keepdims=True)
    self_slot = jnp.sum(jnp.where(listed == me, idx, 0), keepdims=True)
    info = jnp.concatenate([sizes, own_size, self_slot]).astype(jnp.int32)

    layer_step = (neighbors % n_lay - atom_ids[:, None] % n_lay) % n_lay
    earlier = (layer_step[:, :, None] == layer_step[:, None, :]) & (idx[None, None, :] < idx[None, :, None])
    rank = 3 * layer_step + jnp.sum(earlier.astype(jnp.int32), axis=2)
    own_rank = lax.dynamic_index_in_dim(rank, me, 0, keepdims=False)
    lane = jnp.arange(LANES, dtype=jnp.int32)
    wanted = jnp.where(lane[None, :] // shells == own_rank[:, None], listed[:, None] * shells + lane[None, :] % shells, -1)
    one_hot = (wanted[:, :, None] == jnp.arange(atoms * shells, dtype=jnp.int32)).astype(jnp.bfloat16)
    spread = jnp.einsum(
        "wln,nb->wbl", one_hot, basis_proj.reshape(atoms * shells, size), preferred_element_type=jnp.float32
    ).astype(jnp.bfloat16).reshape(slots * size, LANES)
    own_basis = lax.dynamic_index_in_dim(basis_proj, me, 0, keepdims=False)
    own_basis = jnp.pad(own_basis, ((0, 16 - shells), (0, 0)))

    extents = lax.all_gather(pair_extent, ("row", "col", "layer"), axis=0, tiled=True)
    tile_steps = [(dr, dc) for dr in steps for dc in (0, 1, -1)]
    tiles = len(tile_steps)
    tile_rows = jnp.stack([(row + dr) % n_row for dr, _ in tile_steps])
    tile_cols = jnp.stack([(col + dc) % n_col for _, dc in tile_steps])
    order = [(0, k) for k in range(12)] + [(-1, k) for k in range(3, 9)] + [(1, k) for k in range(9, 12)]
    lane_layer = jnp.array([d for d, _ in order], dtype=jnp.int32)
    lane_rank = jnp.array([k for _, k in order], dtype=jnp.int32)
    pair_lay = (lay + lane_layer) % n_lay
    pair_atom = (tile_rows * n_col + tile_cols)[:, None] * n_lay + pair_lay[None, :]
    at_rank = jnp.take(rank, pair_atom, axis=0) == lane_rank[None, :, None]
    pair_other = jnp.sum(jnp.where(at_rank, jnp.take(neighbors, pair_atom, axis=0), 0), axis=2)
    pair_ext = jnp.sum(jnp.where(at_rank, jnp.take(extents, pair_atom, axis=0), 0), axis=2)
    coords = jnp.stack([atom_x, atom_y, atom_z], axis=1)
    total = (jnp.take(coords, pair_atom, axis=0) + jnp.take(coords, pair_other, axis=0)).astype(jnp.float32)
    o_row = pair_other // (n_lay * n_col)
    o_col = pair_other // n_lay % n_col
    o_lay = pair_other % n_lay
    go_row = (o_row - tile_rows[:, None] + 1) % n_row - 1
    go_col = (o_col - tile_cols[:, None] + 1) % n_col - 1
    go_lay = jnp.minimum((o_lay - pair_lay[None, :] + 1) % n_lay - 1, 1)
    base_row = jnp.array([dr for dr, _ in tile_steps], dtype=jnp.float32)[:, None] * BX
    base_col = jnp.array([dc for _, dc in tile_steps], dtype=jnp.float32)[:, None] * BY
    base_lay = lane_layer[None, :].astype(jnp.float32) * BZ
    cent_x = base_row + 0.5 * (total[..., 0] + BX * go_row.astype(jnp.float32))
    cent_y = base_col + 0.5 * (total[..., 1] + BY * go_col.astype(jnp.float32))
    cent_z = base_lay + 0.5 * (total[..., 2] + BZ * go_lay.astype(jnp.float32))
    ext = pair_ext.astype(jnp.float32)
    inverse = (shells / ext) ** 2
    shell = jnp.arange(1, shells + 1).astype(jnp.float32)
    packed = jnp.stack([cent_x, cent_y, cent_z, ext, inverse, inverse], axis=1)
    packed = jnp.broadcast_to(packed[..., None], packed.shape + (shells,))
    divided = jnp.concatenate(
        [jnp.ones((4, shells)), (1.0 / (shell * shell))[None], jnp.ones((1, shells))]
    ).astype(jnp.float32)
    packed = (packed * divided[None, :, None, :]).reshape(tiles, 6, len(order) * shells)
    spare = LANES - len(order) * shells
    lane_geo = jnp.pad(packed, ((0, 0), (0, 2), (0, spare)), constant_values=-1.0)
    sub_geo = lane_geo.transpose(0, 2, 1)
    periods = (float(BX * n_row), float(BY * n_col), float(BZ * n_lay))
    plane, line_z = pl.pallas_call(
        functools.partial(profile_kernel, periods),
        out_shape=(
            jax.ShapeDtypeStruct((tiles, shells, BX * BY, LANES), jnp.bfloat16),
            jax.ShapeDtypeStruct((tiles, shells, LANES, BZ), jnp.bfloat16),
        ),
        in_specs=[VMEM, VMEM],
        out_specs=(VMEM, VMEM),
        compiler_params=pltpu.CompilerParams(vmem_limit_bytes=32 << 20),
        cost_estimate=pl.CostEstimate(flops=30_000_000, bytes_accessed=4_000_000, transcendentals=2_000_000),
        name="profiles",
    )(lane_geo, sub_geo)

    sign_next, coef = pl.pallas_call(
        functools.partial(step_kernel, tuple(starts), tuple(widths), pairs, n_pool),
        out_shape=(
            jax.ShapeDtypeStruct((slots, size, size), jnp.bfloat16),
            jax.ShapeDtypeStruct((8, LANES), jnp.float32),
        ),
        in_specs=[SMEM, SMEM, VMEM, VMEM, VMEM] + [ANY] * len(values),
        out_specs=(VMEM, VMEM),
        scratch_shapes=[
            pltpu.VMEM((n_pool + 1, size, size), jnp.bfloat16),
            pltpu.VMEM((slots * size, slots * size), jnp.bfloat16),
            pltpu.VMEM((size, slots * size), jnp.bfloat16),
            pltpu.VMEM((size, slots * size), jnp.bfloat16),
            pltpu.SemaphoreType.DMA((len(values),)),
        ],
        compiler_params=pltpu.CompilerParams(vmem_limit_bytes=40 << 20),
        cost_estimate=pl.CostEstimate(flops=1_300_000_000, bytes_accessed=8_000_000, transcendentals=0),
        name="square_cube_coefficients",
    )(table, info, own_basis, spread, own, *values)

    per_class = 3 * shells
    below = from_offset(coef, "layer", -1)
    above = from_offset(coef, "layer", 1)
    merged = jnp.concatenate(
        [
            coef[:, : 4 * per_class],
            below[:, per_class : 3 * per_class],
            above[:, 3 * per_class : 4 * per_class],
            jnp.zeros((8, spare), jnp.float32),
        ],
        axis=1,
    )
    received = []
    for dr, dc in tile_steps:
        if dr == 0 and dc == 0:
            received.append(merged)
        elif dr == 0:
            received.append(from_offset(merged, "col", dc))
        elif dc == 0:
            received.append(from_offset(merged, "row", dr))
        else:
            moves = [
                (((i + dr) % n_row) * n_col + (j + dc) % n_col, i * n_col + j)
                for i in range(n_row)
                for j in range(n_col)
            ]
            received.append(lax.ppermute(merged, ("row", "col"), moves))
    density = pl.pallas_call(
        functools.partial(density_kernel, tiles),
        out_shape=jax.ShapeDtypeStruct((BX * BY, BZ), jnp.float32),
        in_specs=[VMEM] * (tiles + 2),
        out_specs=VMEM,
        scratch_shapes=[pltpu.VMEM((BX * BY, tiles * shells * LANES), jnp.bfloat16)],
        compiler_params=pltpu.CompilerParams(vmem_limit_bytes=32 << 20),
        cost_estimate=pl.CostEstimate(flops=310_000_000, bytes_accessed=4_000_000, transcendentals=0),
        name="density",
    )(*received, plane, line_z.reshape(tiles * shells * LANES, BZ))
    return sign_next[None], density.reshape(BX, BY, BZ)


def solution(mesh):
    rows = P(("row", "col", "layer"), None, None, None)
    in_specs = (rows, P(), P(), P(), P(("row", "col", "layer"), None), P(), P(), P())
    out_specs = (rows, P("row", "col", "layer"))
    return jax.shard_map(local, mesh=mesh, in_specs=in_specs, out_specs=out_specs, check_vma=False)
```

```python
import functools

import jax
import jax.numpy as jnp
from jax import lax
from jax.experimental import pallas as pl
from jax.experimental.pallas import tpu as pltpu
from jax.sharding import PartitionSpec as P

BX = 16
BY = 16
BZ = 128
LANES = 128
UNROLL = 4
VMEM = pl.BlockSpec(memory_space=pltpu.VMEM)
SMEM = pl.BlockSpec(memory_space=pltpu.SMEM)
ANY = pl.BlockSpec(memory_space=pl.ANY)


def from_offset(x, axis, step):
    count = lax.axis_size(axis)
    return lax.ppermute(x, axis, [((i + step) % count, i) for i in range(count)])


def from_layer(x, flip):
    count = lax.axis_size("layer")
    return lax.ppermute(x, "layer", [(i ^ flip, i) for i in range(count)])


def column_targets(n_row):
    return 5 if n_row == 2 else 7


def target_place(n_row, step_row, step_lay, row):
    same = jnp.where(step_lay < 3, step_lay, -1)
    if n_row == 2:
        lead = step_lay - row
        across = jnp.where((lead >= 0) & (lead < 2), 3 + lead, -1)
    else:
        across = 3 + step_lay
    return jnp.where(step_row == 0, same, jnp.where(step_row == 1, across, -1))


class Places:
    def __init__(self, n_row, n_col, n_lay):
        self.n_row, self.n_col, self.n_lay = n_row, n_col, n_lay
        self.lay_bits = n_lay.bit_length() - 1
        self.col_bits = n_col.bit_length() - 1
        self.row = lax.axis_index("row")
        self.col = lax.axis_index("col")
        self.lay = lax.axis_index("layer")
        self.me = (((self.row << self.col_bits) + self.col) << self.lay_bits) + self.lay

    def split(self, atom):
        return (
            atom >> (self.lay_bits + self.col_bits),
            (atom >> self.lay_bits) & (self.n_col - 1),
            atom & (self.n_lay - 1),
        )


def pick_kernel(axes, neighbors_ref, sign_ref, out_ref, place_ref):
    at = Places(*axes)
    for i in range(out_ref.shape[0] + 1):
        place_ref[i] = 0
    for u in range(sign_ref.shape[0]):
        row, col, lay = at.split(neighbors_ref[at.me, u])
        place = target_place(at.n_row, (row - at.row) & (at.n_row - 1), (lay - at.lay) & (at.n_lay - 1), at.row)
        place = jnp.where((col == at.col) & (place >= 0), place, out_ref.shape[0])
        place_ref[place] = u
    for i in range(out_ref.shape[0]):
        out_ref[i] = sign_ref[place_ref[i]]


def prepare_kernel(axes, count, n_pick, *refs):
    neighbors_ref, extent_ref, size_ref, x_ref, y_ref, z_ref, basis_ref = refs[:7]
    table_ref, info_ref, geo_ref, spread_ref, own_basis_ref, known, inverse = refs[7:]
    at = Places(*axes)
    slots = extent_ref.shape[1]
    shells = 6
    column_base = count * at.n_lay * slots
    sub = lax.broadcasted_iota(jnp.int32, (8, LANES), 0)
    lane_pair = lax.broadcasted_iota(jnp.int32, (8, LANES), 1) // shells
    hot_row = lax.broadcasted_iota(jnp.int32, (LANES, 16), 0)
    hot_shell = lax.broadcasted_iota(jnp.int32, (LANES, 16), 1)
    geo = jnp.zeros((8, LANES), jnp.int32)
    seen = [jnp.int32(0)] * at.n_lay
    self_slot = jnp.int32(0)
    for w in range(slots):
        atom = neighbors_ref[at.me, w]
        row, col, lay = at.split(atom)
        step_row = (row - at.row) & (at.n_row - 1)
        step_col = (col - at.col) & (at.n_col - 1)
        step_lay = (lay - at.lay) & (at.n_lay - 1)
        rank = jnp.int32(0)
        for k in range(at.n_lay):
            rank = jnp.where(step_lay == k, 3 * k + seen[k], rank)
            seen[k] = seen[k] + (step_lay == k).astype(jnp.int32)
        go_row = ((step_row + 1) & (at.n_row - 1)) - 1
        go_col = ((step_col + 1) & (at.n_col - 1)) - 1
        go_lay = jnp.minimum(((step_lay + 1) & (at.n_lay - 1)) - 1, 1)
        twice_x = x_ref[at.me] + x_ref[atom] + BX * go_row
        twice_y = y_ref[at.me] + y_ref[atom] + BY * go_col
        twice_z = z_ref[at.me] + z_ref[atom] + BZ * go_lay
        values = jnp.where(sub == 0, twice_x, jnp.where(sub == 1, twice_y, jnp.where(sub == 2, twice_z, 2 * extent_ref[0, w])))
        geo = jnp.where(lane_pair == rank, values, geo)
        self_slot = jnp.where(atom == at.me, w, self_slot)
        info_ref[w] = size_ref[atom]
        hot = (hot_row == rank * shells + hot_shell) & (hot_shell < shells)
        spread_ref[w] = jnp.dot(
            hot.astype(jnp.bfloat16), basis_ref[atom], preferred_element_type=jnp.float32
        ).astype(spread_ref.dtype)
        known[0, w] = atom
        known[1, w] = jnp.where(step_col == 0, 0, jnp.where(step_col == 1, 1, 2))
        known[2, w] = jnp.where(step_row == 0, 0, jnp.where(step_row == 1, 1, 2)) * at.n_lay + (lay ^ at.lay)
        inverse[atom] = -1
    geo_ref[...] = 0.5 * geo.astype(jnp.float32)
    own_basis_ref[...] = basis_ref[at.me]
    info_ref[slots] = size_ref[at.me]
    info_ref[slots + 1] = self_slot

    def row_of_pairs(v, total):
        atom = known[0, v]
        side = known[1, v]
        line = known[2, v]
        row, _, lay = at.split(atom)
        for u in range(slots):
            inverse[neighbors_ref[atom, u]] = v * 16 + u
        column_line = column_base + ((side - 1) * count * at.n_lay + line) * n_pick
        for w in range(slots):
            other = known[0, w]
            other_side = known[1, w]
            mark = inverse[other]
            o_row, _, o_lay = at.split(other)
            there = target_place(at.n_row, (o_row - row) & (at.n_row - 1), (o_lay - lay) & (at.n_lay - 1), row)
            back = target_place(at.n_row, (row - o_row) & (at.n_row - 1), (lay - o_lay) & (at.n_lay - 1), o_row)
            from_row = (other_side != 0) | (v <= w)
            from_column = (side == other_side) & (there >= 0) & ((back < 0) | (v <= w))
            chosen = ((mark >> 4) == v) & jnp.where(side == 0, from_row, from_column)
            table_ref[3 * total + 1] = v
            table_ref[3 * total + 2] = w
            table_ref[3 * total + 3] = jnp.where(side == 0, line * slots + (mark & 15), column_line + there)
            total = total + chosen.astype(jnp.int32)
        return total

    total = lax.fori_loop(0, slots, row_of_pairs, jnp.int32(0))
    table_ref[0] = (total + UNROLL - 1) // UNROLL
    for i in range(UNROLL - 1):
        for k in range(3):
            table_ref[3 * (total + i) + 1 + k] = table_ref[3 * (total - 1) + 1 + k]


def step_kernel(offsets, lengths, *refs):
    tab_ref, info_ref, basis_ref, spread_ref, sign_ref = refs[:5]
    piece_refs = refs[5 : 5 + len(offsets)]
    next_ref, coef_ref, pool, gram, own, square, sems = refs[5 + len(offsets) :]
    slots, size = sign_ref.shape[0], sign_ref.shape[1]
    copies = []
    for i, piece in enumerate(piece_refs):
        copy = pltpu.make_async_copy(piece, pool.at[pl.ds(offsets[i], lengths[i])], sems.at[i])
        copy.start()
        copies.append(copy)
    for v in range(slots):
        gram[v * size : (v + 1) * size] = jnp.zeros((size, slots * size), gram.dtype)
    rows = lax.broadcasted_iota(jnp.int32, (size, size), 0)
    lanes = lax.broadcasted_iota(jnp.int32, (size, size), 1)
    own_size = info_ref[slots]
    self_slot = info_ref[slots + 1]
    for w in range(slots):
        kept = (rows < own_size) & (lanes < info_ref[w])
        block = jnp.where(kept, sign_ref[w].astype(jnp.float32), 0.0)
        own[:, w * size : (w + 1) * size] = block.astype(own.dtype)
    for copy in copies:
        copy.wait()

    def place(i, carry):
        for k in range(UNROLL):
            entry = 3 * (i * UNROLL + k)
            p = pl.multiple_of(tab_ref[entry + 1] * size, size)
            q = pl.multiple_of(tab_ref[entry + 2] * size, size)
            block = pool[tab_ref[entry + 3]]
            gram[pl.ds(p, size), pl.ds(q, size)] = block
            gram[pl.ds(q, size), pl.ds(p, size)] = block.T
        return carry

    lax.fori_loop(0, tab_ref[0], place, 0)
    wide = 2 * size
    wide_lanes = lax.broadcasted_iota(jnp.int32, (size, wide), 1)
    wide_rows = lax.broadcasted_iota(jnp.int32, (size, wide), 0)

    def column_kept(n):
        first = info_ref[2 * n]
        second = info_ref[2 * n + 1]
        return (wide_lanes < first) | ((wide_lanes >= size) & (wide_lanes < size + second))

    for n in range(slots // 2):
        part = jnp.dot(own[...], gram[:, n * wide : (n + 1) * wide], preferred_element_type=jnp.float32)
        square[:, n * wide : (n + 1) * wide] = jnp.where(column_kept(n), part, 0.0).astype(square.dtype)
    coef = jnp.zeros((basis_ref.shape[0], LANES), jnp.float32)
    across = (((1,), (1,)), ((), ()))
    for n in range(slots // 2):
        part = jnp.dot(square[...], gram[:, n * wide : (n + 1) * wide], preferred_element_type=jnp.float32)
        cube = jnp.where(column_kept(n), part, 0.0)
        full = 1.5 * own[:, n * wide : (n + 1) * wide].astype(jnp.float32) - 0.5 * cube
        next_ref[2 * n] = full[:, :size].astype(next_ref.dtype)
        next_ref[2 * n + 1] = full[:, size:].astype(next_ref.dtype)
        shift = (self_slot - 2 * n) * size
        is_self = (self_slot >= 2 * n) & (self_slot < 2 * n + 2)
        diag = (wide_lanes == wide_rows + shift) & (wide_rows < own_size) & is_self
        dmat = 0.5 * (jnp.where(diag, 1.0, 0.0) - full)
        high = dmat.astype(jnp.bfloat16)
        low = (dmat - high.astype(jnp.float32)).astype(jnp.bfloat16)
        half = jnp.dot(basis_ref[...], high, preferred_element_type=jnp.float32) + jnp.dot(
            basis_ref[...], low, preferred_element_type=jnp.float32
        )
        half_high = half.astype(jnp.bfloat16)
        half_low = (half - half_high.astype(jnp.float32)).astype(jnp.bfloat16)
        for k in range(2):
            spread = spread_ref[2 * n + k]
            for part in (half_high, half_low):
                coef = coef + lax.dot_general(
                    part[:, k * size : (k + 1) * size], spread, across, preferred_element_type=jnp.float32
                )
    coef_ref[...] = coef[: coef_ref.shape[0]]


def profile_kernel(periods, tile_steps, *refs):
    tiles = len(tile_steps)
    geo_refs = refs[:tiles]
    plane_ref, line_ref = refs[tiles:]
    shells = plane_ref.shape[1]
    cells = plane_ref.shape[2]
    cell = lax.broadcasted_iota(jnp.int32, (cells, LANES), 0)
    grid_x = (cell // BY).astype(jnp.float32)
    grid_y = (cell % BY).astype(jnp.float32)
    grid_z = lax.broadcasted_iota(jnp.int32, (LANES, BZ), 1).astype(jnp.float32)
    lane = lax.broadcasted_iota(jnp.int32, (1, LANES), 1)
    shell = (lane % shells + 1).astype(jnp.float32)
    valid = lane < 21 * shells

    def nearest(offset, period):
        return offset - period * jnp.floor(offset * (1.0 / period) + 0.5)

    for o, (step_row, step_col) in enumerate(tile_steps):
        geo = geo_refs[o][...]
        extent = jnp.where(valid, geo[3:4], 1.0)
        inverse = (shells / extent) * (shells / extent)
        reach = jnp.where(valid, extent, -1.0)
        rate_t = inverse / (shell * shell)
        packed = jnp.concatenate([geo[2:3], reach, rate_t, inverse, jnp.zeros((4, LANES), jnp.float32)], axis=0)
        sub = packed.T
        d_x = nearest(grid_x - (geo[0:1] + float(BX * step_row)), periods[0])
        d_y = nearest(grid_y - (geo[1:2] + float(BY * step_col)), periods[1])
        inside = (jnp.abs(d_x) <= reach) & (jnp.abs(d_y) <= reach)
        squared = d_x * d_x + d_y * d_y
        d_z = nearest(grid_z - sub[:, 0:1], periods[2])
        inside_z = jnp.abs(d_z) <= sub[:, 1:2]
        squared_z = d_z * d_z
        for s in range(shells):
            part = 1.0 / ((s + 1) * (s + 1))
            rate = inverse * part + rate_t
            plane_ref[o, s] = jnp.where(inside, jnp.exp(-rate * squared), 0.0).astype(plane_ref.dtype)
            rate_z = sub[:, 3:4] * part + sub[:, 2:3]
            line_ref[o, s] = jnp.where(inside_z, jnp.exp(-rate_z * squared_z), 0.0).astype(line_ref.dtype)


def density_kernel(tiles, *refs):
    tile_refs = refs[:tiles]
    plane_ref, line_ref, out_ref, terms = refs[tiles:]
    shells = plane_ref.shape[1]
    for o in range(tiles):
        for s in range(shells):
            scaled = plane_ref[o, s].astype(jnp.float32) * tile_refs[o][s : s + 1, :]
            at = (o * shells + s) * LANES
            terms[:, at : at + LANES] = scaled.astype(terms.dtype)
    out_ref[...] = jnp.dot(terms[...], line_ref[...], preferred_element_type=jnp.float32)


def to_tiles(tile, shift, tile_steps, n_row, n_col):
    shells = 6
    span = 3 * shells
    below = from_offset(tile, "layer", -1)
    above = from_offset(tile, "layer", 1)
    merged = jnp.concatenate(
        [
            tile[:, : 4 * span],
            below[:, span : 3 * span],
            above[:, 3 * span : 4 * span],
            jnp.zeros((8, LANES - 7 * span), jnp.float32),
        ],
        axis=1,
    )
    if shift is not None:
        merged = merged + shift
    received = []
    for dr, dc in tile_steps:
        if dr == 0 and dc == 0:
            received.append(merged)
        elif dr == 0:
            received.append(from_offset(merged, "col", dc))
        elif dc == 0:
            received.append(from_offset(merged, "row", dr))
        else:
            moves = [
                (((i + dr) % n_row) * n_col + (j + dc) % n_col, i * n_col + j)
                for i in range(n_row)
                for j in range(n_col)
            ]
            received.append(lax.ppermute(merged, ("row", "col"), moves))
    return received


def local(sign_start, neighbors, atom_size, basis_proj, pair_extent, atom_x, atom_y, atom_z):
    n_row = lax.axis_size("row")
    n_col = lax.axis_size("col")
    n_lay = lax.axis_size("layer")
    assert n_lay == 4 and n_col >= 4 and (n_row == 2 or n_row >= 4)
    assert n_row & (n_row - 1) == 0 and n_col & (n_col - 1) == 0
    axes = (n_row, n_col, n_lay)
    atoms, slots = neighbors.shape
    size = sign_start.shape[2]
    shells = basis_proj.shape[1]
    steps = [0, 1] if n_row == 2 else [0, 1, -1]
    count = len(steps)
    own = sign_start[0]
    half = slots // 2

    rows, tops, ends, ups, downs = {}, {}, {}, {}, {}
    for di in range(1, count):
        rows[di, 0] = from_offset(own, "row", steps[di])
    rows[0, 2] = from_layer(own, 2)
    n_pick = column_targets(n_row)
    picked = pl.pallas_call(
        functools.partial(pick_kernel, axes),
        out_shape=jax.ShapeDtypeStruct((n_pick, size, size), own.dtype),
        in_specs=[SMEM, VMEM],
        out_specs=VMEM,
        scratch_shapes=[pltpu.SMEM((n_pick + 1,), jnp.int32)],
        name="pick_column_blocks",
    )(neighbors, own)
    ups[0, 0] = from_offset(picked, "col", 1)
    downs[0, 0] = from_offset(picked, "col", -1)
    for di in range(1, count):
        tops[di, 2] = from_layer(rows[di, 0][:half], 2)
        ends[di, 2] = from_offset(rows[0, 2][half:], "row", steps[di])
    for di in range(1, count):
        ups[di, 0] = from_offset(ups[0, 0], "row", steps[di])
    downs[0, 2] = from_layer(downs[0, 0], 2)
    for di in range(count):
        ups[di, 2] = from_layer(ups[di, 0], 2)
    for di in range(1, count):
        downs[di, 0] = from_offset(downs[0, 0], "row", steps[di])
        downs[di, 2] = from_offset(downs[0, 2], "row", steps[di])
    values, starts, widths = [], [], []

    def add(value, start, mate):
        for piece, place in ((value, start), (from_layer(value, 1), mate)):
            values.append(piece)
            starts.append(place)
            widths.append(piece.shape[0])

    column_base = count * n_lay * slots
    add(own, 0, slots)
    add(rows[0, 2], 2 * slots, 3 * slots)
    for di in range(1, count):
        base = di * n_lay * slots
        add(rows[di, 0], base, base + slots)
        add(tops[di, 2], base + 2 * slots, base + 3 * slots)
        add(ends[di, 2], base + 2 * slots + half, base + 3 * slots + half)
    for side, parts in enumerate((ups, downs)):
        for di in range(count):
            for flip in (0, 2):
                base = column_base + ((side * count + di) * n_lay + flip) * n_pick
                add(parts[di, flip], base, base + n_pick)
    n_pool = column_base + 2 * count * n_lay * n_pick

    basis = jnp.pad(basis_proj, ((0, 0), (0, 16 - shells), (0, 0)))
    pairs = slots * (slots + 1) // 2
    table, info, geo, spread, own_basis = pl.pallas_call(
        functools.partial(prepare_kernel, axes, count, n_pick),
        out_shape=(
            jax.ShapeDtypeStruct((3 * (pairs + UNROLL) + 1,), jnp.int32),
            jax.ShapeDtypeStruct((slots + 2,), jnp.int32),
            jax.ShapeDtypeStruct((8, LANES), jnp.float32),
            jax.ShapeDtypeStruct((slots, LANES, size), jnp.bfloat16),
            jax.ShapeDtypeStruct((16, size), jnp.bfloat16),
        ),
        in_specs=[SMEM] * 6 + [VMEM],
        out_specs=(SMEM, SMEM, VMEM, VMEM, VMEM),
        scratch_shapes=[pltpu.SMEM((3, slots), jnp.int32), pltpu.SMEM((atoms,), jnp.int32)],
        cost_estimate=pl.CostEstimate(flops=10_000_000, bytes_accessed=1_000_000, transcendentals=0),
        name="prepare",
    )(neighbors, pair_extent, atom_size, atom_x, atom_y, atom_z, basis)

    tile_steps = [(dr, dc) for dr in steps for dc in (0, 1, -1)]
    tiles = len(tile_steps)
    lane = jnp.arange(LANES)
    shift_z = jnp.where(lane < 12 * shells, 0.0, jnp.where(lane < 18 * shells, -float(BZ), float(BZ)))
    shift = jnp.where(jnp.arange(8)[:, None] == 2, shift_z[None, :], 0.0).astype(jnp.float32)
    geos = to_tiles(geo, shift, tile_steps, n_row, n_col)
    periods = (float(BX * n_row), float(BY * n_col), float(BZ * n_lay))
    plane, line = pl.pallas_call(
        functools.partial(profile_kernel, periods, tile_steps),
        out_shape=(
            jax.ShapeDtypeStruct((tiles, shells, BX * BY, LANES), jnp.bfloat16),
            jax.ShapeDtypeStruct((tiles, shells, LANES, BZ), jnp.bfloat16),
        ),
        in_specs=[VMEM] * tiles,
        out_specs=(VMEM, VMEM),
        compiler_params=pltpu.CompilerParams(vmem_limit_bytes=12 << 20),
        cost_estimate=pl.CostEstimate(flops=30_000_000, bytes_accessed=4_000_000, transcendentals=2_000_000),
        name="profiles",
    )(*geos)

    sign_next, coef = pl.pallas_call(
        functools.partial(step_kernel, tuple(starts), tuple(widths)),
        out_shape=(
            jax.ShapeDtypeStruct((slots, size, size), jnp.bfloat16),
            jax.ShapeDtypeStruct((8, LANES), jnp.float32),
        ),
        in_specs=[SMEM, SMEM, VMEM, VMEM, VMEM] + [ANY] * len(values),
        out_specs=(VMEM, VMEM),
        scratch_shapes=[
            pltpu.VMEM((n_pool, size, size), jnp.bfloat16),
            pltpu.VMEM((slots * size, slots * size), jnp.bfloat16),
            pltpu.VMEM((size, slots * size), jnp.bfloat16),
            pltpu.VMEM((size, slots * size), jnp.bfloat16),
            pltpu.SemaphoreType.DMA((len(values),)),
        ],
        compiler_params=pltpu.CompilerParams(vmem_limit_bytes=(10 << 20) + n_pool * size * size * 2),
        cost_estimate=pl.CostEstimate(flops=1_300_000_000, bytes_accessed=8_000_000, transcendentals=0),
        name="square_cube_coefficients",
    )(table, info, own_basis, spread, own, *values)

    received = to_tiles(coef, None, tile_steps, n_row, n_col)
    density = pl.pallas_call(
        functools.partial(density_kernel, tiles),
        out_shape=jax.ShapeDtypeStruct((BX * BY, BZ), jnp.float32),
        in_specs=[VMEM] * (tiles + 2),
        out_specs=VMEM,
        scratch_shapes=[pltpu.VMEM((BX * BY, tiles * shells * LANES), jnp.bfloat16)],
        compiler_params=pltpu.CompilerParams(vmem_limit_bytes=16 << 20),
        cost_estimate=pl.CostEstimate(flops=310_000_000, bytes_accessed=4_000_000, transcendentals=0),
        name="density",
    )(*received, plane, line.reshape(tiles * shells * LANES, BZ))
    return sign_next[None], density.reshape(BX, BY, BZ)


def solution(mesh):
    rows = P(("row", "col", "layer"), None, None, None)
    in_specs = (rows, P(), P(), P(), P(("row", "col", "layer"), None), P(), P(), P())
    out_specs = (rows, P("row", "col", "layer"))
    return jax.shard_map(local, mesh=mesh, in_specs=in_specs, out_specs=out_specs, check_vma=False)
```

```python
import functools

import jax
import jax.numpy as jnp
from jax import lax
from jax.experimental import pallas as pl
from jax.experimental.pallas import tpu as pltpu
from jax.sharding import PartitionSpec as P

BX = 16
BY = 16
BZ = 128
LANES = 128
UNROLL = 4
SHELLS = 6
SPAN = 3 * SHELLS
GEO = 16
VMEM = pl.BlockSpec(memory_space=pltpu.VMEM)
SMEM = pl.BlockSpec(memory_space=pltpu.SMEM)
ANY = pl.BlockSpec(memory_space=pl.ANY)


def from_offset(x, axis, step):
    count = lax.axis_size(axis)
    return lax.ppermute(x, axis, [((i + step) % count, i) for i in range(count)])


def from_layer(x, flip):
    count = lax.axis_size("layer")
    return lax.ppermute(x, "layer", [(i ^ flip, i) for i in range(count)])


def column_targets(n_row):
    return 5 if n_row == 2 else 7


def target_place(n_row, step_row, step_lay, row):
    same = jnp.where(step_lay < 3, step_lay, -1)
    if n_row == 2:
        lead = step_lay - row
        across = jnp.where((lead >= 0) & (lead < 2), 3 + lead, -1)
    else:
        across = 3 + step_lay
    return jnp.where(step_row == 0, same, jnp.where(step_row == 1, across, -1))


class Places:
    def __init__(self, n_row, n_col, n_lay):
        self.n_row, self.n_col, self.n_lay = n_row, n_col, n_lay
        self.lay_bits = n_lay.bit_length() - 1
        self.col_bits = n_col.bit_length() - 1
        self.row = lax.axis_index("row")
        self.col = lax.axis_index("col")
        self.lay = lax.axis_index("layer")
        self.me = (((self.row << self.col_bits) + self.col) << self.lay_bits) + self.lay

    def split(self, atom):
        return (
            atom >> (self.lay_bits + self.col_bits),
            (atom >> self.lay_bits) & (self.n_col - 1),
            atom & (self.n_lay - 1),
        )


def own_ranks(at, neighbors_ref):
    seen = [jnp.int32(0)] * at.n_lay
    listed = []
    for w in range(neighbors_ref.shape[0]):
        atom = neighbors_ref[w, at.me]
        step_lay = (atom - at.lay) & (at.n_lay - 1)
        rank = jnp.int32(0)
        for k in range(at.n_lay):
            rank = jnp.where(step_lay == k, 3 * k + seen[k], rank)
            seen[k] = seen[k] + (step_lay == k).astype(jnp.int32)
        listed.append((atom, rank))
    return listed


def pick_kernel(axes, *refs):
    neighbors_ref, extent_ref, x_ref, y_ref, z_ref, sign_ref, out_ref, geo_ref, place_ref = refs
    at = Places(*axes)
    n_pick = place_ref.shape[0] - 1
    size = sign_ref.shape[1]
    sub = lax.broadcasted_iota(jnp.int32, (GEO, LANES), 0)
    lane_pair = lax.broadcasted_iota(jnp.int32, (GEO, LANES), 1) // SHELLS
    geo = jnp.zeros((GEO, LANES), jnp.int32)
    for i in range(n_pick + 1):
        place_ref[i] = 0
    for w, (atom, rank) in enumerate(own_ranks(at, neighbors_ref)):
        row, col, lay = at.split(atom)
        step_row = (row - at.row) & (at.n_row - 1)
        step_col = (col - at.col) & (at.n_col - 1)
        step_lay = (lay - at.lay) & (at.n_lay - 1)
        place = target_place(at.n_row, step_row, step_lay, at.row)
        place_ref[jnp.where((step_col == 0) & (place >= 0), place, n_pick)] = w
        go_row = ((step_row + 1) & (at.n_row - 1)) - 1
        go_col = ((step_col + 1) & (at.n_col - 1)) - 1
        go_lay = jnp.minimum(((step_lay + 1) & (at.n_lay - 1)) - 1, 1)
        twice_x = x_ref[at.me] + x_ref[atom] + BX * go_row
        twice_y = y_ref[at.me] + y_ref[atom] + BY * go_col
        twice_z = z_ref[at.me] + z_ref[atom] + BZ * go_lay - BZ
        values = jnp.where(sub == 0, twice_x, jnp.where(sub == 1, twice_y, jnp.where(sub == 2, twice_z, extent_ref[0, w])))
        geo = jnp.where(lane_pair == rank, values, geo)
    geo = geo.astype(jnp.float32).astype(geo_ref.dtype)
    geo_ref[...] = geo
    out_ref[n_pick * size : n_pick * size + GEO] = geo
    for i in range(n_pick):
        out_ref[i * size : (i + 1) * size] = sign_ref[place_ref[i]]


def prepare_kernel(axes, count, late_from, *refs):
    neighbors_ref, size_ref, layout_ref, basis_ref = refs[:4]
    early_ref, late_ref, info_ref, spread_ref, own_basis_ref, known, inverse = refs[4:]
    at = Places(*axes)
    slots = neighbors_ref.shape[0]
    atoms = neighbors_ref.shape[1]
    bits = atoms.bit_length() - 1
    lines = count * at.n_lay

    def hot(rows, atom, first):
        sub = lax.broadcasted_iota(jnp.int32, (rows, SHELLS * atoms), 0)
        lane = lax.broadcasted_iota(jnp.int32, (rows, SHELLS * atoms), 1)
        return ((lane & (atoms - 1)) == atom) & (sub == first + (lane >> bits))

    def rows_of(chosen):
        picked = jnp.where(chosen, 1.0, 0.0).astype(jnp.bfloat16)
        return jnp.dot(picked, basis_ref[...], preferred_element_type=jnp.float32).astype(jnp.bfloat16)

    self_slot = jnp.int32(0)
    for w, (atom, rank) in enumerate(own_ranks(at, neighbors_ref)):
        row, col, lay = at.split(atom)
        step_row = (row - at.row) & (at.n_row - 1)
        step_col = (col - at.col) & (at.n_col - 1)
        self_slot = jnp.where(atom == at.me, w, self_slot)
        info_ref[w] = size_ref[atom]
        spread_ref[w] = rows_of(hot(LANES, atom, rank * SHELLS))
        flip = lay ^ at.lay
        known[0, w] = atom
        known[1, w] = jnp.where(step_col == 0, 0, jnp.where(step_col == 1, 1, 2))
        known[2, w] = jnp.where(step_row == 0, 0, jnp.where(step_row == 1, 1, 2)) * at.n_lay + flip
        known[3, w] = jnp.where((step_row != 0) & (flip == 3), 16 + w, w)
        inverse[atom] = -1
    own_basis_ref[...] = rows_of(hot(16, at.me, 0))
    info_ref[slots] = size_ref[at.me]
    info_ref[slots + 1] = self_slot

    def row_of_pairs(v, totals):
        early, late = totals
        atom = known[0, v]
        side = known[1, v]
        line = known[2, v]
        turn = known[3, v]
        row, _, lay = at.split(atom)
        for u in range(slots):
            inverse[neighbors_ref[u, atom]] = v * 16 + u
        top = layout_ref[line]
        end = layout_ref[lines + line]
        beside = layout_ref[(side + 1) * lines + line]
        half = slots // 2
        for w in range(slots):
            other = known[0, w]
            other_side = known[1, w]
            mark = inverse[other]
            slot = mark & 15
            o_row, _, o_lay = at.split(other)
            there = target_place(at.n_row, (o_row - row) & (at.n_row - 1), (o_lay - lay) & (at.n_lay - 1), row)
            back = target_place(at.n_row, (row - o_row) & (at.n_row - 1), (lay - o_lay) & (at.n_lay - 1), o_row)
            from_row = (other_side != 0) | (turn <= known[3, w])
            from_column = (side == other_side) & (there >= 0) & ((back < 0) | (v <= w))
            chosen = ((mark >> 4) == v) & jnp.where(side == 0, from_row, from_column)
            in_row = jnp.where(slot < half, top + slot * LANES, end + (slot - half) * LANES)
            where = jnp.where(side == 0, in_row, beside + there * LANES)
            is_late = where >= late_from
            for ref, total in ((early_ref, early), (late_ref, late)):
                ref[3 * total + 1] = v
                ref[3 * total + 2] = w
                ref[3 * total + 3] = where
            late_ref[3 * late + 3] = where - late_from
            early = early + (chosen & ~is_late).astype(jnp.int32)
            late = late + (chosen & is_late).astype(jnp.int32)
        return early, late

    totals = lax.fori_loop(0, slots, row_of_pairs, (jnp.int32(0), jnp.int32(0)))
    for ref, total in zip((early_ref, late_ref), totals):
        ref[0] = (total + UNROLL - 1) // UNROLL
        last = 3 * jnp.maximum(total - 1, 0) + 1
        for i in range(UNROLL - 1):
            for k in range(3):
                ref[3 * (total + i) + 1 + k] = ref[last + k]


def pack_kernel(moves, inputs, outputs, *refs):
    sems = refs[-1]
    copies = []
    for k, (source, start, rows, target, place) in enumerate(moves):
        copy = pltpu.make_async_copy(
            refs[source].at[pl.ds(start, rows)], refs[inputs + target].at[pl.ds(place, rows)], sems.at[k]
        )
        copy.start()
        copies.append(copy)
    for copy in copies:
        copy.wait()


def pack(values, plans, extra, name):
    moves, shapes = [], []
    for target, plan in enumerate(plans):
        place = 0
        for source, start, rows in plan:
            moves.append((source, start, rows, target, place))
            place += rows
        shapes.append(jax.ShapeDtypeStruct((place, LANES), values[0].dtype))
    inputs = len(values) + len(extra)
    return pl.pallas_call(
        functools.partial(pack_kernel, tuple(moves), inputs, len(plans)),
        out_shape=tuple(shapes),
        in_specs=[ANY] * inputs,
        out_specs=tuple([ANY] * len(plans)),
        scratch_shapes=[pltpu.SemaphoreType.DMA((len(moves),))],
        compiler_params=pltpu.CompilerParams(vmem_limit_bytes=1 << 20),
        cost_estimate=pl.CostEstimate(flops=0, bytes_accessed=3_000_000, transcendentals=0),
        name=name,
    )(*values, *extra)


def fill(piece_refs, pool, sems):
    copies = []
    place = 0
    for i, piece in enumerate(piece_refs):
        rows = piece.shape[0]
        copy = pltpu.make_async_copy(piece, pool.at[pl.ds(place, rows)], sems.at[i])
        copy.start()
        copies.append(copy)
        place += rows
    return copies


def place_pairs(table_ref, pool, gram, size):
    def place(i, carry):
        for k in range(UNROLL):
            entry = 3 * (i * UNROLL + k)
            p = pl.multiple_of(table_ref[entry + 1] * size, size)
            q = pl.multiple_of(table_ref[entry + 2] * size, size)
            block = pool[pl.ds(pl.multiple_of(table_ref[entry + 3], 16), size)]
            gram[pl.ds(p, size), pl.ds(q, size)] = block
            gram[pl.ds(q, size), pl.ds(p, size)] = block.T
        return carry

    lax.fori_loop(0, table_ref[0], place, 0)


def gram_kernel(pieces, *refs):
    table_ref = refs[0]
    piece_refs = refs[1 : 1 + pieces]
    gram, pool, sems = refs[-3:]
    size = LANES
    copies = fill(piece_refs, pool, sems)
    for v in range(gram.shape[0] // size):
        gram[v * size : (v + 1) * size] = jnp.zeros((size, gram.shape[1]), gram.dtype)
    for copy in copies:
        copy.wait()
    place_pairs(table_ref, pool, gram, size)


def step_kernel(pieces, *refs):
    table_ref, info_ref, basis_ref, spread_ref, sign_ref, early_ref = refs[:6]
    piece_refs = refs[6 : 6 + pieces]
    next_ref, coef_ref, pool, gram, own, square, sems = refs[6 + pieces :]
    slots, size = sign_ref.shape[0], sign_ref.shape[1]
    copies = fill(piece_refs, pool, sems)
    for v in range(slots):
        gram[v * size : (v + 1) * size] = early_ref[v * size : (v + 1) * size]
    rows = lax.broadcasted_iota(jnp.int32, (size, size), 0)
    lanes = lax.broadcasted_iota(jnp.int32, (size, size), 1)
    own_size = info_ref[slots]
    self_slot = info_ref[slots + 1]
    for w in range(slots):
        kept = (rows < own_size) & (lanes < info_ref[w])
        block = jnp.where(kept, sign_ref[w].astype(jnp.float32), 0.0)
        own[:, w * size : (w + 1) * size] = block.astype(own.dtype)
    for copy in copies:
        copy.wait()
    place_pairs(table_ref, pool, gram, size)
    wide = 2 * size
    wide_lanes = lax.broadcasted_iota(jnp.int32, (size, wide), 1)
    wide_rows = lax.broadcasted_iota(jnp.int32, (size, wide), 0)

    def column_kept(n):
        first = info_ref[2 * n]
        second = info_ref[2 * n + 1]
        return (wide_lanes < first) | ((wide_lanes >= size) & (wide_lanes < size + second))

    for n in range(slots // 2):
        part = jnp.dot(own[...], gram[:, n * wide : (n + 1) * wide], preferred_element_type=jnp.float32)
        square[:, n * wide : (n + 1) * wide] = jnp.where(column_kept(n), part, 0.0).astype(square.dtype)
    coef = jnp.zeros((basis_ref.shape[0], LANES), jnp.float32)
    across = (((1,), (1,)), ((), ()))
    for n in range(slots // 2):
        part = jnp.dot(square[...], gram[:, n * wide : (n + 1) * wide], preferred_element_type=jnp.float32)
        cube = jnp.where(column_kept(n), part, 0.0)
        full = 1.5 * own[:, n * wide : (n + 1) * wide].astype(jnp.float32) - 0.5 * cube
        next_ref[2 * n] = full[:, :size].astype(next_ref.dtype)
        next_ref[2 * n + 1] = full[:, size:].astype(next_ref.dtype)
        shift = (self_slot - 2 * n) * size
        is_self = (self_slot >= 2 * n) & (self_slot < 2 * n + 2)
        diag = (wide_lanes == wide_rows + shift) & (wide_rows < own_size) & is_self
        dmat = 0.5 * (jnp.where(diag, 1.0, 0.0) - full)
        high = dmat.astype(jnp.bfloat16)
        low = (dmat - high.astype(jnp.float32)).astype(jnp.bfloat16)
        half = jnp.dot(basis_ref[...], high, preferred_element_type=jnp.float32) + jnp.dot(
            basis_ref[...], low, preferred_element_type=jnp.float32
        )
        half_high = half.astype(jnp.bfloat16)
        half_low = (half - half_high.astype(jnp.float32)).astype(jnp.bfloat16)
        for k in range(2):
            spread = spread_ref[2 * n + k]
            for part in (half_high, half_low):
                coef = coef + lax.dot_general(
                    part[:, k * size : (k + 1) * size], spread, across, preferred_element_type=jnp.float32
                )
    coef_ref[...] = coef[: coef_ref.shape[0]]


def profile_kernel(periods, steps, sources, inputs, *refs):
    plane_ref, line_ref, geos, sems = refs[inputs:]
    odd = (lax.axis_index("layer") & 1) == 1
    copies = []
    for o, source in enumerate(sources):
        for k, (buffer, start) in enumerate(source):
            copy = pltpu.make_async_copy(refs[buffer].at[pl.ds(start, GEO)], geos.at[3 * o + k], sems.at[3 * o + k])
            copy.start()
            copies.append(copy)
    cells = plane_ref.shape[2]
    cell = lax.broadcasted_iota(jnp.int32, (cells, LANES), 0)
    grid_x = (cell // BY).astype(jnp.float32)
    grid_y = (cell % BY).astype(jnp.float32)
    grid_z = lax.broadcasted_iota(jnp.int32, (LANES, BZ), 1).astype(jnp.float32)
    lane = lax.broadcasted_iota(jnp.int32, (1, LANES), 1)
    shell = (lane % SHELLS + 1).astype(jnp.float32)
    valid = lane < 7 * SPAN
    from_own = lane < 4 * SPAN
    from_below = lane < 6 * SPAN
    lift = jnp.where(from_own, 0.0, jnp.where(from_below, -float(BZ), float(BZ))) + 0.5 * BZ

    def nearest(offset, period):
        return offset - period * jnp.floor(offset * (1.0 / period) + 0.5)

    for copy in copies:
        copy.wait()
    for o, (step_row, step_col) in enumerate(steps):
        own, first, third = (geos[3 * o + k].astype(jnp.float32) for k in range(3))
        below = jnp.where(odd, first, third)
        above = jnp.where(odd, third, first)
        moved = jnp.where(from_below, pltpu.roll(below, 3 * SPAN, axis=1), pltpu.roll(above, 3 * SPAN, axis=1))
        geo = jnp.where(from_own, own, moved)
        extent = jnp.where(valid, geo[3:4], 1.0)
        inverse = (SHELLS / extent) * (SHELLS / extent)
        reach = jnp.where(valid, extent, -1.0)
        rate_t = inverse / (shell * shell)
        packed = jnp.concatenate(
            [0.5 * geo[2:3] + lift, reach, rate_t, inverse, jnp.zeros((4, LANES), jnp.float32)], axis=0
        )
        sub = packed.T
        d_x = nearest(grid_x - (0.5 * geo[0:1] + float(BX * step_row)), periods[0])
        d_y = nearest(grid_y - (0.5 * geo[1:2] + float(BY * step_col)), periods[1])
        inside = (jnp.abs(d_x) <= reach) & (jnp.abs(d_y) <= reach)
        squared = d_x * d_x + d_y * d_y
        d_z = nearest(grid_z - sub[:, 0:1], periods[2])
        inside_z = jnp.abs(d_z) <= sub[:, 1:2]
        squared_z = d_z * d_z
        for s in range(SHELLS):
            part = 1.0 / ((s + 1) * (s + 1))
            rate = inverse * part + rate_t
            plane_ref[o, s] = jnp.where(inside, jnp.exp(-rate * squared), 0.0).astype(plane_ref.dtype)
            rate_z = sub[:, 3:4] * part + sub[:, 2:3]
            line_ref[o, s] = jnp.where(inside_z, jnp.exp(-rate_z * squared_z), 0.0).astype(line_ref.dtype)


def density_kernel(column_steps, *refs):
    coef_refs = refs[:column_steps]
    plane_ref, line_ref, out_ref, terms = refs[column_steps:]
    for o in range(plane_ref.shape[0]):
        coef = coef_refs[o % column_steps]
        first = 8 * (o // column_steps)
        for s in range(SHELLS):
            scaled = plane_ref[o, s].astype(jnp.float32) * coef[first + s : first + s + 1, :]
            at = (o * SHELLS + s) * LANES
            terms[:, at : at + LANES] = scaled.astype(terms.dtype)
    out_ref[...] = jnp.dot(terms[...], line_ref[...], preferred_element_type=jnp.float32)


def local(sign_start, neighbors, atom_size, basis_proj, pair_extent, atom_x, atom_y, atom_z):
    n_row = lax.axis_size("row")
    n_col = lax.axis_size("col")
    n_lay = lax.axis_size("layer")
    assert n_lay == 4 and n_col >= 4 and (n_row == 2 or n_row >= 4)
    assert n_row & (n_row - 1) == 0 and n_col & (n_col - 1) == 0
    axes = (n_row, n_col, n_lay)
    atoms, slots = neighbors.shape
    size = sign_start.shape[2]
    steps = [0, 1] if n_row == 2 else [0, 1, -1]
    count = len(steps)
    others = range(1, count)
    own = sign_start[0]
    flat = own.reshape(slots * size, size)
    listings = neighbors.T
    full = slots * size
    half = full // 2
    n_pick = column_targets(n_row)
    part = n_pick * size + GEO

    def on_row(value, di):
        return from_offset(value, "row", steps[di])

    x_row = {di: on_row(flat, di) for di in others}
    y_row = from_layer(flat, 2)
    m_row = from_layer(flat, 1)
    picked, geo = pl.pallas_call(
        functools.partial(pick_kernel, axes),
        out_shape=(
            jax.ShapeDtypeStruct((part, size), own.dtype),
            jax.ShapeDtypeStruct((GEO, LANES), own.dtype),
        ),
        in_specs=[SMEM] * 5 + [VMEM],
        out_specs=(VMEM, VMEM),
        scratch_shapes=[pltpu.SMEM((n_pick + 1,), jnp.int32)],
        compiler_params=pltpu.CompilerParams(vmem_limit_bytes=2 << 20),
        name="pick_column_blocks",
    )(listings, pair_extent, atom_x, atom_y, atom_z, own)
    up = from_offset(picked, "col", 1)
    down = from_offset(picked, "col", -1)

    at = {}
    buffers = {}

    def note(name, value, contents):
        buffers[name] = value
        start = 0
        for what, rows in contents:
            if what is not None:
                at[what] = (name, start)
            start += rows

    def row_of(di, flip):
        return [(("top", di, flip), half), (("end", di, flip), half)]

    def side_of(kind, di, flip):
        return [((kind, di, flip), part - GEO), ((kind + " geo", di, flip), GEO)]

    note("own", flat, row_of(0, 0))
    note("mate", m_row, row_of(0, 1))
    note("far", y_row, row_of(0, 2))
    note("up", up, side_of("up", 0, 0))
    note("down", down, side_of("down", 0, 0))
    note("geo", geo, [(("geo", 0, 0), GEO)])
    for di in others:
        note(("x", di), x_row[di], row_of(di, 0))

    names = ["up", "down", "geo", "far"] + [("x", di) for di in others]
    place = {name: i for i, name in enumerate(names)}
    xs = [place["x", di] for di in others]
    plans = [
        [(place["far"], half, half), (0, 0, part), (2, 0, GEO)],
        [(x, 0, half) for x in xs] + [(1, 0, part), (2, 0, GEO)],
        [(x, 0, full) for x in xs] + [(place["far"], 0, full), (0, 0, part), (1, 0, part), (2, 0, GEO)],
    ]

    early_order = ["own", "mate", "far", "up", "down", "geo"] + [("x", di) for di in others]
    early_order += [("two x", di) for di in others] + ["two y", "two m"]
    late_order = [("three x", di) for di in others] + ["three y", "three m"]
    late_order += [("four x", di) for di in others] + ["four y"]

    contents = {}
    for di in others:
        contents["two x", di] = [(("end", di, 2), half)] + side_of("up", di, 0) + [(("geo", di, 0), GEO)]
    contents["two y"] = [(("top", di, 2), half) for di in others] + side_of("down", 0, 2) + [(("geo", 0, 2), GEO)]
    contents["two m"] = sum([row_of(di, 1) for di in others], []) + row_of(0, 3)
    contents["two m"] += side_of("up", 0, 1) + side_of("down", 0, 1) + [(("geo", 0, 1), GEO)]
    for di in others:
        contents["three x", di] = side_of("down", di, 0) + side_of("down", di, 2) + [(("geo", di, 2), GEO)]
    contents["three y"] = side_of("up", 0, 2) + sum([side_of("up", di, 2) for di in others], [])
    contents["three m"] = []
    for di in others:
        contents["three m"] += [(("end", di, 3), half)] + side_of("up", di, 1) + [(("geo", di, 1), GEO)]
    contents["three m"] += [(("top", di, 3), half) for di in others] + side_of("down", 0, 3) + [(("geo", 0, 3), GEO)]
    for di in others:
        contents["four x", di] = side_of("down", di, 1) + side_of("down", di, 3) + [(("geo", di, 3), GEO)]
    contents["four y"] = side_of("up", 0, 3) + sum([side_of("up", di, 3) for di in others], [])
    lengths = {name: sum(rows for _, rows in content) for name, content in contents.items()}
    for name in early_order:
        if name in buffers:
            lengths[name] = buffers[name].shape[0]
    base = {}
    total = 0
    for name in early_order + late_order:
        base[name] = total
        total += lengths[name]
        if name == early_order[-1]:
            late_from = total
    located = dict(at)
    for name, content in contents.items():
        start = 0
        for what, rows in content:
            located[what] = (name, start)
            start += rows
    layout = [
        base[located[kind, di, flip][0]] + located[kind, di, flip][1]
        for kind in ("top", "end", "up", "down")
        for di in range(count)
        for flip in range(n_lay)
    ]
    pairs = slots * (slots + 1) // 2
    entries = 3 * (pairs + UNROLL) + 1
    early_table, late_table, info, spread, own_basis = pl.pallas_call(
        functools.partial(prepare_kernel, axes, count, late_from),
        out_shape=(
            jax.ShapeDtypeStruct((entries,), jnp.int32),
            jax.ShapeDtypeStruct((entries,), jnp.int32),
            jax.ShapeDtypeStruct((slots + 2,), jnp.int32),
            jax.ShapeDtypeStruct((slots, LANES, size), jnp.bfloat16),
            jax.ShapeDtypeStruct((16, size), jnp.bfloat16),
        ),
        in_specs=[SMEM] * 3 + [VMEM],
        out_specs=(SMEM, SMEM, SMEM, VMEM, VMEM),
        scratch_shapes=[pltpu.SMEM((4, slots), jnp.int32), pltpu.SMEM((atoms,), jnp.int32)],
        compiler_params=pltpu.CompilerParams(vmem_limit_bytes=(2 << 20) + atoms * 16384),
        cost_estimate=pl.CostEstimate(flops=1_000_000_000, bytes_accessed=8_000_000, transcendentals=0),
        name="prepare",
    )(
        listings,
        atom_size,
        jnp.array(layout, dtype=jnp.int32),
        basis_proj.transpose(1, 0, 2).reshape(SHELLS * atoms, size),
    )

    two_x, two_y, two_m = pack([buffers[name] for name in names], plans, [own_basis], "pack_two")
    for di in others:
        note(("two x", di), on_row(two_x, di), contents["two x", di])
    note("two y", from_layer(two_y, 2), contents["two y"])
    note("two m", from_layer(two_m, 1), contents["two m"])

    names = ["up", "down", "two y"] + [("two x", di) for di in others]
    place = {name: i for i, name in enumerate(names)}
    y_down = at["down", 0, 2][1]
    x_up = at["up", 1, 0][1]
    xs = [place["two x", di] for di in others]
    plans = [
        [(1, 0, part), (2, y_down, part + GEO)],
        [(0, 0, part)] + [(x, x_up, part) for x in xs],
        [(x, 0, lengths["two x", 1]) for x in xs] + [(2, 0, lengths["two y"])],
    ]
    three_x, three_y, three_m = pack([buffers[name] for name in names], plans, [], "pack_three")
    for di in others:
        note(("three x", di), on_row(three_x, di), contents["three x", di])
    note("three y", from_layer(three_y, 2), contents["three y"])
    note("three m", from_layer(three_m, 1), contents["three m"])

    early_values = [buffers[name] for name in early_order]
    gram = pl.pallas_call(
        functools.partial(gram_kernel, len(early_values)),
        out_shape=jax.ShapeDtypeStruct((full, full), jnp.bfloat16),
        in_specs=[SMEM] + [ANY] * (len(early_values) + 1),
        out_specs=VMEM,
        scratch_shapes=[
            pltpu.VMEM((late_from, LANES), jnp.bfloat16),
            pltpu.SemaphoreType.DMA((len(early_values),)),
        ],
        compiler_params=pltpu.CompilerParams(vmem_limit_bytes=(6 << 20) + late_from * LANES * 2),
        cost_estimate=pl.CostEstimate(flops=1_000_000_000, bytes_accessed=20_000_000, transcendentals=0),
        name="gram_early",
    )(early_table, *early_values, three_x)

    for di in others:
        note(("four x", di), from_layer(buffers["three x", di], 1), contents["four x", di])
    note("four y", from_layer(buffers["three y"], 1), contents["four y"])

    late_values = [buffers[name] for name in late_order]
    sign_next, coef = pl.pallas_call(
        functools.partial(step_kernel, len(late_values)),
        out_shape=(
            jax.ShapeDtypeStruct((slots, size, size), jnp.bfloat16),
            jax.ShapeDtypeStruct((8, LANES), jnp.float32),
        ),
        in_specs=[SMEM, SMEM, VMEM, VMEM, VMEM, VMEM] + [ANY] * len(late_values),
        out_specs=(VMEM, VMEM),
        scratch_shapes=[
            pltpu.VMEM((total - late_from, LANES), jnp.bfloat16),
            pltpu.VMEM((full, full), jnp.bfloat16),
            pltpu.VMEM((size, full), jnp.bfloat16),
            pltpu.VMEM((size, full), jnp.bfloat16),
            pltpu.SemaphoreType.DMA((len(late_values),)),
        ],
        compiler_params=pltpu.CompilerParams(vmem_limit_bytes=(15 << 20) + (total - late_from) * LANES * 2),
        cost_estimate=pl.CostEstimate(flops=1_300_000_000, bytes_accessed=8_000_000, transcendentals=0),
        name="square_cube_coefficients",
    )(late_table, info, own_basis, spread, own, gram, *late_values)

    below = from_offset(coef, "layer", -1)
    above = from_offset(coef, "layer", 1)
    merged = jnp.concatenate(
        [
            coef[:, : 4 * SPAN],
            below[:, SPAN : 3 * SPAN],
            above[:, 3 * SPAN : 4 * SPAN],
            jnp.zeros((8, LANES - 7 * SPAN), jnp.float32),
        ],
        axis=1,
    )
    stacked = jnp.concatenate([merged] + [on_row(merged, di) for di in others], axis=0)
    column_steps = (0, 1, -1)
    received = [stacked] + [from_offset(stacked, "col", dc) for dc in column_steps[1:]]

    tile_steps = [(dr, dc) for dr in steps for dc in column_steps]
    tiles = len(tile_steps)
    used, sources = [], []
    for di in range(count):
        for kind in ("geo", "up geo", "down geo"):
            source = []
            for flip in (0, 1, 3):
                name, start = at[kind, di, flip]
                if name not in used:
                    used.append(name)
                source.append((used.index(name), start))
            sources.append(tuple(source))
    periods = (float(BX * n_row), float(BY * n_col), float(BZ * n_lay))
    plane, line = pl.pallas_call(
        functools.partial(profile_kernel, periods, tile_steps, tuple(sources), len(used)),
        out_shape=(
            jax.ShapeDtypeStruct((tiles, SHELLS, BX * BY, LANES), jnp.bfloat16),
            jax.ShapeDtypeStruct((tiles, SHELLS, LANES, BZ), jnp.bfloat16),
        ),
        in_specs=[ANY] * len(used),
        out_specs=(VMEM, VMEM),
        scratch_shapes=[
            pltpu.VMEM((3 * tiles, GEO, LANES), jnp.bfloat16),
            pltpu.SemaphoreType.DMA((3 * tiles,)),
        ],
        compiler_params=pltpu.CompilerParams(vmem_limit_bytes=10 << 20),
        cost_estimate=pl.CostEstimate(flops=30_000_000, bytes_accessed=4_000_000, transcendentals=2_000_000),
        name="profiles",
    )(*[buffers[name] for name in used])

    density = pl.pallas_call(
        functools.partial(density_kernel, len(column_steps)),
        out_shape=jax.ShapeDtypeStruct((BX * BY, BZ), jnp.float32),
        in_specs=[VMEM] * (len(column_steps) + 2),
        out_specs=VMEM,
        scratch_shapes=[pltpu.VMEM((BX * BY, tiles * SHELLS * LANES), jnp.bfloat16)],
        compiler_params=pltpu.CompilerParams(vmem_limit_bytes=16 << 20),
        cost_estimate=pl.CostEstimate(flops=310_000_000, bytes_accessed=4_000_000, transcendentals=0),
        name="density",
    )(*received, plane, line.reshape(tiles * SHELLS * LANES, BZ))
    return sign_next[None], density.reshape(BX, BY, BZ)


def solution(mesh):
    rows = P(("row", "col", "layer"), None, None, None)
    in_specs = (rows, P(), P(), P(), P(("row", "col", "layer"), None), P(), P(), P())
    out_specs = (rows, P("row", "col", "layer"))
    return jax.shard_map(local, mesh=mesh, in_specs=in_specs, out_specs=out_specs, check_vma=False)
```

```python
import functools

import jax
import jax.numpy as jnp
from jax import lax
from jax.experimental import pallas as pl
from jax.experimental.pallas import tpu as pltpu
from jax.sharding import PartitionSpec as P

BX = 16
BY = 16
BZ = 128
LANES = 128
UNROLL = 4
SHELLS = 6
SPAN = 3 * SHELLS
GEO = 16
VMEM = pl.BlockSpec(memory_space=pltpu.VMEM)
SMEM = pl.BlockSpec(memory_space=pltpu.SMEM)
ANY = pl.BlockSpec(memory_space=pl.ANY)
HBM = pl.BlockSpec(memory_space=pltpu.HBM)


def from_offset(x, axis, step):
    count = lax.axis_size(axis)
    return lax.ppermute(x, axis, [((i + step) % count, i) for i in range(count)])


def from_layer(x, flip):
    count = lax.axis_size("layer")
    return lax.ppermute(x, "layer", [(i ^ flip, i) for i in range(count)])


def column_targets(n_row):
    return 5 if n_row == 2 else 7


def target_place(n_row, step_row, step_lay, row):
    same = jnp.where(step_lay < 3, step_lay, -1)
    if n_row == 2:
        lead = step_lay - row
        across = jnp.where((lead >= 0) & (lead < 2), 3 + lead, -1)
    else:
        across = 3 + step_lay
    return jnp.where(step_row == 0, same, jnp.where(step_row == 1, across, -1))


class Places:
    def __init__(self, n_row, n_col, n_lay):
        self.n_row, self.n_col, self.n_lay = n_row, n_col, n_lay
        self.lay_bits = n_lay.bit_length() - 1
        self.col_bits = n_col.bit_length() - 1
        self.row = lax.axis_index("row")
        self.col = lax.axis_index("col")
        self.lay = lax.axis_index("layer")
        self.me = (((self.row << self.col_bits) + self.col) << self.lay_bits) + self.lay

    def split(self, atom):
        return (
            atom >> (self.lay_bits + self.col_bits),
            (atom >> self.lay_bits) & (self.n_col - 1),
            atom & (self.n_lay - 1),
        )


def own_ranks(at, ints_ref):
    seen = [jnp.int32(0)] * at.n_lay
    listed = []
    for w in range(ints_ref.shape[0] - 5):
        atom = ints_ref[w, at.me]
        step_lay = (atom - at.lay) & (at.n_lay - 1)
        rank = jnp.int32(0)
        for k in range(at.n_lay):
            rank = jnp.where(step_lay == k, 3 * k + seen[k], rank)
            seen[k] = seen[k] + (step_lay == k).astype(jnp.int32)
        listed.append((atom, rank))
    return listed


def pick_kernel(axes, ints_ref, sign_ref, out_ref, geo_ref, place_ref, sems):
    at = Places(*axes)
    slots = sign_ref.shape[0]
    n_pick = place_ref.shape[0] - 1
    size = sign_ref.shape[1]
    for i in range(n_pick + 1):
        place_ref[i] = 0
    ranks = own_ranks(at, ints_ref)
    for w, (atom, _) in enumerate(ranks):
        row, col, lay = at.split(atom)
        place = target_place(at.n_row, (row - at.row) & (at.n_row - 1), (lay - at.lay) & (at.n_lay - 1), at.row)
        place_ref[jnp.where((col == at.col) & (place >= 0), place, n_pick)] = w
    copies = []
    for i in range(n_pick):
        copy = pltpu.make_async_copy(sign_ref.at[place_ref[i]], out_ref.at[pl.ds(i * size, size)], sems.at[i])
        copy.start()
        copies.append(copy)
    sub = lax.broadcasted_iota(jnp.int32, (GEO, LANES), 0)
    lane_pair = lax.broadcasted_iota(jnp.int32, (GEO, LANES), 1) // SHELLS
    geo = jnp.zeros((GEO, LANES), jnp.int32)
    for w, (atom, rank) in enumerate(ranks):
        row, col, lay = at.split(atom)
        go_row = ((row - at.row + 1) & (at.n_row - 1)) - 1
        go_col = ((col - at.col + 1) & (at.n_col - 1)) - 1
        go_lay = jnp.minimum(((lay - at.lay + 1) & (at.n_lay - 1)) - 1, 1)
        twice_x = ints_ref[slots + 1, at.me] + ints_ref[slots + 1, atom] + BX * go_row
        twice_y = ints_ref[slots + 2, at.me] + ints_ref[slots + 2, atom] + BY * go_col
        twice_z = ints_ref[slots + 3, at.me] + ints_ref[slots + 3, atom] + BZ * go_lay - BZ
        extent = ints_ref[slots + 4, w]
        values = jnp.where(sub == 0, twice_x, jnp.where(sub == 1, twice_y, jnp.where(sub == 2, twice_z, extent)))
        geo = jnp.where(lane_pair == rank, values, geo)
    geo = geo.astype(jnp.float32).astype(geo_ref.dtype)
    geo_ref[...] = geo
    out_ref[n_pick * size : n_pick * size + GEO] = geo
    for copy in copies:
        copy.wait()


def prepare_kernel(axes, count, layout, late_from, *refs):
    ints_ref, basis_ref = refs[:2]
    early_ref, late_ref, info_ref, spread_ref, own_basis_ref, known, inverse, layout_ref = refs[-8:]
    at = Places(*axes)
    slots = ints_ref.shape[0] - 5
    atoms = ints_ref.shape[1]
    for i, value in enumerate(layout):
        layout_ref[i] = value
    bits = atoms.bit_length() - 1
    lines = count * at.n_lay

    def hot(rows, atom, first):
        sub = lax.broadcasted_iota(jnp.int32, (rows, SHELLS * atoms), 0)
        lane = lax.broadcasted_iota(jnp.int32, (rows, SHELLS * atoms), 1)
        return ((lane & (atoms - 1)) == atom) & (sub == first + (lane >> bits))

    def rows_of(chosen):
        picked = jnp.where(chosen, 1.0, 0.0).astype(jnp.bfloat16)
        return jnp.dot(picked, basis_ref[...], preferred_element_type=jnp.float32).astype(jnp.bfloat16)

    self_slot = jnp.int32(0)
    for w, (atom, rank) in enumerate(own_ranks(at, ints_ref)):
        row, col, lay = at.split(atom)
        step_row = (row - at.row) & (at.n_row - 1)
        step_col = (col - at.col) & (at.n_col - 1)
        self_slot = jnp.where(atom == at.me, w, self_slot)
        info_ref[w] = ints_ref[slots, atom]
        spread_ref[w] = rows_of(hot(LANES, atom, rank * SHELLS))
        flip = lay ^ at.lay
        known[0, w] = atom
        known[1, w] = jnp.where(step_col == 0, 0, jnp.where(step_col == 1, 1, 2))
        known[2, w] = jnp.where(step_row == 0, 0, jnp.where(step_row == 1, 1, 2)) * at.n_lay + flip
        known[3, w] = jnp.where((step_row != 0) & (flip == 3), 16 + w, w)
        inverse[atom] = -1
    own_basis_ref[...] = rows_of(hot(16, at.me, 0))
    info_ref[slots] = ints_ref[slots, at.me]
    info_ref[slots + 1] = self_slot

    def row_of_pairs(v, totals):
        early, late = totals
        atom = known[0, v]
        side = known[1, v]
        line = known[2, v]
        turn = known[3, v]
        row, _, lay = at.split(atom)
        for u in range(slots):
            inverse[ints_ref[u, atom]] = v * 16 + u
        top = layout_ref[line]
        end = layout_ref[lines + line]
        beside = layout_ref[(side + 1) * lines + line]
        half = slots // 2
        for w in range(slots):
            other = known[0, w]
            other_side = known[1, w]
            mark = inverse[other]
            slot = mark & 15
            o_row, _, o_lay = at.split(other)
            there = target_place(at.n_row, (o_row - row) & (at.n_row - 1), (o_lay - lay) & (at.n_lay - 1), row)
            back = target_place(at.n_row, (row - o_row) & (at.n_row - 1), (lay - o_lay) & (at.n_lay - 1), o_row)
            from_row = (other_side != 0) | (turn <= known[3, w])
            from_column = (side == other_side) & (there >= 0) & ((back < 0) | (v <= w))
            chosen = ((mark >> 4) == v) & jnp.where(side == 0, from_row, from_column)
            in_row = jnp.where(slot < half, top + slot * LANES, end + (slot - half) * LANES)
            where = jnp.where(side == 0, in_row, beside + there * LANES)
            is_late = where >= late_from
            for ref, total in ((early_ref, early), (late_ref, late)):
                ref[3 * total + 1] = v
                ref[3 * total + 2] = w
                ref[3 * total + 3] = where
            late_ref[3 * late + 3] = where - late_from
            early = early + (chosen & ~is_late).astype(jnp.int32)
            late = late + (chosen & is_late).astype(jnp.int32)
        return early, late

    totals = lax.fori_loop(0, slots, row_of_pairs, (jnp.int32(0), jnp.int32(0)))
    for ref, total in zip((early_ref, late_ref), totals):
        ref[0] = (total + UNROLL - 1) // UNROLL
        last = 3 * jnp.maximum(total - 1, 0) + 1
        for i in range(UNROLL - 1):
            for k in range(3):
                ref[3 * (total + i) + 1 + k] = ref[last + k]


def pack_kernel(moves, inputs, outputs, *refs):
    sems = refs[-1]
    copies = []
    for k, (source, start, rows, target, place) in enumerate(moves):
        copy = pltpu.make_async_copy(
            refs[source].at[pl.ds(start, rows)], refs[inputs + target].at[pl.ds(place, rows)], sems.at[k]
        )
        copy.start()
        copies.append(copy)
    for copy in copies:
        copy.wait()


def pack(values, plans, extra, name):
    moves, shapes = [], []
    for target, plan in enumerate(plans):
        place = 0
        for source, start, rows in plan:
            moves.append((source, start, rows, target, place))
            place += rows
        shapes.append(jax.ShapeDtypeStruct((place, LANES), values[0].dtype))
    inputs = len(values) + len(extra)
    return pl.pallas_call(
        functools.partial(pack_kernel, tuple(moves), inputs, len(plans)),
        out_shape=tuple(shapes),
        in_specs=[ANY] * inputs,
        out_specs=tuple([ANY] * len(plans)),
        scratch_shapes=[pltpu.SemaphoreType.DMA((len(moves),))],
        compiler_params=pltpu.CompilerParams(vmem_limit_bytes=1 << 20),
        cost_estimate=pl.CostEstimate(flops=0, bytes_accessed=3_000_000, transcendentals=0),
        name=name,
    )(*values, *extra)


def fill(piece_refs, pool, sems):
    copies = []
    place = 0
    for i, piece in enumerate(piece_refs):
        rows = piece.shape[0]
        copy = pltpu.make_async_copy(piece, pool.at[pl.ds(place, rows)], sems.at[i])
        copy.start()
        copies.append(copy)
        place += rows
    return copies


def place_pairs(table_ref, pool, gram, size):
    def place(i, carry):
        for k in range(UNROLL):
            entry = 3 * (i * UNROLL + k)
            p = pl.multiple_of(table_ref[entry + 1] * size, size)
            q = pl.multiple_of(table_ref[entry + 2] * size, size)
            block = pool[pl.ds(pl.multiple_of(table_ref[entry + 3], 16), size)]
            gram[pl.ds(p, size), pl.ds(q, size)] = block
            gram[pl.ds(q, size), pl.ds(p, size)] = block.T
        return carry

    lax.fori_loop(0, table_ref[0], place, 0)


def gram_kernel(pieces, *refs):
    table_ref = refs[0]
    piece_refs = refs[1 : 1 + pieces]
    gram, pool, sems = refs[-3:]
    size = LANES
    copies = fill(piece_refs, pool, sems)
    for v in range(gram.shape[0] // size):
        gram[v * size : (v + 1) * size] = jnp.zeros((size, gram.shape[1]), gram.dtype)
    for copy in copies:
        copy.wait()
    place_pairs(table_ref, pool, gram, size)


def step_kernel(pieces, *refs):
    table_ref, info_ref, basis_ref, spread_ref, sign_ref, early_ref = refs[:6]
    piece_refs = refs[6 : 6 + pieces]
    next_ref, coef_ref, pool, gram, own, square, sems = refs[-7:]
    slots, size = sign_ref.shape[0], sign_ref.shape[1]
    copies = fill(piece_refs, pool, sems)
    for v in range(slots):
        gram[v * size : (v + 1) * size] = early_ref[v * size : (v + 1) * size]
    rows = lax.broadcasted_iota(jnp.int32, (size, size), 0)
    lanes = lax.broadcasted_iota(jnp.int32, (size, size), 1)
    own_size = info_ref[slots]
    self_slot = info_ref[slots + 1]
    for w in range(slots):
        kept = (rows < own_size) & (lanes < info_ref[w])
        block = jnp.where(kept, sign_ref[w].astype(jnp.float32), 0.0)
        own[:, w * size : (w + 1) * size] = block.astype(own.dtype)
    for copy in copies:
        copy.wait()
    place_pairs(table_ref, pool, gram, size)
    wide = 2 * size
    wide_lanes = lax.broadcasted_iota(jnp.int32, (size, wide), 1)
    wide_rows = lax.broadcasted_iota(jnp.int32, (size, wide), 0)

    def column_kept(n):
        first = info_ref[2 * n]
        second = info_ref[2 * n + 1]
        return (wide_lanes < first) | ((wide_lanes >= size) & (wide_lanes < size + second))

    for n in range(slots // 2):
        part = jnp.dot(own[...], gram[:, n * wide : (n + 1) * wide], preferred_element_type=jnp.float32)
        square[:, n * wide : (n + 1) * wide] = jnp.where(column_kept(n), part, 0.0).astype(square.dtype)
    coef = jnp.zeros((basis_ref.shape[0], LANES), jnp.float32)
    across = (((1,), (1,)), ((), ()))
    for n in range(slots // 2):
        part = jnp.dot(square[...], gram[:, n * wide : (n + 1) * wide], preferred_element_type=jnp.float32)
        cube = jnp.where(column_kept(n), part, 0.0)
        full = 1.5 * own[:, n * wide : (n + 1) * wide].astype(jnp.float32) - 0.5 * cube
        next_ref[2 * n] = full[:, :size].astype(next_ref.dtype)
        next_ref[2 * n + 1] = full[:, size:].astype(next_ref.dtype)
        shift = (self_slot - 2 * n) * size
        is_self = (self_slot >= 2 * n) & (self_slot < 2 * n + 2)
        diag = (wide_lanes == wide_rows + shift) & (wide_rows < own_size) & is_self
        dmat = 0.5 * (jnp.where(diag, 1.0, 0.0) - full)
        high = dmat.astype(jnp.bfloat16)
        low = (dmat - high.astype(jnp.float32)).astype(jnp.bfloat16)
        half = jnp.dot(basis_ref[...], high, preferred_element_type=jnp.float32) + jnp.dot(
            basis_ref[...], low, preferred_element_type=jnp.float32
        )
        half_high = half.astype(jnp.bfloat16)
        half_low = (half - half_high.astype(jnp.float32)).astype(jnp.bfloat16)
        for k in range(2):
            spread = spread_ref[2 * n + k]
            for part in (half_high, half_low):
                coef = coef + lax.dot_general(
                    part[:, k * size : (k + 1) * size], spread, across, preferred_element_type=jnp.float32
                )
    coef_ref[...] = coef[: coef_ref.shape[0]]


def profile_kernel(periods, steps, mate_from, *refs):
    own_ref, mate_ref, third_ref = refs[:3]
    plane_ref, line_ref, geos, sems = refs[-4:]
    odd = (lax.axis_index("layer") & 1) == 1
    rows = len(steps) * GEO
    copies = []
    for k, source in enumerate((own_ref, mate_ref.at[pl.ds(mate_from, rows)], third_ref)):
        copy = pltpu.make_async_copy(source, geos.at[k], sems.at[k])
        copy.start()
        copies.append(copy)
    cells = plane_ref.shape[2]
    cell = lax.broadcasted_iota(jnp.int32, (cells, LANES), 0)
    grid_x = (cell // BY).astype(jnp.float32)
    grid_y = (cell % BY).astype(jnp.float32)
    grid_z = lax.broadcasted_iota(jnp.int32, (LANES, BZ), 1).astype(jnp.float32)
    lane = lax.broadcasted_iota(jnp.int32, (1, LANES), 1)
    shell = (lane % SHELLS + 1).astype(jnp.float32)
    valid = lane < 7 * SPAN
    from_own = lane < 4 * SPAN
    from_below = lane < 6 * SPAN
    lift = jnp.where(from_own, 0.0, jnp.where(from_below, -float(BZ), float(BZ))) + 0.5 * BZ

    def nearest(offset, period):
        return offset - period * jnp.floor(offset * (1.0 / period) + 0.5)

    for copy in copies:
        copy.wait()
    for o, (step_row, step_col) in enumerate(steps):
        own, first, third = (geos[k, o * GEO : (o + 1) * GEO].astype(jnp.float32) for k in range(3))
        below = jnp.where(odd, first, third)
        above = jnp.where(odd, third, first)
        moved = jnp.where(from_below, pltpu.roll(below, 3 * SPAN, axis=1), pltpu.roll(above, 3 * SPAN, axis=1))
        geo = jnp.where(from_own, own, moved)
        extent = jnp.where(valid, geo[3:4], 1.0)
        inverse = (SHELLS / extent) * (SHELLS / extent)
        reach = jnp.where(valid, extent, -1.0)
        rate_t = inverse / (shell * shell)
        packed = jnp.concatenate(
            [0.5 * geo[2:3] + lift, reach, rate_t, inverse, jnp.zeros((4, LANES), jnp.float32)], axis=0
        )
        sub = packed.T
        d_x = nearest(grid_x - (0.5 * geo[0:1] + float(BX * step_row)), periods[0])
        d_y = nearest(grid_y - (0.5 * geo[1:2] + float(BY * step_col)), periods[1])
        inside = (jnp.abs(d_x) <= reach) & (jnp.abs(d_y) <= reach)
        squared = d_x * d_x + d_y * d_y
        d_z = nearest(grid_z - sub[:, 0:1], periods[2])
        inside_z = jnp.abs(d_z) <= sub[:, 1:2]
        squared_z = d_z * d_z
        for s in range(SHELLS):
            part = 1.0 / ((s + 1) * (s + 1))
            rate = inverse * part + rate_t
            plane_ref[o, s] = jnp.where(inside, jnp.exp(-rate * squared), 0.0).astype(plane_ref.dtype)
            rate_z = sub[:, 3:4] * part + sub[:, 2:3]
            line_ref[o, s] = jnp.where(inside_z, jnp.exp(-rate_z * squared_z), 0.0).astype(line_ref.dtype)


def density_kernel(column_steps, *refs):
    coef_refs = refs[:column_steps]
    plane_ref, line_ref, out_ref, terms = refs[column_steps:]
    for o in range(plane_ref.shape[0]):
        coef = coef_refs[o % column_steps]
        first = 8 * (o // column_steps)
        for s in range(SHELLS):
            scaled = plane_ref[o, s].astype(jnp.float32) * coef[first + s : first + s + 1, :]
            at = (o * SHELLS + s) * LANES
            terms[:, at : at + LANES] = scaled.astype(terms.dtype)
    out_ref[...] = jnp.dot(terms[...], line_ref[...], preferred_element_type=jnp.float32)


def local(sign_start, neighbors, atom_size, basis_proj, pair_extent, atom_x, atom_y, atom_z):
    n_row = lax.axis_size("row")
    n_col = lax.axis_size("col")
    n_lay = lax.axis_size("layer")
    assert n_lay == 4 and n_col >= 4 and (n_row == 2 or n_row >= 4)
    assert n_row & (n_row - 1) == 0 and n_col & (n_col - 1) == 0
    axes = (n_row, n_col, n_lay)
    atoms, slots = neighbors.shape
    size = sign_start.shape[2]
    steps = [0, 1] if n_row == 2 else [0, 1, -1]
    count = len(steps)
    others = range(1, count)
    own = sign_start[0]
    flat = own.reshape(slots * size, size)
    ints = jnp.concatenate(
        [
            neighbors.T,
            atom_size[None],
            atom_x[None],
            atom_y[None],
            atom_z[None],
            jnp.pad(pair_extent, ((0, 0), (0, atoms - slots))),
        ],
        axis=0,
    )
    full = slots * size
    half = full // 2
    n_pick = column_targets(n_row)
    part = n_pick * size + GEO

    def on_row(value, di):
        return from_offset(value, "row", steps[di])

    x_row = {di: on_row(flat, di) for di in others}
    y_row = from_layer(flat, 2)
    m_row = from_layer(flat, 1)
    picked, geo = pl.pallas_call(
        functools.partial(pick_kernel, axes),
        out_shape=(
            jax.ShapeDtypeStruct((part, size), own.dtype),
            jax.ShapeDtypeStruct((GEO, LANES), own.dtype),
        ),
        in_specs=[SMEM, HBM],
        out_specs=(VMEM, VMEM),
        scratch_shapes=[pltpu.SMEM((n_pick + 1,), jnp.int32), pltpu.SemaphoreType.DMA((n_pick,))],
        compiler_params=pltpu.CompilerParams(vmem_limit_bytes=2 << 20),
        name="pick_column_blocks",
    )(ints, own)
    up = from_offset(picked, "col", 1)
    down = from_offset(picked, "col", -1)

    at = {}
    buffers = {}

    def note(name, value, contents):
        buffers[name] = value
        start = 0
        for what, rows in contents:
            if what is not None:
                at[what] = (name, start)
            start += rows

    def row_of(di, flip):
        return [(("top", di, flip), half), (("end", di, flip), half)]

    def side_of(kind, di, flip):
        return [((kind, di, flip), part - GEO), ((kind + " geo", di, flip), GEO)]

    note("own", flat, row_of(0, 0))
    note("mate", m_row, row_of(0, 1))
    note("far", y_row, row_of(0, 2))
    note("up", up, side_of("up", 0, 0))
    note("down", down, side_of("down", 0, 0))
    note("geo", geo, [(("geo", 0, 0), GEO)])
    for di in others:
        note(("x", di), x_row[di], row_of(di, 0))

    names = ["up", "down", "geo", "far"] + [("x", di) for di in others]
    place = {name: i for i, name in enumerate(names)}
    xs = [place["x", di] for di in others]
    plans = [
        [(place["far"], half, half), (0, 0, part), (2, 0, GEO), (1, part - GEO, GEO)],
        [(x, 0, half) for x in xs] + [(1, 0, part)],
        [(x, 0, full) for x in xs] + [(place["far"], 0, full), (0, 0, part), (1, 0, part)],
    ]

    two_x, two_y, two_m = pack([buffers[name] for name in names], plans, [], "pack_two")

    early_order = ["own", "mate", "far", "up", "down", "geo"] + [("x", di) for di in others]
    early_order += [("two x", di) for di in others] + ["two y", "two m"]
    late_order = [("three x", di) for di in others] + ["three y", "three m"]
    late_order += [("four x", di) for di in others] + ["four y"]

    contents = {}
    for di in others:
        contents["two x", di] = [(("end", di, 2), half)] + side_of("up", di, 0)
        contents["two x", di] += [(("geo", di, 0), GEO), (("down geo", di, 0), GEO)]
    contents["two y"] = [(("top", di, 2), half) for di in others] + side_of("down", 0, 2)
    contents["two m"] = sum([row_of(di, 1) for di in others], []) + row_of(0, 3)
    contents["two m"] += side_of("up", 0, 1) + side_of("down", 0, 1)
    for di in others:
        contents["three x", di] = side_of("down", di, 0) + side_of("down", di, 2)
    contents["three y"] = side_of("up", 0, 2) + sum([side_of("up", di, 2) for di in others], [])
    contents["three m"] = []
    for di in others:
        contents["three m"] += [(("end", di, 3), half)] + side_of("up", di, 1) + [(None, 2 * GEO)]
    contents["three m"] += [(("top", di, 3), half) for di in others] + side_of("down", 0, 3)
    contents["three m"] += [("geos", count * 3 * GEO)]
    for di in others:
        contents["four x", di] = side_of("down", di, 1) + side_of("down", di, 3)
    contents["four y"] = side_of("up", 0, 3) + sum([side_of("up", di, 3) for di in others], [])
    lengths = {name: sum(rows for _, rows in content) for name, content in contents.items()}
    for name in early_order:
        if name in buffers:
            lengths[name] = buffers[name].shape[0]
    base = {}
    total = 0
    for name in early_order + late_order:
        base[name] = total
        total += lengths[name]
        if name == early_order[-1]:
            late_from = total
    located = dict(at)
    for name, content in contents.items():
        start = 0
        for what, rows in content:
            located[what] = (name, start)
            start += rows
    layout = [
        base[located[kind, di, flip][0]] + located[kind, di, flip][1]
        for kind in ("top", "end", "up", "down")
        for di in range(count)
        for flip in range(n_lay)
    ]
    pairs = slots * (slots + 1) // 2
    entries = 3 * (pairs + UNROLL) + 1
    early_table, late_table, info, spread, own_basis = pl.pallas_call(
        functools.partial(prepare_kernel, axes, count, tuple(layout), late_from),
        out_shape=(
            jax.ShapeDtypeStruct((entries,), jnp.int32),
            jax.ShapeDtypeStruct((entries,), jnp.int32),
            jax.ShapeDtypeStruct((slots + 2,), jnp.int32),
            jax.ShapeDtypeStruct((slots, LANES, size), jnp.bfloat16),
            jax.ShapeDtypeStruct((16, size), jnp.bfloat16),
        ),
        in_specs=[SMEM, VMEM, ANY],
        out_specs=(SMEM, SMEM, SMEM, VMEM, VMEM),
        scratch_shapes=[
            pltpu.SMEM((4, slots), jnp.int32),
            pltpu.SMEM((atoms,), jnp.int32),
            pltpu.SMEM((len(layout),), jnp.int32),
        ],
        compiler_params=pltpu.CompilerParams(vmem_limit_bytes=(2 << 20) + atoms * 16384),
        cost_estimate=pl.CostEstimate(flops=6_000_000_000, bytes_accessed=8_000_000, transcendentals=0),
        name="prepare",
    )(ints, basis_proj.transpose(1, 0, 2).reshape(SHELLS * atoms, size), two_x)

    for di in others:
        note(("two x", di), on_row(two_x, di), contents["two x", di])
    note("two y", from_layer(two_y, 2), contents["two y"])
    note("two m", from_layer(two_m, 1), contents["two m"])

    names = ["up", "down", "two y", "geo"] + [("two x", di) for di in others]
    place = {name: i for i, name in enumerate(names)}
    y_down = at["down", 0, 2][1]
    x_up = at["up", 1, 0][1]
    gather = []
    for di in range(count):
        for kind in ("geo", "up geo", "down geo"):
            name, start = at[kind, di, 0]
            gather.append((place[name], start, GEO))
    xs = [place["two x", di] for di in others]
    plans = [
        [(1, 0, part), (2, y_down, part)],
        [(0, 0, part)] + [(x, x_up, part) for x in xs],
        [(x, 0, lengths["two x", 1]) for x in xs] + [(2, 0, lengths["two y"])] + gather,
        gather,
    ]
    three_x, three_y, three_m, geos = pack([buffers[name] for name in names], plans, [own_basis], "pack_three")
    for di in others:
        note(("three x", di), on_row(three_x, di), contents["three x", di])
    note("three y", from_layer(three_y, 2), contents["three y"])
    note("three m", from_layer(three_m, 1), contents["three m"])
    third_geos = from_layer(geos, 3)

    early_values = [buffers[name] for name in early_order]
    gram = pl.pallas_call(
        functools.partial(gram_kernel, len(early_values)),
        out_shape=jax.ShapeDtypeStruct((full, full), jnp.bfloat16),
        in_specs=[SMEM] + [ANY] * (len(early_values) + 1),
        out_specs=VMEM,
        scratch_shapes=[
            pltpu.VMEM((late_from, LANES), jnp.bfloat16),
            pltpu.SemaphoreType.DMA((len(early_values),)),
        ],
        compiler_params=pltpu.CompilerParams(vmem_limit_bytes=(6 << 20) + late_from * LANES * 2),
        cost_estimate=pl.CostEstimate(flops=1_000_000_000, bytes_accessed=20_000_000, transcendentals=0),
        name="gram_early",
    )(early_table, *early_values, three_x)

    for di in others:
        note(("four x", di), from_layer(buffers["three x", di], 1), contents["four x", di])
    note("four y", from_layer(buffers["three y"], 1), contents["four y"])

    column_steps = (0, 1, -1)
    tile_steps = [(dr, dc) for dr in steps for dc in column_steps]
    tiles = len(tile_steps)
    periods = (float(BX * n_row), float(BY * n_col), float(BZ * n_lay))
    plane, line = pl.pallas_call(
        functools.partial(profile_kernel, periods, tile_steps, at["geos"][1]),
        out_shape=(
            jax.ShapeDtypeStruct((tiles, SHELLS, BX * BY, LANES), jnp.bfloat16),
            jax.ShapeDtypeStruct((tiles, SHELLS, LANES, BZ), jnp.bfloat16),
        ),
        in_specs=[ANY] * 4,
        out_specs=(VMEM, VMEM),
        scratch_shapes=[
            pltpu.VMEM((3, tiles * GEO, LANES), jnp.bfloat16),
            pltpu.SemaphoreType.DMA((3,)),
        ],
        compiler_params=pltpu.CompilerParams(vmem_limit_bytes=10 << 20),
        cost_estimate=pl.CostEstimate(flops=5_000_000_000, bytes_accessed=4_000_000, transcendentals=2_000_000),
        name="profiles",
    )(geos, buffers["three m"], third_geos, gram)

    late_values = [buffers[name] for name in late_order]
    sign_next, coef = pl.pallas_call(
        functools.partial(step_kernel, len(late_values)),
        out_shape=(
            jax.ShapeDtypeStruct((slots, size, size), jnp.bfloat16),
            jax.ShapeDtypeStruct((8, LANES), jnp.float32),
        ),
        in_specs=[SMEM, SMEM, VMEM, VMEM, VMEM, VMEM] + [ANY] * (len(late_values) + 1),
        out_specs=(VMEM, VMEM),
        scratch_shapes=[
            pltpu.VMEM((total - late_from, LANES), jnp.bfloat16),
            pltpu.VMEM((full, full), jnp.bfloat16),
            pltpu.VMEM((size, full), jnp.bfloat16),
            pltpu.VMEM((size, full), jnp.bfloat16),
            pltpu.SemaphoreType.DMA((len(late_values),)),
        ],
        compiler_params=pltpu.CompilerParams(vmem_limit_bytes=(15 << 20) + (total - late_from) * LANES * 2),
        cost_estimate=pl.CostEstimate(flops=1_300_000_000, bytes_accessed=8_000_000, transcendentals=0),
        name="square_cube_coefficients",
    )(late_table, info, own_basis, spread, own, gram, *late_values, line)

    below = from_offset(coef, "layer", -1)
    above = from_offset(coef, "layer", 1)
    merged = jnp.concatenate(
        [
            coef[:, : 4 * SPAN],
            below[:, SPAN : 3 * SPAN],
            above[:, 3 * SPAN : 4 * SPAN],
            jnp.zeros((8, LANES - 7 * SPAN), jnp.float32),
        ],
        axis=1,
    )
    stacked = jnp.concatenate([merged] + [on_row(merged, di) for di in others], axis=0)
    received = [stacked] + [from_offset(stacked, "col", dc) for dc in column_steps[1:]]

    density = pl.pallas_call(
        functools.partial(density_kernel, len(column_steps)),
        out_shape=jax.ShapeDtypeStruct((BX * BY, BZ), jnp.float32),
        in_specs=[VMEM] * (len(column_steps) + 2),
        out_specs=VMEM,
        scratch_shapes=[pltpu.VMEM((BX * BY, tiles * SHELLS * LANES), jnp.bfloat16)],
        compiler_params=pltpu.CompilerParams(vmem_limit_bytes=16 << 20),
        cost_estimate=pl.CostEstimate(flops=310_000_000, bytes_accessed=4_000_000, transcendentals=0),
        name="density",
    )(*received, plane, line.reshape(tiles * SHELLS * LANES, BZ))
    return sign_next[None], density.reshape(BX, BY, BZ)


def solution(mesh):
    rows = P(("row", "col", "layer"), None, None, None)
    in_specs = (rows, P(), P(), P(), P(("row", "col", "layer"), None), P(), P(), P())
    out_specs = (rows, P("row", "col", "layer"))
    return jax.shard_map(local, mesh=mesh, in_specs=in_specs, out_specs=out_specs, check_vma=False)
```

```python
import functools

import jax
import jax.numpy as jnp
from jax import lax
from jax.experimental import pallas as pl
from jax.experimental.pallas import tpu as pltpu
from jax.sharding import PartitionSpec as P

BX = 16
BY = 16
BZ = 128
LANES = 128
UNROLL = 4
SHELLS = 6
SPAN = 3 * SHELLS
GEO = 16
VMEM = pl.BlockSpec(memory_space=pltpu.VMEM)
SMEM = pl.BlockSpec(memory_space=pltpu.SMEM)
ANY = pl.BlockSpec(memory_space=pl.ANY)
HBM = pl.BlockSpec(memory_space=pltpu.HBM)


def from_offset(x, axis, step):
    count = lax.axis_size(axis)
    return lax.ppermute(x, axis, [((i + step) % count, i) for i in range(count)])


def from_row_layer(x, step, mover):
    rows, layers = lax.axis_size("row"), lax.axis_size("layer")
    moves = [
        (((i + step) % rows) * layers + mover(j) % layers, i * layers + j) for i in range(rows) for j in range(layers)
    ]
    return lax.ppermute(x, ("row", "layer"), moves)


def from_layer(x, flip):
    count = lax.axis_size("layer")
    return lax.ppermute(x, "layer", [(i ^ flip, i) for i in range(count)])


def column_targets(n_row):
    return 5 if n_row == 2 else 7


def target_place(n_row, step_row, step_lay, row):
    same = jnp.where(step_lay < 3, step_lay, -1)
    if n_row == 2:
        lead = step_lay - row
        across = jnp.where((lead >= 0) & (lead < 2), 3 + lead, -1)
    else:
        across = 3 + step_lay
    return jnp.where(step_row == 0, same, jnp.where(step_row == 1, across, -1))


class Places:
    def __init__(self, n_row, n_col, n_lay):
        self.n_row, self.n_col, self.n_lay = n_row, n_col, n_lay
        self.lay_bits = n_lay.bit_length() - 1
        self.col_bits = n_col.bit_length() - 1
        self.row = lax.axis_index("row")
        self.col = lax.axis_index("col")
        self.lay = lax.axis_index("layer")
        self.me = (((self.row << self.col_bits) + self.col) << self.lay_bits) + self.lay

    def split(self, atom):
        return (
            atom >> (self.lay_bits + self.col_bits),
            (atom >> self.lay_bits) & (self.n_col - 1),
            atom & (self.n_lay - 1),
        )


def load(sources, targets, sems):
    copies = [pltpu.make_async_copy(a, b, sems.at[i]) for i, (a, b) in enumerate(zip(sources, targets))]
    for copy in copies:
        copy.start()
    for copy in copies:
        copy.wait()


def own_ranks(at, neighbors_ref):
    seen = [jnp.int32(0)] * at.n_lay
    listed = []
    for w in range(neighbors_ref.shape[0]):
        atom = neighbors_ref[w, at.me]
        step_lay = (atom - at.lay) & (at.n_lay - 1)
        rank = jnp.int32(0)
        for k in range(at.n_lay):
            rank = jnp.where(step_lay == k, 3 * k + seen[k], rank)
            seen[k] = seen[k] + (step_lay == k).astype(jnp.int32)
        listed.append((atom, rank))
    return listed


def pick_kernel(axes, *refs):
    sign_ref, out_ref, geo_ref, neighbors_ref, extent_ref, x_ref, y_ref, z_ref, place_ref, loads, sems = refs[5:]
    at = Places(*axes)
    slots = sign_ref.shape[0]
    n_pick = place_ref.shape[0] - 1
    size = sign_ref.shape[1]
    for i in range(n_pick + 1):
        place_ref[i] = 0
    load(refs[:5], (neighbors_ref, extent_ref, x_ref, y_ref, z_ref), loads)
    ranks = own_ranks(at, neighbors_ref)
    for w, (atom, _) in enumerate(ranks):
        row, col, lay = at.split(atom)
        place = target_place(at.n_row, (row - at.row) & (at.n_row - 1), (lay - at.lay) & (at.n_lay - 1), at.row)
        place_ref[jnp.where((col == at.col) & (place >= 0), place, n_pick)] = w
    copies = []
    for i in range(n_pick):
        copy = pltpu.make_async_copy(sign_ref.at[place_ref[i]], out_ref.at[pl.ds(i * size, size)], sems.at[i])
        copy.start()
        copies.append(copy)
    sub = lax.broadcasted_iota(jnp.int32, (GEO, LANES), 0)
    lane_pair = lax.broadcasted_iota(jnp.int32, (GEO, LANES), 1) // SHELLS
    geo = jnp.zeros((GEO, LANES), jnp.int32)
    for w, (atom, rank) in enumerate(ranks):
        row, col, lay = at.split(atom)
        go_row = ((row - at.row + 1) & (at.n_row - 1)) - 1
        go_col = ((col - at.col + 1) & (at.n_col - 1)) - 1
        go_lay = jnp.minimum(((lay - at.lay + 1) & (at.n_lay - 1)) - 1, 1)
        twice_x = x_ref[at.me] + x_ref[atom] + BX * go_row
        twice_y = y_ref[at.me] + y_ref[atom] + BY * go_col
        twice_z = z_ref[at.me] + z_ref[atom] + BZ * go_lay - BZ
        extent = extent_ref[0, w]
        values = jnp.where(sub == 0, twice_x, jnp.where(sub == 1, twice_y, jnp.where(sub == 2, twice_z, extent)))
        geo = jnp.where(lane_pair == rank, values, geo)
    geo = geo.astype(jnp.float32).astype(geo_ref.dtype)
    geo_ref[...] = geo
    out_ref[n_pick * size :] = geo
    for copy in copies:
        copy.wait()


def prepare_kernel(axes, count, layout, late_from, *refs):
    basis_ref = refs[2]
    early_ref, late_ref, info_ref, spread_ref, own_basis_ref = refs[-11:-6]
    neighbors_ref, size_ref, known, inverse, layout_ref, loads = refs[-6:]
    at = Places(*axes)
    load(refs[:2], (neighbors_ref, size_ref), loads)
    slots, atoms = neighbors_ref.shape
    bits = atoms.bit_length() - 1
    for i, value in enumerate(layout):
        layout_ref[i] = value
    lines = count * at.n_lay

    def hot(rows, atom, first):
        sub = lax.broadcasted_iota(jnp.int32, (rows, SHELLS * atoms), 0)
        lane = lax.broadcasted_iota(jnp.int32, (rows, SHELLS * atoms), 1)
        return ((lane & (atoms - 1)) == atom) & (sub == first + (lane >> bits))

    def rows_of(chosen):
        picked = jnp.where(chosen, 1.0, 0.0).astype(jnp.bfloat16)
        return jnp.dot(picked, basis_ref[...], preferred_element_type=jnp.float32).astype(jnp.bfloat16)

    self_slot = jnp.int32(0)
    for w, (atom, rank) in enumerate(own_ranks(at, neighbors_ref)):
        row, col, lay = at.split(atom)
        step_row = (row - at.row) & (at.n_row - 1)
        step_col = (col - at.col) & (at.n_col - 1)
        self_slot = jnp.where(atom == at.me, w, self_slot)
        info_ref[w] = size_ref[atom]
        spread_ref[:, w * LANES : (w + 1) * LANES] = rows_of(hot(LANES, atom, rank * SHELLS))
        flip = lay ^ at.lay
        known[0, w] = atom
        known[1, w] = jnp.where(step_col == 0, 0, jnp.where(step_col == 1, 1, 2))
        known[2, w] = jnp.where(step_row == 0, 0, jnp.where(step_row == 1, 1, 2)) * at.n_lay + flip
        inverse[atom] = -1
    own_basis_ref[...] = rows_of(hot(16, at.me, 0))
    info_ref[slots] = size_ref[at.me]
    info_ref[slots + 1] = self_slot

    def row_of_pairs(v, totals):
        early, late = totals
        atom = known[0, v]
        side = known[1, v]
        line = known[2, v]
        row, _, lay = at.split(atom)
        for u in range(slots):
            inverse[neighbors_ref[u, atom]] = v * 16 + u
        top = layout_ref[line]
        end = layout_ref[lines + line]
        beside = layout_ref[(side + 1) * lines + line]
        half = slots // 2
        for w in range(slots):
            other = known[0, w]
            other_side = known[1, w]
            mark = inverse[other]
            slot = mark & 15
            o_row, _, o_lay = at.split(other)
            there = target_place(at.n_row, (o_row - row) & (at.n_row - 1), (o_lay - lay) & (at.n_lay - 1), row)
            back = target_place(at.n_row, (row - o_row) & (at.n_row - 1), (lay - o_lay) & (at.n_lay - 1), o_row)
            from_row = (other_side != 0) | (v <= w)
            from_column = (side == other_side) & (there >= 0) & ((back < 0) | (v <= w))
            chosen = ((mark >> 4) == v) & jnp.where(side == 0, from_row, from_column)
            in_row = jnp.where(slot < half, top + slot * LANES, end + (slot - half) * LANES)
            where = jnp.where(side == 0, in_row, beside + there * LANES)
            is_late = where >= late_from
            for ref, total in ((early_ref, early), (late_ref, late)):
                ref[3 * total + 1] = v
                ref[3 * total + 2] = w
                ref[3 * total + 3] = where
            late_ref[3 * late + 3] = where - late_from
            early = early + (chosen & ~is_late).astype(jnp.int32)
            late = late + (chosen & is_late).astype(jnp.int32)
        return early, late

    totals = lax.fori_loop(0, slots, row_of_pairs, (jnp.int32(0), jnp.int32(0)))
    for ref, total in zip((early_ref, late_ref), totals):
        ref[0] = (total + UNROLL - 1) // UNROLL
        last = 3 * jnp.maximum(total - 1, 0) + 1
        for i in range(UNROLL - 1):
            for k in range(3):
                ref[3 * (total + i) + 1 + k] = ref[last + k]


def pack_kernel(moves, inputs, outputs, *refs):
    sems = refs[-1]
    copies = []
    for k, (source, start, rows, target, place) in enumerate(moves):
        copy = pltpu.make_async_copy(
            refs[source].at[pl.ds(start, rows)], refs[inputs + target].at[pl.ds(place, rows)], sems.at[k]
        )
        copy.start()
        copies.append(copy)
    for copy in copies:
        copy.wait()


def pack(values, plans, extra, name):
    moves, shapes = [], []
    for target, plan in enumerate(plans):
        place = 0
        for source, start, rows in plan:
            moves.append((source, start, rows, target, place))
            place += rows
        shapes.append(jax.ShapeDtypeStruct((place, LANES), values[0].dtype))
    inputs = len(values) + len(extra)
    return pl.pallas_call(
        functools.partial(pack_kernel, tuple(moves), inputs, len(plans)),
        out_shape=tuple(shapes),
        in_specs=[ANY] * inputs,
        out_specs=tuple([ANY] * len(plans)),
        scratch_shapes=[pltpu.SemaphoreType.DMA((len(moves),))],
        compiler_params=pltpu.CompilerParams(vmem_limit_bytes=1 << 20),
        cost_estimate=pl.CostEstimate(flops=0, bytes_accessed=3_000_000, transcendentals=0),
        name=name,
    )(*values, *extra)


def fill(piece_refs, pool, sems):
    copies = []
    place = 0
    for i, piece in enumerate(piece_refs):
        rows = piece.shape[0]
        copy = pltpu.make_async_copy(piece, pool.at[pl.ds(place, rows)], sems.at[i])
        copy.start()
        copies.append(copy)
        place += rows
    return copies


def place_pairs(table_ref, pool, gram, size):
    def place(i, carry):
        for k in range(UNROLL):
            entry = 3 * (i * UNROLL + k)
            p = pl.multiple_of(table_ref[entry + 1] * size, size)
            q = pl.multiple_of(table_ref[entry + 2] * size, size)
            block = pool[pl.ds(pl.multiple_of(table_ref[entry + 3], 16), size)]
            gram[pl.ds(p, size), pl.ds(q, size)] = block
            gram[pl.ds(q, size), pl.ds(p, size)] = block.T
        return carry

    lax.fori_loop(0, table_ref[0], place, 0)


def gram_kernel(pieces, *refs):
    table_ref = refs[0]
    piece_refs = refs[1 : 1 + pieces]
    gram, pool, sems = refs[-3:]
    size = LANES
    copies = fill(piece_refs, pool, sems)
    for v in range(gram.shape[0] // size):
        gram[v * size : (v + 1) * size] = jnp.zeros((size, gram.shape[1]), gram.dtype)
    for copy in copies:
        copy.wait()
    place_pairs(table_ref, pool, gram, size)


def step_kernel(pieces, *refs):
    table_ref, info_ref, basis_ref, spread_ref, sign_ref, early_ref = refs[:6]
    piece_refs = refs[6 : 6 + pieces]
    next_ref, coef_ref, pool, gram, own, square, sems = refs[-7:]
    slots, size = sign_ref.shape[0], sign_ref.shape[1]
    copies = fill(piece_refs, pool, sems)
    for v in range(slots):
        gram[v * size : (v + 1) * size] = early_ref[v * size : (v + 1) * size]
    rows = lax.broadcasted_iota(jnp.int32, (size, size), 0)
    lanes = lax.broadcasted_iota(jnp.int32, (size, size), 1)
    own_size = info_ref[slots]
    self_slot = info_ref[slots + 1]
    for w in range(slots):
        kept = (rows < own_size) & (lanes < info_ref[w])
        block = jnp.where(kept, sign_ref[w].astype(jnp.float32), 0.0)
        own[:, w * size : (w + 1) * size] = block.astype(own.dtype)
    for copy in copies:
        copy.wait()
    place_pairs(table_ref, pool, gram, size)
    wide = 2 * size
    wide_lanes = lax.broadcasted_iota(jnp.int32, (size, wide), 1)
    wide_rows = lax.broadcasted_iota(jnp.int32, (size, wide), 0)

    def column_kept(n):
        first = info_ref[2 * n]
        second = info_ref[2 * n + 1]
        return (wide_lanes < first) | ((wide_lanes >= size) & (wide_lanes < size + second))

    for n in range(slots // 2):
        part = jnp.dot(own[...], gram[:, n * wide : (n + 1) * wide], preferred_element_type=jnp.float32)
        square[:, n * wide : (n + 1) * wide] = jnp.where(column_kept(n), part, 0.0).astype(square.dtype)
    basis = jnp.concatenate([basis_ref[...], basis_ref[...]], axis=1)
    coef = jnp.zeros((2 * basis_ref.shape[0], LANES), jnp.float32)
    across = (((1,), (1,)), ((), ()))
    for n in range(slots // 2):
        part = jnp.dot(square[...], gram[:, n * wide : (n + 1) * wide], preferred_element_type=jnp.float32)
        cube = jnp.where(column_kept(n), part, 0.0)
        full = 1.5 * own[:, n * wide : (n + 1) * wide].astype(jnp.float32) - 0.5 * cube
        next_ref[2 * n] = full[:, :size].astype(next_ref.dtype)
        next_ref[2 * n + 1] = full[:, size:].astype(next_ref.dtype)
        shift = (self_slot - 2 * n) * size
        is_self = (self_slot >= 2 * n) & (self_slot < 2 * n + 2)
        diag = (wide_lanes == wide_rows + shift) & (wide_rows < own_size) & is_self
        dmat = 0.5 * (jnp.where(diag, 1.0, 0.0) - full)
        high = dmat.astype(jnp.bfloat16)
        low = (dmat - high.astype(jnp.float32)).astype(jnp.bfloat16)
        half = jnp.dot(basis, jnp.concatenate([high, low], axis=0), preferred_element_type=jnp.float32)
        half_high = half.astype(jnp.bfloat16)
        half_low = (half - half_high.astype(jnp.float32)).astype(jnp.bfloat16)
        coef = coef + lax.dot_general(
            jnp.concatenate([half_high, half_low], axis=0),
            spread_ref[:, n * wide : (n + 1) * wide],
            across,
            preferred_element_type=jnp.float32,
        )
    coef = coef[: basis_ref.shape[0]] + coef[basis_ref.shape[0] :]
    coef_ref[...] = coef[: coef_ref.shape[0]]


def profile_kernel(periods, steps, *refs):
    plane_ref, line_ref, geos, sems = refs[-4:]
    odd = (lax.axis_index("layer") & 1) == 1
    copies = []
    for k in range(3):
        copy = pltpu.make_async_copy(refs[k], geos.at[k], sems.at[k])
        copy.start()
        copies.append(copy)
    cells = plane_ref.shape[2]
    cell = lax.broadcasted_iota(jnp.int32, (cells, LANES), 0)
    grid_x = (cell // BY).astype(jnp.float32)
    grid_y = (cell % BY).astype(jnp.float32)
    grid_z = lax.broadcasted_iota(jnp.int32, (LANES, BZ), 1).astype(jnp.float32)
    lane = lax.broadcasted_iota(jnp.int32, (1, LANES), 1)
    shell = (lane % SHELLS + 1).astype(jnp.float32)
    valid = lane < 7 * SPAN
    from_own = lane < 4 * SPAN
    from_below = lane < 6 * SPAN
    lift = jnp.where(from_own, 0.0, jnp.where(from_below, -float(BZ), float(BZ))) + 0.5 * BZ

    def nearest(offset, period):
        return offset - period * jnp.floor(offset * (1.0 / period) + 0.5)

    for copy in copies:
        copy.wait()
    for o, (place, step_row, step_col) in enumerate(steps):
        own, first, third = (geos[k, place * GEO : (place + 1) * GEO].astype(jnp.float32) for k in range(3))
        below = jnp.where(odd, first, third)
        above = jnp.where(odd, third, first)
        moved = jnp.where(from_below, pltpu.roll(below, 3 * SPAN, axis=1), pltpu.roll(above, 3 * SPAN, axis=1))
        geo = jnp.where(from_own, own, moved)
        extent = jnp.where(valid, geo[3:4], 1.0)
        inverse = (SHELLS / extent) * (SHELLS / extent)
        reach = jnp.where(valid, extent, -1.0)
        rate_t = inverse / (shell * shell)
        packed = jnp.concatenate(
            [0.5 * geo[2:3] + lift, reach, rate_t, inverse, jnp.zeros((4, LANES), jnp.float32)], axis=0
        )
        sub = packed.T
        d_x = nearest(grid_x - (0.5 * geo[0:1] + float(BX * step_row)), periods[0])
        d_y = nearest(grid_y - (0.5 * geo[1:2] + float(BY * step_col)), periods[1])
        inside = (jnp.abs(d_x) <= reach) & (jnp.abs(d_y) <= reach)
        squared = d_x * d_x + d_y * d_y
        d_z = nearest(grid_z - sub[:, 0:1], periods[2])
        inside_z = jnp.abs(d_z) <= sub[:, 1:2]
        squared_z = d_z * d_z
        for s in range(SHELLS):
            part = 1.0 / ((s + 1) * (s + 1))
            rate = inverse * part + rate_t
            plane_ref[o, s] = jnp.where(inside, jnp.exp(-rate * squared), 0.0).astype(plane_ref.dtype)
            rate_z = sub[:, 3:4] * part + sub[:, 2:3]
            line_ref[o, s] = jnp.where(inside_z, jnp.exp(-rate_z * squared_z), 0.0).astype(line_ref.dtype)


def density_kernel(tiles, inputs, *refs):
    coef_refs = refs[: inputs - 2]
    plane_ref, line_ref = refs[inputs - 2 : inputs]
    out_ref, terms = refs[-2:]
    for i, (o, source, first) in enumerate(tiles):
        for s in range(SHELLS):
            scaled = plane_ref[o, s].astype(jnp.float32) * coef_refs[source][first + s : first + s + 1, :]
            at = (i * SHELLS + s) * LANES
            terms[:, at : at + LANES] = scaled.astype(terms.dtype)
    start = tiles[0][0] * SHELLS * LANES
    summed = jnp.dot(
        terms[...], line_ref[start : start + len(tiles) * SHELLS * LANES], preferred_element_type=jnp.float32
    )
    if len(refs) > inputs + 2:
        summed = summed + refs[inputs][...]
    out_ref[...] = summed


def local(sign_start, neighbors, atom_size, basis_proj, pair_extent, atom_x, atom_y, atom_z):
    n_row = lax.axis_size("row")
    n_col = lax.axis_size("col")
    n_lay = lax.axis_size("layer")
    assert n_lay == 4 and n_col >= 4 and (n_row == 2 or n_row >= 4)
    assert n_row & (n_row - 1) == 0 and n_col & (n_col - 1) == 0
    axes = (n_row, n_col, n_lay)
    atoms, slots = neighbors.shape
    size = sign_start.shape[2]
    steps = [0, 1] if n_row == 2 else [0, 1, -1]
    count = len(steps)
    others = range(1, count)
    own = sign_start[0]
    flat = own.reshape(slots * size, size)
    listings = neighbors.T
    full = slots * size
    half = full // 2
    n_pick = column_targets(n_row)
    picks = n_pick * size
    part = picks + GEO
    kinds = ("geo", "up geo", "down geo")

    def on_row(value, di):
        return from_offset(value, "row", steps[di])

    picked, geo = pl.pallas_call(
        functools.partial(pick_kernel, axes),
        out_shape=(
            jax.ShapeDtypeStruct((part, size), own.dtype),
            jax.ShapeDtypeStruct((GEO, LANES), own.dtype),
        ),
        in_specs=[HBM] * 6,
        out_specs=(VMEM, VMEM),
        scratch_shapes=[
            pltpu.SMEM((slots, atoms), jnp.int32),
            pltpu.SMEM((1, slots), jnp.int32),
            pltpu.SMEM((atoms,), jnp.int32),
            pltpu.SMEM((atoms,), jnp.int32),
            pltpu.SMEM((atoms,), jnp.int32),
            pltpu.SMEM((n_pick + 1,), jnp.int32),
            pltpu.SemaphoreType.DMA((5,)),
            pltpu.SemaphoreType.DMA((n_pick,)),
        ],
        compiler_params=pltpu.CompilerParams(vmem_limit_bytes=2 << 20),
        name="pick_column_blocks",
    )(listings, pair_extent, atom_x, atom_y, atom_z, own)
    x_row = {di: on_row(flat, di) for di in others}
    far = from_layer(flat, 2)
    up = from_offset(picked, "col", 1)
    down = from_offset(picked, "col", -1)
    halves = pack(
        [far] + [x_row[di] for di in others],
        [[(0, half, half)]] + [[(di, 0, half)] for di in others],
        [],
        "pack_halves",
    )
    ends = {di: on_row(halves[0], di) for di in others}
    tops = {di: from_layer(halves[di], 2) for di in others}
    mate = from_layer(flat, 1)

    beside, geos = pack(
        [up, down, geo],
        [[(0, 0, picks), (1, 0, picks)], [(2, 0, GEO), (0, picks, GEO), (1, picks, GEO)]],
        [ends[di] for di in others] + [tops[di] for di in others],
        "pack_beside",
    )
    side_x = {di: on_row(beside, di) for di in others}
    side_y = from_layer(beside, 2)
    side_d = {di: from_row_layer(beside, steps[di], lambda j: j ^ 2) for di in others}
    geos = jnp.concatenate([geos] + [on_row(geos, di) for di in others], axis=0)
    mate_geos = from_layer(geos, 1)
    third_geos = from_layer(geos, 3)
    rows = [x_row[di] for di in others] + [far] + [ends[di] for di in others] + [tops[di] for di in others]
    rows += [beside]
    to_mate = pack(rows, [[(i, 0, value.shape[0]) for i, value in enumerate(rows)]], [], "pack_mate")[0]
    mate_rows = from_layer(to_mate, 1)

    def row_of(di, flip):
        return [(("top", di, flip), half), (("end", di, flip), half)]

    def side_of(di, flip):
        return [(("up", di, flip), picks), (("down", di, flip), picks)]

    early = [(flat, row_of(0, 0)), (mate, row_of(0, 1)), (far, row_of(0, 2))]
    early += [(x_row[di], row_of(di, 0)) for di in others]
    early += [(ends[di], [(("end", di, 2), half)]) for di in others]
    early += [(tops[di], [(("top", di, 2), half)]) for di in others]
    early += [(beside, side_of(0, 0))]
    content = sum([row_of(di, 1) for di in others], []) + row_of(0, 3)
    content += [(("end", di, 3), half) for di in others] + [(("top", di, 3), half) for di in others]
    early += [(mate_rows, content + side_of(0, 1))]
    located = {}
    total = 0
    for _, content in early:
        for what, length in content:
            located[what] = total
            total += length
    late_from = total
    late = [side_of(di, 0) for di in others] + [side_of(di, 1) for di in others]
    late += [side_of(0, 2), side_of(0, 3)]
    late += [side_of(di, 2) for di in others] + [side_of(di, 3) for di in others]
    for content in late:
        for what, length in content:
            located[what] = total
            total += length
    layout = [
        located[kind, di, flip]
        for kind in ("top", "end", "up", "down")
        for di in range(count)
        for flip in range(n_lay)
    ]

    pairs = slots * (slots + 1) // 2
    entries = 3 * (pairs + UNROLL) + 1
    early_table, late_table, info, spread, own_basis = pl.pallas_call(
        functools.partial(prepare_kernel, axes, count, tuple(layout), late_from),
        out_shape=(
            jax.ShapeDtypeStruct((entries,), jnp.int32),
            jax.ShapeDtypeStruct((entries,), jnp.int32),
            jax.ShapeDtypeStruct((slots + 2,), jnp.int32),
            jax.ShapeDtypeStruct((LANES, full), jnp.bfloat16),
            jax.ShapeDtypeStruct((16, size), jnp.bfloat16),
        ),
        in_specs=[HBM, HBM, VMEM, ANY],
        out_specs=(SMEM, SMEM, SMEM, VMEM, VMEM),
        scratch_shapes=[
            pltpu.SMEM((slots, atoms), jnp.int32),
            pltpu.SMEM((atoms,), jnp.int32),
            pltpu.SMEM((3, slots), jnp.int32),
            pltpu.SMEM((atoms,), jnp.int32),
            pltpu.SMEM((len(layout),), jnp.int32),
            pltpu.SemaphoreType.DMA((2,)),
        ],
        compiler_params=pltpu.CompilerParams(vmem_limit_bytes=(2 << 20) + atoms * 16384),
        cost_estimate=pl.CostEstimate(flops=6_000_000_000, bytes_accessed=8_000_000, transcendentals=0),
        name="prepare",
    )(listings, atom_size, basis_proj.transpose(1, 0, 2).reshape(SHELLS * atoms, size), beside)

    early_values = [value for value, _ in early]
    gram = pl.pallas_call(
        functools.partial(gram_kernel, len(early_values)),
        out_shape=jax.ShapeDtypeStruct((full, full), jnp.bfloat16),
        in_specs=[SMEM] + [ANY] * len(early_values),
        out_specs=VMEM,
        scratch_shapes=[
            pltpu.VMEM((late_from, LANES), jnp.bfloat16),
            pltpu.SemaphoreType.DMA((len(early_values),)),
        ],
        compiler_params=pltpu.CompilerParams(vmem_limit_bytes=(6 << 20) + late_from * LANES * 2),
        cost_estimate=pl.CostEstimate(flops=4_000_000_000, bytes_accessed=20_000_000, transcendentals=0),
        name="gram_early",
    )(early_table, *early_values)

    diagonal = [side_d[di] for di in others]
    if len(diagonal) == 1:
        diagonal = pack(diagonal, [[(0, 0, 2 * picks)]], [gram], "pack_diagonal")
    late_values = [side_x[di] for di in others] + [from_layer(side_x[di], 1) for di in others]
    late_values += [side_y, from_layer(side_y, 1)]
    late_values += diagonal
    late_values += [from_layer(value, 1) for value in diagonal]

    column_steps = (0, 1, -1)
    tile_steps = [(di * 3 + k, steps[di], dc) for k, dc in enumerate(column_steps) for di in range(count)]
    tiles = len(tile_steps)
    periods = (float(BX * n_row), float(BY * n_col), float(BZ * n_lay))
    plane, line = pl.pallas_call(
        functools.partial(profile_kernel, periods, tile_steps),
        out_shape=(
            jax.ShapeDtypeStruct((tiles, SHELLS, BX * BY, LANES), jnp.bfloat16),
            jax.ShapeDtypeStruct((tiles, SHELLS, LANES, BZ), jnp.bfloat16),
        ),
        in_specs=[ANY] * 4,
        out_specs=(VMEM, VMEM),
        scratch_shapes=[
            pltpu.VMEM((3, tiles * GEO, LANES), jnp.bfloat16),
            pltpu.SemaphoreType.DMA((3,)),
        ],
        compiler_params=pltpu.CompilerParams(vmem_limit_bytes=10 << 20),
        cost_estimate=pl.CostEstimate(flops=5_000_000_000, bytes_accessed=4_000_000, transcendentals=2_000_000),
        name="profiles",
    )(geos, mate_geos, third_geos, gram)

    sign_next, coef = pl.pallas_call(
        functools.partial(step_kernel, len(late_values)),
        out_shape=(
            jax.ShapeDtypeStruct((slots, size, size), jnp.bfloat16),
            jax.ShapeDtypeStruct((8, LANES), jnp.float32),
        ),
        in_specs=[SMEM, SMEM, VMEM, VMEM, VMEM, VMEM] + [ANY] * (len(late_values) + 1),
        out_specs=(VMEM, VMEM),
        scratch_shapes=[
            pltpu.VMEM((total - late_from, LANES), jnp.bfloat16),
            pltpu.VMEM((full, full), jnp.bfloat16),
            pltpu.VMEM((size, full), jnp.bfloat16),
            pltpu.VMEM((size, full), jnp.bfloat16),
            pltpu.SemaphoreType.DMA((len(late_values),)),
        ],
        compiler_params=pltpu.CompilerParams(vmem_limit_bytes=(15 << 20) + (total - late_from) * LANES * 2),
        cost_estimate=pl.CostEstimate(flops=1_300_000_000, bytes_accessed=8_000_000, transcendentals=0),
        name="square_cube_coefficients",
    )(late_table, info, own_basis, spread, own, gram, *late_values, line)

    triples = [(coef, from_offset(coef, "layer", -1), from_offset(coef, "layer", 1))]
    for di in others:
        step = steps[di]
        triples.append(
            (
                on_row(coef, di),
                from_row_layer(coef, step, lambda j: j - 1),
                from_row_layer(coef, step, lambda j: j + 1),
            )
        )
    stacked = jnp.concatenate(
        [
            jnp.concatenate(
                [
                    here[:, : 4 * SPAN],
                    below[:, SPAN : 3 * SPAN],
                    above[:, 3 * SPAN : 4 * SPAN],
                    jnp.zeros((8, LANES - 7 * SPAN), jnp.float32),
                ],
                axis=1,
            )
            for here, below, above in triples
        ],
        axis=0,
    )
    received = [from_offset(stacked, "col", dc) for dc in column_steps[1:]]
    line = line.reshape(tiles * SHELLS * LANES, BZ)

    def density_of(parts, coefs, extra, name):
        inputs = len(coefs) + 2
        return pl.pallas_call(
            functools.partial(density_kernel, tuple(parts), inputs),
            out_shape=jax.ShapeDtypeStruct((BX * BY, BZ), jnp.float32),
            in_specs=[VMEM] * (inputs + len(extra)),
            out_specs=VMEM,
            scratch_shapes=[pltpu.VMEM((BX * BY, len(parts) * SHELLS * LANES), jnp.bfloat16)],
            compiler_params=pltpu.CompilerParams(vmem_limit_bytes=16 << 20),
            cost_estimate=pl.CostEstimate(flops=310_000_000, bytes_accessed=4_000_000, transcendentals=0),
            name=name,
        )(*coefs, plane, line, *extra)

    density = density_of([(di, 0, 8 * di) for di in range(count)], [stacked], [], "density_column")
    sides = [((k + 1) * count + di, k, 8 * di) for k in range(2) for di in range(count)]
    density = density_of(sides, received, [density], "density_sides")
    return sign_next[None], density.reshape(BX, BY, BZ)


def solution(mesh):
    rows = P(("row", "col", "layer"), None, None, None)
    in_specs = (rows, P(), P(), P(), P(("row", "col", "layer"), None), P(), P(), P())
    out_specs = (rows, P("row", "col", "layer"))
    return jax.shard_map(local, mesh=mesh, in_specs=in_specs, out_specs=out_specs, check_vma=False)
```

```python
import functools

import jax
import jax.numpy as jnp
from jax import lax
from jax.experimental import pallas as pl
from jax.experimental.pallas import tpu as pltpu
from jax.sharding import PartitionSpec as P

BX = 16
BY = 16
BZ = 128
LANES = 128
UNROLL = 4
SHELLS = 6
SPAN = 3 * SHELLS
GEO = 16
VMEM = pl.BlockSpec(memory_space=pltpu.VMEM)
SMEM = pl.BlockSpec(memory_space=pltpu.SMEM)
ANY = pl.BlockSpec(memory_space=pl.ANY)
HBM = pl.BlockSpec(memory_space=pltpu.HBM)


def from_offset(x, axis, step):
    count = lax.axis_size(axis)
    return lax.ppermute(x, axis, [((i + step) % count, i) for i in range(count)])


def from_row_layer(x, step, mover):
    rows, layers = lax.axis_size("row"), lax.axis_size("layer")
    moves = [
        (((i + step) % rows) * layers + mover(j) % layers, i * layers + j) for i in range(rows) for j in range(layers)
    ]
    return lax.ppermute(x, ("row", "layer"), moves)


def from_layer(x, flip):
    count = lax.axis_size("layer")
    return lax.ppermute(x, "layer", [(i ^ flip, i) for i in range(count)])


def column_targets(n_row):
    return 5 if n_row == 2 else 7


def target_place(n_row, step_row, step_lay, row):
    same = jnp.where(step_lay < 3, step_lay, -1)
    if n_row == 2:
        lead = step_lay - row
        across = jnp.where((lead >= 0) & (lead < 2), 3 + lead, -1)
    else:
        across = 3 + step_lay
    return jnp.where(step_row == 0, same, jnp.where(step_row == 1, across, -1))


class Places:
    def __init__(self, n_row, n_col, n_lay):
        self.n_row, self.n_col, self.n_lay = n_row, n_col, n_lay
        self.lay_bits = n_lay.bit_length() - 1
        self.col_bits = n_col.bit_length() - 1
        self.row = lax.axis_index("row")
        self.col = lax.axis_index("col")
        self.lay = lax.axis_index("layer")
        self.me = (((self.row << self.col_bits) + self.col) << self.lay_bits) + self.lay

    def split(self, atom):
        return (
            atom >> (self.lay_bits + self.col_bits),
            (atom >> self.lay_bits) & (self.n_col - 1),
            atom & (self.n_lay - 1),
        )


def load(sources, targets, sems):
    copies = [pltpu.make_async_copy(a, b, sems.at[i]) for i, (a, b) in enumerate(zip(sources, targets))]
    for copy in copies:
        copy.start()
    for copy in copies:
        copy.wait()


def own_ranks(at, neighbors_ref):
    seen = [jnp.int32(0)] * at.n_lay
    listed = []
    for w in range(neighbors_ref.shape[0]):
        atom = neighbors_ref[w, at.me]
        step_lay = (atom - at.lay) & (at.n_lay - 1)
        rank = jnp.int32(0)
        for k in range(at.n_lay):
            rank = jnp.where(step_lay == k, 3 * k + seen[k], rank)
            seen[k] = seen[k] + (step_lay == k).astype(jnp.int32)
        listed.append((atom, rank))
    return listed


def pick_kernel(axes, *refs):
    sign_ref, out_ref, geo_ref, neighbors_ref, extent_ref, x_ref, y_ref, z_ref, place_ref, loads, sems = refs[5:]
    at = Places(*axes)
    slots = sign_ref.shape[0]
    n_pick = place_ref.shape[0] - 1
    size = sign_ref.shape[1]
    for i in range(n_pick + 1):
        place_ref[i] = 0
    load(refs[:5], (neighbors_ref, extent_ref, x_ref, y_ref, z_ref), loads)
    ranks = own_ranks(at, neighbors_ref)
    for w, (atom, _) in enumerate(ranks):
        row, col, lay = at.split(atom)
        place = target_place(at.n_row, (row - at.row) & (at.n_row - 1), (lay - at.lay) & (at.n_lay - 1), at.row)
        place_ref[jnp.where((col == at.col) & (place >= 0), place, n_pick)] = w
    copies = []
    for i in range(n_pick):
        copy = pltpu.make_async_copy(sign_ref.at[place_ref[i]], out_ref.at[pl.ds(i * size, size)], sems.at[i])
        copy.start()
        copies.append(copy)
    sub = lax.broadcasted_iota(jnp.int32, (GEO, LANES), 0)
    lane_pair = lax.broadcasted_iota(jnp.int32, (GEO, LANES), 1) // SHELLS
    geo = jnp.zeros((GEO, LANES), jnp.int32)
    for w, (atom, rank) in enumerate(ranks):
        row, col, lay = at.split(atom)
        go_row = ((row - at.row + 1) & (at.n_row - 1)) - 1
        go_col = ((col - at.col + 1) & (at.n_col - 1)) - 1
        go_lay = jnp.minimum(((lay - at.lay + 1) & (at.n_lay - 1)) - 1, 1)
        twice_x = x_ref[at.me] + x_ref[atom] + BX * go_row
        twice_y = y_ref[at.me] + y_ref[atom] + BY * go_col
        twice_z = z_ref[at.me] + z_ref[atom] + BZ * go_lay - BZ
        extent = extent_ref[0, w]
        values = jnp.where(sub == 0, twice_x, jnp.where(sub == 1, twice_y, jnp.where(sub == 2, twice_z, extent)))
        geo = jnp.where(lane_pair == rank, values, geo)
    geo = geo.astype(jnp.float32).astype(geo_ref.dtype)
    geo_ref[...] = geo
    out_ref[n_pick * size :] = geo
    for copy in copies:
        copy.wait()


def prepare_kernel(axes, count, layout, late_from, *refs):
    basis_ref = refs[2]
    early_ref, late_ref, info_ref, spread_ref, own_basis_ref = refs[-11:-6]
    neighbors_ref, size_ref, known, inverse, layout_ref, loads = refs[-6:]
    at = Places(*axes)
    load(refs[:2], (neighbors_ref, size_ref), loads)
    slots, atoms = neighbors_ref.shape
    bits = atoms.bit_length() - 1
    for i, value in enumerate(layout):
        layout_ref[i] = value
    lines = count * at.n_lay

    def hot(rows, atom, first):
        sub = lax.broadcasted_iota(jnp.int32, (rows, SHELLS * atoms), 0)
        lane = lax.broadcasted_iota(jnp.int32, (rows, SHELLS * atoms), 1)
        return ((lane & (atoms - 1)) == atom) & (sub == first + (lane >> bits))

    def rows_of(chosen):
        picked = jnp.where(chosen, 1.0, 0.0).astype(jnp.bfloat16)
        return jnp.dot(picked, basis_ref[...], preferred_element_type=jnp.float32).astype(jnp.bfloat16)

    self_slot = jnp.int32(0)
    for w, (atom, rank) in enumerate(own_ranks(at, neighbors_ref)):
        row, col, lay = at.split(atom)
        step_row = (row - at.row) & (at.n_row - 1)
        step_col = (col - at.col) & (at.n_col - 1)
        self_slot = jnp.where(atom == at.me, w, self_slot)
        info_ref[w] = size_ref[atom]
        spread_ref[:, w * LANES : (w + 1) * LANES] = rows_of(hot(LANES, atom, rank * SHELLS))
        flip = lay ^ at.lay
        known[0, w] = atom
        known[1, w] = jnp.where(step_col == 0, 0, jnp.where(step_col == 1, 1, 2))
        known[2, w] = jnp.where(step_row == 0, 0, jnp.where(step_row == 1, 1, 2)) * at.n_lay + flip
        inverse[atom] = -1
    own_basis_ref[...] = rows_of(hot(16, at.me, 0))
    info_ref[slots] = size_ref[at.me]
    info_ref[slots + 1] = self_slot

    def row_of_pairs(v, totals):
        early, late = totals
        atom = known[0, v]
        side = known[1, v]
        line = known[2, v]
        row, _, lay = at.split(atom)
        for u in range(slots):
            inverse[neighbors_ref[u, atom]] = v * 16 + u
        top = layout_ref[line]
        end = layout_ref[lines + line]
        beside = layout_ref[(side + 1) * lines + line]
        half = slots // 2
        for w in range(slots):
            other = known[0, w]
            other_side = known[1, w]
            mark = inverse[other]
            slot = mark & 15
            o_row, _, o_lay = at.split(other)
            there = target_place(at.n_row, (o_row - row) & (at.n_row - 1), (o_lay - lay) & (at.n_lay - 1), row)
            back = target_place(at.n_row, (row - o_row) & (at.n_row - 1), (lay - o_lay) & (at.n_lay - 1), o_row)
            from_row = (other_side != 0) | (v <= w)
            from_column = (side == other_side) & (there >= 0) & ((back < 0) | (v <= w))
            chosen = ((mark >> 4) == v) & jnp.where(side == 0, from_row, from_column)
            in_row = jnp.where(slot < half, top + slot * LANES, end + (slot - half) * LANES)
            where = jnp.where(side == 0, in_row, beside + there * LANES)
            is_late = where >= late_from
            for ref, total in ((early_ref, early), (late_ref, late)):
                ref[3 * total + 1] = v
                ref[3 * total + 2] = w
                ref[3 * total + 3] = where
            late_ref[3 * late + 3] = where - late_from
            early = early + (chosen & ~is_late).astype(jnp.int32)
            late = late + (chosen & is_late).astype(jnp.int32)
        return early, late

    totals = lax.fori_loop(0, slots, row_of_pairs, (jnp.int32(0), jnp.int32(0)))
    for ref, total in zip((early_ref, late_ref), totals):
        ref[0] = (total + UNROLL - 1) // UNROLL
        last = 3 * jnp.maximum(total - 1, 0) + 1
        for i in range(UNROLL - 1):
            for k in range(3):
                ref[3 * (total + i) + 1 + k] = ref[last + k]


def pack_kernel(moves, inputs, outputs, *refs):
    sems = refs[-1]
    copies = []
    for k, (source, start, rows, target, place) in enumerate(moves):
        copy = pltpu.make_async_copy(
            refs[source].at[pl.ds(start, rows)], refs[inputs + target].at[pl.ds(place, rows)], sems.at[k]
        )
        copy.start()
        copies.append(copy)
    for copy in copies:
        copy.wait()


def pack(values, plans, extra, name):
    moves, shapes = [], []
    for target, plan in enumerate(plans):
        place = 0
        for source, start, rows in plan:
            moves.append((source, start, rows, target, place))
            place += rows
        shapes.append(jax.ShapeDtypeStruct((place, LANES), values[0].dtype))
    inputs = len(values) + len(extra)
    return pl.pallas_call(
        functools.partial(pack_kernel, tuple(moves), inputs, len(plans)),
        out_shape=tuple(shapes),
        in_specs=[ANY] * inputs,
        out_specs=tuple([ANY] * len(plans)),
        scratch_shapes=[pltpu.SemaphoreType.DMA((len(moves),))],
        compiler_params=pltpu.CompilerParams(vmem_limit_bytes=1 << 20),
        cost_estimate=pl.CostEstimate(flops=0, bytes_accessed=1000, transcendentals=0),
        name=name,
    )(*values, *extra)


def fill(piece_refs, pool, sems):
    copies = []
    place = 0
    for i, piece in enumerate(piece_refs):
        rows = piece.shape[0]
        copy = pltpu.make_async_copy(piece, pool.at[pl.ds(place, rows)], sems.at[i])
        copy.start()
        copies.append(copy)
        place += rows
    return copies


def place_pairs(table_ref, pool, gram, size):
    def place(i, carry):
        for k in range(UNROLL):
            entry = 3 * (i * UNROLL + k)
            p = pl.multiple_of(table_ref[entry + 1] * size, size)
            q = pl.multiple_of(table_ref[entry + 2] * size, size)
            block = pool[pl.ds(pl.multiple_of(table_ref[entry + 3], 16), size)]
            gram[pl.ds(p, size), pl.ds(q, size)] = block
            gram[pl.ds(q, size), pl.ds(p, size)] = block.T
        return carry

    lax.fori_loop(0, table_ref[0], place, 0)


def gram_kernel(pieces, *refs):
    table_ref = refs[0]
    piece_refs = refs[1 : 1 + pieces]
    gram, pool, sems = refs[-3:]
    size = LANES
    copies = fill(piece_refs, pool, sems)
    for v in range(gram.shape[0] // size):
        gram[v * size : (v + 1) * size] = jnp.zeros((size, gram.shape[1]), gram.dtype)
    for copy in copies:
        copy.wait()
    place_pairs(table_ref, pool, gram, size)


def step_kernel(pieces, *refs):
    table_ref, info_ref, basis_ref, spread_ref, sign_ref, early_ref = refs[:6]
    piece_refs = refs[6 : 6 + pieces]
    next_ref, coef_ref, pool, gram, own, square, sems = refs[-7:]
    slots, size = sign_ref.shape[0], sign_ref.shape[1]
    copies = fill(piece_refs, pool, sems)
    for v in range(slots):
        gram[v * size : (v + 1) * size] = early_ref[v * size : (v + 1) * size]
    rows = lax.broadcasted_iota(jnp.int32, (size, size), 0)
    lanes = lax.broadcasted_iota(jnp.int32, (size, size), 1)
    own_size = info_ref[slots]
    self_slot = info_ref[slots + 1]
    for w in range(slots):
        kept = (rows < own_size) & (lanes < info_ref[w])
        block = jnp.where(kept, sign_ref[w].astype(jnp.float32), 0.0)
        own[:, w * size : (w + 1) * size] = block.astype(own.dtype)
    for copy in copies:
        copy.wait()
    place_pairs(table_ref, pool, gram, size)
    wide = 2 * size
    wide_lanes = lax.broadcasted_iota(jnp.int32, (size, wide), 1)
    wide_rows = lax.broadcasted_iota(jnp.int32, (size, wide), 0)

    def column_kept(n):
        first = info_ref[2 * n]
        second = info_ref[2 * n + 1]
        return (wide_lanes < first) | ((wide_lanes >= size) & (wide_lanes < size + second))

    for n in range(slots // 2):
        part = jnp.dot(own[...], gram[:, n * wide : (n + 1) * wide], preferred_element_type=jnp.float32)
        square[:, n * wide : (n + 1) * wide] = jnp.where(column_kept(n), part, 0.0).astype(square.dtype)
    basis = jnp.concatenate([basis_ref[...], basis_ref[...]], axis=1)
    coef = jnp.zeros((2 * basis_ref.shape[0], LANES), jnp.float32)
    across = (((1,), (1,)), ((), ()))
    for n in range(slots // 2):
        part = jnp.dot(square[...], gram[:, n * wide : (n + 1) * wide], preferred_element_type=jnp.float32)
        cube = jnp.where(column_kept(n), part, 0.0)
        full = 1.5 * own[:, n * wide : (n + 1) * wide].astype(jnp.float32) - 0.5 * cube
        next_ref[2 * n] = full[:, :size].astype(next_ref.dtype)
        next_ref[2 * n + 1] = full[:, size:].astype(next_ref.dtype)
        shift = (self_slot - 2 * n) * size
        is_self = (self_slot >= 2 * n) & (self_slot < 2 * n + 2)
        diag = (wide_lanes == wide_rows + shift) & (wide_rows < own_size) & is_self
        dmat = 0.5 * (jnp.where(diag, 1.0, 0.0) - full)
        high = dmat.astype(jnp.bfloat16)
        low = (dmat - high.astype(jnp.float32)).astype(jnp.bfloat16)
        half = jnp.dot(basis, jnp.concatenate([high, low], axis=0), preferred_element_type=jnp.float32)
        half_high = half.astype(jnp.bfloat16)
        half_low = (half - half_high.astype(jnp.float32)).astype(jnp.bfloat16)
        coef = coef + lax.dot_general(
            jnp.concatenate([half_high, half_low], axis=0),
            spread_ref[:, n * wide : (n + 1) * wide],
            across,
            preferred_element_type=jnp.float32,
        )
    coef = coef[: basis_ref.shape[0]] + coef[basis_ref.shape[0] :]
    coef_ref[...] = coef[: coef_ref.shape[0]]


def profile_kernel(periods, steps, *refs):
    plane_ref, line_ref, geos, sems = refs[-4:]
    odd = (lax.axis_index("layer") & 1) == 1
    copies = []
    for k in range(3):
        copy = pltpu.make_async_copy(refs[k], geos.at[k], sems.at[k])
        copy.start()
        copies.append(copy)
    cells = plane_ref.shape[2]
    cell = lax.broadcasted_iota(jnp.int32, (cells, LANES), 0)
    grid_x = (cell // BY).astype(jnp.float32)
    grid_y = (cell % BY).astype(jnp.float32)
    grid_z = lax.broadcasted_iota(jnp.int32, (LANES, BZ), 1).astype(jnp.float32)
    lane = lax.broadcasted_iota(jnp.int32, (1, LANES), 1)
    shell = (lane % SHELLS + 1).astype(jnp.float32)
    valid = lane < 7 * SPAN
    from_own = lane < 4 * SPAN
    from_below = lane < 6 * SPAN
    lift = jnp.where(from_own, 0.0, jnp.where(from_below, -float(BZ), float(BZ))) + 0.5 * BZ

    def nearest(offset, period):
        return offset - period * jnp.floor(offset * (1.0 / period) + 0.5)

    for copy in copies:
        copy.wait()
    for o, (place, step_row, step_col) in enumerate(steps):
        own, first, third = (geos[k, place * GEO : (place + 1) * GEO].astype(jnp.float32) for k in range(3))
        below = jnp.where(odd, first, third)
        above = jnp.where(odd, third, first)
        moved = jnp.where(from_below, pltpu.roll(below, 3 * SPAN, axis=1), pltpu.roll(above, 3 * SPAN, axis=1))
        geo = jnp.where(from_own, own, moved)
        extent = jnp.where(valid, geo[3:4], 1.0)
        inverse = (SHELLS / extent) * (SHELLS / extent)
        reach = jnp.where(valid, extent, -1.0)
        rate_t = inverse / (shell * shell)
        packed = jnp.concatenate(
            [0.5 * geo[2:3] + lift, reach, rate_t, inverse, jnp.zeros((4, LANES), jnp.float32)], axis=0
        )
        sub = packed.T
        d_x = nearest(grid_x - (0.5 * geo[0:1] + float(BX * step_row)), periods[0])
        d_y = nearest(grid_y - (0.5 * geo[1:2] + float(BY * step_col)), periods[1])
        inside = (jnp.abs(d_x) <= reach) & (jnp.abs(d_y) <= reach)
        squared = d_x * d_x + d_y * d_y
        d_z = nearest(grid_z - sub[:, 0:1], periods[2])
        inside_z = jnp.abs(d_z) <= sub[:, 1:2]
        squared_z = d_z * d_z
        for s in range(SHELLS):
            part = 1.0 / ((s + 1) * (s + 1))
            rate = inverse * part + rate_t
            plane_ref[o, s] = jnp.where(inside, jnp.exp(-rate * squared), 0.0).astype(plane_ref.dtype)
            rate_z = sub[:, 3:4] * part + sub[:, 2:3]
            line_ref[o, s] = jnp.where(inside_z, jnp.exp(-rate_z * squared_z), 0.0).astype(line_ref.dtype)


def density_kernel(tiles, inputs, *refs):
    coef_refs = refs[: inputs - 2]
    plane_ref, line_ref = refs[inputs - 2 : inputs]
    out_ref, terms = refs[-2:]
    for i, (o, source, first) in enumerate(tiles):
        for s in range(SHELLS):
            scaled = plane_ref[o, s].astype(jnp.float32) * coef_refs[source][first + s : first + s + 1, :]
            at = (i * SHELLS + s) * LANES
            terms[:, at : at + LANES] = scaled.astype(terms.dtype)
    start = tiles[0][0] * SHELLS * LANES
    summed = jnp.dot(
        terms[...], line_ref[start : start + len(tiles) * SHELLS * LANES], preferred_element_type=jnp.float32
    )
    if len(refs) > inputs + 2:
        summed = summed + refs[inputs][...]
    out_ref[...] = summed


def local(sign_start, neighbors, atom_size, basis_proj, pair_extent, atom_x, atom_y, atom_z):
    n_row = lax.axis_size("row")
    n_col = lax.axis_size("col")
    n_lay = lax.axis_size("layer")
    assert n_lay == 4 and n_col >= 4 and (n_row == 2 or n_row >= 4)
    assert n_row & (n_row - 1) == 0 and n_col & (n_col - 1) == 0
    axes = (n_row, n_col, n_lay)
    atoms, slots = neighbors.shape
    size = sign_start.shape[2]
    steps = [0, 1] if n_row == 2 else [0, 1, -1]
    count = len(steps)
    others = range(1, count)
    own = sign_start[0]
    flat = own.reshape(slots * size, size)
    listings = neighbors.T
    full = slots * size
    half = full // 2
    n_pick = column_targets(n_row)
    picks = n_pick * size
    part = picks + GEO
    kinds = ("geo", "up geo", "down geo")

    def on_row(value, di):
        return from_offset(value, "row", steps[di])

    picked, geo = pl.pallas_call(
        functools.partial(pick_kernel, axes),
        out_shape=(
            jax.ShapeDtypeStruct((part, size), own.dtype),
            jax.ShapeDtypeStruct((GEO, LANES), own.dtype),
        ),
        in_specs=[HBM] * 6,
        out_specs=(VMEM, VMEM),
        scratch_shapes=[
            pltpu.SMEM((slots, atoms), jnp.int32),
            pltpu.SMEM((1, slots), jnp.int32),
            pltpu.SMEM((atoms,), jnp.int32),
            pltpu.SMEM((atoms,), jnp.int32),
            pltpu.SMEM((atoms,), jnp.int32),
            pltpu.SMEM((n_pick + 1,), jnp.int32),
            pltpu.SemaphoreType.DMA((5,)),
            pltpu.SemaphoreType.DMA((n_pick,)),
        ],
        compiler_params=pltpu.CompilerParams(vmem_limit_bytes=60 << 20),
        name="pick_column_blocks",
    )(listings, pair_extent, atom_x, atom_y, atom_z, own)
    x_row = {di: on_row(flat, di) for di in others}
    far = from_layer(flat, 2)
    up = from_offset(picked, "col", 1)
    down = from_offset(picked, "col", -1)
    quarter = half // 2
    halves = pack(
        [far] + [x_row[di] for di in others],
        [[(0, half + k * quarter, quarter)] for k in range(2)]
        + [[(di, k * quarter, quarter)] for di in others for k in range(2)],
        [],
        "pack_halves",
    )
    ends = {(di, k): on_row(halves[k], di) for di in others for k in range(2)}
    tops = {(di, k): from_layer(halves[2 * di + k], 2) for di in others for k in range(2)}
    corners = [(di, k) for di in others for k in range(2)]
    mate = from_layer(flat, 1)

    beside = pack(
        [up, down, geo],
        [[(0, 0, picks), (1, 0, picks), (2, 0, GEO), (0, picks, GEO), (1, picks, GEO)]],
        [ends[key] for key in corners] + [tops[key] for key in corners],
        "pack_beside",
    )[0]
    side_x = {di: on_row(beside, di) for di in others}
    side_y = from_layer(beside, 2)
    side_d = {di: from_row_layer(beside, steps[di], lambda j: j ^ 2) for di in others}
    mate_side = from_layer(beside, 1)

    def row_of(di, flip):
        return [(("top", di, flip), half), (("end", di, flip), half)]

    def side_of(di, flip):
        return [(("up", di, flip), picks), (("down", di, flip), picks), (None, 3 * GEO)]

    early = [(flat, row_of(0, 0)), (mate, row_of(0, 1)), (far, row_of(0, 2))]
    early += [(x_row[di], row_of(di, 0)) for di in others]
    for name, parts in (("end", ends), ("top", tops)):
        for di in others:
            early += [(parts[di, 0], [((name, di, 2), quarter)]), (parts[di, 1], [(None, quarter)])]
    early += [(beside, side_of(0, 0))]
    content = sum([row_of(di, 1) for di in others], []) + row_of(0, 3)
    content += [(("end", di, 3), half) for di in others] + [(("top", di, 3), half) for di in others]
    early += [(None, content), (mate_side, side_of(0, 1))]
    located = {}
    total = 0
    for _, content in early:
        for what, length in content:
            located[what] = total
            total += length
    late_from = total
    late = [side_of(di, 0) for di in others] + [side_of(di, 1) for di in others]
    late += [side_of(0, 2), side_of(0, 3)]
    late += [side_of(di, 2) for di in others] + [side_of(di, 3) for di in others]
    for content in late:
        for what, length in content:
            located[what] = total
            total += length
    layout = [
        located[kind, di, flip]
        for kind in ("top", "end", "up", "down")
        for di in range(count)
        for flip in range(n_lay)
    ]

    pairs = slots * (slots + 1) // 2
    entries = 3 * (pairs + UNROLL) + 1
    early_table, late_table, info, spread, own_basis = pl.pallas_call(
        functools.partial(prepare_kernel, axes, count, tuple(layout), late_from),
        out_shape=(
            jax.ShapeDtypeStruct((entries,), jnp.int32),
            jax.ShapeDtypeStruct((entries,), jnp.int32),
            jax.ShapeDtypeStruct((slots + 2,), jnp.int32),
            jax.ShapeDtypeStruct((LANES, full), jnp.bfloat16),
            jax.ShapeDtypeStruct((16, size), jnp.bfloat16),
        ),
        in_specs=[HBM, HBM, VMEM, ANY],
        out_specs=(SMEM, SMEM, SMEM, VMEM, VMEM),
        scratch_shapes=[
            pltpu.SMEM((slots, atoms), jnp.int32),
            pltpu.SMEM((atoms,), jnp.int32),
            pltpu.SMEM((3, slots), jnp.int32),
            pltpu.SMEM((atoms,), jnp.int32),
            pltpu.SMEM((len(layout),), jnp.int32),
            pltpu.SemaphoreType.DMA((2,)),
        ],
        compiler_params=pltpu.CompilerParams(vmem_limit_bytes=(2 << 20) + atoms * 16384),
        cost_estimate=pl.CostEstimate(flops=1000, bytes_accessed=1000, transcendentals=0),
        name="prepare",
    )(listings, atom_size, basis_proj.transpose(1, 0, 2).reshape(SHELLS * atoms, size), beside)

    rows = [x_row[di] for di in others] + [far] + [ends[key] for key in corners] + [tops[key] for key in corners]
    to_mate = pack(rows, [[(i, 0, value.shape[0]) for i, value in enumerate(rows)]], [beside], "pack_mate")[0]
    mate_rows = from_layer(to_mate, 1)

    geos = pack(
        [beside] + [side_x[di] for di in others], [[(di, 2 * picks, 3 * GEO) for di in range(count)]], [own_basis], "pack_geos"
    )[0]
    mate_geos = from_layer(geos, 1)
    third_geos = from_layer(geos, 3)

    early_values = [mate_rows if value is None else value for value, _ in early]
    gram = pl.pallas_call(
        functools.partial(gram_kernel, len(early_values)),
        out_shape=jax.ShapeDtypeStruct((full, full), jnp.bfloat16),
        in_specs=[SMEM] + [ANY] * (len(early_values) + 2),
        out_specs=VMEM,
        scratch_shapes=[
            pltpu.VMEM((late_from, LANES), jnp.bfloat16),
            pltpu.SemaphoreType.DMA((len(early_values),)),
        ],
        compiler_params=pltpu.CompilerParams(vmem_limit_bytes=(6 << 20) + late_from * LANES * 2),
        cost_estimate=pl.CostEstimate(flops=1000, bytes_accessed=1000, transcendentals=0),
        name="gram_early",
    )(early_table, *early_values, mate_geos, third_geos)

    diagonal = [side_d[di] for di in others]
    if len(diagonal) == 1:
        diagonal = pack(diagonal, [[(0, 0, 2 * picks + 3 * GEO)]], [gram], "pack_diagonal")
    late_values = [side_x[di] for di in others] + [from_layer(side_x[di], 1) for di in others]
    late_values += [side_y, from_layer(side_y, 1)]
    late_values += diagonal
    late_values += [from_layer(value, 1) for value in diagonal]

    column_steps = (0, 1, -1)
    tile_steps = [(di * 3 + k, steps[di], dc) for k, dc in enumerate(column_steps) for di in range(count)]
    tiles = len(tile_steps)
    periods = (float(BX * n_row), float(BY * n_col), float(BZ * n_lay))
    plane, line = pl.pallas_call(
        functools.partial(profile_kernel, periods, tile_steps),
        out_shape=(
            jax.ShapeDtypeStruct((tiles, SHELLS, BX * BY, LANES), jnp.bfloat16),
            jax.ShapeDtypeStruct((tiles, SHELLS, LANES, BZ), jnp.bfloat16),
        ),
        in_specs=[ANY] * 4,
        out_specs=(VMEM, VMEM),
        scratch_shapes=[
            pltpu.VMEM((3, tiles * GEO, LANES), jnp.bfloat16),
            pltpu.SemaphoreType.DMA((3,)),
        ],
        compiler_params=pltpu.CompilerParams(vmem_limit_bytes=10 << 20),
        cost_estimate=pl.CostEstimate(flops=1000, bytes_accessed=1000, transcendentals=0),
        name="profiles",
    )(geos, mate_geos, third_geos, gram)

    sign_next, coef = pl.pallas_call(
        functools.partial(step_kernel, len(late_values)),
        out_shape=(
            jax.ShapeDtypeStruct((slots, size, size), jnp.bfloat16),
            jax.ShapeDtypeStruct((8, LANES), jnp.float32),
        ),
        in_specs=[SMEM, SMEM, VMEM, VMEM, VMEM, VMEM] + [ANY] * (len(late_values) + 1),
        out_specs=(VMEM, VMEM),
        scratch_shapes=[
            pltpu.VMEM((total - late_from, LANES), jnp.bfloat16),
            pltpu.VMEM((full, full), jnp.bfloat16),
            pltpu.VMEM((size, full), jnp.bfloat16),
            pltpu.VMEM((size, full), jnp.bfloat16),
            pltpu.SemaphoreType.DMA((len(late_values),)),
        ],
        compiler_params=pltpu.CompilerParams(vmem_limit_bytes=(15 << 20) + (total - late_from) * LANES * 2),
        cost_estimate=pl.CostEstimate(flops=1_300_000_000, bytes_accessed=8_000_000, transcendentals=0),
        name="square_cube_coefficients",
    )(late_table, info, own_basis, spread, own, gram, *late_values, line)

    triples = [(coef, from_offset(coef, "layer", -1), from_offset(coef, "layer", 1))]
    for di in others:
        step = steps[di]
        triples.append(
            (
                on_row(coef, di),
                from_row_layer(coef, step, lambda j: j - 1),
                from_row_layer(coef, step, lambda j: j + 1),
            )
        )
    stacked = jnp.concatenate(
        [
            jnp.concatenate(
                [
                    here[:, : 4 * SPAN],
                    below[:, SPAN : 3 * SPAN],
                    above[:, 3 * SPAN : 4 * SPAN],
                    jnp.zeros((8, LANES - 7 * SPAN), jnp.float32),
                ],
                axis=1,
            )
            for here, below, above in triples
        ],
        axis=0,
    )
    received = [from_offset(stacked, "col", dc) for dc in column_steps[1:]]
    line = line.reshape(tiles * SHELLS * LANES, BZ)

    def density_of(parts, coefs, extra, name):
        inputs = len(coefs) + 2
        return pl.pallas_call(
            functools.partial(density_kernel, tuple(parts), inputs),
            out_shape=jax.ShapeDtypeStruct((BX * BY, BZ), jnp.float32),
            in_specs=[VMEM] * (inputs + len(extra)),
            out_specs=VMEM,
            scratch_shapes=[pltpu.VMEM((BX * BY, len(parts) * SHELLS * LANES), jnp.bfloat16)],
            compiler_params=pltpu.CompilerParams(vmem_limit_bytes=16 << 20),
            cost_estimate=pl.CostEstimate(flops=310_000_000, bytes_accessed=4_000_000, transcendentals=0),
            name=name,
        )(*coefs, plane, line, *extra)

    density = density_of([(di, 0, 8 * di) for di in range(count)], [stacked], [], "density_column")
    sides = [((k + 1) * count + di, k, 8 * di) for k in range(2) for di in range(count)]
    density = density_of(sides, received, [density], "density_sides")
    return sign_next[None], density.reshape(BX, BY, BZ)


def solution(mesh):
    rows = P(("row", "col", "layer"), None, None, None)
    in_specs = (rows, P(), P(), P(), P(("row", "col", "layer"), None), P(), P(), P())
    out_specs = (rows, P("row", "col", "layer"))
    return jax.shard_map(local, mesh=mesh, in_specs=in_specs, out_specs=out_specs, check_vma=False)
```

```python
import functools

import jax
import jax.numpy as jnp
from jax import lax
from jax.experimental import pallas as pl
from jax.experimental.pallas import tpu as pltpu
from jax.sharding import PartitionSpec as P

BX = 16
BY = 16
BZ = 128
LANES = 128
UNROLL = 4
SHELLS = 6
SPAN = 3 * SHELLS
GEO = 16
VMEM = pl.BlockSpec(memory_space=pltpu.VMEM)
SMEM = pl.BlockSpec(memory_space=pltpu.SMEM)
ANY = pl.BlockSpec(memory_space=pl.ANY)
HBM = pl.BlockSpec(memory_space=pltpu.HBM)


def from_offset(x, axis, step):
    count = lax.axis_size(axis)
    return lax.ppermute(x, axis, [((i + step) % count, i) for i in range(count)])


def from_layer(x, flip):
    count = lax.axis_size("layer")
    return lax.ppermute(x, "layer", [(i ^ flip, i) for i in range(count)])


def column_targets(n_row):
    return 5 if n_row == 2 else 7


def target_place(n_row, step_row, step_lay, row):
    same = jnp.where(step_lay < 3, step_lay, -1)
    if n_row == 2:
        lead = step_lay - row
        across = jnp.where((lead >= 0) & (lead < 2), 3 + lead, -1)
    else:
        across = 3 + step_lay
    return jnp.where(step_row == 0, same, jnp.where(step_row == 1, across, -1))


class Places:
    def __init__(self, n_row, n_col, n_lay):
        self.n_row, self.n_col, self.n_lay = n_row, n_col, n_lay
        self.lay_bits = n_lay.bit_length() - 1
        self.col_bits = n_col.bit_length() - 1
        self.row = lax.axis_index("row")
        self.col = lax.axis_index("col")
        self.lay = lax.axis_index("layer")
        self.me = (((self.row << self.col_bits) + self.col) << self.lay_bits) + self.lay

    def split(self, atom):
        return (
            atom >> (self.lay_bits + self.col_bits),
            (atom >> self.lay_bits) & (self.n_col - 1),
            atom & (self.n_lay - 1),
        )


def load(sources, targets, sems):
    copies = [pltpu.make_async_copy(a, b, sems.at[i]) for i, (a, b) in enumerate(zip(sources, targets))]
    for copy in copies:
        copy.start()
    for copy in copies:
        copy.wait()


def own_ranks(at, neighbors_ref):
    seen = [jnp.int32(0)] * at.n_lay
    listed = []
    for w in range(neighbors_ref.shape[0]):
        atom = neighbors_ref[w, at.me]
        step_lay = (atom - at.lay) & (at.n_lay - 1)
        rank = jnp.int32(0)
        for k in range(at.n_lay):
            rank = jnp.where(step_lay == k, 3 * k + seen[k], rank)
            seen[k] = seen[k] + (step_lay == k).astype(jnp.int32)
        listed.append((atom, rank))
    return listed


def pick_kernel(axes, *refs):
    sign_ref, out_ref, geo_ref, neighbors_ref, extent_ref, x_ref, y_ref, z_ref, place_ref, loads, sems = refs[5:]
    at = Places(*axes)
    slots = sign_ref.shape[0]
    n_pick = place_ref.shape[0] - 1
    size = sign_ref.shape[1]
    for i in range(n_pick + 1):
        place_ref[i] = 0
    load(refs[:5], (neighbors_ref, extent_ref, x_ref, y_ref, z_ref), loads)
    ranks = own_ranks(at, neighbors_ref)
    for w, (atom, _) in enumerate(ranks):
        row, col, lay = at.split(atom)
        place = target_place(at.n_row, (row - at.row) & (at.n_row - 1), (lay - at.lay) & (at.n_lay - 1), at.row)
        place_ref[jnp.where((col == at.col) & (place >= 0), place, n_pick)] = w
    copies = []
    for i in range(n_pick):
        copy = pltpu.make_async_copy(sign_ref.at[place_ref[i]], out_ref.at[pl.ds(i * size, size)], sems.at[i])
        copy.start()
        copies.append(copy)
    sub = lax.broadcasted_iota(jnp.int32, (GEO, LANES), 0)
    lane_pair = lax.broadcasted_iota(jnp.int32, (GEO, LANES), 1) // SHELLS
    geo = jnp.zeros((GEO, LANES), jnp.int32)
    for w, (atom, rank) in enumerate(ranks):
        row, col, lay = at.split(atom)
        go_row = ((row - at.row + 1) & (at.n_row - 1)) - 1
        go_col = ((col - at.col + 1) & (at.n_col - 1)) - 1
        go_lay = jnp.minimum(((lay - at.lay + 1) & (at.n_lay - 1)) - 1, 1)
        twice_x = x_ref[at.me] + x_ref[atom] + BX * go_row
        twice_y = y_ref[at.me] + y_ref[atom] + BY * go_col
        twice_z = z_ref[at.me] + z_ref[atom] + BZ * go_lay - BZ
        extent = extent_ref[0, w]
        values = jnp.where(sub == 0, twice_x, jnp.where(sub == 1, twice_y, jnp.where(sub == 2, twice_z, extent)))
        geo = jnp.where(lane_pair == rank, values, geo)
    geo = geo.astype(jnp.float32).astype(geo_ref.dtype)
    geo_ref[...] = geo
    out_ref[n_pick * size :] = geo
    for copy in copies:
        copy.wait()


def prepare_kernel(axes, count, layout, late_from, *refs):
    basis_ref = refs[2]
    early_ref, late_ref, info_ref, spread_ref, own_basis_ref = refs[-11:-6]
    neighbors_ref, size_ref, known, inverse, layout_ref, loads = refs[-6:]
    at = Places(*axes)
    load(refs[:2], (neighbors_ref, size_ref), loads)
    slots, atoms = neighbors_ref.shape
    bits = atoms.bit_length() - 1
    for i, value in enumerate(layout):
        layout_ref[i] = value
    lines = count * at.n_lay

    def hot(rows, atom, first):
        sub = lax.broadcasted_iota(jnp.int32, (rows, SHELLS * atoms), 0)
        lane = lax.broadcasted_iota(jnp.int32, (rows, SHELLS * atoms), 1)
        return ((lane & (atoms - 1)) == atom) & (sub == first + (lane >> bits))

    def rows_of(chosen):
        picked = jnp.where(chosen, 1.0, 0.0).astype(jnp.bfloat16)
        return jnp.dot(picked, basis_ref[...], preferred_element_type=jnp.float32).astype(jnp.bfloat16)

    self_slot = jnp.int32(0)
    for w, (atom, rank) in enumerate(own_ranks(at, neighbors_ref)):
        row, col, lay = at.split(atom)
        step_row = (row - at.row) & (at.n_row - 1)
        step_col = (col - at.col) & (at.n_col - 1)
        self_slot = jnp.where(atom == at.me, w, self_slot)
        info_ref[w] = size_ref[atom]
        spread_ref[:, w * LANES : (w + 1) * LANES] = rows_of(hot(LANES, atom, rank * SHELLS))
        flip = lay ^ at.lay
        known[0, w] = atom
        known[1, w] = jnp.where(step_col == 0, 0, jnp.where(step_col == 1, 1, 2))
        known[2, w] = jnp.where(step_row == 0, 0, jnp.where(step_row == 1, 1, 2)) * at.n_lay + flip
        known[3, w] = jnp.where((step_row != 0) & (flip == 3), 16 + w, w)
        inverse[atom] = -1
    own_basis_ref[...] = rows_of(hot(16, at.me, 0))
    info_ref[slots] = size_ref[at.me]
    info_ref[slots + 1] = self_slot

    def row_of_pairs(v, totals):
        early, late = totals
        atom = known[0, v]
        side = known[1, v]
        line = known[2, v]
        turn = known[3, v]
        row, _, lay = at.split(atom)
        for u in range(slots):
            inverse[neighbors_ref[u, atom]] = v * 16 + u
        top = layout_ref[line]
        end = layout_ref[lines + line]
        beside = layout_ref[(side + 1) * lines + line]
        half = slots // 2
        for w in range(slots):
            other = known[0, w]
            other_side = known[1, w]
            mark = inverse[other]
            slot = mark & 15
            o_row, _, o_lay = at.split(other)
            there = target_place(at.n_row, (o_row - row) & (at.n_row - 1), (o_lay - lay) & (at.n_lay - 1), row)
            back = target_place(at.n_row, (row - o_row) & (at.n_row - 1), (lay - o_lay) & (at.n_lay - 1), o_row)
            from_row = (other_side != 0) | (turn <= known[3, w])
            from_column = (side == other_side) & (there >= 0) & ((back < 0) | (v <= w))
            chosen = ((mark >> 4) == v) & jnp.where(side == 0, from_row, from_column)
            in_row = jnp.where(slot < half, top + slot * LANES, end + (slot - half) * LANES)
            where = jnp.where(side == 0, in_row, beside + there * LANES)
            is_late = where >= late_from
            for ref, total in ((early_ref, early), (late_ref, late)):
                ref[3 * total + 1] = v
                ref[3 * total + 2] = w
                ref[3 * total + 3] = where
            late_ref[3 * late + 3] = where - late_from
            early = early + (chosen & ~is_late).astype(jnp.int32)
            late = late + (chosen & is_late).astype(jnp.int32)
        return early, late

    totals = lax.fori_loop(0, slots, row_of_pairs, (jnp.int32(0), jnp.int32(0)))
    for ref, total in zip((early_ref, late_ref), totals):
        ref[0] = (total + UNROLL - 1) // UNROLL
        last = 3 * jnp.maximum(total - 1, 0) + 1
        for i in range(UNROLL - 1):
            for k in range(3):
                ref[3 * (total + i) + 1 + k] = ref[last + k]


def pack_kernel(moves, inputs, outputs, *refs):
    sems = refs[-1]
    copies = []
    for k, (source, start, rows, target, place) in enumerate(moves):
        copy = pltpu.make_async_copy(
            refs[source].at[pl.ds(start, rows)], refs[inputs + target].at[pl.ds(place, rows)], sems.at[k]
        )
        copy.start()
        copies.append(copy)
    for copy in copies:
        copy.wait()


def pack(values, plans, extra, name):
    moves, shapes = [], []
    for target, plan in enumerate(plans):
        place = 0
        for source, start, rows in plan:
            moves.append((source, start, rows, target, place))
            place += rows
        shapes.append(jax.ShapeDtypeStruct((place, LANES), values[0].dtype))
    inputs = len(values) + len(extra)
    return pl.pallas_call(
        functools.partial(pack_kernel, tuple(moves), inputs, len(plans)),
        out_shape=tuple(shapes),
        in_specs=[ANY] * inputs,
        out_specs=tuple([ANY] * len(plans)),
        scratch_shapes=[pltpu.SemaphoreType.DMA((len(moves),))],
        compiler_params=pltpu.CompilerParams(vmem_limit_bytes=1 << 20),
        cost_estimate=pl.CostEstimate(flops=0, bytes_accessed=3_000_000, transcendentals=0),
        name=name,
    )(*values, *extra)


def fill(piece_refs, pool, sems):
    copies = []
    place = 0
    for i, piece in enumerate(piece_refs):
        rows = piece.shape[0]
        copy = pltpu.make_async_copy(piece, pool.at[pl.ds(place, rows)], sems.at[i])
        copy.start()
        copies.append(copy)
        place += rows
    return copies


def place_pairs(table_ref, pool, gram, size):
    def place(i, carry):
        for k in range(UNROLL):
            entry = 3 * (i * UNROLL + k)
            p = pl.multiple_of(table_ref[entry + 1] * size, size)
            q = pl.multiple_of(table_ref[entry + 2] * size, size)
            block = pool[pl.ds(pl.multiple_of(table_ref[entry + 3], 16), size)]
            gram[pl.ds(p, size), pl.ds(q, size)] = block
            gram[pl.ds(q, size), pl.ds(p, size)] = block.T
        return carry

    lax.fori_loop(0, table_ref[0], place, 0)


def gram_kernel(pieces, *refs):
    table_ref = refs[0]
    piece_refs = refs[1 : 1 + pieces]
    gram, pool, sems = refs[-3:]
    size = LANES
    copies = fill(piece_refs, pool, sems)
    for v in range(gram.shape[0] // size):
        gram[v * size : (v + 1) * size] = jnp.zeros((size, gram.shape[1]), gram.dtype)
    for copy in copies:
        copy.wait()
    place_pairs(table_ref, pool, gram, size)


def step_kernel(pieces, *refs):
    table_ref, info_ref, basis_ref, spread_ref, sign_ref, early_ref = refs[:6]
    piece_refs = refs[6 : 6 + pieces]
    next_ref, coef_ref, pool, gram, own, square, sems = refs[-7:]
    slots, size = sign_ref.shape[0], sign_ref.shape[1]
    copies = fill(piece_refs, pool, sems)
    for v in range(slots):
        gram[v * size : (v + 1) * size] = early_ref[v * size : (v + 1) * size]
    rows = lax.broadcasted_iota(jnp.int32, (size, size), 0)
    lanes = lax.broadcasted_iota(jnp.int32, (size, size), 1)
    own_size = info_ref[slots]
    self_slot = info_ref[slots + 1]
    for w in range(slots):
        kept = (rows < own_size) & (lanes < info_ref[w])
        block = jnp.where(kept, sign_ref[w].astype(jnp.float32), 0.0)
        own[:, w * size : (w + 1) * size] = block.astype(own.dtype)
    for copy in copies:
        copy.wait()
    place_pairs(table_ref, pool, gram, size)
    wide = 2 * size
    wide_lanes = lax.broadcasted_iota(jnp.int32, (size, wide), 1)
    wide_rows = lax.broadcasted_iota(jnp.int32, (size, wide), 0)

    def column_kept(n):
        first = info_ref[2 * n]
        second = info_ref[2 * n + 1]
        return (wide_lanes < first) | ((wide_lanes >= size) & (wide_lanes < size + second))

    for n in range(slots // 2):
        part = jnp.dot(own[...], gram[:, n * wide : (n + 1) * wide], preferred_element_type=jnp.float32)
        square[:, n * wide : (n + 1) * wide] = jnp.where(column_kept(n), part, 0.0).astype(square.dtype)
    basis = jnp.concatenate([basis_ref[...], basis_ref[...]], axis=1)
    coef = jnp.zeros((2 * basis_ref.shape[0], LANES), jnp.float32)
    across = (((1,), (1,)), ((), ()))
    for n in range(slots // 2):
        part = jnp.dot(square[...], gram[:, n * wide : (n + 1) * wide], preferred_element_type=jnp.float32)
        cube = jnp.where(column_kept(n), part, 0.0)
        full = 1.5 * own[:, n * wide : (n + 1) * wide].astype(jnp.float32) - 0.5 * cube
        next_ref[2 * n] = full[:, :size].astype(next_ref.dtype)
        next_ref[2 * n + 1] = full[:, size:].astype(next_ref.dtype)
        shift = (self_slot - 2 * n) * size
        is_self = (self_slot >= 2 * n) & (self_slot < 2 * n + 2)
        diag = (wide_lanes == wide_rows + shift) & (wide_rows < own_size) & is_self
        dmat = 0.5 * (jnp.where(diag, 1.0, 0.0) - full)
        high = dmat.astype(jnp.bfloat16)
        low = (dmat - high.astype(jnp.float32)).astype(jnp.bfloat16)
        half = jnp.dot(basis, jnp.concatenate([high, low], axis=0), preferred_element_type=jnp.float32)
        half_high = half.astype(jnp.bfloat16)
        half_low = (half - half_high.astype(jnp.float32)).astype(jnp.bfloat16)
        coef = coef + lax.dot_general(
            jnp.concatenate([half_high, half_low], axis=0),
            spread_ref[:, n * wide : (n + 1) * wide],
            across,
            preferred_element_type=jnp.float32,
        )
    coef = coef[: basis_ref.shape[0]] + coef[basis_ref.shape[0] :]
    coef_ref[...] = coef[: coef_ref.shape[0]]


def profile_kernel(periods, steps, mate_from, *refs):
    own_ref, mate_ref, third_ref = refs[:3]
    plane_ref, line_ref, geos, sems = refs[-4:]
    odd = (lax.axis_index("layer") & 1) == 1
    rows = len(steps) * GEO
    copies = []
    for k, source in enumerate((own_ref, mate_ref.at[pl.ds(mate_from, rows)], third_ref)):
        copy = pltpu.make_async_copy(source, geos.at[k], sems.at[k])
        copy.start()
        copies.append(copy)
    cells = plane_ref.shape[2]
    cell = lax.broadcasted_iota(jnp.int32, (cells, LANES), 0)
    grid_x = (cell // BY).astype(jnp.float32)
    grid_y = (cell % BY).astype(jnp.float32)
    grid_z = lax.broadcasted_iota(jnp.int32, (LANES, BZ), 1).astype(jnp.float32)
    lane = lax.broadcasted_iota(jnp.int32, (1, LANES), 1)
    shell = (lane % SHELLS + 1).astype(jnp.float32)
    valid = lane < 7 * SPAN
    from_own = lane < 4 * SPAN
    from_below = lane < 6 * SPAN
    lift = jnp.where(from_own, 0.0, jnp.where(from_below, -float(BZ), float(BZ))) + 0.5 * BZ

    def nearest(offset, period):
        return offset - period * jnp.floor(offset * (1.0 / period) + 0.5)

    for copy in copies:
        copy.wait()
    for o, (step_row, step_col) in enumerate(steps):
        own, first, third = (geos[k, o * GEO : (o + 1) * GEO].astype(jnp.float32) for k in range(3))
        below = jnp.where(odd, first, third)
        above = jnp.where(odd, third, first)
        moved = jnp.where(from_below, pltpu.roll(below, 3 * SPAN, axis=1), pltpu.roll(above, 3 * SPAN, axis=1))
        geo = jnp.where(from_own, own, moved)
        extent = jnp.where(valid, geo[3:4], 1.0)
        inverse = (SHELLS / extent) * (SHELLS / extent)
        reach = jnp.where(valid, extent, -1.0)
        rate_t = inverse / (shell * shell)
        packed = jnp.concatenate(
            [0.5 * geo[2:3] + lift, reach, rate_t, inverse, jnp.zeros((4, LANES), jnp.float32)], axis=0
        )
        sub = packed.T
        d_x = nearest(grid_x - (0.5 * geo[0:1] + float(BX * step_row)), periods[0])
        d_y = nearest(grid_y - (0.5 * geo[1:2] + float(BY * step_col)), periods[1])
        inside = (jnp.abs(d_x) <= reach) & (jnp.abs(d_y) <= reach)
        squared = d_x * d_x + d_y * d_y
        d_z = nearest(grid_z - sub[:, 0:1], periods[2])
        inside_z = jnp.abs(d_z) <= sub[:, 1:2]
        squared_z = d_z * d_z
        for s in range(SHELLS):
            part = 1.0 / ((s + 1) * (s + 1))
            rate = inverse * part + rate_t
            plane_ref[o, s] = jnp.where(inside, jnp.exp(-rate * squared), 0.0).astype(plane_ref.dtype)
            rate_z = sub[:, 3:4] * part + sub[:, 2:3]
            line_ref[o, s] = jnp.where(inside_z, jnp.exp(-rate_z * squared_z), 0.0).astype(line_ref.dtype)


def density_kernel(column_steps, *refs):
    coef_refs = refs[:column_steps]
    plane_ref, line_ref, out_ref, terms = refs[column_steps:]
    for o in range(plane_ref.shape[0]):
        coef = coef_refs[o % column_steps]
        first = 8 * (o // column_steps)
        for s in range(SHELLS):
            scaled = plane_ref[o, s].astype(jnp.float32) * coef[first + s : first + s + 1, :]
            at = (o * SHELLS + s) * LANES
            terms[:, at : at + LANES] = scaled.astype(terms.dtype)
    out_ref[...] = jnp.dot(terms[...], line_ref[...], preferred_element_type=jnp.float32)


def local(sign_start, neighbors, atom_size, basis_proj, pair_extent, atom_x, atom_y, atom_z):
    n_row = lax.axis_size("row")
    n_col = lax.axis_size("col")
    n_lay = lax.axis_size("layer")
    assert n_lay == 4 and n_col >= 4 and (n_row == 2 or n_row >= 4)
    assert n_row & (n_row - 1) == 0 and n_col & (n_col - 1) == 0
    axes = (n_row, n_col, n_lay)
    atoms, slots = neighbors.shape
    size = sign_start.shape[2]
    steps = [0, 1] if n_row == 2 else [0, 1, -1]
    count = len(steps)
    others = range(1, count)
    own = sign_start[0]
    flat = own.reshape(slots * size, size)
    listings = neighbors.T
    full = slots * size
    half = full // 2
    n_pick = column_targets(n_row)
    part = n_pick * size + GEO

    def on_row(value, di):
        return from_offset(value, "row", steps[di])

    x_row = {di: on_row(flat, di) for di in others}
    y_row = from_layer(flat, 2)
    m_row = from_layer(flat, 1)
    picked, geo = pl.pallas_call(
        functools.partial(pick_kernel, axes),
        out_shape=(
            jax.ShapeDtypeStruct((part, size), own.dtype),
            jax.ShapeDtypeStruct((GEO, LANES), own.dtype),
        ),
        in_specs=[HBM] * 6,
        out_specs=(VMEM, VMEM),
        scratch_shapes=[
            pltpu.SMEM((slots, atoms), jnp.int32),
            pltpu.SMEM((1, slots), jnp.int32),
            pltpu.SMEM((atoms,), jnp.int32),
            pltpu.SMEM((atoms,), jnp.int32),
            pltpu.SMEM((atoms,), jnp.int32),
            pltpu.SMEM((n_pick + 1,), jnp.int32),
            pltpu.SemaphoreType.DMA((5,)),
            pltpu.SemaphoreType.DMA((n_pick,)),
        ],
        compiler_params=pltpu.CompilerParams(vmem_limit_bytes=60 << 20),
        name="pick_column_blocks",
    )(listings, pair_extent, atom_x, atom_y, atom_z, own)
    up = from_offset(picked, "col", 1)
    down = from_offset(picked, "col", -1)

    at = {}
    buffers = {}

    def note(name, value, contents):
        buffers[name] = value
        start = 0
        for what, rows in contents:
            if what is not None:
                at[what] = (name, start)
            start += rows

    def row_of(di, flip):
        return [(("top", di, flip), half), (("end", di, flip), half)]

    def side_of(kind, di, flip):
        return [((kind, di, flip), part - GEO), ((kind + " geo", di, flip), GEO)]

    note("own", flat, row_of(0, 0))
    note("mate", m_row, row_of(0, 1))
    note("far", y_row, row_of(0, 2))
    note("up", up, side_of("up", 0, 0))
    note("down", down, side_of("down", 0, 0))
    note("geo", geo, [(("geo", 0, 0), GEO)])
    for di in others:
        note(("x", di), x_row[di], row_of(di, 0))

    names = ["up", "down", "geo", "far"] + [("x", di) for di in others]
    place = {name: i for i, name in enumerate(names)}
    xs = [place["x", di] for di in others]
    plans = [
        [(place["far"], half, half), (0, 0, part), (2, 0, GEO), (1, part - GEO, GEO)],
        [(x, 0, half) for x in xs] + [(1, 0, part)],
        [(x, 0, full) for x in xs] + [(place["far"], 0, full), (0, 0, part), (1, 0, part)],
    ]

    two_x, two_y = pack([buffers[name] for name in names], plans[:2], [m_row], "pack_two")

    early_order = ["own", "mate", "far", "up", "down", "geo"] + [("x", di) for di in others]
    early_order += [("two x", di) for di in others] + ["two y", "two m"]
    late_order = [("three x", di) for di in others] + ["three y", "three m"]
    late_order += ["four"]

    contents = {}
    for di in others:
        contents["two x", di] = [(("end", di, 2), half)] + side_of("up", di, 0)
        contents["two x", di] += [(("geo", di, 0), GEO), (("down geo", di, 0), GEO)]
    contents["two y"] = [(("top", di, 2), half) for di in others] + side_of("down", 0, 2)
    contents["two m"] = sum([row_of(di, 1) for di in others], []) + row_of(0, 3)
    contents["two m"] += side_of("up", 0, 1) + side_of("down", 0, 1)
    for di in others:
        contents["three x", di] = side_of("down", di, 0) + side_of("down", di, 2)
    contents["three y"] = side_of("up", 0, 2) + sum([side_of("up", di, 2) for di in others], [])
    contents["three m"] = []
    for di in others:
        contents["three m"] += [(("end", di, 3), half)] + side_of("up", di, 1) + [(None, 2 * GEO)]
    contents["three m"] += [(("top", di, 3), half) for di in others] + side_of("down", 0, 3)
    contents["three m"] += [("geos", count * 3 * GEO)]
    contents["four"] = []
    for di in others:
        contents["four"] += side_of("down", di, 1) + side_of("down", di, 3)
    contents["four"] += side_of("up", 0, 3) + sum([side_of("up", di, 3) for di in others], [])
    lengths = {name: sum(rows for _, rows in content) for name, content in contents.items()}
    for name in early_order:
        if name in buffers:
            lengths[name] = buffers[name].shape[0]
    base = {}
    total = 0
    for name in early_order + late_order:
        base[name] = total
        total += lengths[name]
        if name == early_order[-1]:
            late_from = total
    located = dict(at)
    for name, content in contents.items():
        start = 0
        for what, rows in content:
            located[what] = (name, start)
            start += rows
    layout = [
        base[located[kind, di, flip][0]] + located[kind, di, flip][1]
        for kind in ("top", "end", "up", "down")
        for di in range(count)
        for flip in range(n_lay)
    ]
    pairs = slots * (slots + 1) // 2
    entries = 3 * (pairs + UNROLL) + 1
    early_table, late_table, info, spread, own_basis = pl.pallas_call(
        functools.partial(prepare_kernel, axes, count, tuple(layout), late_from),
        out_shape=(
            jax.ShapeDtypeStruct((entries,), jnp.int32),
            jax.ShapeDtypeStruct((entries,), jnp.int32),
            jax.ShapeDtypeStruct((slots + 2,), jnp.int32),
            jax.ShapeDtypeStruct((LANES, full), jnp.bfloat16),
            jax.ShapeDtypeStruct((16, size), jnp.bfloat16),
        ),
        in_specs=[HBM, HBM, VMEM, ANY],
        out_specs=(SMEM, SMEM, SMEM, VMEM, VMEM),
        scratch_shapes=[
            pltpu.SMEM((slots, atoms), jnp.int32),
            pltpu.SMEM((atoms,), jnp.int32),
            pltpu.SMEM((4, slots), jnp.int32),
            pltpu.SMEM((atoms,), jnp.int32),
            pltpu.SMEM((len(layout),), jnp.int32),
            pltpu.SemaphoreType.DMA((2,)),
        ],
        compiler_params=pltpu.CompilerParams(vmem_limit_bytes=(2 << 20) + atoms * 16384),
        cost_estimate=pl.CostEstimate(flops=6_000_000_000, bytes_accessed=8_000_000, transcendentals=0),
        name="prepare",
    )(listings, atom_size, basis_proj.transpose(1, 0, 2).reshape(SHELLS * atoms, size), two_x)

    for di in others:
        note(("two x", di), on_row(two_x, di), contents["two x", di])
    note("two y", from_layer(two_y, 2), contents["two y"])
    two_m = pack([buffers[name] for name in names], plans[2:], [two_x], "pack_two_mate")[0]
    note("two m", from_layer(two_m, 1), contents["two m"])

    names = ["up", "down", "two y", "geo"] + [("two x", di) for di in others]
    place = {name: i for i, name in enumerate(names)}
    y_down = at["down", 0, 2][1]
    x_up = at["up", 1, 0][1]
    gather = []
    for di in range(count):
        for kind in ("geo", "up geo", "down geo"):
            name, start = at[kind, di, 0]
            gather.append((place[name], start, GEO))
    xs = [place["two x", di] for di in others]
    plans = [
        [(1, 0, part), (2, y_down, part)],
        [(0, 0, part)] + [(x, x_up, part) for x in xs],
        [(x, 0, lengths["two x", 1]) for x in xs] + [(2, 0, lengths["two y"])] + gather,
        gather,
    ]
    three_x, three_y, three_m, geos = pack([buffers[name] for name in names], plans, [own_basis], "pack_three")
    for di in others:
        note(("three x", di), on_row(three_x, di), contents["three x", di])
    note("three y", from_layer(three_y, 2), contents["three y"])
    note("three m", from_layer(three_m, 1), contents["three m"])
    third_geos = from_layer(geos, 3)

    early_values = [buffers[name] for name in early_order]
    gram = pl.pallas_call(
        functools.partial(gram_kernel, len(early_values)),
        out_shape=jax.ShapeDtypeStruct((full, full), jnp.bfloat16),
        in_specs=[SMEM] + [ANY] * (len(early_values) + 2),
        out_specs=VMEM,
        scratch_shapes=[
            pltpu.VMEM((late_from, LANES), jnp.bfloat16),
            pltpu.SemaphoreType.DMA((len(early_values),)),
        ],
        compiler_params=pltpu.CompilerParams(vmem_limit_bytes=(6 << 20) + late_from * LANES * 2),
        cost_estimate=pl.CostEstimate(flops=1000, bytes_accessed=1000, transcendentals=0),
        name="gram_early",
    )(early_table, *early_values, three_x, third_geos)

    thirds = [buffers["three x", di] for di in others] + [buffers["three y"]]
    four = pack(thirds, [[(i, 0, value.shape[0]) for i, value in enumerate(thirds)]], [gram], "pack_four")[0]
    note("four", from_layer(four, 1), contents["four"])

    column_steps = (0, 1, -1)
    tile_steps = [(dr, dc) for dr in steps for dc in column_steps]
    tiles = len(tile_steps)
    periods = (float(BX * n_row), float(BY * n_col), float(BZ * n_lay))
    plane, line = pl.pallas_call(
        functools.partial(profile_kernel, periods, tile_steps, at["geos"][1]),
        out_shape=(
            jax.ShapeDtypeStruct((tiles, SHELLS, BX * BY, LANES), jnp.bfloat16),
            jax.ShapeDtypeStruct((tiles, SHELLS, LANES, BZ), jnp.bfloat16),
        ),
        in_specs=[ANY] * 4,
        out_specs=(VMEM, VMEM),
        scratch_shapes=[
            pltpu.VMEM((3, tiles * GEO, LANES), jnp.bfloat16),
            pltpu.SemaphoreType.DMA((3,)),
        ],
        compiler_params=pltpu.CompilerParams(vmem_limit_bytes=10 << 20),
        cost_estimate=pl.CostEstimate(flops=5_000_000_000, bytes_accessed=4_000_000, transcendentals=2_000_000),
        name="profiles",
    )(geos, buffers["three m"], third_geos, gram)

    late_values = [buffers[name] for name in late_order]
    sign_next, coef = pl.pallas_call(
        functools.partial(step_kernel, len(late_values)),
        out_shape=(
            jax.ShapeDtypeStruct((slots, size, size), jnp.bfloat16),
            jax.ShapeDtypeStruct((8, LANES), jnp.float32),
        ),
        in_specs=[SMEM, SMEM, VMEM, VMEM, VMEM, VMEM] + [ANY] * (len(late_values) + 1),
        out_specs=(VMEM, VMEM),
        scratch_shapes=[
            pltpu.VMEM((total - late_from, LANES), jnp.bfloat16),
            pltpu.VMEM((full, full), jnp.bfloat16),
            pltpu.VMEM((size, full), jnp.bfloat16),
            pltpu.VMEM((size, full), jnp.bfloat16),
            pltpu.SemaphoreType.DMA((len(late_values),)),
        ],
        compiler_params=pltpu.CompilerParams(vmem_limit_bytes=(15 << 20) + (total - late_from) * LANES * 2),
        cost_estimate=pl.CostEstimate(flops=1_300_000_000, bytes_accessed=8_000_000, transcendentals=0),
        name="square_cube_coefficients",
    )(late_table, info, own_basis, spread, own, gram, *late_values, line)

    below = from_offset(coef, "layer", -1)
    above = from_offset(coef, "layer", 1)
    merged = jnp.concatenate(
        [
            coef[:, : 4 * SPAN],
            below[:, SPAN : 3 * SPAN],
            above[:, 3 * SPAN : 4 * SPAN],
            jnp.zeros((8, LANES - 7 * SPAN), jnp.float32),
        ],
        axis=1,
    )
    stacked = jnp.concatenate([merged] + [on_row(merged, di) for di in others], axis=0)
    received = [stacked] + [from_offset(stacked, "col", dc) for dc in column_steps[1:]]

    density = pl.pallas_call(
        functools.partial(density_kernel, len(column_steps)),
        out_shape=jax.ShapeDtypeStruct((BX * BY, BZ), jnp.float32),
        in_specs=[VMEM] * (len(column_steps) + 2),
        out_specs=VMEM,
        scratch_shapes=[pltpu.VMEM((BX * BY, tiles * SHELLS * LANES), jnp.bfloat16)],
        compiler_params=pltpu.CompilerParams(vmem_limit_bytes=16 << 20),
        cost_estimate=pl.CostEstimate(flops=310_000_000, bytes_accessed=4_000_000, transcendentals=0),
        name="density",
    )(*received, plane, line.reshape(tiles * SHELLS * LANES, BZ))
    return sign_next[None], density.reshape(BX, BY, BZ)


def solution(mesh):
    rows = P(("row", "col", "layer"), None, None, None)
    in_specs = (rows, P(), P(), P(), P(("row", "col", "layer"), None), P(), P(), P())
    out_specs = (rows, P("row", "col", "layer"))
    return jax.shard_map(local, mesh=mesh, in_specs=in_specs, out_specs=out_specs, check_vma=False)
```

```python
import functools

import jax
import jax.numpy as jnp
from jax import lax
from jax.experimental import pallas as pl
from jax.experimental.pallas import tpu as pltpu
from jax.sharding import PartitionSpec as P

BX = 16
BY = 16
BZ = 128
LANES = 128
UNROLL = 4
SHELLS = 6
SPAN = 3 * SHELLS
GEO = 16
VMEM = pl.BlockSpec(memory_space=pltpu.VMEM)
SMEM = pl.BlockSpec(memory_space=pltpu.SMEM)
ANY = pl.BlockSpec(memory_space=pl.ANY)
HBM = pl.BlockSpec(memory_space=pltpu.HBM)


def from_offset(x, axis, step):
    count = lax.axis_size(axis)
    return lax.ppermute(x, axis, [((i + step) % count, i) for i in range(count)])


def from_layer(x, flip):
    count = lax.axis_size("layer")
    return lax.ppermute(x, "layer", [(i ^ flip, i) for i in range(count)])


def column_targets(n_row):
    return 5 if n_row == 2 else 7


def target_place(n_row, step_row, step_lay, row):
    same = jnp.where(step_lay < 3, step_lay, -1)
    if n_row == 2:
        lead = step_lay - row
        across = jnp.where((lead >= 0) & (lead < 2), 3 + lead, -1)
    else:
        across = 3 + step_lay
    return jnp.where(step_row == 0, same, jnp.where(step_row == 1, across, -1))


class Places:
    def __init__(self, n_row, n_col, n_lay):
        self.n_row, self.n_col, self.n_lay = n_row, n_col, n_lay
        self.lay_bits = n_lay.bit_length() - 1
        self.col_bits = n_col.bit_length() - 1
        self.row = lax.axis_index("row")
        self.col = lax.axis_index("col")
        self.lay = lax.axis_index("layer")
        self.me = (((self.row << self.col_bits) + self.col) << self.lay_bits) + self.lay

    def split(self, atom):
        return (
            atom >> (self.lay_bits + self.col_bits),
            (atom >> self.lay_bits) & (self.n_col - 1),
            atom & (self.n_lay - 1),
        )


def load(sources, targets, sems):
    copies = [pltpu.make_async_copy(a, b, sems.at[i]) for i, (a, b) in enumerate(zip(sources, targets))]
    for copy in copies:
        copy.start()
    for copy in copies:
        copy.wait()


def own_ranks(at, neighbors_ref):
    seen = [jnp.int32(0)] * at.n_lay
    listed = []
    for w in range(neighbors_ref.shape[0]):
        atom = neighbors_ref[w, at.me]
        step_lay = (atom - at.lay) & (at.n_lay - 1)
        rank = jnp.int32(0)
        for k in range(at.n_lay):
            rank = jnp.where(step_lay == k, 3 * k + seen[k], rank)
            seen[k] = seen[k] + (step_lay == k).astype(jnp.int32)
        listed.append((atom, rank))
    return listed


def pick_kernel(axes, *refs):
    sign_ref, out_ref, geo_ref, neighbors_ref, extent_ref, x_ref, y_ref, z_ref, place_ref, loads, sems = refs[5:]
    at = Places(*axes)
    slots = sign_ref.shape[0]
    n_pick = place_ref.shape[0] - 1
    size = sign_ref.shape[1]
    for i in range(n_pick + 1):
        place_ref[i] = 0
    load(refs[:5], (neighbors_ref, extent_ref, x_ref, y_ref, z_ref), loads)
    ranks = own_ranks(at, neighbors_ref)
    for w, (atom, _) in enumerate(ranks):
        row, col, lay = at.split(atom)
        place = target_place(at.n_row, (row - at.row) & (at.n_row - 1), (lay - at.lay) & (at.n_lay - 1), at.row)
        place_ref[jnp.where((col == at.col) & (place >= 0), place, n_pick)] = w
    copies = []
    for i in range(n_pick):
        copy = pltpu.make_async_copy(sign_ref.at[place_ref[i]], out_ref.at[pl.ds(i * size, size)], sems.at[i])
        copy.start()
        copies.append(copy)
    sub = lax.broadcasted_iota(jnp.int32, (GEO, LANES), 0)
    lane_pair = lax.broadcasted_iota(jnp.int32, (GEO, LANES), 1) // SHELLS
    geo = jnp.zeros((GEO, LANES), jnp.int32)
    for w, (atom, rank) in enumerate(ranks):
        row, col, lay = at.split(atom)
        go_row = ((row - at.row + 1) & (at.n_row - 1)) - 1
        go_col = ((col - at.col + 1) & (at.n_col - 1)) - 1
        go_lay = jnp.minimum(((lay - at.lay + 1) & (at.n_lay - 1)) - 1, 1)
        twice_x = x_ref[at.me] + x_ref[atom] + BX * go_row
        twice_y = y_ref[at.me] + y_ref[atom] + BY * go_col
        twice_z = z_ref[at.me] + z_ref[atom] + BZ * go_lay - BZ
        extent = extent_ref[0, w]
        values = jnp.where(sub == 0, twice_x, jnp.where(sub == 1, twice_y, jnp.where(sub == 2, twice_z, extent)))
        geo = jnp.where(lane_pair == rank, values, geo)
    geo = geo.astype(jnp.float32).astype(geo_ref.dtype)
    geo_ref[...] = geo
    out_ref[n_pick * size : n_pick * size + GEO] = geo
    for copy in copies:
        copy.wait()


def prepare_kernel(axes, count, layout, late_from, *refs):
    basis_ref = refs[2]
    early_ref, late_ref, info_ref, spread_ref, own_basis_ref = refs[-11:-6]
    neighbors_ref, size_ref, known, inverse, layout_ref, loads = refs[-6:]
    at = Places(*axes)
    load(refs[:2], (neighbors_ref, size_ref), loads)
    slots, atoms = neighbors_ref.shape
    bits = atoms.bit_length() - 1
    for i, value in enumerate(layout):
        layout_ref[i] = value
    lines = count * at.n_lay

    def hot(rows, atom, first):
        sub = lax.broadcasted_iota(jnp.int32, (rows, SHELLS * atoms), 0)
        lane = lax.broadcasted_iota(jnp.int32, (rows, SHELLS * atoms), 1)
        return ((lane & (atoms - 1)) == atom) & (sub == first + (lane >> bits))

    def rows_of(chosen):
        picked = jnp.where(chosen, 1.0, 0.0).astype(jnp.bfloat16)
        return jnp.dot(picked, basis_ref[...], preferred_element_type=jnp.float32).astype(jnp.bfloat16)

    self_slot = jnp.int32(0)
    for w, (atom, rank) in enumerate(own_ranks(at, neighbors_ref)):
        row, col, lay = at.split(atom)
        step_row = (row - at.row) & (at.n_row - 1)
        step_col = (col - at.col) & (at.n_col - 1)
        self_slot = jnp.where(atom == at.me, w, self_slot)
        info_ref[w] = size_ref[atom]
        spread_ref[:, w * LANES : (w + 1) * LANES] = rows_of(hot(LANES, atom, rank * SHELLS))
        flip = lay ^ at.lay
        known[0, w] = atom
        known[1, w] = jnp.where(step_col == 0, 0, jnp.where(step_col == 1, 1, 2))
        known[2, w] = jnp.where(step_row == 0, 0, jnp.where(step_row == 1, 1, 2)) * at.n_lay + flip
        inverse[atom] = -1
    own_basis_ref[...] = rows_of(hot(16, at.me, 0))
    info_ref[slots] = size_ref[at.me]
    info_ref[slots + 1] = self_slot

    def row_of_pairs(v, totals):
        early, late = totals
        atom = known[0, v]
        side = known[1, v]
        line = known[2, v]
        row, _, lay = at.split(atom)
        for u in range(slots):
            inverse[neighbors_ref[u, atom]] = v * 16 + u
        top = layout_ref[line]
        end = layout_ref[lines + line]
        beside = layout_ref[(side + 1) * lines + line]
        half = slots // 2
        for w in range(slots):
            other = known[0, w]
            other_side = known[1, w]
            mark = inverse[other]
            slot = mark & 15
            o_row, _, o_lay = at.split(other)
            there = target_place(at.n_row, (o_row - row) & (at.n_row - 1), (o_lay - lay) & (at.n_lay - 1), row)
            back = target_place(at.n_row, (row - o_row) & (at.n_row - 1), (lay - o_lay) & (at.n_lay - 1), o_row)
            from_row = (other_side != 0) | (v <= w)
            from_column = (side == other_side) & (there >= 0) & ((back < 0) | (v <= w))
            chosen = ((mark >> 4) == v) & jnp.where(side == 0, from_row, from_column)
            in_row = jnp.where(slot < half, top + slot * LANES, end + (slot - half) * LANES)
            where = jnp.where(side == 0, in_row, beside + there * LANES)
            is_late = where >= late_from
            for ref, total in ((early_ref, early), (late_ref, late)):
                ref[3 * total + 1] = v
                ref[3 * total + 2] = w
                ref[3 * total + 3] = where
            late_ref[3 * late + 3] = where - late_from
            early = early + (chosen & ~is_late).astype(jnp.int32)
            late = late + (chosen & is_late).astype(jnp.int32)
        return early, late

    totals = lax.fori_loop(0, slots, row_of_pairs, (jnp.int32(0), jnp.int32(0)))
    for ref, total in zip((early_ref, late_ref), totals):
        ref[0] = (total + UNROLL - 1) // UNROLL
        last = 3 * jnp.maximum(total - 1, 0) + 1
        for i in range(UNROLL - 1):
            for k in range(3):
                ref[3 * (total + i) + 1 + k] = ref[last + k]


def pack_kernel(moves, inputs, outputs, *refs):
    sems = refs[-1]
    copies = []
    for k, (source, start, rows, target, place) in enumerate(moves):
        copy = pltpu.make_async_copy(
            refs[source].at[pl.ds(start, rows)], refs[inputs + target].at[pl.ds(place, rows)], sems.at[k]
        )
        copy.start()
        copies.append(copy)
    for copy in copies:
        copy.wait()


def pack(values, plans, extra, name):
    moves, shapes = [], []
    for target, plan in enumerate(plans):
        place = 0
        for source, start, rows in plan:
            moves.append((source, start, rows, target, place))
            place += rows
        shapes.append(jax.ShapeDtypeStruct((place, LANES), values[0].dtype))
    inputs = len(values) + len(extra)
    return pl.pallas_call(
        functools.partial(pack_kernel, tuple(moves), inputs, len(plans)),
        out_shape=tuple(shapes),
        in_specs=[ANY] * inputs,
        out_specs=tuple([ANY] * len(plans)),
        scratch_shapes=[pltpu.SemaphoreType.DMA((len(moves),))],
        compiler_params=pltpu.CompilerParams(vmem_limit_bytes=1 << 20),
        cost_estimate=pl.CostEstimate(flops=0, bytes_accessed=3_000_000, transcendentals=0),
        name=name,
    )(*values, *extra)


def fill(piece_refs, pool, sems):
    copies = []
    place = 0
    for i, piece in enumerate(piece_refs):
        rows = piece.shape[0]
        copy = pltpu.make_async_copy(piece, pool.at[pl.ds(place, rows)], sems.at[i])
        copy.start()
        copies.append(copy)
        place += rows
    return copies


def place_pairs(table_ref, pool, gram, size):
    def place(i, carry):
        for k in range(UNROLL):
            entry = 3 * (i * UNROLL + k)
            p = pl.multiple_of(table_ref[entry + 1] * size, size)
            q = pl.multiple_of(table_ref[entry + 2] * size, size)
            block = pool[pl.ds(pl.multiple_of(table_ref[entry + 3], 16), size)]
            gram[pl.ds(p, size), pl.ds(q, size)] = block
            gram[pl.ds(q, size), pl.ds(p, size)] = block.T
        return carry

    lax.fori_loop(0, table_ref[0], place, 0)


def gram_kernel(pieces, *refs):
    table_ref = refs[0]
    piece_refs = refs[1 : 1 + pieces]
    gram, pool, sems = refs[-3:]
    size = LANES
    copies = fill(piece_refs, pool, sems)
    for v in range(gram.shape[0] // size):
        gram[v * size : (v + 1) * size] = jnp.zeros((size, gram.shape[1]), gram.dtype)
    for copy in copies:
        copy.wait()
    place_pairs(table_ref, pool, gram, size)


def step_kernel(pieces, *refs):
    table_ref, info_ref, basis_ref, spread_ref, sign_ref, early_ref = refs[:6]
    piece_refs = refs[6 : 6 + pieces]
    next_ref, coef_ref, pool, gram, own, square, sems = refs[-7:]
    slots, size = sign_ref.shape[0], sign_ref.shape[1]
    copies = fill(piece_refs, pool, sems)
    for v in range(slots):
        gram[v * size : (v + 1) * size] = early_ref[v * size : (v + 1) * size]
    rows = lax.broadcasted_iota(jnp.int32, (size, size), 0)
    lanes = lax.broadcasted_iota(jnp.int32, (size, size), 1)
    own_size = info_ref[slots]
    self_slot = info_ref[slots + 1]
    for w in range(slots):
        kept = (rows < own_size) & (lanes < info_ref[w])
        block = jnp.where(kept, sign_ref[w].astype(jnp.float32), 0.0)
        own[:, w * size : (w + 1) * size] = block.astype(own.dtype)
    for copy in copies:
        copy.wait()
    place_pairs(table_ref, pool, gram, size)
    wide = 2 * size
    wide_lanes = lax.broadcasted_iota(jnp.int32, (size, wide), 1)
    wide_rows = lax.broadcasted_iota(jnp.int32, (size, wide), 0)

    def column_kept(n):
        first = info_ref[2 * n]
        second = info_ref[2 * n + 1]
        return (wide_lanes < first) | ((wide_lanes >= size) & (wide_lanes < size + second))

    for n in range(slots // 2):
        part = jnp.dot(own[...], gram[:, n * wide : (n + 1) * wide], preferred_element_type=jnp.float32)
        square[:, n * wide : (n + 1) * wide] = jnp.where(column_kept(n), part, 0.0).astype(square.dtype)
    basis = jnp.concatenate([basis_ref[...], basis_ref[...]], axis=1)
    coef = jnp.zeros((2 * basis_ref.shape[0], LANES), jnp.float32)
    across = (((1,), (1,)), ((), ()))
    for n in range(slots // 2):
        part = jnp.dot(square[...], gram[:, n * wide : (n + 1) * wide], preferred_element_type=jnp.float32)
        cube = jnp.where(column_kept(n), part, 0.0)
        full = 1.5 * own[:, n * wide : (n + 1) * wide].astype(jnp.float32) - 0.5 * cube
        next_ref[2 * n] = full[:, :size].astype(next_ref.dtype)
        next_ref[2 * n + 1] = full[:, size:].astype(next_ref.dtype)
        shift = (self_slot - 2 * n) * size
        is_self = (self_slot >= 2 * n) & (self_slot < 2 * n + 2)
        diag = (wide_lanes == wide_rows + shift) & (wide_rows < own_size) & is_self
        dmat = 0.5 * (jnp.where(diag, 1.0, 0.0) - full)
        high = dmat.astype(jnp.bfloat16)
        low = (dmat - high.astype(jnp.float32)).astype(jnp.bfloat16)
        half = jnp.dot(basis, jnp.concatenate([high, low], axis=0), preferred_element_type=jnp.float32)
        half_high = half.astype(jnp.bfloat16)
        half_low = (half - half_high.astype(jnp.float32)).astype(jnp.bfloat16)
        coef = coef + lax.dot_general(
            jnp.concatenate([half_high, half_low], axis=0),
            spread_ref[:, n * wide : (n + 1) * wide],
            across,
            preferred_element_type=jnp.float32,
        )
    coef = coef[: basis_ref.shape[0]] + coef[basis_ref.shape[0] :]
    coef_ref[...] = coef[: coef_ref.shape[0]]


def profile_kernel(periods, steps, mate_from, *refs):
    own_ref, mate_ref, third_ref = refs[:3]
    plane_ref, line_ref, geos, sems = refs[-4:]
    odd = (lax.axis_index("layer") & 1) == 1
    rows = len(steps) * GEO
    copies = []
    for k, source in enumerate((own_ref, mate_ref.at[pl.ds(mate_from, rows)], third_ref)):
        copy = pltpu.make_async_copy(source, geos.at[k], sems.at[k])
        copy.start()
        copies.append(copy)
    cells = plane_ref.shape[2]
    cell = lax.broadcasted_iota(jnp.int32, (cells, LANES), 0)
    grid_x = (cell // BY).astype(jnp.float32)
    grid_y = (cell % BY).astype(jnp.float32)
    grid_z = lax.broadcasted_iota(jnp.int32, (LANES, BZ), 1).astype(jnp.float32)
    lane = lax.broadcasted_iota(jnp.int32, (1, LANES), 1)
    shell = (lane % SHELLS + 1).astype(jnp.float32)
    valid = lane < 7 * SPAN
    from_own = lane < 4 * SPAN
    from_below = lane < 6 * SPAN
    lift = jnp.where(from_own, 0.0, jnp.where(from_below, -float(BZ), float(BZ))) + 0.5 * BZ

    def nearest(offset, period):
        return offset - period * jnp.floor(offset * (1.0 / period) + 0.5)

    for copy in copies:
        copy.wait()
    for o, (step_row, step_col) in enumerate(steps):
        own, first, third = (geos[k, o * GEO : (o + 1) * GEO].astype(jnp.float32) for k in range(3))
        below = jnp.where(odd, first, third)
        above = jnp.where(odd, third, first)
        moved = jnp.where(from_below, pltpu.roll(below, 3 * SPAN, axis=1), pltpu.roll(above, 3 * SPAN, axis=1))
        geo = jnp.where(from_own, own, moved)
        extent = jnp.where(valid, geo[3:4], 1.0)
        inverse = (SHELLS / extent) * (SHELLS / extent)
        reach = jnp.where(valid, extent, -1.0)
        rate_t = inverse / (shell * shell)
        packed = jnp.concatenate(
            [0.5 * geo[2:3] + lift, reach, rate_t, inverse, jnp.zeros((4, LANES), jnp.float32)], axis=0
        )
        sub = packed.T
        d_x = nearest(grid_x - (0.5 * geo[0:1] + float(BX * step_row)), periods[0])
        d_y = nearest(grid_y - (0.5 * geo[1:2] + float(BY * step_col)), periods[1])
        inside = (jnp.abs(d_x) <= reach) & (jnp.abs(d_y) <= reach)
        squared = d_x * d_x + d_y * d_y
        d_z = nearest(grid_z - sub[:, 0:1], periods[2])
        inside_z = jnp.abs(d_z) <= sub[:, 1:2]
        squared_z = d_z * d_z
        for s in range(SHELLS):
            part = 1.0 / ((s + 1) * (s + 1))
            rate = inverse * part + rate_t
            plane_ref[o, s] = jnp.where(inside, jnp.exp(-rate * squared), 0.0).astype(plane_ref.dtype)
            rate_z = sub[:, 3:4] * part + sub[:, 2:3]
            line_ref[o, s] = jnp.where(inside_z, jnp.exp(-rate_z * squared_z), 0.0).astype(line_ref.dtype)


def density_kernel(column_steps, *refs):
    coef_refs = refs[:column_steps]
    plane_ref, line_ref, out_ref, terms = refs[column_steps:]
    for o in range(plane_ref.shape[0]):
        coef = coef_refs[o % column_steps]
        first = 8 * (o // column_steps)
        for s in range(SHELLS):
            scaled = plane_ref[o, s].astype(jnp.float32) * coef[first + s : first + s + 1, :]
            at = (o * SHELLS + s) * LANES
            terms[:, at : at + LANES] = scaled.astype(terms.dtype)
    out_ref[...] = jnp.dot(terms[...], line_ref[...], preferred_element_type=jnp.float32)


def local(sign_start, neighbors, atom_size, basis_proj, pair_extent, atom_x, atom_y, atom_z):
    n_row = lax.axis_size("row")
    n_col = lax.axis_size("col")
    n_lay = lax.axis_size("layer")
    assert n_lay == 4 and n_col >= 4 and (n_row == 2 or n_row >= 4)
    assert n_row & (n_row - 1) == 0 and n_col & (n_col - 1) == 0
    axes = (n_row, n_col, n_lay)
    atoms, slots = neighbors.shape
    size = sign_start.shape[2]
    steps = [0, 1] if n_row == 2 else [0, 1, -1]
    count = len(steps)
    others = range(1, count)
    own = sign_start[0]
    flat = own.reshape(slots * size, size)
    listings = neighbors.T
    full = slots * size
    half = full // 2
    n_pick = column_targets(n_row)
    picks = n_pick * size
    part = picks + GEO

    def on_row(value, di):
        return from_offset(value, "row", steps[di])

    x_row = {di: on_row(flat, di) for di in others}
    y_row = from_layer(flat, 2)
    m_row = from_layer(flat, 1)
    picked, geo = pl.pallas_call(
        functools.partial(pick_kernel, axes),
        out_shape=(
            jax.ShapeDtypeStruct((max(part, half + GEO), size), own.dtype),
            jax.ShapeDtypeStruct((GEO, LANES), own.dtype),
        ),
        in_specs=[HBM] * 6,
        out_specs=(VMEM, VMEM),
        scratch_shapes=[
            pltpu.SMEM((slots, atoms), jnp.int32),
            pltpu.SMEM((1, slots), jnp.int32),
            pltpu.SMEM((atoms,), jnp.int32),
            pltpu.SMEM((atoms,), jnp.int32),
            pltpu.SMEM((atoms,), jnp.int32),
            pltpu.SMEM((n_pick + 1,), jnp.int32),
            pltpu.SemaphoreType.DMA((5,)),
            pltpu.SemaphoreType.DMA((n_pick,)),
        ],
        compiler_params=pltpu.CompilerParams(vmem_limit_bytes=60 << 20),
        name="pick_column_blocks",
    )(listings, pair_extent, atom_x, atom_y, atom_z, own)
    up = from_offset(picked, "col", 1)
    down = from_offset(picked, "col", -1)

    halves = pack(
        [y_row] + [x_row[di] for di in others],
        [[(0, half, half)]] + [[(di, 0, half)] for di in others],
        [],
        "pack_halves",
    )
    ends = {di: on_row(halves[0], di) for di in others}
    tops = {di: from_layer(halves[di], 2) for di in others}

    at = {}
    buffers = {}

    def note(name, value, contents):
        buffers[name] = value
        start = 0
        for what, rows in contents:
            if what is not None:
                at[what] = (name, start)
            start += rows

    def row_of(di, flip):
        return [(("top", di, flip), half), (("end", di, flip), half)]

    def side_of(kind, di, flip):
        return [((kind, di, flip), picks)]

    note("own", flat, row_of(0, 0))
    note("mate", m_row, row_of(0, 1))
    note("far", y_row, row_of(0, 2))
    note("up", up, side_of("up", 0, 0) + [(("up geo", 0, 0), GEO)])
    note("down", down, side_of("down", 0, 0) + [(("down geo", 0, 0), GEO)])
    note("geo", geo, [(("geo", 0, 0), GEO)])
    for di in others:
        note(("x", di), x_row[di], row_of(di, 0))
        note(("end", di), ends[di], [(("end", di, 2), half)])
        note(("top", di), tops[di], [(("top", di, 2), half)])

    corners = [("end", di) for di in others] + [("top", di) for di in others]
    crossing = [("x", di) for di in others] + ["far"] + corners
    names = ["up", "down", "geo"] + crossing
    plans = [
        [(0, 0, picks), (2, 0, GEO), (0, picks, GEO), (1, picks, GEO)],
        [(1, 0, picks)],
        [(i + 3, 0, buffers[name].shape[0]) for i, name in enumerate(crossing)] + [(0, 0, picks), (1, 0, picks)],
    ]
    two_x, two_y = pack(
        [buffers[name] for name in names[:3]], plans[:2], [buffers[name] for name in corners] + [m_row], "pack_two"
    )

    early_order = ["own", "mate", "far", "up", "down", "geo"] + [("x", di) for di in others]
    early_order += corners + [("two x", di) for di in others] + ["two y", "two m"]
    late_order = [("three x", di) for di in others] + ["three y", "three m"]
    late_order += ["four"]

    contents = {}
    for di in others:
        contents["two x", di] = side_of("up", di, 0) + [(("geo", di, 0), GEO)]
        contents["two x", di] += [(("up geo", di, 0), GEO), (("down geo", di, 0), GEO)]
    contents["two y"] = side_of("down", 0, 2)
    contents["two m"] = sum([row_of(di, 1) for di in others], []) + row_of(0, 3)
    contents["two m"] += [(("end", di, 3), half) for di in others] + [(("top", di, 3), half) for di in others]
    contents["two m"] += side_of("up", 0, 1) + side_of("down", 0, 1)
    for di in others:
        contents["three x", di] = side_of("down", di, 0) + side_of("down", di, 2)
    contents["three y"] = side_of("up", 0, 2) + sum([side_of("up", di, 2) for di in others], [])
    contents["three m"] = sum([side_of("up", di, 1) for di in others], []) + side_of("down", 0, 3)
    contents["three m"] += [("geos", count * 3 * GEO)]
    contents["four"] = []
    for di in others:
        contents["four"] += side_of("down", di, 1) + side_of("down", di, 3)
    contents["four"] += side_of("up", 0, 3) + sum([side_of("up", di, 3) for di in others], [])
    lengths = {name: sum(rows for _, rows in content) for name, content in contents.items()}
    for name in early_order:
        if name in buffers:
            lengths[name] = buffers[name].shape[0]
    base = {}
    total = 0
    for name in early_order + late_order:
        base[name] = total
        total += lengths[name]
        if name == early_order[-1]:
            late_from = total
    located = dict(at)
    for name, content in contents.items():
        start = 0
        for what, rows in content:
            located[what] = (name, start)
            start += rows
    layout = [
        base[located[kind, di, flip][0]] + located[kind, di, flip][1]
        for kind in ("top", "end", "up", "down")
        for di in range(count)
        for flip in range(n_lay)
    ]
    pairs = slots * (slots + 1) // 2
    entries = 3 * (pairs + UNROLL) + 1
    early_table, late_table, info, spread, own_basis = pl.pallas_call(
        functools.partial(prepare_kernel, axes, count, tuple(layout), late_from),
        out_shape=(
            jax.ShapeDtypeStruct((entries,), jnp.int32),
            jax.ShapeDtypeStruct((entries,), jnp.int32),
            jax.ShapeDtypeStruct((slots + 2,), jnp.int32),
            jax.ShapeDtypeStruct((LANES, full), jnp.bfloat16),
            jax.ShapeDtypeStruct((16, size), jnp.bfloat16),
        ),
        in_specs=[HBM, HBM, VMEM, ANY],
        out_specs=(SMEM, SMEM, SMEM, VMEM, VMEM),
        scratch_shapes=[
            pltpu.SMEM((slots, atoms), jnp.int32),
            pltpu.SMEM((atoms,), jnp.int32),
            pltpu.SMEM((3, slots), jnp.int32),
            pltpu.SMEM((atoms,), jnp.int32),
            pltpu.SMEM((len(layout),), jnp.int32),
            pltpu.SemaphoreType.DMA((2,)),
        ],
        compiler_params=pltpu.CompilerParams(vmem_limit_bytes=(2 << 20) + atoms * 16384),
        cost_estimate=pl.CostEstimate(flops=6_000_000_000, bytes_accessed=8_000_000, transcendentals=0),
        name="prepare",
    )(listings, atom_size, basis_proj.transpose(1, 0, 2).reshape(SHELLS * atoms, size), two_x)

    for di in others:
        note(("two x", di), on_row(two_x, di), contents["two x", di])
    note("two y", from_layer(two_y, 2), contents["two y"])
    two_m = pack([buffers[name] for name in names], plans[2:], [two_x], "pack_two_mate")[0]
    note("two m", from_layer(two_m, 1), contents["two m"])

    names = ["up", "down", "two y", "geo"] + [("two x", di) for di in others]
    place = {name: i for i, name in enumerate(names)}
    gather = []
    for di in range(count):
        for kind in ("geo", "up geo", "down geo"):
            name, start = at[kind, di, 0]
            gather.append((place[name], start, GEO))
    xs = [place["two x", di] for di in others]
    plans = [
        [(1, 0, picks), (2, 0, picks)],
        [(0, 0, picks)] + [(x, 0, picks) for x in xs],
        [(x, 0, picks) for x in xs] + [(2, 0, picks)] + gather,
        gather,
    ]
    three_x, three_y, three_m, geos = pack([buffers[name] for name in names], plans, [own_basis], "pack_three")
    for di in others:
        note(("three x", di), on_row(three_x, di), contents["three x", di])
    note("three y", from_layer(three_y, 2), contents["three y"])
    note("three m", from_layer(three_m, 1), contents["three m"])
    third_geos = from_layer(geos, 3)

    early_values = [buffers[name] for name in early_order]
    gram = pl.pallas_call(
        functools.partial(gram_kernel, len(early_values)),
        out_shape=jax.ShapeDtypeStruct((full, full), jnp.bfloat16),
        in_specs=[SMEM] + [ANY] * (len(early_values) + 1),
        out_specs=VMEM,
        scratch_shapes=[
            pltpu.VMEM((late_from, LANES), jnp.bfloat16),
            pltpu.SemaphoreType.DMA((len(early_values),)),
        ],
        compiler_params=pltpu.CompilerParams(vmem_limit_bytes=(6 << 20) + late_from * LANES * 2),
        cost_estimate=pl.CostEstimate(flops=1000, bytes_accessed=1000, transcendentals=0),
        name="gram_early",
    )(early_table, *early_values, three_x)

    thirds = [buffers["three x", di] for di in others] + [buffers["three y"]]
    four = pack(thirds, [[(i, 0, value.shape[0]) for i, value in enumerate(thirds)]], [gram, third_geos], "pack_four")[0]
    note("four", from_layer(four, 1), contents["four"])

    column_steps = (0, 1, -1)
    tile_steps = [(dr, dc) for dr in steps for dc in column_steps]
    tiles = len(tile_steps)
    periods = (float(BX * n_row), float(BY * n_col), float(BZ * n_lay))
    plane, line = pl.pallas_call(
        functools.partial(profile_kernel, periods, tile_steps, at["geos"][1]),
        out_shape=(
            jax.ShapeDtypeStruct((tiles, SHELLS, BX * BY, LANES), jnp.bfloat16),
            jax.ShapeDtypeStruct((tiles, SHELLS, LANES, BZ), jnp.bfloat16),
        ),
        in_specs=[ANY] * 4,
        out_specs=(VMEM, VMEM),
        scratch_shapes=[
            pltpu.VMEM((3, tiles * GEO, LANES), jnp.bfloat16),
            pltpu.SemaphoreType.DMA((3,)),
        ],
        compiler_params=pltpu.CompilerParams(vmem_limit_bytes=10 << 20),
        cost_estimate=pl.CostEstimate(flops=5_000_000_000, bytes_accessed=4_000_000, transcendentals=2_000_000),
        name="profiles",
    )(geos, buffers["three m"], third_geos, gram)

    late_values = [buffers[name] for name in late_order]
    sign_next, coef = pl.pallas_call(
        functools.partial(step_kernel, len(late_values)),
        out_shape=(
            jax.ShapeDtypeStruct((slots, size, size), jnp.bfloat16),
            jax.ShapeDtypeStruct((8, LANES), jnp.float32),
        ),
        in_specs=[SMEM, SMEM, VMEM, VMEM, VMEM, VMEM] + [ANY] * (len(late_values) + 1),
        out_specs=(VMEM, VMEM),
        scratch_shapes=[
            pltpu.VMEM((total - late_from, LANES), jnp.bfloat16),
            pltpu.VMEM((full, full), jnp.bfloat16),
            pltpu.VMEM((size, full), jnp.bfloat16),
            pltpu.VMEM((size, full), jnp.bfloat16),
            pltpu.SemaphoreType.DMA((len(late_values),)),
        ],
        compiler_params=pltpu.CompilerParams(vmem_limit_bytes=(15 << 20) + (total - late_from) * LANES * 2),
        cost_estimate=pl.CostEstimate(flops=1_300_000_000, bytes_accessed=8_000_000, transcendentals=0),
        name="square_cube_coefficients",
    )(late_table, info, own_basis, spread, own, gram, *late_values, line)

    below = from_offset(coef, "layer", -1)
    above = from_offset(coef, "layer", 1)
    merged = jnp.concatenate(
        [
            coef[:, : 4 * SPAN],
            below[:, SPAN : 3 * SPAN],
            above[:, 3 * SPAN : 4 * SPAN],
            jnp.zeros((8, LANES - 7 * SPAN), jnp.float32),
        ],
        axis=1,
    )
    stacked = jnp.concatenate([merged] + [on_row(merged, di) for di in others], axis=0)
    received = [stacked] + [from_offset(stacked, "col", dc) for dc in column_steps[1:]]

    density = pl.pallas_call(
        functools.partial(density_kernel, len(column_steps)),
        out_shape=jax.ShapeDtypeStruct((BX * BY, BZ), jnp.float32),
        in_specs=[VMEM] * (len(column_steps) + 2),
        out_specs=VMEM,
        scratch_shapes=[pltpu.VMEM((BX * BY, tiles * SHELLS * LANES), jnp.bfloat16)],
        compiler_params=pltpu.CompilerParams(vmem_limit_bytes=16 << 20),
        cost_estimate=pl.CostEstimate(flops=310_000_000, bytes_accessed=4_000_000, transcendentals=0),
        name="density",
    )(*received, plane, line.reshape(tiles * SHELLS * LANES, BZ))
    return sign_next[None], density.reshape(BX, BY, BZ)


def solution(mesh):
    rows = P(("row", "col", "layer"), None, None, None)
    in_specs = (rows, P(), P(), P(), P(("row", "col", "layer"), None), P(), P(), P())
    out_specs = (rows, P("row", "col", "layer"))
    return jax.shard_map(local, mesh=mesh, in_specs=in_specs, out_specs=out_specs, check_vma=False)
```

```python
import functools

import jax
import jax.numpy as jnp
from jax import lax
from jax.experimental import pallas as pl
from jax.experimental.pallas import tpu as pltpu
from jax.sharding import PartitionSpec as P

BX = 16
BY = 16
BZ = 128
LANES = 128
UNROLL = 4
SHELLS = 6
SPAN = 3 * SHELLS
GEO = 16
VMEM = pl.BlockSpec(memory_space=pltpu.VMEM)
SMEM = pl.BlockSpec(memory_space=pltpu.SMEM)
ANY = pl.BlockSpec(memory_space=pl.ANY)
HBM = pl.BlockSpec(memory_space=pltpu.HBM)


def from_offset(x, axis, step):
    count = lax.axis_size(axis)
    return lax.ppermute(x, axis, [((i + step) % count, i) for i in range(count)])


def from_layer(x, flip):
    count = lax.axis_size("layer")
    return lax.ppermute(x, "layer", [(i ^ flip, i) for i in range(count)])


def column_targets(n_row):
    return 5 if n_row == 2 else 7


def target_place(n_row, step_row, step_lay, row):
    same = jnp.where(step_lay < 3, step_lay, -1)
    if n_row == 2:
        lead = step_lay - row
        across = jnp.where((lead >= 0) & (lead < 2), 3 + lead, -1)
    else:
        across = 3 + step_lay
    return jnp.where(step_row == 0, same, jnp.where(step_row == 1, across, -1))


class Places:
    def __init__(self, n_row, n_col, n_lay):
        self.n_row, self.n_col, self.n_lay = n_row, n_col, n_lay
        self.lay_bits = n_lay.bit_length() - 1
        self.col_bits = n_col.bit_length() - 1
        self.row = lax.axis_index("row")
        self.col = lax.axis_index("col")
        self.lay = lax.axis_index("layer")
        self.me = (((self.row << self.col_bits) + self.col) << self.lay_bits) + self.lay

    def split(self, atom):
        return (
            atom >> (self.lay_bits + self.col_bits),
            (atom >> self.lay_bits) & (self.n_col - 1),
            atom & (self.n_lay - 1),
        )


def load(sources, targets, sems):
    copies = [pltpu.make_async_copy(a, b, sems.at[i]) for i, (a, b) in enumerate(zip(sources, targets))]
    for copy in copies:
        copy.start()
    for copy in copies:
        copy.wait()


def own_ranks(at, neighbors_ref):
    seen = [jnp.int32(0)] * at.n_lay
    listed = []
    for w in range(neighbors_ref.shape[0]):
        atom = neighbors_ref[w, at.me]
        step_lay = (atom - at.lay) & (at.n_lay - 1)
        rank = jnp.int32(0)
        for k in range(at.n_lay):
            rank = jnp.where(step_lay == k, 3 * k + seen[k], rank)
            seen[k] = seen[k] + (step_lay == k).astype(jnp.int32)
        listed.append((atom, rank))
    return listed


def pick_kernel(axes, *refs):
    sign_ref, out_ref, geo_ref, neighbors_ref, extent_ref, x_ref, y_ref, z_ref, place_ref, loads, sems = refs[5:]
    at = Places(*axes)
    slots = sign_ref.shape[0]
    n_pick = place_ref.shape[0] - 1
    size = sign_ref.shape[1]
    for i in range(n_pick + 1):
        place_ref[i] = 0
    load(refs[:5], (neighbors_ref, extent_ref, x_ref, y_ref, z_ref), loads)
    ranks = own_ranks(at, neighbors_ref)
    for w, (atom, _) in enumerate(ranks):
        row, col, lay = at.split(atom)
        place = target_place(at.n_row, (row - at.row) & (at.n_row - 1), (lay - at.lay) & (at.n_lay - 1), at.row)
        place_ref[jnp.where((col == at.col) & (place >= 0), place, n_pick)] = w
    copies = []
    for i in range(n_pick):
        copy = pltpu.make_async_copy(sign_ref.at[place_ref[i]], out_ref.at[pl.ds(i * size, size)], sems.at[i])
        copy.start()
        copies.append(copy)
    sub = lax.broadcasted_iota(jnp.int32, (GEO, LANES), 0)
    lane_pair = lax.broadcasted_iota(jnp.int32, (GEO, LANES), 1) // SHELLS
    geo = jnp.zeros((GEO, LANES), jnp.int32)
    for w, (atom, rank) in enumerate(ranks):
        row, col, lay = at.split(atom)
        go_row = ((row - at.row + 1) & (at.n_row - 1)) - 1
        go_col = ((col - at.col + 1) & (at.n_col - 1)) - 1
        go_lay = jnp.minimum(((lay - at.lay + 1) & (at.n_lay - 1)) - 1, 1)
        twice_x = x_ref[at.me] + x_ref[atom] + BX * go_row
        twice_y = y_ref[at.me] + y_ref[atom] + BY * go_col
        twice_z = z_ref[at.me] + z_ref[atom] + BZ * go_lay - BZ
        extent = extent_ref[0, w]
        values = jnp.where(sub == 0, twice_x, jnp.where(sub == 1, twice_y, jnp.where(sub == 2, twice_z, extent)))
        geo = jnp.where(lane_pair == rank, values, geo)
    geo = geo.astype(jnp.float32).astype(geo_ref.dtype)
    geo_ref[...] = geo
    out_ref[n_pick * size : n_pick * size + GEO] = geo
    for copy in copies:
        copy.wait()


def prepare_kernel(axes, count, layout, late_from, *refs):
    basis_ref = refs[2]
    early_ref, late_ref, info_ref, spread_ref, own_basis_ref = refs[-11:-6]
    neighbors_ref, size_ref, known, inverse, layout_ref, loads = refs[-6:]
    at = Places(*axes)
    load(refs[:2], (neighbors_ref, size_ref), loads)
    slots, atoms = neighbors_ref.shape
    bits = atoms.bit_length() - 1
    for i, value in enumerate(layout):
        layout_ref[i] = value
    lines = count * at.n_lay

    def hot(rows, atom, first):
        sub = lax.broadcasted_iota(jnp.int32, (rows, SHELLS * atoms), 0)
        lane = lax.broadcasted_iota(jnp.int32, (rows, SHELLS * atoms), 1)
        return ((lane & (atoms - 1)) == atom) & (sub == first + (lane >> bits))

    def rows_of(chosen):
        picked = jnp.where(chosen, 1.0, 0.0).astype(jnp.bfloat16)
        return jnp.dot(picked, basis_ref[...], preferred_element_type=jnp.float32).astype(jnp.bfloat16)

    self_slot = jnp.int32(0)
    for w, (atom, rank) in enumerate(own_ranks(at, neighbors_ref)):
        row, col, lay = at.split(atom)
        step_row = (row - at.row) & (at.n_row - 1)
        step_col = (col - at.col) & (at.n_col - 1)
        self_slot = jnp.where(atom == at.me, w, self_slot)
        info_ref[w] = size_ref[atom]
        spread_ref[:, w * LANES : (w + 1) * LANES] = rows_of(hot(LANES, atom, rank * SHELLS))
        flip = lay ^ at.lay
        known[0, w] = atom
        known[1, w] = jnp.where(step_col == 0, 0, jnp.where(step_col == 1, 1, 2))
        known[2, w] = jnp.where(step_row == 0, 0, jnp.where(step_row == 1, 1, 2)) * at.n_lay + flip
        inverse[atom] = -1
    own_basis_ref[...] = rows_of(hot(16, at.me, 0))
    info_ref[slots] = size_ref[at.me]
    info_ref[slots + 1] = self_slot

    def row_of_pairs(v, totals):
        early, late = totals
        atom = known[0, v]
        side = known[1, v]
        line = known[2, v]
        for u in range(slots):
            inverse[neighbors_ref[u, atom]] = v * 16 + u

        def from_row(totals):
            total, late = totals
            for w in range(slots):
                mark = inverse[known[0, w]]
                chosen = ((mark >> 4) == v) & ((known[1, w] != 0) | (v <= w))
                where = layout_ref[line * slots + (mark & 15)]
                is_late = where >= late_from
                entry = v + 16 * w
                early_ref[total + 1] = entry + 256 * where
                late_ref[late + 1] = entry + 256 * (where - late_from)
                total = total + (chosen & ~is_late).astype(jnp.int32)
                late = late + (chosen & is_late).astype(jnp.int32)
            return total, late

        def from_column(totals):
            early, late = totals
            row, _, lay = at.split(atom)
            beside = layout_ref[lines * slots + (side - 1) * lines + line]
            for w in range(slots):
                other = known[0, w]
                mark = inverse[other]
                o_row, _, o_lay = at.split(other)
                d_row = (o_row - row) & (at.n_row - 1)
                d_lay = (o_lay - lay) & (at.n_lay - 1)
                there = target_place(at.n_row, d_row, d_lay, row)
                back = target_place(at.n_row, -d_row & (at.n_row - 1), -d_lay & (at.n_lay - 1), o_row)
                chosen = ((mark >> 4) == v) & (side == known[1, w]) & (there >= 0) & ((back < 0) | (v <= w))
                where = beside + there * LANES
                is_late = where >= late_from
                entry = v + 16 * w
                early_ref[early + 1] = entry + 256 * where
                late_ref[late + 1] = entry + 256 * (where - late_from)
                early = early + (chosen & ~is_late).astype(jnp.int32)
                late = late + (chosen & is_late).astype(jnp.int32)
            return early, late

        return lax.cond(side == 0, from_row, from_column, (early, late))

    totals = lax.fori_loop(0, slots, row_of_pairs, (jnp.int32(0), jnp.int32(0)))
    for ref, total in zip((early_ref, late_ref), totals):
        ref[0] = (total + UNROLL - 1) // UNROLL
        for i in range(UNROLL - 1):
            ref[total + i + 1] = ref[jnp.maximum(total, 1)]


def pack_kernel(moves, inputs, outputs, *refs):
    sems = refs[-1]
    copies = []
    for k, (source, start, rows, target, place) in enumerate(moves):
        copy = pltpu.make_async_copy(
            refs[source].at[pl.ds(start, rows)], refs[inputs + target].at[pl.ds(place, rows)], sems.at[k]
        )
        copy.start()
        copies.append(copy)
    for copy in copies:
        copy.wait()


def pack(values, plans, extra, name):
    moves, shapes = [], []
    for target, plan in enumerate(plans):
        place = 0
        for source, start, rows in plan:
            moves.append((source, start, rows, target, place))
            place += rows
        shapes.append(jax.ShapeDtypeStruct((place, LANES), values[0].dtype))
    inputs = len(values) + len(extra)
    return pl.pallas_call(
        functools.partial(pack_kernel, tuple(moves), inputs, len(plans)),
        out_shape=tuple(shapes),
        in_specs=[ANY] * inputs,
        out_specs=tuple([ANY] * len(plans)),
        scratch_shapes=[pltpu.SemaphoreType.DMA((len(moves),))],
        compiler_params=pltpu.CompilerParams(vmem_limit_bytes=1 << 20),
        cost_estimate=pl.CostEstimate(flops=0, bytes_accessed=3_000_000, transcendentals=0),
        name=name,
    )(*values, *extra)


def fill(piece_refs, pool, sems):
    copies = []
    place = 0
    for i, piece in enumerate(piece_refs):
        rows = piece.shape[0]
        copy = pltpu.make_async_copy(piece, pool.at[pl.ds(place, rows)], sems.at[i])
        copy.start()
        copies.append(copy)
        place += rows
    return copies


def place_pairs(table_ref, pool, gram, size):
    def place(i, carry):
        for k in range(UNROLL):
            entry = table_ref[i * UNROLL + k + 1]
            p = pl.multiple_of((entry & 15) * size, size)
            q = pl.multiple_of(((entry >> 4) & 15) * size, size)
            block = pool[pl.ds(pl.multiple_of(entry >> 8, 16), size)]
            gram[pl.ds(p, size), pl.ds(q, size)] = block
            gram[pl.ds(q, size), pl.ds(p, size)] = block.T
        return carry

    lax.fori_loop(0, table_ref[0], place, 0)


def gram_kernel(pieces, *refs):
    table_ref = refs[0]
    piece_refs = refs[1 : 1 + pieces]
    gram, pool, sems = refs[-3:]
    size = LANES
    copies = fill(piece_refs, pool, sems)
    for v in range(gram.shape[0] // size):
        gram[v * size : (v + 1) * size] = jnp.zeros((size, gram.shape[1]), gram.dtype)
    for copy in copies:
        copy.wait()
    place_pairs(table_ref, pool, gram, size)


def step_kernel(pieces, *refs):
    table_ref, info_ref, basis_ref, spread_ref, sign_ref, early_ref = refs[:6]
    piece_refs = refs[6 : 6 + pieces]
    next_ref, coef_ref, pool, gram, own, square, sems = refs[-7:]
    slots, size = sign_ref.shape[0], sign_ref.shape[1]
    copies = fill(piece_refs, pool, sems)
    for v in range(slots):
        gram[v * size : (v + 1) * size] = early_ref[v * size : (v + 1) * size]
    rows = lax.broadcasted_iota(jnp.int32, (size, size), 0)
    lanes = lax.broadcasted_iota(jnp.int32, (size, size), 1)
    own_size = info_ref[slots]
    self_slot = info_ref[slots + 1]
    for w in range(slots):
        kept = (rows < own_size) & (lanes < info_ref[w])
        block = jnp.where(kept, sign_ref[w].astype(jnp.float32), 0.0)
        own[:, w * size : (w + 1) * size] = block.astype(own.dtype)
    for copy in copies:
        copy.wait()
    place_pairs(table_ref, pool, gram, size)
    wide = 2 * size
    wide_lanes = lax.broadcasted_iota(jnp.int32, (size, wide), 1)
    wide_rows = lax.broadcasted_iota(jnp.int32, (size, wide), 0)

    def column_kept(n):
        first = info_ref[2 * n]
        second = info_ref[2 * n + 1]
        return (wide_lanes < first) | ((wide_lanes >= size) & (wide_lanes < size + second))

    for n in range(slots // 2):
        part = jnp.dot(own[...], gram[:, n * wide : (n + 1) * wide], preferred_element_type=jnp.float32)
        square[:, n * wide : (n + 1) * wide] = jnp.where(column_kept(n), part, 0.0).astype(square.dtype)
    basis = jnp.concatenate([basis_ref[...], basis_ref[...]], axis=1)
    coef = jnp.zeros((2 * basis_ref.shape[0], LANES), jnp.float32)
    across = (((1,), (1,)), ((), ()))
    for n in range(slots // 2):
        part = jnp.dot(square[...], gram[:, n * wide : (n + 1) * wide], preferred_element_type=jnp.float32)
        cube = jnp.where(column_kept(n), part, 0.0)
        full = 1.5 * own[:, n * wide : (n + 1) * wide].astype(jnp.float32) - 0.5 * cube
        next_ref[2 * n] = full[:, :size].astype(next_ref.dtype)
        next_ref[2 * n + 1] = full[:, size:].astype(next_ref.dtype)
        shift = (self_slot - 2 * n) * size
        is_self = (self_slot >= 2 * n) & (self_slot < 2 * n + 2)
        diag = (wide_lanes == wide_rows + shift) & (wide_rows < own_size) & is_self
        dmat = 0.5 * (jnp.where(diag, 1.0, 0.0) - full)
        high = dmat.astype(jnp.bfloat16)
        low = (dmat - high.astype(jnp.float32)).astype(jnp.bfloat16)
        half = jnp.dot(basis, jnp.concatenate([high, low], axis=0), preferred_element_type=jnp.float32)
        half_high = half.astype(jnp.bfloat16)
        half_low = (half - half_high.astype(jnp.float32)).astype(jnp.bfloat16)
        coef = coef + lax.dot_general(
            jnp.concatenate([half_high, half_low], axis=0),
            spread_ref[:, n * wide : (n + 1) * wide],
            across,
            preferred_element_type=jnp.float32,
        )
    coef = coef[: basis_ref.shape[0]] + coef[basis_ref.shape[0] :]
    coef_ref[...] = coef[: coef_ref.shape[0]]


def profile_kernel(periods, steps, mate_from, *refs):
    own_ref, mate_ref, third_ref = refs[:3]
    plane_ref, line_ref, geos, sems = refs[-4:]
    odd = (lax.axis_index("layer") & 1) == 1
    rows = len(steps) * GEO
    copies = []
    for k, source in enumerate((own_ref, mate_ref.at[pl.ds(mate_from, rows)], third_ref)):
        copy = pltpu.make_async_copy(source, geos.at[k], sems.at[k])
        copy.start()
        copies.append(copy)
    cells = plane_ref.shape[2]
    cell = lax.broadcasted_iota(jnp.int32, (cells, LANES), 0)
    grid_x = (cell // BY).astype(jnp.float32)
    grid_y = (cell % BY).astype(jnp.float32)
    grid_z = lax.broadcasted_iota(jnp.int32, (LANES, BZ), 1).astype(jnp.float32)
    lane = lax.broadcasted_iota(jnp.int32, (1, LANES), 1)
    shell = (lane % SHELLS + 1).astype(jnp.float32)
    valid = lane < 7 * SPAN
    from_own = lane < 4 * SPAN
    from_below = lane < 6 * SPAN
    lift = jnp.where(from_own, 0.0, jnp.where(from_below, -float(BZ), float(BZ))) + 0.5 * BZ

    def nearest(offset, period):
        return offset - period * jnp.floor(offset * (1.0 / period) + 0.5)

    for copy in copies:
        copy.wait()
    for o, (step_row, step_col) in enumerate(steps):
        own, first, third = (geos[k, o * GEO : (o + 1) * GEO].astype(jnp.float32) for k in range(3))
        below = jnp.where(odd, first, third)
        above = jnp.where(odd, third, first)
        moved = jnp.where(from_below, pltpu.roll(below, 3 * SPAN, axis=1), pltpu.roll(above, 3 * SPAN, axis=1))
        geo = jnp.where(from_own, own, moved)
        extent = jnp.where(valid, geo[3:4], 1.0)
        inverse = (SHELLS / extent) * (SHELLS / extent)
        reach = jnp.where(valid, extent, -1.0)
        rate_t = inverse / (shell * shell)
        packed = jnp.concatenate(
            [0.5 * geo[2:3] + lift, reach, rate_t, inverse, jnp.zeros((4, LANES), jnp.float32)], axis=0
        )
        sub = packed.T
        d_x = nearest(grid_x - (0.5 * geo[0:1] + float(BX * step_row)), periods[0])
        d_y = nearest(grid_y - (0.5 * geo[1:2] + float(BY * step_col)), periods[1])
        inside = (jnp.abs(d_x) <= reach) & (jnp.abs(d_y) <= reach)
        squared = d_x * d_x + d_y * d_y
        d_z = nearest(grid_z - sub[:, 0:1], periods[2])
        inside_z = jnp.abs(d_z) <= sub[:, 1:2]
        squared_z = d_z * d_z
        for s in range(SHELLS):
            part = 1.0 / ((s + 1) * (s + 1))
            rate = inverse * part + rate_t
            plane_ref[o, s] = jnp.where(inside, jnp.exp(-rate * squared), 0.0).astype(plane_ref.dtype)
            rate_z = sub[:, 3:4] * part + sub[:, 2:3]
            line_ref[o, s] = jnp.where(inside_z, jnp.exp(-rate_z * squared_z), 0.0).astype(line_ref.dtype)


def density_kernel(column_steps, last, *refs):
    own_ref, up_ref, down_ref, around_ref, plane_ref, line_ref, out_ref, terms = refs
    col = lax.axis_index("col")
    coef_refs = [
        own_ref[...],
        jnp.where(col == last, around_ref[...], up_ref[...]),
        jnp.where(col == 0, around_ref[...], down_ref[...]),
    ]
    for o in range(plane_ref.shape[0]):
        coef = coef_refs[o % column_steps]
        first = 8 * (o // column_steps)
        for s in range(SHELLS):
            scaled = plane_ref[o, s].astype(jnp.float32) * coef[first + s : first + s + 1, :]
            at = (o * SHELLS + s) * LANES
            terms[:, at : at + LANES] = scaled.astype(terms.dtype)
    out_ref[...] = jnp.dot(terms[...], line_ref[...], preferred_element_type=jnp.float32)


def local(sign_start, neighbors, atom_size, basis_proj, pair_extent, atom_x, atom_y, atom_z):
    n_row = lax.axis_size("row")
    n_col = lax.axis_size("col")
    n_lay = lax.axis_size("layer")
    assert n_lay == 4 and n_col >= 4 and (n_row == 2 or n_row >= 4)
    assert n_row & (n_row - 1) == 0 and n_col & (n_col - 1) == 0
    axes = (n_row, n_col, n_lay)
    atoms, slots = neighbors.shape
    size = sign_start.shape[2]
    steps = [0, 1] if n_row == 2 else [0, 1, -1]
    count = len(steps)
    others = range(1, count)
    own = sign_start[0]
    flat = own.reshape(slots * size, size)
    listings = neighbors.T
    full = slots * size
    half = full // 2
    most = half - size
    n_pick = column_targets(n_row)
    picks = n_pick * size
    part = picks + GEO

    def on_row(value, di):
        return from_offset(value, "row", steps[di])

    x_row = {di: on_row(flat, di) for di in others}
    y_row = from_layer(flat, 2)
    m_row = from_layer(flat, 1)
    picked, geo = pl.pallas_call(
        functools.partial(pick_kernel, axes),
        out_shape=(
            jax.ShapeDtypeStruct((part, size), own.dtype),
            jax.ShapeDtypeStruct((GEO, LANES), own.dtype),
        ),
        in_specs=[HBM] * 6,
        out_specs=(VMEM, VMEM),
        scratch_shapes=[
            pltpu.SMEM((slots, atoms), jnp.int32),
            pltpu.SMEM((1, slots), jnp.int32),
            pltpu.SMEM((atoms,), jnp.int32),
            pltpu.SMEM((atoms,), jnp.int32),
            pltpu.SMEM((atoms,), jnp.int32),
            pltpu.SMEM((n_pick + 1,), jnp.int32),
            pltpu.SemaphoreType.DMA((5,)),
            pltpu.SemaphoreType.DMA((n_pick,)),
        ],
        compiler_params=pltpu.CompilerParams(vmem_limit_bytes=60 << 20),
        name="pick_column_blocks",
    )(listings, pair_extent, atom_x, atom_y, atom_z, own)
    up = from_offset(picked, "col", 1)
    down = from_offset(picked, "col", -1)

    halves = pack(
        [y_row] + [x_row[di] for di in others],
        [[(0, half, most)]] + [[(di, 0, most)] for di in others],
        [],
        "pack_halves",
    )
    ends = {di: on_row(halves[0], di) for di in others}
    tops = {di: from_layer(halves[di], 2) for di in others}

    at = {}
    buffers = {}

    def note(name, value, contents):
        buffers[name] = value
        start = 0
        for what, rows in contents:
            if what is not None:
                at[what] = (name, start)
            start += rows

    def row_of(di, flip, start=0, stop=slots):
        return [(("row", slot, di, flip), size) for slot in range(start, stop)]

    halfway = slots // 2

    def side_of(kind, di, flip):
        return [((kind, di, flip), picks)]

    note("own", flat, row_of(0, 0))
    note("mate", m_row, row_of(0, 1))
    note("far", y_row, row_of(0, 2))
    note("up", up, side_of("up", 0, 0) + [(("up geo", 0, 0), GEO)])
    note("down", down, side_of("down", 0, 0) + [(("down geo", 0, 0), GEO)])
    note("geo", geo, [(("geo", 0, 0), GEO)])
    for di in others:
        note(("x", di), x_row[di], row_of(di, 0))
        note(("end", di), ends[di], row_of(di, 2, halfway, slots - 1))
        note(("top", di), tops[di], row_of(di, 2, 0, halfway - 1))

    corners = [("end", di) for di in others] + [("top", di) for di in others]
    names = ["up", "down", "geo", "far"] + [("x", di) for di in others]
    plans = [
        [(0, 0, picks), (3, full - size, size), (2, 0, GEO), (0, picks, GEO), (1, picks, GEO)],
        [(1, 0, picks)] + [(di + 3, most, size) for di in others],
    ]
    two_x, two_y = pack(
        [buffers[name] for name in names], plans, [buffers[name] for name in corners] + [m_row], "pack_two"
    )
    to_mate = corners + ["up", "down"]
    plans = [[(i, 0, picks if name in ("up", "down") else most) for i, name in enumerate(to_mate)]]
    two_m = pack([buffers[name] for name in to_mate], plans, [], "pack_two_mate")[0]
    for di in others:
        note(("mate x", di), from_layer(x_row[di], 1), row_of(di, 1))
    note("mate far", from_layer(y_row, 1), row_of(0, 3))

    early_order = ["own", "mate", "far", "up", "down", "geo"] + [("x", di) for di in others]
    early_order += [("mate x", di) for di in others] + ["mate far"]
    early_order += corners + [("two x", di) for di in others] + ["two y", "two m"]
    late_order = [("three x", di) for di in others] + ["three y", "three m"]
    late_order += ["four"]

    contents = {}
    for di in others:
        contents["two x", di] = side_of("up", di, 0) + row_of(di, 2, slots - 1, slots) + [(("geo", di, 0), GEO)]
        contents["two x", di] += [(("up geo", di, 0), GEO), (("down geo", di, 0), GEO)]
    contents["two y"] = side_of("down", 0, 2)
    contents["two y"] += sum([row_of(di, 2, halfway - 1, halfway) for di in others], [])
    contents["two m"] = sum([row_of(di, 3, halfway, slots - 1) for di in others], [])
    contents["two m"] += sum([row_of(di, 3, 0, halfway - 1) for di in others], [])
    contents["two m"] += side_of("up", 0, 1) + side_of("down", 0, 1)
    for di in others:
        contents["three x", di] = side_of("down", di, 0) + side_of("down", di, 2)
    contents["three y"] = side_of("up", 0, 2) + sum([side_of("up", di, 2) for di in others], [])
    contents["three m"] = []
    for di in others:
        contents["three m"] += side_of("up", di, 1) + row_of(di, 3, slots - 1, slots)
    contents["three m"] += side_of("down", 0, 3)
    contents["three m"] += sum([row_of(di, 3, halfway - 1, halfway) for di in others], [])
    contents["three m"] += [("geos", count * 3 * GEO)]
    contents["four"] = []
    for di in others:
        contents["four"] += side_of("down", di, 1) + side_of("down", di, 3)
    contents["four"] += side_of("up", 0, 3) + sum([side_of("up", di, 3) for di in others], [])
    lengths = {name: sum(rows for _, rows in content) for name, content in contents.items()}
    for name in early_order:
        if name in buffers:
            lengths[name] = buffers[name].shape[0]
    base = {}
    total = 0
    for name in early_order + late_order:
        base[name] = total
        total += lengths[name]
        if name == early_order[-1]:
            late_from = total
    located = dict(at)
    for name, content in contents.items():
        start = 0
        for what, rows in content:
            located[what] = (name, start)
            start += rows
    layout = [
        base[located["row", slot, di, flip][0]] + located["row", slot, di, flip][1]
        for di in range(count)
        for flip in range(n_lay)
        for slot in range(slots)
    ]
    layout += [
        base[located[kind, di, flip][0]] + located[kind, di, flip][1]
        for kind in ("up", "down")
        for di in range(count)
        for flip in range(n_lay)
    ]
    pairs = slots * (slots + 1) // 2
    entries = pairs + UNROLL + 1
    early_table, late_table, info, spread, own_basis = pl.pallas_call(
        functools.partial(prepare_kernel, axes, count, tuple(layout), late_from),
        out_shape=(
            jax.ShapeDtypeStruct((entries,), jnp.int32),
            jax.ShapeDtypeStruct((entries,), jnp.int32),
            jax.ShapeDtypeStruct((slots + 2,), jnp.int32),
            jax.ShapeDtypeStruct((LANES, full), jnp.bfloat16),
            jax.ShapeDtypeStruct((16, size), jnp.bfloat16),
        ),
        in_specs=[HBM, HBM, VMEM, ANY],
        out_specs=(SMEM, SMEM, SMEM, VMEM, VMEM),
        scratch_shapes=[
            pltpu.SMEM((slots, atoms), jnp.int32),
            pltpu.SMEM((atoms,), jnp.int32),
            pltpu.SMEM((3, slots), jnp.int32),
            pltpu.SMEM((atoms,), jnp.int32),
            pltpu.SMEM((len(layout),), jnp.int32),
            pltpu.SemaphoreType.DMA((2,)),
        ],
        compiler_params=pltpu.CompilerParams(vmem_limit_bytes=(2 << 20) + atoms * 16384),
        cost_estimate=pl.CostEstimate(flops=6_000_000_000, bytes_accessed=8_000_000, transcendentals=0),
        name="prepare",
    )(listings, atom_size, basis_proj.transpose(1, 0, 2).reshape(SHELLS * atoms, size), two_x)

    for di in others:
        note(("two x", di), on_row(two_x, di), contents["two x", di])
    note("two y", from_layer(two_y, 2), contents["two y"])
    note("two m", from_layer(two_m, 1), contents["two m"])

    names = ["up", "down", "two y", "geo"] + [("two x", di) for di in others]
    place = {name: i for i, name in enumerate(names)}
    gather = []
    for di in range(count):
        for kind in ("geo", "up geo", "down geo"):
            name, start = at[kind, di, 0]
            gather.append((place[name], start, GEO))
    xs = [place["two x", di] for di in others]
    plans = [
        [(1, 0, picks), (2, 0, picks)],
        [(0, 0, picks)] + [(x, 0, picks) for x in xs],
        [(x, 0, picks + size) for x in xs] + [(2, 0, lengths["two y"])] + gather,
        gather,
    ]
    three_x, three_y, three_m, geos = pack([buffers[name] for name in names], plans, [own_basis], "pack_three")
    for di in others:
        note(("three x", di), on_row(three_x, di), contents["three x", di])
    note("three y", from_layer(three_y, 2), contents["three y"])
    note("three m", from_layer(three_m, 1), contents["three m"])
    third_geos = from_layer(geos, 3)

    early_values = [buffers[name] for name in early_order]
    gram = pl.pallas_call(
        functools.partial(gram_kernel, len(early_values)),
        out_shape=jax.ShapeDtypeStruct((full, full), jnp.bfloat16),
        in_specs=[SMEM] + [ANY] * (len(early_values) + 1),
        out_specs=VMEM,
        scratch_shapes=[
            pltpu.VMEM((late_from, LANES), jnp.bfloat16),
            pltpu.SemaphoreType.DMA((len(early_values),)),
        ],
        compiler_params=pltpu.CompilerParams(vmem_limit_bytes=(6 << 20) + late_from * LANES * 2),
        cost_estimate=pl.CostEstimate(flops=1000, bytes_accessed=1000, transcendentals=0),
        name="gram_early",
    )(early_table, *early_values, three_x)

    thirds = [buffers["three x", di] for di in others] + [buffers["three y"]]
    four = pack(thirds, [[(i, 0, value.shape[0]) for i, value in enumerate(thirds)]], [gram, third_geos], "pack_four")[0]
    note("four", from_layer(four, 1), contents["four"])

    column_steps = (0, 1, -1)
    tile_steps = [(dr, dc) for dr in steps for dc in column_steps]
    tiles = len(tile_steps)
    periods = (float(BX * n_row), float(BY * n_col), float(BZ * n_lay))
    plane, line = pl.pallas_call(
        functools.partial(profile_kernel, periods, tile_steps, at["geos"][1]),
        out_shape=(
            jax.ShapeDtypeStruct((tiles, SHELLS, BX * BY, LANES), jnp.bfloat16),
            jax.ShapeDtypeStruct((tiles, SHELLS, LANES, BZ), jnp.bfloat16),
        ),
        in_specs=[ANY] * 4,
        out_specs=(VMEM, VMEM),
        scratch_shapes=[
            pltpu.VMEM((3, tiles * GEO, LANES), jnp.bfloat16),
            pltpu.SemaphoreType.DMA((3,)),
        ],
        compiler_params=pltpu.CompilerParams(vmem_limit_bytes=10 << 20),
        cost_estimate=pl.CostEstimate(flops=5_000_000_000, bytes_accessed=4_000_000, transcendentals=2_000_000),
        name="profiles",
    )(geos, buffers["three m"], third_geos, gram)

    late_values = [buffers[name] for name in late_order]
    sign_next, coef = pl.pallas_call(
        functools.partial(step_kernel, len(late_values)),
        out_shape=(
            jax.ShapeDtypeStruct((slots, size, size), jnp.bfloat16),
            jax.ShapeDtypeStruct((8, LANES), jnp.float32),
        ),
        in_specs=[SMEM, SMEM, VMEM, VMEM, VMEM, VMEM] + [ANY] * (len(late_values) + 1),
        out_specs=(VMEM, VMEM),
        scratch_shapes=[
            pltpu.VMEM((total - late_from, LANES), jnp.bfloat16),
            pltpu.VMEM((full, full), jnp.bfloat16),
            pltpu.VMEM((size, full), jnp.bfloat16),
            pltpu.VMEM((size, full), jnp.bfloat16),
            pltpu.SemaphoreType.DMA((len(late_values),)),
        ],
        compiler_params=pltpu.CompilerParams(vmem_limit_bytes=(15 << 20) + (total - late_from) * LANES * 2),
        cost_estimate=pl.CostEstimate(flops=1_300_000_000, bytes_accessed=8_000_000, transcendentals=0),
        name="square_cube_coefficients",
    )(late_table, info, own_basis, spread, own, gram, *late_values, line)

    mate_coef = from_layer(coef, 1)
    third_coef = from_layer(coef, 3)
    odd = lax.axis_index("layer") % 2 == 1
    below = jnp.where(odd, mate_coef, third_coef)
    above = jnp.where(odd, third_coef, mate_coef)
    merged = jnp.concatenate(
        [
            coef[:, : 4 * SPAN],
            below[:, SPAN : 3 * SPAN],
            above[:, 3 * SPAN : 4 * SPAN],
            jnp.zeros((8, LANES - 7 * SPAN), jnp.float32),
        ],
        axis=1,
    )
    stacked = jnp.concatenate([merged] + [on_row(merged, di) for di in others], axis=0)
    last = n_col - 1
    from_up = lax.ppermute(stacked, "col", [(i + 1, i) for i in range(last)])
    from_down = lax.ppermute(stacked, "col", [(i, i + 1) for i in range(last)])
    around = lax.ppermute(stacked, "col", [(0, last), (last, 0)])
    received = [stacked, from_up, from_down, around]

    density = pl.pallas_call(
        functools.partial(density_kernel, len(column_steps), last),
        out_shape=jax.ShapeDtypeStruct((BX * BY, BZ), jnp.float32),
        in_specs=[VMEM] * (len(received) + 2),
        out_specs=VMEM,
        scratch_shapes=[pltpu.VMEM((BX * BY, tiles * SHELLS * LANES), jnp.bfloat16)],
        compiler_params=pltpu.CompilerParams(vmem_limit_bytes=16 << 20),
        cost_estimate=pl.CostEstimate(flops=310_000_000, bytes_accessed=4_000_000, transcendentals=0),
        name="density",
    )(*received, plane, line.reshape(tiles * SHELLS * LANES, BZ))
    return sign_next[None], density.reshape(BX, BY, BZ)


def solution(mesh):
    rows = P(("row", "col", "layer"), None, None, None)
    in_specs = (rows, P(), P(), P(), P(("row", "col", "layer"), None), P(), P(), P())
    out_specs = (rows, P("row", "col", "layer"))
    return jax.shard_map(local, mesh=mesh, in_specs=in_specs, out_specs=out_specs, check_vma=False)
```

```python
import functools

import jax
import jax.numpy as jnp
from jax import lax
from jax.experimental import pallas as pl
from jax.experimental.pallas import tpu as pltpu
from jax.sharding import PartitionSpec as P

BX = 16
BY = 16
BZ = 128
LANES = 128
UNROLL = 4
SHELLS = 6
SPAN = 3 * SHELLS
GEO = 16
VMEM = pl.BlockSpec(memory_space=pltpu.VMEM)
SMEM = pl.BlockSpec(memory_space=pltpu.SMEM)
ANY = pl.BlockSpec(memory_space=pl.ANY)
HBM = pl.BlockSpec(memory_space=pltpu.HBM)


def from_offset(x, axis, step):
    count = lax.axis_size(axis)
    return lax.ppermute(x, axis, [((i + step) % count, i) for i in range(count)])


def from_column(x, side):
    count = lax.axis_size("col")
    step = [1 if (i + side) % 2 == 0 else -1 for i in range(count)]
    return lax.ppermute(x, "col", [((i + step[i]) % count, i) for i in range(count)])


def from_layer(x, flip):
    count = lax.axis_size("layer")
    return lax.ppermute(x, "layer", [(i ^ flip, i) for i in range(count)])


def column_targets(n_row):
    return 5 if n_row == 2 else 7


def target_place(n_row, step_row, step_lay, row):
    same = jnp.where(step_lay < 3, step_lay, -1)
    if n_row == 2:
        lead = step_lay - row
        across = jnp.where((lead >= 0) & (lead < 2), 3 + lead, -1)
    else:
        across = 3 + step_lay
    return jnp.where(step_row == 0, same, jnp.where(step_row == 1, across, -1))


class Places:
    def __init__(self, n_row, n_col, n_lay):
        self.n_row, self.n_col, self.n_lay = n_row, n_col, n_lay
        self.lay_bits = n_lay.bit_length() - 1
        self.col_bits = n_col.bit_length() - 1
        self.row = lax.axis_index("row")
        self.col = lax.axis_index("col")
        self.lay = lax.axis_index("layer")
        self.me = (((self.row << self.col_bits) + self.col) << self.lay_bits) + self.lay

    def split(self, atom):
        return (
            atom >> (self.lay_bits + self.col_bits),
            (atom >> self.lay_bits) & (self.n_col - 1),
            atom & (self.n_lay - 1),
        )


def load(sources, targets, sems):
    copies = [pltpu.make_async_copy(a, b, sems.at[i]) for i, (a, b) in enumerate(zip(sources, targets))]
    for copy in copies:
        copy.start()
    for copy in copies:
        copy.wait()


def own_ranks(at, neighbors_ref):
    seen = [jnp.int32(0)] * at.n_lay
    listed = []
    for w in range(neighbors_ref.shape[0]):
        atom = neighbors_ref[w, at.me]
        step_lay = (atom - at.lay) & (at.n_lay - 1)
        rank = jnp.int32(0)
        for k in range(at.n_lay):
            rank = jnp.where(step_lay == k, 3 * k + seen[k], rank)
            seen[k] = seen[k] + (step_lay == k).astype(jnp.int32)
        listed.append((atom, rank))
    return listed


def pick_kernel(axes, *refs):
    sign_ref, out_ref, neighbors_ref, extent_ref, x_ref, y_ref, z_ref, place_ref, loads, sems = refs[5:]
    at = Places(*axes)
    slots = sign_ref.shape[0]
    n_pick = place_ref.shape[0] - 1
    size = sign_ref.shape[1]
    for i in range(n_pick + 1):
        place_ref[i] = 0
    load(refs[:5], (neighbors_ref, extent_ref, x_ref, y_ref, z_ref), loads)
    ranks = own_ranks(at, neighbors_ref)
    for w, (atom, _) in enumerate(ranks):
        row, col, lay = at.split(atom)
        place = target_place(at.n_row, (row - at.row) & (at.n_row - 1), (lay - at.lay) & (at.n_lay - 1), at.row)
        place_ref[jnp.where((col == at.col) & (place >= 0), place, n_pick)] = w
    copies = []
    for i in range(n_pick):
        copy = pltpu.make_async_copy(sign_ref.at[place_ref[i]], out_ref.at[pl.ds(i * size, size)], sems.at[i])
        copy.start()
        copies.append(copy)
    sub = lax.broadcasted_iota(jnp.int32, (GEO, LANES), 0)
    lane_pair = lax.broadcasted_iota(jnp.int32, (GEO, LANES), 1) // SHELLS
    geo = jnp.zeros((GEO, LANES), jnp.int32)
    for w, (atom, rank) in enumerate(ranks):
        row, col, lay = at.split(atom)
        go_row = ((row - at.row + 1) & (at.n_row - 1)) - 1
        go_col = ((col - at.col + 1) & (at.n_col - 1)) - 1
        go_lay = jnp.minimum(((lay - at.lay + 1) & (at.n_lay - 1)) - 1, 1)
        twice_x = x_ref[at.me] + x_ref[atom] + BX * go_row
        twice_y = y_ref[at.me] + y_ref[atom] + BY * go_col
        twice_z = z_ref[at.me] + z_ref[atom] + BZ * go_lay - BZ
        extent = extent_ref[0, w]
        values = jnp.where(sub == 0, twice_x, jnp.where(sub == 1, twice_y, jnp.where(sub == 2, twice_z, extent)))
        geo = jnp.where(lane_pair == rank, values, geo)
    out_ref[n_pick * size :] = geo.astype(jnp.float32).astype(out_ref.dtype)
    for copy in copies:
        copy.wait()


def prepare_kernel(axes, count, layout, late_from, *refs):
    basis_ref = refs[2]
    early_ref, late_ref, info_ref, spread_ref, own_basis_ref = refs[-11:-6]
    neighbors_ref, size_ref, known, inverse, layout_ref, loads = refs[-6:]
    at = Places(*axes)
    load(refs[:2], (neighbors_ref, size_ref), loads)
    slots, atoms = neighbors_ref.shape
    bits = atoms.bit_length() - 1
    for i, value in enumerate(layout):
        layout_ref[i] = value
    lines = count * at.n_lay

    def hot(rows, atom, first):
        sub = lax.broadcasted_iota(jnp.int32, (rows, SHELLS * atoms), 0)
        lane = lax.broadcasted_iota(jnp.int32, (rows, SHELLS * atoms), 1)
        return ((lane & (atoms - 1)) == atom) & (sub == first + (lane >> bits))

    def rows_of(chosen):
        picked = jnp.where(chosen, 1.0, 0.0).astype(jnp.bfloat16)
        return jnp.dot(picked, basis_ref[...], preferred_element_type=jnp.float32).astype(jnp.bfloat16)

    self_slot = jnp.int32(0)
    for w, (atom, rank) in enumerate(own_ranks(at, neighbors_ref)):
        row, col, lay = at.split(atom)
        step_row = (row - at.row) & (at.n_row - 1)
        self_slot = jnp.where(atom == at.me, w, self_slot)
        info_ref[w] = size_ref[atom]
        spread_ref[:, w * LANES : (w + 1) * LANES] = rows_of(hot(LANES, atom, rank * SHELLS))
        flip = lay ^ at.lay
        known[0, w] = atom
        known[1, w] = jnp.where(col == at.col, 0, jnp.where(col == (at.col ^ 1), 1, 2))
        known[2, w] = jnp.where(step_row == 0, 0, jnp.where(step_row == 1, 1, 2)) * at.n_lay + flip
        inverse[atom] = -1
    own_basis_ref[...] = rows_of(hot(16, at.me, 0))
    info_ref[slots] = size_ref[at.me]
    info_ref[slots + 1] = self_slot

    def row_of_pairs(v, totals):
        early, late = totals
        atom = known[0, v]
        side = known[1, v]
        line = known[2, v]
        for u in range(slots):
            inverse[neighbors_ref[u, atom]] = v * 16 + u

        def from_row(totals):
            total, late = totals
            for w in range(slots):
                mark = inverse[known[0, w]]
                chosen = ((mark >> 4) == v) & ((known[1, w] != 0) | (v <= w))
                where = layout_ref[line * slots + (mark & 15)]
                is_late = where >= late_from
                entry = v + 16 * w
                early_ref[total + 1] = entry + 256 * where
                late_ref[late + 1] = entry + 256 * (where - late_from)
                total = total + (chosen & ~is_late).astype(jnp.int32)
                late = late + (chosen & is_late).astype(jnp.int32)
            return total, late

        def from_column(totals):
            early, late = totals
            row, _, lay = at.split(atom)
            beside = layout_ref[lines * slots + (side - 1) * lines + line]
            for w in range(slots):
                other = known[0, w]
                mark = inverse[other]
                o_row, _, o_lay = at.split(other)
                d_row = (o_row - row) & (at.n_row - 1)
                d_lay = (o_lay - lay) & (at.n_lay - 1)
                there = target_place(at.n_row, d_row, d_lay, row)
                back = target_place(at.n_row, -d_row & (at.n_row - 1), -d_lay & (at.n_lay - 1), o_row)
                chosen = ((mark >> 4) == v) & (side == known[1, w]) & (there >= 0) & ((back < 0) | (v <= w))
                where = beside + there * LANES
                is_late = where >= late_from
                entry = v + 16 * w
                early_ref[early + 1] = entry + 256 * where
                late_ref[late + 1] = entry + 256 * (where - late_from)
                early = early + (chosen & ~is_late).astype(jnp.int32)
                late = late + (chosen & is_late).astype(jnp.int32)
            return early, late

        return lax.cond(side == 0, from_row, from_column, (early, late))

    totals = lax.fori_loop(0, slots, row_of_pairs, (jnp.int32(0), jnp.int32(0)))
    for ref, total in zip((early_ref, late_ref), totals):
        ref[0] = (total + UNROLL - 1) // UNROLL
        for i in range(UNROLL - 1):
            ref[total + i + 1] = ref[jnp.maximum(total, 1)]


def pack_kernel(moves, inputs, outputs, *refs):
    sems = refs[-1]
    copies = []
    for k, (source, start, rows, target, place) in enumerate(moves):
        copy = pltpu.make_async_copy(
            refs[source].at[pl.ds(start, rows)], refs[inputs + target].at[pl.ds(place, rows)], sems.at[k]
        )
        copy.start()
        copies.append(copy)
    for copy in copies:
        copy.wait()


def pack(values, plans, extra, name):
    moves, shapes = [], []
    for target, plan in enumerate(plans):
        place = 0
        for source, start, rows in plan:
            moves.append((source, start, rows, target, place))
            place += rows
        shapes.append(jax.ShapeDtypeStruct((place, LANES), values[0].dtype))
    inputs = len(values) + len(extra)
    return pl.pallas_call(
        functools.partial(pack_kernel, tuple(moves), inputs, len(plans)),
        out_shape=tuple(shapes),
        in_specs=[ANY] * inputs,
        out_specs=tuple([ANY] * len(plans)),
        scratch_shapes=[pltpu.SemaphoreType.DMA((len(moves),))],
        compiler_params=pltpu.CompilerParams(vmem_limit_bytes=1 << 20),
        cost_estimate=pl.CostEstimate(flops=0, bytes_accessed=3_000_000, transcendentals=0),
        name=name,
    )(*values, *extra)


def fill(piece_refs, pool, sems):
    copies = []
    place = 0
    for i, piece in enumerate(piece_refs):
        rows = piece.shape[0]
        copy = pltpu.make_async_copy(piece, pool.at[pl.ds(place, rows)], sems.at[i])
        copy.start()
        copies.append(copy)
        place += rows
    return copies


def place_pairs(table_ref, pool, gram, size):
    def place(i, carry):
        for k in range(UNROLL):
            entry = table_ref[i * UNROLL + k + 1]
            p = pl.multiple_of((entry & 15) * size, size)
            q = pl.multiple_of(((entry >> 4) & 15) * size, size)
            block = pool[pl.ds(pl.multiple_of(entry >> 8, 16), size)]
            gram[pl.ds(p, size), pl.ds(q, size)] = block
            gram[pl.ds(q, size), pl.ds(p, size)] = block.T
        return carry

    lax.fori_loop(0, table_ref[0], place, 0)


def gram_kernel(pieces, *refs):
    table_ref = refs[0]
    piece_refs = refs[1 : 1 + pieces]
    gram, pool, sems = refs[-3:]
    size = LANES
    copies = fill(piece_refs, pool, sems)
    for v in range(gram.shape[0] // size):
        gram[v * size : (v + 1) * size] = jnp.zeros((size, gram.shape[1]), gram.dtype)
    for copy in copies:
        copy.wait()
    place_pairs(table_ref, pool, gram, size)


def step_kernel(pieces, *refs):
    table_ref, info_ref, basis_ref, spread_ref, sign_ref, early_ref = refs[:6]
    piece_refs = refs[6 : 6 + pieces]
    next_ref, coef_ref, pool, gram, own, square, sems = refs[-7:]
    slots, size = sign_ref.shape[0], sign_ref.shape[1]
    copies = fill(piece_refs, pool, sems)
    for v in range(slots):
        gram[v * size : (v + 1) * size] = early_ref[v * size : (v + 1) * size]
    rows = lax.broadcasted_iota(jnp.int32, (size, size), 0)
    lanes = lax.broadcasted_iota(jnp.int32, (size, size), 1)
    own_size = info_ref[slots]
    self_slot = info_ref[slots + 1]
    for w in range(slots):
        kept = (rows < own_size) & (lanes < info_ref[w])
        block = jnp.where(kept, sign_ref[w].astype(jnp.float32), 0.0)
        own[:, w * size : (w + 1) * size] = block.astype(own.dtype)
    for copy in copies:
        copy.wait()
    place_pairs(table_ref, pool, gram, size)
    wide = 2 * size
    wide_lanes = lax.broadcasted_iota(jnp.int32, (size, wide), 1)
    wide_rows = lax.broadcasted_iota(jnp.int32, (size, wide), 0)

    def column_kept(n):
        first = info_ref[2 * n]
        second = info_ref[2 * n + 1]
        return (wide_lanes < first) | ((wide_lanes >= size) & (wide_lanes < size + second))

    for n in range(slots // 2):
        part = jnp.dot(own[...], gram[:, n * wide : (n + 1) * wide], preferred_element_type=jnp.float32)
        square[:, n * wide : (n + 1) * wide] = jnp.where(column_kept(n), part, 0.0).astype(square.dtype)
    basis = jnp.concatenate([basis_ref[...], basis_ref[...]], axis=1)
    coef = jnp.zeros((2 * basis_ref.shape[0], LANES), jnp.float32)
    across = (((1,), (1,)), ((), ()))
    for n in range(slots // 2):
        part = jnp.dot(square[...], gram[:, n * wide : (n + 1) * wide], preferred_element_type=jnp.float32)
        cube = jnp.where(column_kept(n), part, 0.0)
        full = 1.5 * own[:, n * wide : (n + 1) * wide].astype(jnp.float32) - 0.5 * cube
        next_ref[2 * n] = full[:, :size].astype(next_ref.dtype)
        next_ref[2 * n + 1] = full[:, size:].astype(next_ref.dtype)
        shift = (self_slot - 2 * n) * size
        is_self = (self_slot >= 2 * n) & (self_slot < 2 * n + 2)
        diag = (wide_lanes == wide_rows + shift) & (wide_rows < own_size) & is_self
        dmat = 0.5 * (jnp.where(diag, 1.0, 0.0) - full)
        high = dmat.astype(jnp.bfloat16)
        low = (dmat - high.astype(jnp.float32)).astype(jnp.bfloat16)
        half = jnp.dot(basis, jnp.concatenate([high, low], axis=0), preferred_element_type=jnp.float32)
        half_high = half.astype(jnp.bfloat16)
        half_low = (half - half_high.astype(jnp.float32)).astype(jnp.bfloat16)
        coef = coef + lax.dot_general(
            jnp.concatenate([half_high, half_low], axis=0),
            spread_ref[:, n * wide : (n + 1) * wide],
            across,
            preferred_element_type=jnp.float32,
        )
    coef = coef[: basis_ref.shape[0]] + coef[basis_ref.shape[0] :]
    coef_ref[...] = coef[: coef_ref.shape[0]]


def profile_kernel(periods, steps, mate_from, *refs):
    own_ref, mate_ref, third_ref = refs[:3]
    plane_ref, line_ref, geos, sems = refs[-4:]
    odd = (lax.axis_index("layer") & 1) == 1
    rows = len(steps) * GEO
    copies = []
    for k, source in enumerate((own_ref, mate_ref.at[pl.ds(mate_from, rows)], third_ref)):
        copy = pltpu.make_async_copy(source, geos.at[k], sems.at[k])
        copy.start()
        copies.append(copy)
    cells = plane_ref.shape[2]
    cell = lax.broadcasted_iota(jnp.int32, (cells, LANES), 0)
    grid_x = (cell // BY).astype(jnp.float32)
    grid_y = (cell % BY).astype(jnp.float32)
    grid_z = lax.broadcasted_iota(jnp.int32, (LANES, BZ), 1).astype(jnp.float32)
    lane = lax.broadcasted_iota(jnp.int32, (1, LANES), 1)
    shell = (lane % SHELLS + 1).astype(jnp.float32)
    valid = lane < 7 * SPAN
    from_own = lane < 4 * SPAN
    from_below = lane < 6 * SPAN
    lift = jnp.where(from_own, 0.0, jnp.where(from_below, -float(BZ), float(BZ))) + 0.5 * BZ

    def nearest(offset, period):
        return offset - period * jnp.floor(offset * (1.0 / period) + 0.5)

    for copy in copies:
        copy.wait()
    ahead = 1.0 - 2.0 * (lax.axis_index("col") & 1).astype(jnp.float32)
    for o, (step_row, side) in enumerate(steps):
        own, first, third = (geos[k, o * GEO : (o + 1) * GEO].astype(jnp.float32) for k in range(3))
        below = jnp.where(odd, first, third)
        above = jnp.where(odd, third, first)
        moved = jnp.where(from_below, pltpu.roll(below, 3 * SPAN, axis=1), pltpu.roll(above, 3 * SPAN, axis=1))
        geo = jnp.where(from_own, own, moved)
        extent = jnp.where(valid, geo[3:4], 1.0)
        inverse = (SHELLS / extent) * (SHELLS / extent)
        reach = jnp.where(valid, extent, -1.0)
        rate_t = inverse / (shell * shell)
        packed = jnp.concatenate(
            [0.5 * geo[2:3] + lift, reach, rate_t, inverse, jnp.zeros((4, LANES), jnp.float32)], axis=0
        )
        sub = packed.T
        d_x = nearest(grid_x - (0.5 * geo[0:1] + float(BX * step_row)), periods[0])
        d_y = nearest(grid_y - (0.5 * geo[1:2] + float(BY * side) * ahead), periods[1])
        inside = (jnp.abs(d_x) <= reach) & (jnp.abs(d_y) <= reach)
        squared = d_x * d_x + d_y * d_y
        d_z = nearest(grid_z - sub[:, 0:1], periods[2])
        inside_z = jnp.abs(d_z) <= sub[:, 1:2]
        squared_z = d_z * d_z
        for s in range(SHELLS):
            part = 1.0 / ((s + 1) * (s + 1))
            rate = inverse * part + rate_t
            plane_ref[o, s] = jnp.where(inside, jnp.exp(-rate * squared), 0.0).astype(plane_ref.dtype)
            rate_z = sub[:, 3:4] * part + sub[:, 2:3]
            line_ref[o, s] = jnp.where(inside_z, jnp.exp(-rate_z * squared_z), 0.0).astype(line_ref.dtype)


def density_kernel(column_steps, *refs):
    coef_refs = refs[:column_steps]
    plane_ref, line_ref, out_ref, terms = refs[column_steps:]
    for o in range(plane_ref.shape[0]):
        coef = coef_refs[o % column_steps]
        first = 8 * (o // column_steps)
        for s in range(SHELLS):
            scaled = plane_ref[o, s].astype(jnp.float32) * coef[first + s : first + s + 1, :]
            at = (o * SHELLS + s) * LANES
            terms[:, at : at + LANES] = scaled.astype(terms.dtype)
    out_ref[...] = jnp.dot(terms[...], line_ref[...], preferred_element_type=jnp.float32)


def local(sign_start, neighbors, atom_size, basis_proj, pair_extent, atom_x, atom_y, atom_z):
    n_row = lax.axis_size("row")
    n_col = lax.axis_size("col")
    n_lay = lax.axis_size("layer")
    assert n_lay == 4 and n_col >= 4 and (n_row == 2 or n_row >= 4)
    assert n_row & (n_row - 1) == 0 and n_col & (n_col - 1) == 0
    axes = (n_row, n_col, n_lay)
    atoms, slots = neighbors.shape
    size = sign_start.shape[2]
    steps = [0, 1] if n_row == 2 else [0, 1, -1]
    count = len(steps)
    others = range(1, count)
    own = sign_start[0]
    flat = own.reshape(slots * size, size)
    listings = neighbors.T
    full = slots * size
    half = full // 2
    most = half - size
    n_pick = column_targets(n_row)
    picks = n_pick * size
    part = picks + GEO

    def on_row(value, di):
        return from_offset(value, "row", steps[di])

    x_row = {di: on_row(flat, di) for di in others}
    y_row = from_layer(flat, 2)
    m_row = from_layer(flat, 1)
    picked = pl.pallas_call(
        functools.partial(pick_kernel, axes),
        out_shape=jax.ShapeDtypeStruct((part, size), own.dtype),
        in_specs=[HBM] * 6,
        out_specs=VMEM,
        scratch_shapes=[
            pltpu.SMEM((slots, atoms), jnp.int32),
            pltpu.SMEM((1, slots), jnp.int32),
            pltpu.SMEM((atoms,), jnp.int32),
            pltpu.SMEM((atoms,), jnp.int32),
            pltpu.SMEM((atoms,), jnp.int32),
            pltpu.SMEM((n_pick + 1,), jnp.int32),
            pltpu.SemaphoreType.DMA((5,)),
            pltpu.SemaphoreType.DMA((n_pick,)),
        ],
        compiler_params=pltpu.CompilerParams(vmem_limit_bytes=60 << 20),
        name="pick_column_blocks",
    )(listings, pair_extent, atom_x, atom_y, atom_z, own)
    up = from_column(picked, 0)
    down = from_column(picked, 1)

    halves = pack(
        [y_row] + [x_row[di] for di in others] + [picked],
        [[(0, half, most)]] + [[(di, 0, most)] for di in others] + [[(count, picks, GEO)]],
        [],
        "pack_halves",
    )
    ends = {di: on_row(halves[0], di) for di in others}
    tops = {di: from_layer(halves[di], 2) for di in others}

    at = {}
    buffers = {}

    def note(name, value, contents):
        buffers[name] = value
        start = 0
        for what, rows in contents:
            if what is not None:
                at[what] = (name, start)
            start += rows

    def row_of(di, flip, start=0, stop=slots):
        return [(("row", slot, di, flip), size) for slot in range(start, stop)]

    halfway = slots // 2

    def side_of(kind, di, flip):
        return [((kind, di, flip), picks)]

    note("own", flat, row_of(0, 0))
    note("mate", m_row, row_of(0, 1))
    note("far", y_row, row_of(0, 2))
    note("up", up, side_of("up", 0, 0) + [(("up geo", 0, 0), GEO)])
    note("down", down, side_of("down", 0, 0) + [(("down geo", 0, 0), GEO)])
    note("geo", halves[count], [(("geo", 0, 0), GEO)])
    for di in others:
        note(("x", di), x_row[di], row_of(di, 0))
        note(("end", di), ends[di], row_of(di, 2, halfway, slots - 1))
        note(("top", di), tops[di], row_of(di, 2, 0, halfway - 1))

    corners = [("end", di) for di in others] + [("top", di) for di in others]
    names = ["up", "down", "geo", "far"] + [("x", di) for di in others]
    plans = [
        [(0, 0, picks), (3, full - size, size), (2, 0, GEO), (0, picks, GEO), (1, picks, GEO)],
        [(1, 0, picks)] + [(di + 3, most, size) for di in others],
        [(2, 0, GEO), (0, picks, GEO), (1, picks, GEO)],
    ]
    two_x, two_y, geos = pack([buffers[name] for name in names], plans, [m_row], "pack_two")
    to_mate = corners + ["up", "down"]
    plans = [[(i, 0, picks if name in ("up", "down") else most) for i, name in enumerate(to_mate)]]
    two_m = pack([buffers[name] for name in to_mate], plans, [], "pack_two_mate")[0]
    for di in others:
        note(("mate x", di), from_layer(x_row[di], 1), row_of(di, 1))
    note("mate far", from_layer(y_row, 1), row_of(0, 3))

    early_order = ["own", "mate", "far", "up", "down", "geo"] + [("x", di) for di in others]
    early_order += [("mate x", di) for di in others] + ["mate far"]
    early_order += corners + [("two x", di) for di in others] + ["two y", "two m"]
    late_order = [("three x", di) for di in others] + ["three y", "three m"]
    late_order += ["four"]

    contents = {}
    for di in others:
        contents["two x", di] = side_of("up", di, 0) + row_of(di, 2, slots - 1, slots) + [(("geo", di, 0), GEO)]
        contents["two x", di] += [(("up geo", di, 0), GEO), (("down geo", di, 0), GEO)]
    contents["two y"] = side_of("down", 0, 2)
    contents["two y"] += sum([row_of(di, 2, halfway - 1, halfway) for di in others], [])
    contents["two m"] = sum([row_of(di, 3, halfway, slots - 1) for di in others], [])
    contents["two m"] += sum([row_of(di, 3, 0, halfway - 1) for di in others], [])
    contents["two m"] += side_of("up", 0, 1) + side_of("down", 0, 1)
    for di in others:
        contents["three x", di] = side_of("down", di, 0) + side_of("down", di, 2)
    contents["three y"] = side_of("up", 0, 2) + sum([side_of("up", di, 2) for di in others], [])
    contents["three m"] = []
    for di in others:
        contents["three m"] += side_of("up", di, 1) + row_of(di, 3, slots - 1, slots)
    contents["three m"] += side_of("down", 0, 3)
    contents["three m"] += sum([row_of(di, 3, halfway - 1, halfway) for di in others], [])
    contents["three m"] += [("geos", count * 3 * GEO)]
    contents["four"] = []
    for di in others:
        contents["four"] += side_of("down", di, 1) + side_of("down", di, 3)
    contents["four"] += side_of("up", 0, 3) + sum([side_of("up", di, 3) for di in others], [])
    lengths = {name: sum(rows for _, rows in content) for name, content in contents.items()}
    for name in early_order:
        if name in buffers:
            lengths[name] = buffers[name].shape[0]
    base = {}
    total = 0
    for name in early_order + late_order:
        base[name] = total
        total += lengths[name]
        if name == early_order[-1]:
            late_from = total
    located = dict(at)
    for name, content in contents.items():
        start = 0
        for what, rows in content:
            located[what] = (name, start)
            start += rows
    layout = [
        base[located["row", slot, di, flip][0]] + located["row", slot, di, flip][1]
        for di in range(count)
        for flip in range(n_lay)
        for slot in range(slots)
    ]
    layout += [
        base[located[kind, di, flip][0]] + located[kind, di, flip][1]
        for kind in ("up", "down")
        for di in range(count)
        for flip in range(n_lay)
    ]
    pairs = slots * (slots + 1) // 2
    entries = pairs + UNROLL + 1
    early_table, late_table, info, spread, own_basis = pl.pallas_call(
        functools.partial(prepare_kernel, axes, count, tuple(layout), late_from),
        out_shape=(
            jax.ShapeDtypeStruct((entries,), jnp.int32),
            jax.ShapeDtypeStruct((entries,), jnp.int32),
            jax.ShapeDtypeStruct((slots + 2,), jnp.int32),
            jax.ShapeDtypeStruct((LANES, full), jnp.bfloat16),
            jax.ShapeDtypeStruct((16, size), jnp.bfloat16),
        ),
        in_specs=[HBM, HBM, VMEM, ANY] + [ANY] * len(corners),
        out_specs=(SMEM, SMEM, SMEM, VMEM, VMEM),
        scratch_shapes=[
            pltpu.SMEM((slots, atoms), jnp.int32),
            pltpu.SMEM((atoms,), jnp.int32),
            pltpu.SMEM((3, slots), jnp.int32),
            pltpu.SMEM((atoms,), jnp.int32),
            pltpu.SMEM((len(layout),), jnp.int32),
            pltpu.SemaphoreType.DMA((2,)),
        ],
        compiler_params=pltpu.CompilerParams(vmem_limit_bytes=(2 << 20) + atoms * 16384),
        cost_estimate=pl.CostEstimate(flops=6_000_000_000, bytes_accessed=8_000_000, transcendentals=0),
        name="prepare",
    )(listings, atom_size, basis_proj.transpose(1, 0, 2).reshape(SHELLS * atoms, size), two_x, *[buffers[name] for name in corners])

    for di in others:
        note(("two x", di), on_row(two_x, di), contents["two x", di])
    note("two y", from_layer(two_y, 2), contents["two y"])
    note("two m", from_layer(two_m, 1), contents["two m"])

    buffers["geos"] = geos
    names = ["up", "down", "two y", "geos"] + [("two x", di) for di in others]
    place = {name: i for i, name in enumerate(names)}
    gather = [(place["geos"], 0, 3 * GEO)] + [(place["two x", di], picks + size, 3 * GEO) for di in others]
    xs = [place["two x", di] for di in others]
    plans = [
        [(1, 0, picks), (2, 0, picks)],
        [(0, 0, picks)] + [(x, 0, picks) for x in xs],
        [(x, 0, picks + size) for x in xs] + [(2, 0, lengths["two y"])] + gather,
        gather,
    ]
    three_x, three_y, three_m, geos = pack([buffers[name] for name in names], plans, [own_basis], "pack_three")
    for di in others:
        note(("three x", di), on_row(three_x, di), contents["three x", di])
    note("three y", from_layer(three_y, 2), contents["three y"])
    note("three m", from_layer(three_m, 1), contents["three m"])
    third_geos = from_layer(geos, 3)

    early_values = [buffers[name] for name in early_order]
    gram = pl.pallas_call(
        functools.partial(gram_kernel, len(early_values)),
        out_shape=jax.ShapeDtypeStruct((full, full), jnp.bfloat16),
        in_specs=[SMEM] + [ANY] * (len(early_values) + 1),
        out_specs=VMEM,
        scratch_shapes=[
            pltpu.VMEM((late_from, LANES), jnp.bfloat16),
            pltpu.SemaphoreType.DMA((len(early_values),)),
        ],
        compiler_params=pltpu.CompilerParams(vmem_limit_bytes=(6 << 20) + late_from * LANES * 2),
        cost_estimate=pl.CostEstimate(flops=1000, bytes_accessed=1000, transcendentals=0),
        name="gram_early",
    )(early_table, *early_values, three_x)

    thirds = [buffers["three x", di] for di in others] + [buffers["three y"]]
    four = pack(thirds, [[(i, 0, value.shape[0]) for i, value in enumerate(thirds)]], [gram, third_geos], "pack_four")[0]
    note("four", from_layer(four, 1), contents["four"])

    column_steps = (0, 1, -1)
    tile_steps = [(dr, dc) for dr in steps for dc in column_steps]
    tiles = len(tile_steps)
    periods = (float(BX * n_row), float(BY * n_col), float(BZ * n_lay))
    plane, line = pl.pallas_call(
        functools.partial(profile_kernel, periods, tile_steps, at["geos"][1]),
        out_shape=(
            jax.ShapeDtypeStruct((tiles, SHELLS, BX * BY, LANES), jnp.bfloat16),
            jax.ShapeDtypeStruct((tiles, SHELLS, LANES, BZ), jnp.bfloat16),
        ),
        in_specs=[ANY] * 4,
        out_specs=(VMEM, VMEM),
        scratch_shapes=[
            pltpu.VMEM((3, tiles * GEO, LANES), jnp.bfloat16),
            pltpu.SemaphoreType.DMA((3,)),
        ],
        compiler_params=pltpu.CompilerParams(vmem_limit_bytes=10 << 20),
        cost_estimate=pl.CostEstimate(flops=5_000_000_000, bytes_accessed=4_000_000, transcendentals=2_000_000),
        name="profiles",
    )(geos, buffers["three m"], third_geos, gram)

    late_values = [buffers[name] for name in late_order]
    sign_next, coef = pl.pallas_call(
        functools.partial(step_kernel, len(late_values)),
        out_shape=(
            jax.ShapeDtypeStruct((slots, size, size), jnp.bfloat16),
            jax.ShapeDtypeStruct((8, LANES), jnp.float32),
        ),
        in_specs=[SMEM, SMEM, VMEM, VMEM, VMEM, VMEM] + [ANY] * (len(late_values) + 1),
        out_specs=(VMEM, VMEM),
        scratch_shapes=[
            pltpu.VMEM((total - late_from, LANES), jnp.bfloat16),
            pltpu.VMEM((full, full), jnp.bfloat16),
            pltpu.VMEM((size, full), jnp.bfloat16),
            pltpu.VMEM((size, full), jnp.bfloat16),
            pltpu.SemaphoreType.DMA((len(late_values),)),
        ],
        compiler_params=pltpu.CompilerParams(vmem_limit_bytes=(15 << 20) + (total - late_from) * LANES * 2),
        cost_estimate=pl.CostEstimate(flops=1_300_000_000, bytes_accessed=8_000_000, transcendentals=0),
        name="square_cube_coefficients",
    )(late_table, info, own_basis, spread, own, gram, *late_values, line)

    mate_coef = from_layer(coef, 1)
    third_coef = from_layer(coef, 3)
    odd = lax.axis_index("layer") % 2 == 1
    below = jnp.where(odd, mate_coef, third_coef)
    above = jnp.where(odd, third_coef, mate_coef)
    merged = jnp.concatenate(
        [
            coef[:, : 4 * SPAN],
            below[:, SPAN : 3 * SPAN],
            above[:, 3 * SPAN : 4 * SPAN],
            jnp.zeros((8, LANES - 7 * SPAN), jnp.float32),
        ],
        axis=1,
    )
    stacked = jnp.concatenate([merged] + [on_row(merged, di) for di in others], axis=0)
    received = [stacked, from_column(stacked, 0), from_column(stacked, 1)]

    density = pl.pallas_call(
        functools.partial(density_kernel, len(column_steps)),
        out_shape=jax.ShapeDtypeStruct((BX * BY, BZ), jnp.float32),
        in_specs=[VMEM] * (len(received) + 2),
        out_specs=VMEM,
        scratch_shapes=[pltpu.VMEM((BX * BY, tiles * SHELLS * LANES), jnp.bfloat16)],
        compiler_params=pltpu.CompilerParams(vmem_limit_bytes=16 << 20),
        cost_estimate=pl.CostEstimate(flops=310_000_000, bytes_accessed=4_000_000, transcendentals=0),
        name="density",
    )(*received, plane, line.reshape(tiles * SHELLS * LANES, BZ))
    return sign_next[None], density.reshape(BX, BY, BZ)


def solution(mesh):
    rows = P(("row", "col", "layer"), None, None, None)
    in_specs = (rows, P(), P(), P(), P(("row", "col", "layer"), None), P(), P(), P())
    out_specs = (rows, P("row", "col", "layer"))
    return jax.shard_map(local, mesh=mesh, in_specs=in_specs, out_specs=out_specs, check_vma=False)
```

```python
import functools

import jax
import jax.numpy as jnp
from jax import lax
from jax.experimental import pallas as pl
from jax.experimental.pallas import tpu as pltpu
from jax.sharding import PartitionSpec as P

BX = 16
BY = 16
BZ = 128
LANES = 128
UNROLL = 4
SHELLS = 6
SPAN = 3 * SHELLS
GEO = 16
VMEM = pl.BlockSpec(memory_space=pltpu.VMEM)
SMEM = pl.BlockSpec(memory_space=pltpu.SMEM)
ANY = pl.BlockSpec(memory_space=pl.ANY)
HBM = pl.BlockSpec(memory_space=pltpu.HBM)


def from_offset(x, axis, step):
    count = lax.axis_size(axis)
    return lax.ppermute(x, axis, [((i + step) % count, i) for i in range(count)])


def from_column(x, side):
    count = lax.axis_size("col")
    step = [1 if (i + side) % 2 == 0 else -1 for i in range(count)]
    return lax.ppermute(x, "col", [((i + step[i]) % count, i) for i in range(count)])


def from_layer(x, flip):
    count = lax.axis_size("layer")
    return lax.ppermute(x, "layer", [(i ^ flip, i) for i in range(count)])


def column_targets(n_row):
    return 5 if n_row == 2 else 7


def target_place(n_row, step_row, step_lay, row):
    same = jnp.where(step_lay < 3, step_lay, -1)
    if n_row == 2:
        lead = step_lay - row
        across = jnp.where((lead >= 0) & (lead < 2), 3 + lead, -1)
    else:
        across = 3 + step_lay
    return jnp.where(step_row == 0, same, jnp.where(step_row == 1, across, -1))


class Places:
    def __init__(self, n_row, n_col, n_lay):
        self.n_row, self.n_col, self.n_lay = n_row, n_col, n_lay
        self.lay_bits = n_lay.bit_length() - 1
        self.col_bits = n_col.bit_length() - 1
        self.row = lax.axis_index("row")
        self.col = lax.axis_index("col")
        self.lay = lax.axis_index("layer")
        self.me = (((self.row << self.col_bits) + self.col) << self.lay_bits) + self.lay

    def split(self, atom):
        return (
            atom >> (self.lay_bits + self.col_bits),
            (atom >> self.lay_bits) & (self.n_col - 1),
            atom & (self.n_lay - 1),
        )


def load(sources, targets, sems):
    copies = [pltpu.make_async_copy(a, b, sems.at[i]) for i, (a, b) in enumerate(zip(sources, targets))]
    for copy in copies:
        copy.start()
    for copy in copies:
        copy.wait()


def own_ranks(at, neighbors_ref):
    seen = [jnp.int32(0)] * at.n_lay
    listed = []
    for w in range(neighbors_ref.shape[0]):
        atom = neighbors_ref[w, at.me]
        step_lay = (atom - at.lay) & (at.n_lay - 1)
        rank = jnp.int32(0)
        for k in range(at.n_lay):
            rank = jnp.where(step_lay == k, 3 * k + seen[k], rank)
            seen[k] = seen[k] + (step_lay == k).astype(jnp.int32)
        listed.append((atom, rank))
    return listed


def pick_kernel(axes, *refs):
    sign_ref, out_ref, neighbors_ref, extent_ref, x_ref, y_ref, z_ref, place_ref, loads, sems = refs[5:]
    at = Places(*axes)
    slots = sign_ref.shape[0]
    n_pick = place_ref.shape[0] - 1
    size = sign_ref.shape[1]
    for i in range(n_pick + 1):
        place_ref[i] = 0
    load(refs[:5], (neighbors_ref, extent_ref, x_ref, y_ref, z_ref), loads)
    ranks = own_ranks(at, neighbors_ref)
    for w, (atom, _) in enumerate(ranks):
        row, col, lay = at.split(atom)
        place = target_place(at.n_row, (row - at.row) & (at.n_row - 1), (lay - at.lay) & (at.n_lay - 1), at.row)
        place_ref[jnp.where((col == at.col) & (place >= 0), place, n_pick)] = w
    copies = []
    for i in range(n_pick):
        copy = pltpu.make_async_copy(sign_ref.at[place_ref[i]], out_ref.at[pl.ds(i * size, size)], sems.at[i])
        copy.start()
        copies.append(copy)
    sub = lax.broadcasted_iota(jnp.int32, (GEO, LANES), 0)
    lane_pair = lax.broadcasted_iota(jnp.int32, (GEO, LANES), 1) // SHELLS
    geo = jnp.zeros((GEO, LANES), jnp.int32)
    for w, (atom, rank) in enumerate(ranks):
        row, col, lay = at.split(atom)
        go_row = ((row - at.row + 1) & (at.n_row - 1)) - 1
        go_col = ((col - at.col + 1) & (at.n_col - 1)) - 1
        go_lay = jnp.minimum(((lay - at.lay + 1) & (at.n_lay - 1)) - 1, 1)
        twice_x = x_ref[at.me] + x_ref[atom] + BX * go_row
        twice_y = y_ref[at.me] + y_ref[atom] + BY * go_col
        twice_z = z_ref[at.me] + z_ref[atom] + BZ * go_lay - BZ
        extent = extent_ref[0, w]
        values = jnp.where(sub == 0, twice_x, jnp.where(sub == 1, twice_y, jnp.where(sub == 2, twice_z, extent)))
        geo = jnp.where(lane_pair == rank, values, geo)
    out_ref[n_pick * size :] = geo.astype(jnp.float32).astype(out_ref.dtype)
    for copy in copies:
        copy.wait()


def prepare_kernel(axes, count, layout, late_from, *refs):
    basis_ref = refs[2]
    early_ref, late_ref, info_ref, spread_ref, own_basis_ref = refs[-11:-6]
    neighbors_ref, size_ref, known, inverse, layout_ref, loads = refs[-6:]
    at = Places(*axes)
    load(refs[:2], (neighbors_ref, size_ref), loads)
    slots, atoms = neighbors_ref.shape
    bits = atoms.bit_length() - 1
    for i, value in enumerate(layout):
        layout_ref[i] = value
    lines = count * at.n_lay

    def hot(rows, atom, first):
        sub = lax.broadcasted_iota(jnp.int32, (rows, SHELLS * atoms), 0)
        lane = lax.broadcasted_iota(jnp.int32, (rows, SHELLS * atoms), 1)
        return ((lane & (atoms - 1)) == atom) & (sub == first + (lane >> bits))

    def rows_of(chosen):
        picked = jnp.where(chosen, 1.0, 0.0).astype(jnp.bfloat16)
        return jnp.dot(picked, basis_ref[...], preferred_element_type=jnp.float32).astype(jnp.bfloat16)

    self_slot = jnp.int32(0)
    for w, (atom, rank) in enumerate(own_ranks(at, neighbors_ref)):
        row, col, lay = at.split(atom)
        step_row = (row - at.row) & (at.n_row - 1)
        self_slot = jnp.where(atom == at.me, w, self_slot)
        info_ref[w] = size_ref[atom]
        spread_ref[:, w * LANES : (w + 1) * LANES] = rows_of(hot(LANES, atom, rank * SHELLS))
        flip = lay ^ at.lay
        known[0, w] = atom
        known[1, w] = jnp.where(col == at.col, 0, jnp.where(col == (at.col ^ 1), 1, 2))
        known[2, w] = jnp.where(step_row == 0, 0, jnp.where(step_row == 1, 1, 2)) * at.n_lay + flip
        inverse[atom] = -1
    own_basis_ref[...] = rows_of(hot(16, at.me, 0))
    info_ref[slots] = size_ref[at.me]
    info_ref[slots + 1] = self_slot

    def row_of_pairs(v, totals):
        early, late = totals
        atom = known[0, v]
        side = known[1, v]
        line = known[2, v]
        for u in range(slots):
            inverse[neighbors_ref[u, atom]] = v * 16 + u

        def from_row(totals):
            total, late = totals
            for w in range(slots):
                mark = inverse[known[0, w]]
                chosen = ((mark >> 4) == v) & ((known[1, w] != 0) | (v <= w))
                where = layout_ref[line * slots + (mark & 15)]
                is_late = where >= late_from
                entry = v + 16 * w
                early_ref[total + 1] = entry + 256 * where
                late_ref[late + 1] = entry + 256 * (where - late_from)
                total = total + (chosen & ~is_late).astype(jnp.int32)
                late = late + (chosen & is_late).astype(jnp.int32)
            return total, late

        def from_column(totals):
            early, late = totals
            row, _, lay = at.split(atom)
            beside = layout_ref[lines * slots + (side - 1) * lines + line]
            for w in range(slots):
                other = known[0, w]
                mark = inverse[other]
                o_row, _, o_lay = at.split(other)
                d_row = (o_row - row) & (at.n_row - 1)
                d_lay = (o_lay - lay) & (at.n_lay - 1)
                there = target_place(at.n_row, d_row, d_lay, row)
                back = target_place(at.n_row, -d_row & (at.n_row - 1), -d_lay & (at.n_lay - 1), o_row)
                chosen = ((mark >> 4) == v) & (side == known[1, w]) & (there >= 0) & ((back < 0) | (v <= w))
                where = beside + there * LANES
                is_late = where >= late_from
                entry = v + 16 * w
                early_ref[early + 1] = entry + 256 * where
                late_ref[late + 1] = entry + 256 * (where - late_from)
                early = early + (chosen & ~is_late).astype(jnp.int32)
                late = late + (chosen & is_late).astype(jnp.int32)
            return early, late

        return lax.cond(side == 0, from_row, from_column, (early, late))

    totals = lax.fori_loop(0, slots, row_of_pairs, (jnp.int32(0), jnp.int32(0)))
    for ref, total in zip((early_ref, late_ref), totals):
        ref[0] = (total + UNROLL - 1) // UNROLL
        for i in range(UNROLL - 1):
            ref[total + i + 1] = ref[jnp.maximum(total, 1)]


def pack_kernel(moves, inputs, *refs):
    for source, start, rows, target, place in moves:
        refs[inputs + target][place : place + rows] = refs[source][start : start + rows]


def pack(values, plans, extra, name):
    moves, shapes = [], []
    for target, plan in enumerate(plans):
        place = 0
        for source, start, rows in plan:
            moves.append((source, start, rows, target, place))
            place += rows
        shapes.append(jax.ShapeDtypeStruct((place, LANES), values[0].dtype))
    inputs = len(values) + len(extra)
    return pl.pallas_call(
        functools.partial(pack_kernel, tuple(moves), inputs),
        out_shape=tuple(shapes),
        in_specs=[VMEM] * len(values) + [ANY] * len(extra),
        out_specs=tuple([VMEM] * len(plans)),
        compiler_params=pltpu.CompilerParams(
            vmem_limit_bytes=(1 << 20) + 256 * sum(x.shape[0] for x in list(values) + shapes)
        ),
        cost_estimate=pl.CostEstimate(flops=0, bytes_accessed=3_000_000, transcendentals=0),
        name=name,
    )(*values, *extra)


def fill(piece_refs, pool):
    place = 0
    for piece in piece_refs:
        rows = piece.shape[0]
        pool[place : place + rows] = piece[...]
        place += rows


def place_pairs(table_ref, pool, gram, size):
    def place(i, carry):
        for k in range(UNROLL):
            entry = table_ref[i * UNROLL + k + 1]
            p = pl.multiple_of((entry & 15) * size, size)
            q = pl.multiple_of(((entry >> 4) & 15) * size, size)
            block = pool[pl.ds(pl.multiple_of(entry >> 8, 16), size)]
            gram[pl.ds(p, size), pl.ds(q, size)] = block
            gram[pl.ds(q, size), pl.ds(p, size)] = block.T
        return carry

    lax.fori_loop(0, table_ref[0], place, 0)


def gram_kernel(pieces, *refs):
    table_ref = refs[0]
    piece_refs = refs[1 : 1 + pieces]
    gram, pool = refs[-2:]
    size = LANES
    fill(piece_refs, pool)
    for v in range(gram.shape[0] // size):
        gram[v * size : (v + 1) * size] = jnp.zeros((size, gram.shape[1]), gram.dtype)
    place_pairs(table_ref, pool, gram, size)


def step_kernel(pieces, *refs):
    table_ref, info_ref, basis_ref, spread_ref, sign_ref, early_ref = refs[:6]
    piece_refs = refs[6 : 6 + pieces]
    next_ref, coef_ref, pool, gram, own, square = refs[-6:]
    slots, size = sign_ref.shape[0], sign_ref.shape[1]
    fill(piece_refs, pool)
    for v in range(slots):
        gram[v * size : (v + 1) * size] = early_ref[v * size : (v + 1) * size]
    rows = lax.broadcasted_iota(jnp.int32, (size, size), 0)
    lanes = lax.broadcasted_iota(jnp.int32, (size, size), 1)
    own_size = info_ref[slots]
    self_slot = info_ref[slots + 1]
    for w in range(slots):
        kept = (rows < own_size) & (lanes < info_ref[w])
        block = jnp.where(kept, sign_ref[w].astype(jnp.float32), 0.0)
        own[:, w * size : (w + 1) * size] = block.astype(own.dtype)
    place_pairs(table_ref, pool, gram, size)
    wide = 2 * size
    wide_lanes = lax.broadcasted_iota(jnp.int32, (size, wide), 1)
    wide_rows = lax.broadcasted_iota(jnp.int32, (size, wide), 0)

    def column_kept(n):
        first = info_ref[2 * n]
        second = info_ref[2 * n + 1]
        return (wide_lanes < first) | ((wide_lanes >= size) & (wide_lanes < size + second))

    for n in range(slots // 2):
        part = jnp.dot(own[...], gram[:, n * wide : (n + 1) * wide], preferred_element_type=jnp.float32)
        square[:, n * wide : (n + 1) * wide] = jnp.where(column_kept(n), part, 0.0).astype(square.dtype)
    basis = jnp.concatenate([basis_ref[...], basis_ref[...]], axis=1)
    coef = jnp.zeros((2 * basis_ref.shape[0], LANES), jnp.float32)
    across = (((1,), (1,)), ((), ()))
    for n in range(slots // 2):
        part = jnp.dot(square[...], gram[:, n * wide : (n + 1) * wide], preferred_element_type=jnp.float32)
        cube = jnp.where(column_kept(n), part, 0.0)
        full = 1.5 * own[:, n * wide : (n + 1) * wide].astype(jnp.float32) - 0.5 * cube
        next_ref[2 * n] = full[:, :size].astype(next_ref.dtype)
        next_ref[2 * n + 1] = full[:, size:].astype(next_ref.dtype)
        shift = (self_slot - 2 * n) * size
        is_self = (self_slot >= 2 * n) & (self_slot < 2 * n + 2)
        diag = (wide_lanes == wide_rows + shift) & (wide_rows < own_size) & is_self
        dmat = 0.5 * (jnp.where(diag, 1.0, 0.0) - full)
        high = dmat.astype(jnp.bfloat16)
        low = (dmat - high.astype(jnp.float32)).astype(jnp.bfloat16)
        half = jnp.dot(basis, jnp.concatenate([high, low], axis=0), preferred_element_type=jnp.float32)
        half_high = half.astype(jnp.bfloat16)
        half_low = (half - half_high.astype(jnp.float32)).astype(jnp.bfloat16)
        coef = coef + lax.dot_general(
            jnp.concatenate([half_high, half_low], axis=0),
            spread_ref[:, n * wide : (n + 1) * wide],
            across,
            preferred_element_type=jnp.float32,
        )
    coef = coef[: basis_ref.shape[0]] + coef[basis_ref.shape[0] :]
    coef_ref[...] = coef[: coef_ref.shape[0]]


def profile_kernel(periods, steps, mate_from, *refs):
    own_ref, mate_ref, third_ref = refs[:3]
    plane_ref, line_ref, geos, sems = refs[-4:]
    odd = (lax.axis_index("layer") & 1) == 1
    rows = len(steps) * GEO
    copies = []
    for k, source in enumerate((own_ref, mate_ref.at[pl.ds(mate_from, rows)], third_ref)):
        copy = pltpu.make_async_copy(source, geos.at[k], sems.at[k])
        copy.start()
        copies.append(copy)
    cells = plane_ref.shape[2]
    cell = lax.broadcasted_iota(jnp.int32, (cells, LANES), 0)
    grid_x = (cell // BY).astype(jnp.float32)
    grid_y = (cell % BY).astype(jnp.float32)
    grid_z = lax.broadcasted_iota(jnp.int32, (LANES, BZ), 1).astype(jnp.float32)
    lane = lax.broadcasted_iota(jnp.int32, (1, LANES), 1)
    shell = (lane % SHELLS + 1).astype(jnp.float32)
    valid = lane < 7 * SPAN
    from_own = lane < 4 * SPAN
    from_below = lane < 6 * SPAN
    lift = jnp.where(from_own, 0.0, jnp.where(from_below, -float(BZ), float(BZ))) + 0.5 * BZ

    def nearest(offset, period):
        return offset - period * jnp.floor(offset * (1.0 / period) + 0.5)

    for copy in copies:
        copy.wait()
    ahead = 1.0 - 2.0 * (lax.axis_index("col") & 1).astype(jnp.float32)
    for o, (step_row, side) in enumerate(steps):
        own, first, third = (geos[k, o * GEO : (o + 1) * GEO].astype(jnp.float32) for k in range(3))
        below = jnp.where(odd, first, third)
        above = jnp.where(odd, third, first)
        moved = jnp.where(from_below, pltpu.roll(below, 3 * SPAN, axis=1), pltpu.roll(above, 3 * SPAN, axis=1))
        geo = jnp.where(from_own, own, moved)
        extent = jnp.where(valid, geo[3:4], 1.0)
        inverse = (SHELLS / extent) * (SHELLS / extent)
        reach = jnp.where(valid, extent, -1.0)
        rate_t = inverse / (shell * shell)
        packed = jnp.concatenate(
            [0.5 * geo[2:3] + lift, reach, rate_t, inverse, jnp.zeros((4, LANES), jnp.float32)], axis=0
        )
        sub = packed.T
        d_x = nearest(grid_x - (0.5 * geo[0:1] + float(BX * step_row)), periods[0])
        d_y = nearest(grid_y - (0.5 * geo[1:2] + float(BY * side) * ahead), periods[1])
        inside = (jnp.abs(d_x) <= reach) & (jnp.abs(d_y) <= reach)
        squared = d_x * d_x + d_y * d_y
        d_z = nearest(grid_z - sub[:, 0:1], periods[2])
        inside_z = jnp.abs(d_z) <= sub[:, 1:2]
        squared_z = d_z * d_z
        for s in range(SHELLS):
            part = 1.0 / ((s + 1) * (s + 1))
            rate = inverse * part + rate_t
            plane_ref[o, s] = jnp.where(inside, jnp.exp(-rate * squared), 0.0).astype(plane_ref.dtype)
            rate_z = sub[:, 3:4] * part + sub[:, 2:3]
            line_ref[o, s] = jnp.where(inside_z, jnp.exp(-rate_z * squared_z), 0.0).astype(line_ref.dtype)


def density_kernel(column_steps, *refs):
    coef_refs = refs[:column_steps]
    plane_ref, line_ref, out_ref, terms = refs[column_steps:]
    for o in range(plane_ref.shape[0]):
        coef = coef_refs[-o % column_steps]
        first = 8 * (o // column_steps)
        for s in range(SHELLS):
            scaled = plane_ref[o, s].astype(jnp.float32) * coef[first + s : first + s + 1, :]
            at = (o * SHELLS + s) * LANES
            terms[:, at : at + LANES] = scaled.astype(terms.dtype)
    out_ref[...] = jnp.dot(terms[...], line_ref[...], preferred_element_type=jnp.float32)


def local(sign_start, neighbors, atom_size, basis_proj, pair_extent, atom_x, atom_y, atom_z):
    n_row = lax.axis_size("row")
    n_col = lax.axis_size("col")
    n_lay = lax.axis_size("layer")
    assert n_lay == 4 and n_col >= 4 and (n_row == 2 or n_row >= 4)
    assert n_row & (n_row - 1) == 0 and n_col & (n_col - 1) == 0
    axes = (n_row, n_col, n_lay)
    atoms, slots = neighbors.shape
    size = sign_start.shape[2]
    steps = [0, 1] if n_row == 2 else [0, 1, -1]
    count = len(steps)
    others = range(1, count)
    own = sign_start[0]
    flat = own.reshape(slots * size, size)
    listings = neighbors.T
    full = slots * size
    half = full // 2
    most = half - size
    n_pick = column_targets(n_row)
    picks = n_pick * size
    part = picks + GEO

    def on_row(value, di):
        return from_offset(value, "row", steps[di])

    x_row = {di: on_row(flat, di) for di in others}
    y_row = from_layer(flat, 2)
    m_row = from_layer(flat, 1)
    picked = pl.pallas_call(
        functools.partial(pick_kernel, axes),
        out_shape=jax.ShapeDtypeStruct((part, size), own.dtype),
        in_specs=[HBM] * 6,
        out_specs=VMEM,
        scratch_shapes=[
            pltpu.SMEM((slots, atoms), jnp.int32),
            pltpu.SMEM((1, slots), jnp.int32),
            pltpu.SMEM((atoms,), jnp.int32),
            pltpu.SMEM((atoms,), jnp.int32),
            pltpu.SMEM((atoms,), jnp.int32),
            pltpu.SMEM((n_pick + 1,), jnp.int32),
            pltpu.SemaphoreType.DMA((5,)),
            pltpu.SemaphoreType.DMA((n_pick,)),
        ],
        compiler_params=pltpu.CompilerParams(vmem_limit_bytes=60 << 20),
        name="pick_column_blocks",
    )(listings, pair_extent, atom_x, atom_y, atom_z, own)
    down = from_column(picked, 1)
    up = from_column(picked, 0)

    halves = pack(
        [y_row] + [x_row[di] for di in others] + [picked],
        [[(0, half, most)]] + [[(di, 0, most)] for di in others] + [[(count, picks, GEO)]],
        [],
        "pack_halves",
    )
    ends = {di: on_row(halves[0], di) for di in others}
    tops = {di: from_layer(halves[di], 2) for di in others}

    at = {}
    buffers = {}

    def note(name, value, contents):
        buffers[name] = value
        start = 0
        for what, rows in contents:
            if what is not None:
                at[what] = (name, start)
            start += rows

    def row_of(di, flip, start=0, stop=slots):
        return [(("row", slot, di, flip), size) for slot in range(start, stop)]

    halfway = slots // 2

    def side_of(kind, di, flip):
        return [((kind, di, flip), picks)]

    note("own", flat, row_of(0, 0))
    note("mate", m_row, row_of(0, 1))
    note("far", y_row, row_of(0, 2))
    note("up", up, side_of("up", 0, 0) + [(("up geo", 0, 0), GEO)])
    note("down", down, side_of("down", 0, 0) + [(("down geo", 0, 0), GEO)])
    note("geo", halves[count], [(("geo", 0, 0), GEO)])
    for di in others:
        note(("x", di), x_row[di], row_of(di, 0))
        note(("end", di), ends[di], row_of(di, 2, halfway, slots - 1))
        note(("top", di), tops[di], row_of(di, 2, 0, halfway - 1))

    corners = [("end", di) for di in others] + [("top", di) for di in others]
    names = ["down", "up", "geo", "far"] + [("x", di) for di in others]
    plans = [
        [(1, 0, picks), (3, full - size, size), (2, 0, GEO), (1, picks, GEO), (0, picks, GEO)],
        [(0, 0, picks)] + [(di + 3, most, size) for di in others],
        [(2, 0, GEO), (1, picks, GEO), (0, picks, GEO)],
    ]
    two_x, two_y, geos = pack([buffers[name] for name in names], plans, [m_row], "pack_two")
    to_mate = corners + ["up", "down"]
    plans = [[(i, 0, picks if name in ("up", "down") else most) for i, name in enumerate(to_mate)]]
    two_m = pack([buffers[name] for name in to_mate], plans, [], "pack_two_mate")[0]
    for di in others:
        note(("mate x", di), from_layer(x_row[di], 1), row_of(di, 1))
    note("mate far", from_layer(y_row, 1), row_of(0, 3))

    early_order = ["own", "mate", "far", "up", "down", "geo"] + [("x", di) for di in others]
    early_order += [("mate x", di) for di in others] + ["mate far"]
    early_order += corners + [("two x", di) for di in others] + ["two y", "two m"]
    late_order = [("three x", di) for di in others] + ["three y", "three m"]
    late_order += ["four"]

    contents = {}
    for di in others:
        contents["two x", di] = side_of("up", di, 0) + row_of(di, 2, slots - 1, slots) + [(("geo", di, 0), GEO)]
        contents["two x", di] += [(("up geo", di, 0), GEO), (("down geo", di, 0), GEO)]
    contents["two y"] = side_of("down", 0, 2)
    contents["two y"] += sum([row_of(di, 2, halfway - 1, halfway) for di in others], [])
    contents["two m"] = sum([row_of(di, 3, halfway, slots - 1) for di in others], [])
    contents["two m"] += sum([row_of(di, 3, 0, halfway - 1) for di in others], [])
    contents["two m"] += side_of("up", 0, 1) + side_of("down", 0, 1)
    for di in others:
        contents["three x", di] = side_of("down", di, 0) + side_of("down", di, 2)
    contents["three y"] = side_of("up", 0, 2) + sum([side_of("up", di, 2) for di in others], [])
    contents["three m"] = []
    for di in others:
        contents["three m"] += side_of("up", di, 1) + row_of(di, 3, slots - 1, slots)
    contents["three m"] += side_of("down", 0, 3)
    contents["three m"] += sum([row_of(di, 3, halfway - 1, halfway) for di in others], [])
    contents["three m"] += [("geos", count * 3 * GEO)]
    contents["four"] = []
    for di in others:
        contents["four"] += side_of("down", di, 1) + side_of("down", di, 3)
    contents["four"] += side_of("up", 0, 3) + sum([side_of("up", di, 3) for di in others], [])
    lengths = {name: sum(rows for _, rows in content) for name, content in contents.items()}
    for name in early_order:
        if name in buffers:
            lengths[name] = buffers[name].shape[0]
    base = {}
    total = 0
    for name in early_order + late_order:
        base[name] = total
        total += lengths[name]
        if name == early_order[-1]:
            late_from = total
    located = dict(at)
    for name, content in contents.items():
        start = 0
        for what, rows in content:
            located[what] = (name, start)
            start += rows
    layout = [
        base[located["row", slot, di, flip][0]] + located["row", slot, di, flip][1]
        for di in range(count)
        for flip in range(n_lay)
        for slot in range(slots)
    ]
    layout += [
        base[located[kind, di, flip][0]] + located[kind, di, flip][1]
        for kind in ("up", "down")
        for di in range(count)
        for flip in range(n_lay)
    ]
    pairs = slots * (slots + 1) // 2
    entries = pairs + UNROLL + 1
    early_table, late_table, info, spread, own_basis = pl.pallas_call(
        functools.partial(prepare_kernel, axes, count, tuple(layout), late_from),
        out_shape=(
            jax.ShapeDtypeStruct((entries,), jnp.int32),
            jax.ShapeDtypeStruct((entries,), jnp.int32),
            jax.ShapeDtypeStruct((slots + 2,), jnp.int32),
            jax.ShapeDtypeStruct((LANES, full), jnp.bfloat16),
            jax.ShapeDtypeStruct((16, size), jnp.bfloat16),
        ),
        in_specs=[HBM, HBM, VMEM, ANY] + [ANY] * len(corners),
        out_specs=(SMEM, SMEM, SMEM, VMEM, VMEM),
        scratch_shapes=[
            pltpu.SMEM((slots, atoms), jnp.int32),
            pltpu.SMEM((atoms,), jnp.int32),
            pltpu.SMEM((3, slots), jnp.int32),
            pltpu.SMEM((atoms,), jnp.int32),
            pltpu.SMEM((len(layout),), jnp.int32),
            pltpu.SemaphoreType.DMA((2,)),
        ],
        compiler_params=pltpu.CompilerParams(vmem_limit_bytes=(2 << 20) + atoms * 16384),
        cost_estimate=pl.CostEstimate(flops=6_000_000_000, bytes_accessed=8_000_000, transcendentals=0),
        name="prepare",
    )(listings, atom_size, basis_proj.transpose(1, 0, 2).reshape(SHELLS * atoms, size), two_x, *[buffers[name] for name in corners])

    for di in others:
        note(("two x", di), on_row(two_x, di), contents["two x", di])
    note("two y", from_layer(two_y, 2), contents["two y"])
    note("two m", from_layer(two_m, 1), contents["two m"])

    buffers["geos"] = geos
    names = ["up", "down", "two y", "geos"] + [("two x", di) for di in others]
    place = {name: i for i, name in enumerate(names)}
    gather = [(place["geos"], 0, 3 * GEO)] + [(place["two x", di], picks + size, 3 * GEO) for di in others]
    xs = [place["two x", di] for di in others]
    plans = [
        [(1, 0, picks), (2, 0, picks)],
        [(0, 0, picks)] + [(x, 0, picks) for x in xs],
        [(x, 0, picks + size) for x in xs] + [(2, 0, lengths["two y"])] + gather,
        gather,
    ]
    three_x, three_y, three_m, geos = pack([buffers[name] for name in names], plans, [own_basis], "pack_three")
    for di in others:
        note(("three x", di), on_row(three_x, di), contents["three x", di])
    note("three y", from_layer(three_y, 2), contents["three y"])
    note("three m", from_layer(three_m, 1), contents["three m"])
    third_geos = from_layer(geos, 3)

    early_values = [buffers[name] for name in early_order]
    gram = pl.pallas_call(
        functools.partial(gram_kernel, len(early_values)),
        out_shape=jax.ShapeDtypeStruct((full, full), jnp.bfloat16),
        in_specs=[SMEM] + [VMEM] * len(early_values) + [ANY],
        out_specs=VMEM,
        scratch_shapes=[pltpu.VMEM((late_from, LANES), jnp.bfloat16)],
        compiler_params=pltpu.CompilerParams(vmem_limit_bytes=(6 << 20) + 2 * late_from * LANES * 2),
        cost_estimate=pl.CostEstimate(flops=1000, bytes_accessed=1000, transcendentals=0),
        name="gram_early",
    )(early_table, *early_values, three_x)

    thirds = [buffers["three x", di] for di in others] + [buffers["three y"]]
    four = pack(thirds, [[(i, 0, value.shape[0]) for i, value in enumerate(thirds)]], [gram, third_geos], "pack_four")[0]
    note("four", from_layer(four, 1), contents["four"])

    column_steps = (0, 1, -1)
    tile_steps = [(dr, dc) for dr in steps for dc in column_steps]
    tiles = len(tile_steps)
    periods = (float(BX * n_row), float(BY * n_col), float(BZ * n_lay))
    plane, line = pl.pallas_call(
        functools.partial(profile_kernel, periods, tile_steps, at["geos"][1]),
        out_shape=(
            jax.ShapeDtypeStruct((tiles, SHELLS, BX * BY, LANES), jnp.bfloat16),
            jax.ShapeDtypeStruct((tiles, SHELLS, LANES, BZ), jnp.bfloat16),
        ),
        in_specs=[ANY] * 4,
        out_specs=(VMEM, VMEM),
        scratch_shapes=[
            pltpu.VMEM((3, tiles * GEO, LANES), jnp.bfloat16),
            pltpu.SemaphoreType.DMA((3,)),
        ],
        compiler_params=pltpu.CompilerParams(vmem_limit_bytes=10 << 20),
        cost_estimate=pl.CostEstimate(flops=5_000_000_000, bytes_accessed=4_000_000, transcendentals=2_000_000),
        name="profiles",
    )(geos, buffers["three m"], third_geos, gram)

    late_values = [buffers[name] for name in late_order]
    sign_next, coef = pl.pallas_call(
        functools.partial(step_kernel, len(late_values)),
        out_shape=(
            jax.ShapeDtypeStruct((slots, size, size), jnp.bfloat16),
            jax.ShapeDtypeStruct((8, LANES), jnp.float32),
        ),
        in_specs=[SMEM, SMEM, VMEM, VMEM, VMEM, VMEM] + [VMEM] * len(late_values) + [ANY],
        out_specs=(VMEM, VMEM),
        scratch_shapes=[
            pltpu.VMEM((total - late_from, LANES), jnp.bfloat16),
            pltpu.VMEM((full, full), jnp.bfloat16),
            pltpu.VMEM((size, full), jnp.bfloat16),
            pltpu.VMEM((size, full), jnp.bfloat16),
        ],
        compiler_params=pltpu.CompilerParams(vmem_limit_bytes=(15 << 20) + 2 * (total - late_from) * LANES * 2),
        cost_estimate=pl.CostEstimate(flops=1_300_000_000, bytes_accessed=8_000_000, transcendentals=0),
        name="square_cube_coefficients",
    )(late_table, info, own_basis, spread, own, gram, *late_values, line)

    mate_coef = from_layer(coef, 1)
    third_coef = from_layer(coef, 3)
    odd = lax.axis_index("layer") % 2 == 1
    below = jnp.where(odd, mate_coef, third_coef)
    above = jnp.where(odd, third_coef, mate_coef)
    merged = jnp.concatenate(
        [
            coef[:, : 4 * SPAN],
            below[:, SPAN : 3 * SPAN],
            above[:, 3 * SPAN : 4 * SPAN],
            jnp.zeros((8, LANES - 7 * SPAN), jnp.float32),
        ],
        axis=1,
    )
    stacked = jnp.concatenate([merged] + [on_row(merged, di) for di in others], axis=0)
    far_side = from_column(stacked, 1)
    received = [stacked, far_side, from_column(stacked, 0)]

    density = pl.pallas_call(
        functools.partial(density_kernel, len(column_steps)),
        out_shape=jax.ShapeDtypeStruct((BX * BY, BZ), jnp.float32),
        in_specs=[VMEM] * (len(received) + 2),
        out_specs=VMEM,
        scratch_shapes=[pltpu.VMEM((BX * BY, tiles * SHELLS * LANES), jnp.bfloat16)],
        compiler_params=pltpu.CompilerParams(vmem_limit_bytes=16 << 20),
        cost_estimate=pl.CostEstimate(flops=310_000_000, bytes_accessed=4_000_000, transcendentals=0),
        name="density",
    )(*received, plane, line.reshape(tiles * SHELLS * LANES, BZ))
    return sign_next[None], density.reshape(BX, BY, BZ)


def solution(mesh):
    rows = P(("row", "col", "layer"), None, None, None)
    in_specs = (rows, P(), P(), P(), P(("row", "col", "layer"), None), P(), P(), P())
    out_specs = (rows, P("row", "col", "layer"))
    return jax.shard_map(local, mesh=mesh, in_specs=in_specs, out_specs=out_specs, check_vma=False)
```

```python
import functools

import jax
import jax.numpy as jnp
from jax import lax
from jax.experimental import pallas as pl
from jax.experimental.pallas import tpu as pltpu
from jax.sharding import PartitionSpec as P

BX = 16
BY = 16
BZ = 128
LANES = 128
UNROLL = 4
SHELLS = 6
SPAN = 3 * SHELLS
GEO = 16
VMEM = pl.BlockSpec(memory_space=pltpu.VMEM)
SMEM = pl.BlockSpec(memory_space=pltpu.SMEM)
ANY = pl.BlockSpec(memory_space=pl.ANY)
HBM = pl.BlockSpec(memory_space=pltpu.HBM)


def from_offset(x, axis, step):
    count = lax.axis_size(axis)
    return lax.ppermute(x, axis, [((i + step) % count, i) for i in range(count)])


def from_column(x, side):
    count = lax.axis_size("col")
    step = [1 if (i + side) % 2 == 0 else -1 for i in range(count)]
    return lax.ppermute(x, "col", [((i + step[i]) % count, i) for i in range(count)])


def from_layer(x, flip):
    count = lax.axis_size("layer")
    return lax.ppermute(x, "layer", [(i ^ flip, i) for i in range(count)])


def column_targets(n_row):
    return 5 if n_row == 2 else 7


def target_place(n_row, step_row, step_lay, row):
    same = jnp.where(step_lay < 3, step_lay, -1)
    if n_row == 2:
        lead = step_lay - row
        across = jnp.where((lead >= 0) & (lead < 2), 3 + lead, -1)
    else:
        across = 3 + step_lay
    return jnp.where(step_row == 0, same, jnp.where(step_row == 1, across, -1))


class Places:
    def __init__(self, n_row, n_col, n_lay):
        self.n_row, self.n_col, self.n_lay = n_row, n_col, n_lay
        self.lay_bits = n_lay.bit_length() - 1
        self.col_bits = n_col.bit_length() - 1
        self.row = lax.axis_index("row")
        self.col = lax.axis_index("col")
        self.lay = lax.axis_index("layer")
        self.me = (((self.row << self.col_bits) + self.col) << self.lay_bits) + self.lay

    def split(self, atom):
        return (
            atom >> (self.lay_bits + self.col_bits),
            (atom >> self.lay_bits) & (self.n_col - 1),
            atom & (self.n_lay - 1),
        )


def load(sources, targets, sems):
    copies = [pltpu.make_async_copy(a, b, sems.at[i]) for i, (a, b) in enumerate(zip(sources, targets))]
    for copy in copies:
        copy.start()
    for copy in copies:
        copy.wait()


def own_ranks(at, neighbors_ref):
    seen = [jnp.int32(0)] * at.n_lay
    listed = []
    for w in range(neighbors_ref.shape[0]):
        atom = neighbors_ref[w, at.me]
        step_lay = (atom - at.lay) & (at.n_lay - 1)
        rank = jnp.int32(0)
        for k in range(at.n_lay):
            rank = jnp.where(step_lay == k, 3 * k + seen[k], rank)
            seen[k] = seen[k] + (step_lay == k).astype(jnp.int32)
        listed.append((atom, rank))
    return listed


def pick_kernel(axes, *refs):
    sign_ref, out_ref, neighbors_ref, extent_ref, x_ref, y_ref, z_ref, place_ref, loads, sems = refs[5:]
    at = Places(*axes)
    slots = sign_ref.shape[0]
    n_pick = place_ref.shape[0] - 1
    size = sign_ref.shape[1]
    for i in range(n_pick + 1):
        place_ref[i] = 0
    load(refs[:5], (neighbors_ref, extent_ref, x_ref, y_ref, z_ref), loads)
    ranks = own_ranks(at, neighbors_ref)
    for w, (atom, _) in enumerate(ranks):
        row, col, lay = at.split(atom)
        place = target_place(at.n_row, (row - at.row) & (at.n_row - 1), (lay - at.lay) & (at.n_lay - 1), at.row)
        place_ref[jnp.where((col == at.col) & (place >= 0), place, n_pick)] = w
    copies = []
    for i in range(n_pick):
        copy = pltpu.make_async_copy(sign_ref.at[place_ref[i]], out_ref.at[pl.ds(i * size, size)], sems.at[i])
        copy.start()
        copies.append(copy)
    sub = lax.broadcasted_iota(jnp.int32, (GEO, LANES), 0)
    lane_pair = lax.broadcasted_iota(jnp.int32, (GEO, LANES), 1) // SHELLS
    geo = jnp.zeros((GEO, LANES), jnp.int32)
    for w, (atom, rank) in enumerate(ranks):
        row, col, lay = at.split(atom)
        go_row = ((row - at.row + 1) & (at.n_row - 1)) - 1
        go_col = ((col - at.col + 1) & (at.n_col - 1)) - 1
        go_lay = jnp.minimum(((lay - at.lay + 1) & (at.n_lay - 1)) - 1, 1)
        twice_x = x_ref[at.me] + x_ref[atom] + BX * go_row
        twice_y = y_ref[at.me] + y_ref[atom] + BY * go_col
        twice_z = z_ref[at.me] + z_ref[atom] + BZ * go_lay - BZ
        extent = extent_ref[0, w]
        values = jnp.where(sub == 0, twice_x, jnp.where(sub == 1, twice_y, jnp.where(sub == 2, twice_z, extent)))
        geo = jnp.where(lane_pair == rank, values, geo)
    out_ref[n_pick * size :] = geo.astype(jnp.float32).astype(out_ref.dtype)
    for copy in copies:
        copy.wait()


def spread_kernel(axes, *refs):
    basis_ref = refs[1]
    spread_ref, own_basis_ref, neighbors_ref, loads = refs[-4:]
    at = Places(*axes)
    load(refs[:1], (neighbors_ref,), loads)
    slots, atoms = neighbors_ref.shape
    bits = atoms.bit_length() - 1

    def hot(rows, atom, first):
        sub = lax.broadcasted_iota(jnp.int32, (rows, SHELLS * atoms), 0)
        lane = lax.broadcasted_iota(jnp.int32, (rows, SHELLS * atoms), 1)
        return ((lane & (atoms - 1)) == atom) & (sub == first + (lane >> bits))

    def rows_of(chosen):
        picked = jnp.where(chosen, 1.0, 0.0).astype(jnp.bfloat16)
        return jnp.dot(picked, basis_ref[...], preferred_element_type=jnp.float32).astype(jnp.bfloat16)

    for w, (atom, rank) in enumerate(own_ranks(at, neighbors_ref)):
        spread_ref[:, w * LANES : (w + 1) * LANES] = rows_of(hot(LANES, atom, rank * SHELLS))
    own_basis_ref[...] = rows_of(hot(16, at.me, 0))


def prepare_kernel(axes, count, layout, late_from, *refs):
    early_ref, late_ref, info_ref, neighbors_ref, size_ref, known, inverse, layout_ref, loads = refs[-9:]
    at = Places(*axes)
    load(refs[:2], (neighbors_ref, size_ref), loads)
    slots = neighbors_ref.shape[0]
    lines = count * at.n_lay
    for i, value in enumerate(layout):
        layout_ref[i] = value
    self_slot = jnp.int32(0)
    for w in range(slots):
        atom = neighbors_ref[w, at.me]
        row, col, lay = at.split(atom)
        step_row = (row - at.row) & (at.n_row - 1)
        self_slot = jnp.where(atom == at.me, w, self_slot)
        info_ref[w] = size_ref[atom]
        known[0, w] = atom
        known[1, w] = jnp.where(col == at.col, 0, jnp.where(col == (at.col ^ 1), 1, 2))
        known[2, w] = jnp.where(step_row == 0, 0, jnp.where(step_row == 1, 1, 2)) * at.n_lay + (lay ^ at.lay)
        inverse[atom] = -1
    info_ref[slots] = size_ref[at.me]
    info_ref[slots + 1] = self_slot

    def row_of_pairs(v, totals):
        early, late = totals
        atom = known[0, v]
        side = known[1, v]
        line = known[2, v]
        for u in range(slots):
            inverse[neighbors_ref[u, atom]] = v * 16 + u

        def from_row(totals):
            total, late = totals
            for w in range(slots):
                mark = inverse[known[0, w]]
                chosen = ((mark >> 4) == v) & ((known[1, w] != 0) | (v <= w))
                where = layout_ref[line * slots + (mark & 15)]
                is_late = where >= late_from
                entry = v + 16 * w
                early_ref[total + 1] = entry + 256 * where
                late_ref[late + 1] = entry + 256 * (where - late_from)
                total = total + (chosen & ~is_late).astype(jnp.int32)
                late = late + (chosen & is_late).astype(jnp.int32)
            return total, late

        def from_column(totals):
            early, late = totals
            row, _, lay = at.split(atom)
            beside = layout_ref[lines * slots + (side - 1) * lines + line]
            for w in range(slots):
                other = known[0, w]
                mark = inverse[other]
                o_row, _, o_lay = at.split(other)
                d_row = (o_row - row) & (at.n_row - 1)
                d_lay = (o_lay - lay) & (at.n_lay - 1)
                there = target_place(at.n_row, d_row, d_lay, row)
                back = target_place(at.n_row, -d_row & (at.n_row - 1), -d_lay & (at.n_lay - 1), o_row)
                chosen = ((mark >> 4) == v) & (side == known[1, w]) & (there >= 0) & ((back < 0) | (v <= w))
                where = beside + there * LANES
                is_late = where >= late_from
                entry = v + 16 * w
                early_ref[early + 1] = entry + 256 * where
                late_ref[late + 1] = entry + 256 * (where - late_from)
                early = early + (chosen & ~is_late).astype(jnp.int32)
                late = late + (chosen & is_late).astype(jnp.int32)
            return early, late

        return lax.cond(side == 0, from_row, from_column, (early, late))

    totals = lax.fori_loop(0, slots, row_of_pairs, (jnp.int32(0), jnp.int32(0)))
    for ref, total in zip((early_ref, late_ref), totals):
        ref[0] = (total + UNROLL - 1) // UNROLL
        for i in range(UNROLL - 1):
            ref[total + i + 1] = ref[jnp.maximum(total, 1)]


def pack_kernel(moves, inputs, *refs):
    for source, start, rows, target, place in moves:
        refs[inputs + target][place : place + rows] = refs[source][start : start + rows]


def pack(values, plans, extra, name, cost=0):
    moves, shapes = [], []
    for target, plan in enumerate(plans):
        place = 0
        for source, start, rows in plan:
            moves.append((source, start, rows, target, place))
            place += rows
        shapes.append(jax.ShapeDtypeStruct((place, LANES), values[0].dtype))
    inputs = len(values) + len(extra)
    return pl.pallas_call(
        functools.partial(pack_kernel, tuple(moves), inputs),
        out_shape=tuple(shapes),
        in_specs=[VMEM] * len(values) + [ANY] * len(extra),
        out_specs=tuple([VMEM] * len(plans)),
        compiler_params=pltpu.CompilerParams(
            vmem_limit_bytes=(1 << 20) + 256 * sum(x.shape[0] for x in list(values) + shapes)
        ),
        cost_estimate=pl.CostEstimate(flops=cost, bytes_accessed=1000, transcendentals=0),
        name=name,
    )(*values, *extra)


def fill(piece_refs, pool):
    place = 0
    for piece in piece_refs:
        rows = piece.shape[0]
        pool[place : place + rows] = piece[...]
        place += rows


def place_pairs(table_ref, pool, gram, size):
    def place(i, carry):
        for k in range(UNROLL):
            entry = table_ref[i * UNROLL + k + 1]
            p = pl.multiple_of((entry & 15) * size, size)
            q = pl.multiple_of(((entry >> 4) & 15) * size, size)
            block = pool[pl.ds(pl.multiple_of(entry >> 8, 16), size)]
            gram[pl.ds(p, size), pl.ds(q, size)] = block
            gram[pl.ds(q, size), pl.ds(p, size)] = block.T
        return carry

    lax.fori_loop(0, table_ref[0], place, 0)


def gram_kernel(pieces, *refs):
    table_ref = refs[0]
    piece_refs = refs[1 : 1 + pieces]
    gram, pool = refs[-2:]
    size = LANES
    fill(piece_refs, pool)
    for v in range(gram.shape[0] // size):
        gram[v * size : (v + 1) * size] = jnp.zeros((size, gram.shape[1]), gram.dtype)
    place_pairs(table_ref, pool, gram, size)


def step_kernel(pieces, *refs):
    table_ref, info_ref, basis_ref, spread_ref, sign_ref, early_ref = refs[:6]
    piece_refs = refs[6 : 6 + pieces]
    next_ref, coef_ref, pool, gram, own, square = refs[-6:]
    slots, size = sign_ref.shape[0], sign_ref.shape[1]
    fill(piece_refs, pool)
    for v in range(slots):
        gram[v * size : (v + 1) * size] = early_ref[v * size : (v + 1) * size]
    rows = lax.broadcasted_iota(jnp.int32, (size, size), 0)
    lanes = lax.broadcasted_iota(jnp.int32, (size, size), 1)
    own_size = info_ref[slots]
    self_slot = info_ref[slots + 1]
    for w in range(slots):
        kept = (rows < own_size) & (lanes < info_ref[w])
        block = jnp.where(kept, sign_ref[w].astype(jnp.float32), 0.0)
        own[:, w * size : (w + 1) * size] = block.astype(own.dtype)
    place_pairs(table_ref, pool, gram, size)
    wide = 2 * size
    wide_lanes = lax.broadcasted_iota(jnp.int32, (size, wide), 1)
    wide_rows = lax.broadcasted_iota(jnp.int32, (size, wide), 0)

    def column_kept(n):
        first = info_ref[2 * n]
        second = info_ref[2 * n + 1]
        return (wide_lanes < first) | ((wide_lanes >= size) & (wide_lanes < size + second))

    for n in range(slots // 2):
        part = jnp.dot(own[...], gram[:, n * wide : (n + 1) * wide], preferred_element_type=jnp.float32)
        square[:, n * wide : (n + 1) * wide] = jnp.where(column_kept(n), part, 0.0).astype(square.dtype)
    basis = jnp.concatenate([basis_ref[...], basis_ref[...]], axis=1)
    coef = jnp.zeros((2 * basis_ref.shape[0], LANES), jnp.float32)
    across = (((1,), (1,)), ((), ()))
    for n in range(slots // 2):
        part = jnp.dot(square[...], gram[:, n * wide : (n + 1) * wide], preferred_element_type=jnp.float32)
        cube = jnp.where(column_kept(n), part, 0.0)
        full = 1.5 * own[:, n * wide : (n + 1) * wide].astype(jnp.float32) - 0.5 * cube
        next_ref[2 * n] = full[:, :size].astype(next_ref.dtype)
        next_ref[2 * n + 1] = full[:, size:].astype(next_ref.dtype)
        shift = (self_slot - 2 * n) * size
        is_self = (self_slot >= 2 * n) & (self_slot < 2 * n + 2)
        diag = (wide_lanes == wide_rows + shift) & (wide_rows < own_size) & is_self
        dmat = 0.5 * (jnp.where(diag, 1.0, 0.0) - full)
        high = dmat.astype(jnp.bfloat16)
        low = (dmat - high.astype(jnp.float32)).astype(jnp.bfloat16)
        half = jnp.dot(basis, jnp.concatenate([high, low], axis=0), preferred_element_type=jnp.float32)
        half_high = half.astype(jnp.bfloat16)
        half_low = (half - half_high.astype(jnp.float32)).astype(jnp.bfloat16)
        coef = coef + lax.dot_general(
            jnp.concatenate([half_high, half_low], axis=0),
            spread_ref[:, n * wide : (n + 1) * wide],
            across,
            preferred_element_type=jnp.float32,
        )
    coef = coef[: basis_ref.shape[0]] + coef[basis_ref.shape[0] :]
    coef_ref[...] = coef[: coef_ref.shape[0]]


def profile_kernel(periods, steps, mate_from, *refs):
    own_ref, mate_ref, third_ref = refs[:3]
    plane_ref, line_ref, geos, sems = refs[-4:]
    odd = (lax.axis_index("layer") & 1) == 1
    rows = len(steps) * GEO
    copies = []
    for k, source in enumerate((own_ref, mate_ref.at[pl.ds(mate_from, rows)], third_ref)):
        copy = pltpu.make_async_copy(source, geos.at[k], sems.at[k])
        copy.start()
        copies.append(copy)
    steps_x = lax.broadcasted_iota(jnp.int32, (BX, LANES), 0).astype(jnp.float32)
    steps_y = lax.broadcasted_iota(jnp.int32, (BY, LANES), 0).astype(jnp.float32)
    grid_z = lax.broadcasted_iota(jnp.int32, (LANES, BZ), 1).astype(jnp.float32)
    lane = lax.broadcasted_iota(jnp.int32, (1, LANES), 1)
    shell = (lane % SHELLS + 1).astype(jnp.float32)
    valid = lane < 7 * SPAN
    from_own = lane < 4 * SPAN
    from_below = lane < 6 * SPAN
    lift = jnp.where(from_own, 0.0, jnp.where(from_below, -float(BZ), float(BZ))) + 0.5 * BZ

    def nearest(offset, period):
        return offset - period * jnp.floor(offset * (1.0 / period) + 0.5)

    for copy in copies:
        copy.wait()
    ahead = 1.0 - 2.0 * (lax.axis_index("col") & 1).astype(jnp.float32)
    for o, (step_row, side) in enumerate(steps):
        own, first, third = (geos[k, o * GEO : (o + 1) * GEO].astype(jnp.float32) for k in range(3))
        below = jnp.where(odd, first, third)
        above = jnp.where(odd, third, first)
        moved = jnp.where(from_below, pltpu.roll(below, 3 * SPAN, axis=1), pltpu.roll(above, 3 * SPAN, axis=1))
        geo = jnp.where(from_own, own, moved)
        extent = jnp.where(valid, geo[3:4], 1.0)
        inverse = (SHELLS / extent) * (SHELLS / extent)
        reach = jnp.where(valid, extent, -1.0)
        rate_t = inverse / (shell * shell)
        packed = jnp.concatenate(
            [0.5 * geo[2:3] + lift, reach, rate_t, inverse, jnp.zeros((4, LANES), jnp.float32)], axis=0
        )
        sub = packed.T
        d_x = nearest(steps_x - (0.5 * geo[0:1] + float(BX * step_row)), periods[0])
        d_y = nearest(steps_y - (0.5 * geo[1:2] + float(BY * side) * ahead), periods[1])
        inside_x = jnp.abs(d_x) <= reach
        inside_y = jnp.abs(d_y) <= reach
        squared_x = d_x * d_x
        squared_y = d_y * d_y
        d_z = nearest(grid_z - sub[:, 0:1], periods[2])
        inside_z = jnp.abs(d_z) <= sub[:, 1:2]
        squared_z = d_z * d_z
        for s in range(SHELLS):
            part = 1.0 / ((s + 1) * (s + 1))
            rate = inverse * part + rate_t
            along_x = jnp.where(inside_x, jnp.exp(-rate * squared_x), 0.0)
            along_y = jnp.where(inside_y, jnp.exp(-rate * squared_y), 0.0)
            for x in range(BX):
                plane_ref[o, s, x * BY : (x + 1) * BY] = (along_x[x : x + 1] * along_y).astype(plane_ref.dtype)
            rate_z = sub[:, 3:4] * part + sub[:, 2:3]
            line_ref[o, s] = jnp.where(inside_z, jnp.exp(-rate_z * squared_z), 0.0).astype(line_ref.dtype)


def density_kernel(column_steps, *refs):
    coef_refs = refs[:column_steps]
    plane_ref, line_ref, out_ref, terms = refs[column_steps:]
    for o in range(plane_ref.shape[0]):
        coef = coef_refs[-o % column_steps]
        first = 8 * (o // column_steps)
        for s in range(SHELLS):
            scaled = plane_ref[o, s].astype(jnp.float32) * coef[first + s : first + s + 1, :]
            at = (o * SHELLS + s) * LANES
            terms[:, at : at + LANES] = scaled.astype(terms.dtype)
    out_ref[...] = jnp.dot(terms[...], line_ref[...], preferred_element_type=jnp.float32)


def local(sign_start, neighbors, atom_size, basis_proj, pair_extent, atom_x, atom_y, atom_z):
    n_row = lax.axis_size("row")
    n_col = lax.axis_size("col")
    n_lay = lax.axis_size("layer")
    assert n_lay == 4 and n_col >= 4 and (n_row == 2 or n_row >= 4)
    assert n_row & (n_row - 1) == 0 and n_col & (n_col - 1) == 0
    axes = (n_row, n_col, n_lay)
    atoms, slots = neighbors.shape
    size = sign_start.shape[2]
    steps = [0, 1] if n_row == 2 else [0, 1, -1]
    count = len(steps)
    others = range(1, count)
    own = sign_start[0]
    flat = own.reshape(slots * size, size)
    listings = neighbors.T
    full = slots * size
    half = full // 2
    most = half - size
    n_pick = column_targets(n_row)
    picks = n_pick * size
    part = picks + GEO

    def on_row(value, di):
        return from_offset(value, "row", steps[di])

    x_row = {di: on_row(flat, di) for di in others}
    y_row = from_layer(flat, 2)
    m_row = from_layer(flat, 1)
    picked = pl.pallas_call(
        functools.partial(pick_kernel, axes),
        out_shape=jax.ShapeDtypeStruct((part, size), own.dtype),
        in_specs=[HBM] * 6,
        out_specs=VMEM,
        scratch_shapes=[
            pltpu.SMEM((slots, atoms), jnp.int32),
            pltpu.SMEM((1, slots), jnp.int32),
            pltpu.SMEM((atoms,), jnp.int32),
            pltpu.SMEM((atoms,), jnp.int32),
            pltpu.SMEM((atoms,), jnp.int32),
            pltpu.SMEM((n_pick + 1,), jnp.int32),
            pltpu.SemaphoreType.DMA((5,)),
            pltpu.SemaphoreType.DMA((n_pick,)),
        ],
        compiler_params=pltpu.CompilerParams(vmem_limit_bytes=60 << 20),
        name="pick_column_blocks",
    )(listings, pair_extent, atom_x, atom_y, atom_z, own)
    down = from_column(picked, 1)
    up = from_column(picked, 0)

    halves = pack(
        [y_row] + [x_row[di] for di in others] + [picked],
        [[(0, half, most)]] + [[(di, 0, most)] for di in others] + [[(count, picks, GEO)]],
        [],
        "pack_halves",
    )
    ends = {di: on_row(halves[0], di) for di in others}
    tops = {di: from_layer(halves[di], 2) for di in others}

    at = {}
    buffers = {}

    def note(name, value, contents):
        buffers[name] = value
        start = 0
        for what, rows in contents:
            if what is not None:
                at[what] = (name, start)
            start += rows

    def row_of(di, flip, start=0, stop=slots):
        return [(("row", slot, di, flip), size) for slot in range(start, stop)]

    halfway = slots // 2

    def side_of(kind, di, flip):
        return [((kind, di, flip), picks)]

    note("own", flat, row_of(0, 0))
    note("mate", m_row, row_of(0, 1))
    note("far", y_row, row_of(0, 2))
    note("up", up, side_of("up", 0, 0) + [(("up geo", 0, 0), GEO)])
    note("down", down, side_of("down", 0, 0) + [(("down geo", 0, 0), GEO)])
    note("geo", halves[count], [(("geo", 0, 0), GEO)])
    for di in others:
        note(("x", di), x_row[di], row_of(di, 0))
        note(("end", di), ends[di], row_of(di, 2, halfway, slots - 1))
        note(("top", di), tops[di], row_of(di, 2, 0, halfway - 1))

    corners = [("end", di) for di in others] + [("top", di) for di in others]
    names = ["down", "up", "geo", "far"] + [("x", di) for di in others]
    plans = [
        [(1, 0, picks), (0, 0, picks), (3, full - size, size), (2, 0, GEO), (1, picks, GEO), (0, picks, GEO)],
        [(1, 0, picks), (0, 0, picks)] + [(di + 3, most, size) for di in others] + [(2, 0, GEO), (1, picks, GEO), (0, picks, GEO)],
        [(2, 0, GEO), (1, picks, GEO), (0, picks, GEO)],
    ]
    two_x, two_y, geos = pack([buffers[name] for name in names], plans, [m_row], "pack_two")
    to_mate = corners + ["up", "down"]
    for di in others:
        note(("mate x", di), from_layer(x_row[di], 1), row_of(di, 1))
    note("mate far", from_layer(y_row, 1), row_of(0, 3))

    early_order = ["own", "mate", "far", "up", "down", "geo"] + [("x", di) for di in others]
    early_order += [("mate x", di) for di in others] + ["mate far"]
    early_order += corners + [("two x", di) for di in others] + ["two y", "two m"]
    late_order = [("three x", di) for di in others] + ["three y", "three m"]
    late_order += ["four"]

    contents = {}
    for di in others:
        contents["two x", di] = side_of("up", di, 0) + side_of("down", di, 0)
        contents["two x", di] += row_of(di, 2, slots - 1, slots) + [(("geo", di, 0), GEO)]
        contents["two x", di] += [(("up geo", di, 0), GEO), (("down geo", di, 0), GEO)]
    contents["two y"] = side_of("up", 0, 2) + side_of("down", 0, 2)
    contents["two y"] += sum([row_of(di, 2, halfway - 1, halfway) for di in others], []) + [(None, 3 * GEO)]
    contents["two m"] = sum([row_of(di, 3, halfway, slots - 1) for di in others], [])
    contents["two m"] += sum([row_of(di, 3, 0, halfway - 1) for di in others], [])
    contents["two m"] += side_of("up", 0, 1) + side_of("down", 0, 1)
    for di in others:
        contents["three x", di] = side_of("up", di, 2)
    contents["three y"] = sum([side_of("down", di, 2) for di in others], [])
    contents["three m"] = []
    for di in others:
        contents["three m"] += side_of("up", di, 1) + side_of("down", di, 1) + row_of(di, 3, slots - 1, slots)
    contents["three m"] += side_of("up", 0, 3) + side_of("down", 0, 3)
    contents["three m"] += sum([row_of(di, 3, halfway - 1, halfway) for di in others], []) + [(None, 3 * GEO)]
    contents["three m"] += [("geos", count * 3 * GEO)]
    contents["four"] = sum([side_of("up", di, 3) for di in others], [])
    contents["four"] += sum([side_of("down", di, 3) for di in others], [])
    lengths = {name: sum(rows for _, rows in content) for name, content in contents.items()}
    for name in early_order:
        if name in buffers:
            lengths[name] = buffers[name].shape[0]
    base = {}
    total = 0
    for name in early_order + late_order:
        base[name] = total
        total += lengths[name]
        if name == early_order[-1]:
            late_from = total
    located = dict(at)
    for name, content in contents.items():
        start = 0
        for what, rows in content:
            located[what] = (name, start)
            start += rows
    layout = [
        base[located["row", slot, di, flip][0]] + located["row", slot, di, flip][1]
        for di in range(count)
        for flip in range(n_lay)
        for slot in range(slots)
    ]
    layout += [
        base[located[kind, di, flip][0]] + located[kind, di, flip][1]
        for kind in ("up", "down")
        for di in range(count)
        for flip in range(n_lay)
    ]
    pairs = slots * (slots + 1) // 2
    entries = pairs + UNROLL + 1
    early_table, late_table, info = pl.pallas_call(
        functools.partial(prepare_kernel, axes, count, tuple(layout), late_from),
        out_shape=(
            jax.ShapeDtypeStruct((entries,), jnp.int32),
            jax.ShapeDtypeStruct((entries,), jnp.int32),
            jax.ShapeDtypeStruct((slots + 2,), jnp.int32),
        ),
        in_specs=[HBM, HBM, ANY],
        out_specs=(SMEM, SMEM, SMEM),
        scratch_shapes=[
            pltpu.SMEM((slots, atoms), jnp.int32),
            pltpu.SMEM((atoms,), jnp.int32),
            pltpu.SMEM((3, slots), jnp.int32),
            pltpu.SMEM((atoms,), jnp.int32),
            pltpu.SMEM((len(layout),), jnp.int32),
            pltpu.SemaphoreType.DMA((2,)),
        ],
        compiler_params=pltpu.CompilerParams(vmem_limit_bytes=1 << 20),
        cost_estimate=pl.CostEstimate(flops=1000, bytes_accessed=1000, transcendentals=0),
        name="prepare",
    )(listings, atom_size, two_x)

    plans = [[(i, 0, picks if name in ("up", "down") else most) for i, name in enumerate(to_mate)]]
    two_m = pack([buffers[name] for name in to_mate], plans, [], "pack_two_mate", 3_000_000_000)[0]
    for di in others:
        note(("two x", di), on_row(two_x, di), contents["two x", di])
    note("two y", from_layer(two_y, 2), contents["two y"])
    early_mates = ["mate far"] + [("mate x", di) for di in others]
    note("two m", from_layer(two_m, 1), contents["two m"])

    buffers["geos"] = geos
    names = ["two y", "geos"] + [("two x", di) for di in others]
    place = {name: i for i, name in enumerate(names)}
    gather = [(place["geos"], 0, 3 * GEO)] + [(place["two x", di], 2 * picks + size, 3 * GEO) for di in others]
    xs = [place["two x", di] for di in others]
    plans = [
        [(0, 0, picks)],
        [(x, picks, picks) for x in xs],
        [(x, 0, 2 * picks + size) for x in xs] + [(0, 0, lengths["two y"])] + gather,
        gather,
    ]
    three_x, three_y, three_m, geos = pack([buffers[name] for name in names], plans, [buffers[name] for name in early_mates] + [two_m, info], "pack_three")
    for di in others:
        note(("three x", di), on_row(three_x, di), contents["three x", di])
    note("three y", from_layer(three_y, 2), contents["three y"])
    note("three m", from_layer(three_m, 1), contents["three m"])
    third_geos = from_layer(geos, 3)

    spread, own_basis = pl.pallas_call(
        functools.partial(spread_kernel, axes),
        out_shape=(
            jax.ShapeDtypeStruct((LANES, full), jnp.bfloat16),
            jax.ShapeDtypeStruct((16, size), jnp.bfloat16),
        ),
        in_specs=[HBM, VMEM, ANY],
        out_specs=(VMEM, VMEM),
        scratch_shapes=[pltpu.SMEM((slots, atoms), jnp.int32), pltpu.SemaphoreType.DMA((1,))],
        compiler_params=pltpu.CompilerParams(vmem_limit_bytes=(2 << 20) + atoms * 16384),
        cost_estimate=pl.CostEstimate(flops=1000, bytes_accessed=1000, transcendentals=0),
        name="spread_basis",
    )(listings, basis_proj.transpose(1, 0, 2).reshape(SHELLS * atoms, size), three_x)

    early_values = [buffers[name] for name in early_order]
    gram = pl.pallas_call(
        functools.partial(gram_kernel, len(early_values)),
        out_shape=jax.ShapeDtypeStruct((full, full), jnp.bfloat16),
        in_specs=[SMEM] + [VMEM] * len(early_values) + [ANY],
        out_specs=VMEM,
        scratch_shapes=[pltpu.VMEM((late_from, LANES), jnp.bfloat16)],
        compiler_params=pltpu.CompilerParams(vmem_limit_bytes=(6 << 20) + 2 * late_from * LANES * 2),
        cost_estimate=pl.CostEstimate(flops=1000, bytes_accessed=1000, transcendentals=0),
        name="gram_early",
    )(early_table, *early_values, three_x)

    thirds = [buffers["three x", di] for di in others] + [buffers["three y"]]
    four = pack(thirds, [[(i, 0, value.shape[0]) for i, value in enumerate(thirds)]], [gram, third_geos, own_basis], "pack_four")[0]
    note("four", from_layer(four, 1), contents["four"])

    column_steps = (0, 1, -1)
    tile_steps = [(dr, dc) for dr in steps for dc in column_steps]
    tiles = len(tile_steps)
    periods = (float(BX * n_row), float(BY * n_col), float(BZ * n_lay))
    plane, line = pl.pallas_call(
        functools.partial(profile_kernel, periods, tile_steps, at["geos"][1]),
        out_shape=(
            jax.ShapeDtypeStruct((tiles, SHELLS, BX * BY, LANES), jnp.bfloat16),
            jax.ShapeDtypeStruct((tiles, SHELLS, LANES, BZ), jnp.bfloat16),
        ),
        in_specs=[ANY] * 4,
        out_specs=(VMEM, VMEM),
        scratch_shapes=[
            pltpu.VMEM((3, tiles * GEO, LANES), jnp.bfloat16),
            pltpu.SemaphoreType.DMA((3,)),
        ],
        compiler_params=pltpu.CompilerParams(vmem_limit_bytes=10 << 20),
        cost_estimate=pl.CostEstimate(flops=5_000_000_000, bytes_accessed=4_000_000, transcendentals=2_000_000),
        name="profiles",
    )(geos, buffers["three m"], third_geos, gram)

    late_values = [buffers[name] for name in late_order]
    sign_next, coef = pl.pallas_call(
        functools.partial(step_kernel, len(late_values)),
        out_shape=(
            jax.ShapeDtypeStruct((slots, size, size), jnp.bfloat16),
            jax.ShapeDtypeStruct((8, LANES), jnp.float32),
        ),
        in_specs=[SMEM, SMEM, VMEM, VMEM, VMEM, VMEM] + [VMEM] * len(late_values) + [ANY],
        out_specs=(VMEM, VMEM),
        scratch_shapes=[
            pltpu.VMEM((total - late_from, LANES), jnp.bfloat16),
            pltpu.VMEM((full, full), jnp.bfloat16),
            pltpu.VMEM((size, full), jnp.bfloat16),
            pltpu.VMEM((size, full), jnp.bfloat16),
        ],
        compiler_params=pltpu.CompilerParams(vmem_limit_bytes=(15 << 20) + 2 * (total - late_from) * LANES * 2),
        cost_estimate=pl.CostEstimate(flops=1_300_000_000, bytes_accessed=8_000_000, transcendentals=0),
        name="square_cube_coefficients",
    )(late_table, info, own_basis, spread, own, gram, *late_values, line)

    mate_coef = from_layer(coef, 1)
    third_coef = from_layer(coef, 3)
    odd = lax.axis_index("layer") % 2 == 1
    below = jnp.where(odd, mate_coef, third_coef)
    above = jnp.where(odd, third_coef, mate_coef)
    merged = jnp.concatenate(
        [
            coef[:, : 4 * SPAN],
            below[:, SPAN : 3 * SPAN],
            above[:, 3 * SPAN : 4 * SPAN],
            jnp.zeros((8, LANES - 7 * SPAN), jnp.float32),
        ],
        axis=1,
    )
    stacked = jnp.concatenate([merged] + [on_row(merged, di) for di in others], axis=0)
    far_side = from_column(stacked, 1)
    received = [stacked, far_side, from_column(stacked, 0)]

    density = pl.pallas_call(
        functools.partial(density_kernel, len(column_steps)),
        out_shape=jax.ShapeDtypeStruct((BX * BY, BZ), jnp.float32),
        in_specs=[VMEM] * (len(received) + 2),
        out_specs=VMEM,
        scratch_shapes=[pltpu.VMEM((BX * BY, tiles * SHELLS * LANES), jnp.bfloat16)],
        compiler_params=pltpu.CompilerParams(vmem_limit_bytes=16 << 20),
        cost_estimate=pl.CostEstimate(flops=310_000_000, bytes_accessed=4_000_000, transcendentals=0),
        name="density",
    )(*received, plane, line.reshape(tiles * SHELLS * LANES, BZ))
    return sign_next[None], density.reshape(BX, BY, BZ)


def solution(mesh):
    rows = P(("row", "col", "layer"), None, None, None)
    in_specs = (rows, P(), P(), P(), P(("row", "col", "layer"), None), P(), P(), P())
    out_specs = (rows, P("row", "col", "layer"))
    return jax.shard_map(local, mesh=mesh, in_specs=in_specs, out_specs=out_specs, check_vma=False)
```

```python
import functools

import jax
import jax.numpy as jnp
from jax import lax
from jax.experimental import pallas as pl
from jax.experimental.pallas import tpu as pltpu
from jax.sharding import PartitionSpec as P

BX = 16
BY = 16
BZ = 128
LANES = 128
UNROLL = 4
SHELLS = 6
SPAN = 3 * SHELLS
GEO = 16
VMEM = pl.BlockSpec(memory_space=pltpu.VMEM)
SMEM = pl.BlockSpec(memory_space=pltpu.SMEM)
ANY = pl.BlockSpec(memory_space=pl.ANY)
HBM = pl.BlockSpec(memory_space=pltpu.HBM)


def from_offset(x, axis, step):
    count = lax.axis_size(axis)
    return lax.ppermute(x, axis, [((i + step) % count, i) for i in range(count)])


def from_column(x, side):
    count = lax.axis_size("col")
    step = [1 if (i + side) % 2 == 0 else -1 for i in range(count)]
    return lax.ppermute(x, "col", [((i + step[i]) % count, i) for i in range(count)])


def from_layer(x, flip):
    count = lax.axis_size("layer")
    return lax.ppermute(x, "layer", [(i ^ flip, i) for i in range(count)])


def column_targets(n_row):
    return 5 if n_row == 2 else 7


def target_place(n_row, step_row, step_lay, row):
    same = jnp.where(step_lay < 3, step_lay, -1)
    if n_row == 2:
        lead = step_lay - row
        across = jnp.where((lead >= 0) & (lead < 2), 3 + lead, -1)
    else:
        across = 3 + step_lay
    return jnp.where(step_row == 0, same, jnp.where(step_row == 1, across, -1))


class Places:
    def __init__(self, n_row, n_col, n_lay):
        self.n_row, self.n_col, self.n_lay = n_row, n_col, n_lay
        self.lay_bits = n_lay.bit_length() - 1
        self.col_bits = n_col.bit_length() - 1
        self.row = lax.axis_index("row")
        self.col = lax.axis_index("col")
        self.lay = lax.axis_index("layer")
        self.me = (((self.row << self.col_bits) + self.col) << self.lay_bits) + self.lay

    def split(self, atom):
        return (
            atom >> (self.lay_bits + self.col_bits),
            (atom >> self.lay_bits) & (self.n_col - 1),
            atom & (self.n_lay - 1),
        )


def load(sources, targets, sems):
    copies = [pltpu.make_async_copy(a, b, sems.at[i]) for i, (a, b) in enumerate(zip(sources, targets))]
    for copy in copies:
        copy.start()
    for copy in copies:
        copy.wait()


def own_ranks(at, neighbors_ref):
    seen = [jnp.int32(0)] * at.n_lay
    listed = []
    for w in range(neighbors_ref.shape[0]):
        atom = neighbors_ref[w, at.me]
        step_lay = (atom - at.lay) & (at.n_lay - 1)
        rank = jnp.int32(0)
        for k in range(at.n_lay):
            rank = jnp.where(step_lay == k, 3 * k + seen[k], rank)
            seen[k] = seen[k] + (step_lay == k).astype(jnp.int32)
        listed.append((atom, rank))
    return listed


def pick_kernel(axes, *refs):
    sign_ref, out_ref, neighbors_ref, extent_ref, x_ref, y_ref, z_ref, place_ref, loads, sems = refs[5:]
    at = Places(*axes)
    slots = sign_ref.shape[0]
    n_pick = place_ref.shape[0] - 1
    size = sign_ref.shape[1]
    for i in range(n_pick + 1):
        place_ref[i] = 0
    load(refs[:5], (neighbors_ref, extent_ref, x_ref, y_ref, z_ref), loads)
    ranks = own_ranks(at, neighbors_ref)
    for w, (atom, _) in enumerate(ranks):
        row, col, lay = at.split(atom)
        place = target_place(at.n_row, (row - at.row) & (at.n_row - 1), (lay - at.lay) & (at.n_lay - 1), at.row)
        place_ref[jnp.where((col == at.col) & (place >= 0), place, n_pick)] = w
    copies = []
    for i in range(n_pick):
        copy = pltpu.make_async_copy(sign_ref.at[place_ref[i]], out_ref.at[pl.ds(i * size, size)], sems.at[i])
        copy.start()
        copies.append(copy)
    sub = lax.broadcasted_iota(jnp.int32, (GEO, LANES), 0)
    lane_pair = lax.broadcasted_iota(jnp.int32, (GEO, LANES), 1) // SHELLS
    geo = jnp.zeros((GEO, LANES), jnp.int32)
    for w, (atom, rank) in enumerate(ranks):
        row, col, lay = at.split(atom)
        go_row = ((row - at.row + 1) & (at.n_row - 1)) - 1
        go_col = ((col - at.col + 1) & (at.n_col - 1)) - 1
        go_lay = jnp.minimum(((lay - at.lay + 1) & (at.n_lay - 1)) - 1, 1)
        twice_x = x_ref[at.me] + x_ref[atom] + BX * go_row
        twice_y = y_ref[at.me] + y_ref[atom] + BY * go_col
        twice_z = z_ref[at.me] + z_ref[atom] + BZ * go_lay - BZ
        extent = extent_ref[0, w]
        values = jnp.where(sub == 0, twice_x, jnp.where(sub == 1, twice_y, jnp.where(sub == 2, twice_z, extent)))
        geo = jnp.where(lane_pair == rank, values, geo)
    out_ref[n_pick * size :] = geo.astype(jnp.float32).astype(out_ref.dtype)
    for copy in copies:
        copy.wait()


def spread_kernel(axes, *refs):
    basis_ref = refs[1]
    spread_ref, own_basis_ref, neighbors_ref, loads = refs[-4:]
    at = Places(*axes)
    load(refs[:1], (neighbors_ref,), loads)
    slots, atoms = neighbors_ref.shape
    bits = atoms.bit_length() - 1

    def hot(rows, atom, first):
        sub = lax.broadcasted_iota(jnp.int32, (rows, SHELLS * atoms), 0)
        lane = lax.broadcasted_iota(jnp.int32, (rows, SHELLS * atoms), 1)
        return ((lane & (atoms - 1)) == atom) & (sub == first + (lane >> bits))

    def rows_of(chosen):
        picked = jnp.where(chosen, 1.0, 0.0).astype(jnp.bfloat16)
        return jnp.dot(picked, basis_ref[...], preferred_element_type=jnp.float32).astype(jnp.bfloat16)

    for w, (atom, rank) in enumerate(own_ranks(at, neighbors_ref)):
        spread_ref[:, w * LANES : (w + 1) * LANES] = rows_of(hot(LANES, atom, rank * SHELLS))
    own_basis_ref[...] = rows_of(hot(16, at.me, 0))


def prepare_kernel(axes, count, layout, late_from, *refs):
    early_ref, late_ref, info_ref, neighbors_ref, size_ref, known, inverse, layout_ref, loads = refs[-9:]
    at = Places(*axes)
    load(refs[:2], (neighbors_ref, size_ref), loads)
    slots = neighbors_ref.shape[0]
    lines = count * at.n_lay
    for i, value in enumerate(layout):
        layout_ref[i] = value
    self_slot = jnp.int32(0)
    for w in range(slots):
        atom = neighbors_ref[w, at.me]
        row, col, lay = at.split(atom)
        step_row = (row - at.row) & (at.n_row - 1)
        self_slot = jnp.where(atom == at.me, w, self_slot)
        info_ref[w] = size_ref[atom]
        known[0, w] = atom
        known[1, w] = jnp.where(col == at.col, 0, jnp.where(col == (at.col ^ 1), 1, 2))
        known[2, w] = jnp.where(step_row == 0, 0, jnp.where(step_row == 1, 1, 2)) * at.n_lay + (lay ^ at.lay)
        inverse[atom] = -1
    info_ref[slots] = size_ref[at.me]
    info_ref[slots + 1] = self_slot

    def row_of_pairs(v, totals):
        early, late = totals
        atom = known[0, v]
        side = known[1, v]
        line = known[2, v]
        for u in range(slots):
            inverse[neighbors_ref[u, atom]] = v * 16 + u

        def from_row(totals):
            total, late = totals
            for w in range(slots):
                mark = inverse[known[0, w]]
                chosen = ((mark >> 4) == v) & ((known[1, w] != 0) | (v <= w))
                where = layout_ref[line * slots + (mark & 15)]
                is_late = where >= late_from
                entry = v + 16 * w
                early_ref[total + 1] = entry + 256 * where
                late_ref[late + 1] = entry + 256 * (where - late_from)
                total = total + (chosen & ~is_late).astype(jnp.int32)
                late = late + (chosen & is_late).astype(jnp.int32)
            return total, late

        def from_column(totals):
            early, late = totals
            row, _, lay = at.split(atom)
            beside = layout_ref[lines * slots + (side - 1) * lines + line]
            for w in range(slots):
                other = known[0, w]
                mark = inverse[other]
                o_row, _, o_lay = at.split(other)
                d_row = (o_row - row) & (at.n_row - 1)
                d_lay = (o_lay - lay) & (at.n_lay - 1)
                there = target_place(at.n_row, d_row, d_lay, row)
                back = target_place(at.n_row, -d_row & (at.n_row - 1), -d_lay & (at.n_lay - 1), o_row)
                chosen = ((mark >> 4) == v) & (side == known[1, w]) & (there >= 0) & ((back < 0) | (v <= w))
                where = beside + there * LANES
                is_late = where >= late_from
                entry = v + 16 * w
                early_ref[early + 1] = entry + 256 * where
                late_ref[late + 1] = entry + 256 * (where - late_from)
                early = early + (chosen & ~is_late).astype(jnp.int32)
                late = late + (chosen & is_late).astype(jnp.int32)
            return early, late

        return lax.cond(side == 0, from_row, from_column, (early, late))

    totals = lax.fori_loop(0, slots, row_of_pairs, (jnp.int32(0), jnp.int32(0)))
    for ref, total in zip((early_ref, late_ref), totals):
        ref[0] = (total + UNROLL - 1) // UNROLL
        for i in range(UNROLL - 1):
            ref[total + i + 1] = ref[jnp.maximum(total, 1)]


def pack_kernel(moves, inputs, *refs):
    for source, start, rows, target, place in moves:
        refs[inputs + target][place : place + rows] = refs[source][start : start + rows]


def pack(values, plans, extra, name, cost=0):
    moves, shapes = [], []
    for target, plan in enumerate(plans):
        place = 0
        for source, start, rows in plan:
            moves.append((source, start, rows, target, place))
            place += rows
        shapes.append(jax.ShapeDtypeStruct((place, LANES), values[0].dtype))
    inputs = len(values) + len(extra)
    return pl.pallas_call(
        functools.partial(pack_kernel, tuple(moves), inputs),
        out_shape=tuple(shapes),
        in_specs=[VMEM] * len(values) + [ANY] * len(extra),
        out_specs=tuple([VMEM] * len(plans)),
        compiler_params=pltpu.CompilerParams(
            vmem_limit_bytes=(1 << 20) + 256 * sum(x.shape[0] for x in list(values) + shapes)
        ),
        cost_estimate=pl.CostEstimate(flops=cost, bytes_accessed=1000, transcendentals=0),
        name=name,
    )(*values, *extra)


def fill(piece_refs, pool):
    place = 0
    for piece in piece_refs:
        rows = piece.shape[0]
        pool[place : place + rows] = piece[...]
        place += rows


def place_pairs(table_ref, pool, gram, size):
    def place(i, carry):
        for k in range(UNROLL):
            entry = table_ref[i * UNROLL + k + 1]
            p = pl.multiple_of((entry & 15) * size, size)
            q = pl.multiple_of(((entry >> 4) & 15) * size, size)
            block = pool[pl.ds(pl.multiple_of(entry >> 8, 16), size)]
            gram[pl.ds(p, size), pl.ds(q, size)] = block
            gram[pl.ds(q, size), pl.ds(p, size)] = block.T
        return carry

    lax.fori_loop(0, table_ref[0], place, 0)


def gram_kernel(pieces, *refs):
    table_ref = refs[0]
    piece_refs = refs[1 : 1 + pieces]
    gram, pool = refs[-2:]
    size = LANES
    fill(piece_refs, pool)
    for v in range(gram.shape[0] // size):
        gram[v * size : (v + 1) * size] = jnp.zeros((size, gram.shape[1]), gram.dtype)
    place_pairs(table_ref, pool, gram, size)


def step_kernel(pieces, *refs):
    table_ref, info_ref, basis_ref, spread_ref, sign_ref, early_ref = refs[:6]
    piece_refs = refs[6 : 6 + pieces]
    next_ref, coef_ref, pool, gram, own, square = refs[-6:]
    slots, size = sign_ref.shape[0], sign_ref.shape[1]
    fill(piece_refs, pool)
    for v in range(slots):
        gram[v * size : (v + 1) * size] = early_ref[v * size : (v + 1) * size]
    rows = lax.broadcasted_iota(jnp.int32, (size, size), 0)
    lanes = lax.broadcasted_iota(jnp.int32, (size, size), 1)
    own_size = info_ref[slots]
    self_slot = info_ref[slots + 1]
    for w in range(slots):
        kept = (rows < own_size) & (lanes < info_ref[w])
        block = jnp.where(kept, sign_ref[w].astype(jnp.float32), 0.0)
        own[:, w * size : (w + 1) * size] = block.astype(own.dtype)
    place_pairs(table_ref, pool, gram, size)
    wide = 2 * size
    wide_lanes = lax.broadcasted_iota(jnp.int32, (size, wide), 1)
    wide_rows = lax.broadcasted_iota(jnp.int32, (size, wide), 0)

    def column_kept(n):
        first = info_ref[2 * n]
        second = info_ref[2 * n + 1]
        return (wide_lanes < first) | ((wide_lanes >= size) & (wide_lanes < size + second))

    for n in range(slots // 2):
        part = jnp.dot(own[...], gram[:, n * wide : (n + 1) * wide], preferred_element_type=jnp.float32)
        square[:, n * wide : (n + 1) * wide] = jnp.where(column_kept(n), part, 0.0).astype(square.dtype)
    basis = jnp.concatenate([basis_ref[...], basis_ref[...]], axis=1)
    coef = jnp.zeros((2 * basis_ref.shape[0], LANES), jnp.float32)
    across = (((1,), (1,)), ((), ()))
    for n in range(slots // 2):
        part = jnp.dot(square[...], gram[:, n * wide : (n + 1) * wide], preferred_element_type=jnp.float32)
        cube = jnp.where(column_kept(n), part, 0.0)
        full = 1.5 * own[:, n * wide : (n + 1) * wide].astype(jnp.float32) - 0.5 * cube
        next_ref[2 * n] = full[:, :size].astype(next_ref.dtype)
        next_ref[2 * n + 1] = full[:, size:].astype(next_ref.dtype)
        shift = (self_slot - 2 * n) * size
        is_self = (self_slot >= 2 * n) & (self_slot < 2 * n + 2)
        diag = (wide_lanes == wide_rows + shift) & (wide_rows < own_size) & is_self
        dmat = 0.5 * (jnp.where(diag, 1.0, 0.0) - full)
        high = dmat.astype(jnp.bfloat16)
        low = (dmat - high.astype(jnp.float32)).astype(jnp.bfloat16)
        half = jnp.dot(basis, jnp.concatenate([high, low], axis=0), preferred_element_type=jnp.float32)
        half_high = half.astype(jnp.bfloat16)
        half_low = (half - half_high.astype(jnp.float32)).astype(jnp.bfloat16)
        coef = coef + lax.dot_general(
            jnp.concatenate([half_high, half_low], axis=0),
            spread_ref[:, n * wide : (n + 1) * wide],
            across,
            preferred_element_type=jnp.float32,
        )
    coef = coef[: basis_ref.shape[0]] + coef[basis_ref.shape[0] :]
    coef_ref[...] = coef[: coef_ref.shape[0]]


def profile_kernel(periods, steps, mate_from, *refs):
    own_ref, mate_ref, third_ref = refs[:3]
    plane_ref, line_ref, geos, sems = refs[-4:]
    odd = (lax.axis_index("layer") & 1) == 1
    rows = len(steps) * GEO
    copies = []
    for k, source in enumerate((own_ref, mate_ref.at[pl.ds(mate_from, rows)], third_ref)):
        copy = pltpu.make_async_copy(source, geos.at[k], sems.at[k])
        copy.start()
        copies.append(copy)
    steps_x = lax.broadcasted_iota(jnp.int32, (BX, LANES), 0).astype(jnp.float32)
    steps_y = lax.broadcasted_iota(jnp.int32, (BY, LANES), 0).astype(jnp.float32)
    grid_z = lax.broadcasted_iota(jnp.int32, (LANES, BZ), 1).astype(jnp.float32)
    lane = lax.broadcasted_iota(jnp.int32, (1, LANES), 1)
    shell = (lane % SHELLS + 1).astype(jnp.float32)
    valid = lane < 7 * SPAN
    from_own = lane < 4 * SPAN
    from_below = lane < 6 * SPAN
    lift = jnp.where(from_own, 0.0, jnp.where(from_below, -float(BZ), float(BZ))) + 0.5 * BZ

    def nearest(offset, period):
        return offset - period * jnp.floor(offset * (1.0 / period) + 0.5)

    for copy in copies:
        copy.wait()
    ahead = 1.0 - 2.0 * (lax.axis_index("col") & 1).astype(jnp.float32)
    for o, (step_row, side) in enumerate(steps):
        own, first, third = (geos[k, o * GEO : (o + 1) * GEO].astype(jnp.float32) for k in range(3))
        below = jnp.where(odd, first, third)
        above = jnp.where(odd, third, first)
        moved = jnp.where(from_below, pltpu.roll(below, 3 * SPAN, axis=1), pltpu.roll(above, 3 * SPAN, axis=1))
        geo = jnp.where(from_own, own, moved)
        extent = jnp.where(valid, geo[3:4], 1.0)
        inverse = (SHELLS / extent) * (SHELLS / extent)
        reach = jnp.where(valid, extent, -1.0)
        rate_t = inverse / (shell * shell)
        packed = jnp.concatenate(
            [0.5 * geo[2:3] + lift, reach, rate_t, inverse, jnp.zeros((4, LANES), jnp.float32)], axis=0
        )
        sub = packed.T
        d_x = nearest(steps_x - (0.5 * geo[0:1] + float(BX * step_row)), periods[0])
        d_y = nearest(steps_y - (0.5 * geo[1:2] + float(BY * side) * ahead), periods[1])
        inside_x = jnp.abs(d_x) <= reach
        inside_y = jnp.abs(d_y) <= reach
        squared_x = d_x * d_x
        squared_y = d_y * d_y
        d_z = nearest(grid_z - sub[:, 0:1], periods[2])
        inside_z = jnp.abs(d_z) <= sub[:, 1:2]
        squared_z = d_z * d_z
        for s in range(SHELLS):
            part = 1.0 / ((s + 1) * (s + 1))
            rate = inverse * part + rate_t
            along_x = jnp.where(inside_x, jnp.exp(-rate * squared_x), 0.0)
            along_y = jnp.where(inside_y, jnp.exp(-rate * squared_y), 0.0)
            for x in range(BX):
                plane_ref[o, s, x * BY : (x + 1) * BY] = (along_x[x : x + 1] * along_y).astype(plane_ref.dtype)
            rate_z = sub[:, 3:4] * part + sub[:, 2:3]
            line_ref[o, s] = jnp.where(inside_z, jnp.exp(-rate_z * squared_z), 0.0).astype(line_ref.dtype)


def density_kernel(column_steps, *refs):
    coef_refs = refs[:column_steps]
    plane_ref, line_ref, out_ref, terms = refs[column_steps:]
    for o in range(plane_ref.shape[0]):
        coef = coef_refs[-o % column_steps]
        first = 8 * (o // column_steps)
        for s in range(SHELLS):
            scaled = plane_ref[o, s].astype(jnp.float32) * coef[first + s : first + s + 1, :]
            at = (o * SHELLS + s) * LANES
            terms[:, at : at + LANES] = scaled.astype(terms.dtype)
    out_ref[...] = jnp.dot(terms[...], line_ref[...], preferred_element_type=jnp.float32)


def local(sign_start, neighbors, atom_size, basis_proj, pair_extent, atom_x, atom_y, atom_z):
    n_row = lax.axis_size("row")
    n_col = lax.axis_size("col")
    n_lay = lax.axis_size("layer")
    assert n_lay == 4 and n_col >= 4 and (n_row == 2 or n_row >= 4)
    assert n_row & (n_row - 1) == 0 and n_col & (n_col - 1) == 0
    axes = (n_row, n_col, n_lay)
    atoms, slots = neighbors.shape
    size = sign_start.shape[2]
    steps = [0, 1] if n_row == 2 else [0, 1, -1]
    count = len(steps)
    others = range(1, count)
    own = sign_start[0]
    flat = own.reshape(slots * size, size)
    listings = neighbors.T
    full = slots * size
    half = full // 2
    most = half - size
    n_pick = column_targets(n_row)
    picks = n_pick * size
    part = picks + GEO

    def on_row(value, di):
        return from_offset(value, "row", steps[di])

    x_row = {di: on_row(flat, di) for di in others}
    y_row = from_layer(flat, 2)
    m_row = from_layer(flat, 1)
    picked = pl.pallas_call(
        functools.partial(pick_kernel, axes),
        out_shape=jax.ShapeDtypeStruct((part, size), own.dtype),
        in_specs=[HBM] * 6,
        out_specs=VMEM,
        scratch_shapes=[
            pltpu.SMEM((slots, atoms), jnp.int32),
            pltpu.SMEM((1, slots), jnp.int32),
            pltpu.SMEM((atoms,), jnp.int32),
            pltpu.SMEM((atoms,), jnp.int32),
            pltpu.SMEM((atoms,), jnp.int32),
            pltpu.SMEM((n_pick + 1,), jnp.int32),
            pltpu.SemaphoreType.DMA((5,)),
            pltpu.SemaphoreType.DMA((n_pick,)),
        ],
        compiler_params=pltpu.CompilerParams(vmem_limit_bytes=60 << 20),
        name="pick_column_blocks",
    )(listings, pair_extent, atom_x, atom_y, atom_z, own)
    down = from_column(picked, 1)
    up = from_column(picked, 0)

    halves = pack(
        [y_row] + [x_row[di] for di in others] + [picked],
        [[(0, half, most)]] + [[(di, 0, most)] for di in others] + [[(count, picks, GEO)]],
        [],
        "pack_halves",
    )
    ends = {di: on_row(halves[0], di) for di in others}
    tops = {di: from_layer(halves[di], 2) for di in others}

    at = {}
    buffers = {}

    def note(name, value, contents):
        buffers[name] = value
        start = 0
        for what, rows in contents:
            if what is not None:
                at[what] = (name, start)
            start += rows

    def row_of(di, flip, start=0, stop=slots):
        return [(("row", slot, di, flip), size) for slot in range(start, stop)]

    halfway = slots // 2

    def side_of(kind, di, flip):
        return [((kind, di, flip), picks)]

    note("own", flat, row_of(0, 0))
    note("mate", m_row, row_of(0, 1))
    note("far", y_row, row_of(0, 2))
    note("up", up, side_of("up", 0, 0) + [(("up geo", 0, 0), GEO)])
    note("down", down, side_of("down", 0, 0) + [(("down geo", 0, 0), GEO)])
    note("geo", halves[count], [(("geo", 0, 0), GEO)])
    for di in others:
        note(("x", di), x_row[di], row_of(di, 0))
        note(("end", di), ends[di], row_of(di, 2, halfway, slots - 1))
        note(("top", di), tops[di], row_of(di, 2, 0, halfway - 1))

    corners = [("end", di) for di in others] + [("top", di) for di in others]
    names = ["down", "up", "geo", "far"] + [("x", di) for di in others]
    plans = [
        [(1, 0, picks), (0, 0, picks), (3, full - size, size), (2, 0, GEO), (1, picks, GEO), (0, picks, GEO)],
        [(1, 0, picks), (0, 0, picks)] + [(di + 3, most, size) for di in others] + [(2, 0, GEO), (1, picks, GEO), (0, picks, GEO)],
        [(2, 0, GEO), (1, picks, GEO), (0, picks, GEO)],
    ]
    two_x, two_y, geos = pack([buffers[name] for name in names], plans, [m_row], "pack_two")
    to_mate = corners + ["up", "down"]
    for di in others:
        note(("mate x", di), from_layer(x_row[di], 1), row_of(di, 1))
    note("mate far", from_layer(y_row, 1), row_of(0, 3))

    early_order = ["own", "mate", "far", "up", "down", "geo"] + [("x", di) for di in others]
    early_order += [("mate x", di) for di in others] + ["mate far"]
    early_order += corners + [("two x", di) for di in others] + ["two y", "two m"]
    late_order = [("three x", di) for di in others] + ["three y", "three m"]
    late_order += ["four"]

    contents = {}
    for di in others:
        contents["two x", di] = side_of("up", di, 0) + side_of("down", di, 0)
        contents["two x", di] += row_of(di, 2, slots - 1, slots) + [(("geo", di, 0), GEO)]
        contents["two x", di] += [(("up geo", di, 0), GEO), (("down geo", di, 0), GEO)]
    contents["two y"] = side_of("up", 0, 2) + side_of("down", 0, 2)
    contents["two y"] += sum([row_of(di, 2, halfway - 1, halfway) for di in others], []) + [(None, 3 * GEO)]
    contents["two m"] = sum([row_of(di, 3, halfway, slots - 1) for di in others], [])
    contents["two m"] += sum([row_of(di, 3, 0, halfway - 1) for di in others], [])
    contents["two m"] += side_of("up", 0, 1) + side_of("down", 0, 1)
    for di in others:
        contents["three x", di] = side_of("up", di, 2)
    contents["three y"] = sum([side_of("down", di, 2) for di in others], [])
    contents["three m"] = []
    for di in others:
        contents["three m"] += side_of("up", di, 1) + side_of("down", di, 1) + row_of(di, 3, slots - 1, slots)
    contents["three m"] += side_of("up", 0, 3) + side_of("down", 0, 3)
    contents["three m"] += sum([row_of(di, 3, halfway - 1, halfway) for di in others], []) + [(None, 3 * GEO)]
    contents["three m"] += [("geos", count * 3 * GEO)]
    contents["four"] = sum([side_of("up", di, 3) for di in others], [])
    contents["four"] += sum([side_of("down", di, 3) for di in others], [])
    lengths = {name: sum(rows for _, rows in content) for name, content in contents.items()}
    for name in early_order:
        if name in buffers:
            lengths[name] = buffers[name].shape[0]
    base = {}
    total = 0
    for name in early_order + late_order:
        base[name] = total
        total += lengths[name]
        if name == early_order[-1]:
            late_from = total
    located = dict(at)
    for name, content in contents.items():
        start = 0
        for what, rows in content:
            located[what] = (name, start)
            start += rows
    layout = [
        base[located["row", slot, di, flip][0]] + located["row", slot, di, flip][1]
        for di in range(count)
        for flip in range(n_lay)
        for slot in range(slots)
    ]
    layout += [
        base[located[kind, di, flip][0]] + located[kind, di, flip][1]
        for kind in ("up", "down")
        for di in range(count)
        for flip in range(n_lay)
    ]
    pairs = slots * (slots + 1) // 2
    entries = pairs + UNROLL + 1
    early_table, late_table, info = pl.pallas_call(
        functools.partial(prepare_kernel, axes, count, tuple(layout), late_from),
        out_shape=(
            jax.ShapeDtypeStruct((entries,), jnp.int32),
            jax.ShapeDtypeStruct((entries,), jnp.int32),
            jax.ShapeDtypeStruct((slots + 2,), jnp.int32),
        ),
        in_specs=[HBM, HBM, ANY],
        out_specs=(SMEM, SMEM, SMEM),
        scratch_shapes=[
            pltpu.SMEM((slots, atoms), jnp.int32),
            pltpu.SMEM((atoms,), jnp.int32),
            pltpu.SMEM((3, slots), jnp.int32),
            pltpu.SMEM((atoms,), jnp.int32),
            pltpu.SMEM((len(layout),), jnp.int32),
            pltpu.SemaphoreType.DMA((2,)),
        ],
        compiler_params=pltpu.CompilerParams(vmem_limit_bytes=1 << 20),
        cost_estimate=pl.CostEstimate(flops=1000, bytes_accessed=1000, transcendentals=0),
        name="prepare",
    )(listings, atom_size, two_x)

    plans = [[(i, 0, picks if name in ("up", "down") else most) for i, name in enumerate(to_mate)]]
    two_m = pack([buffers[name] for name in to_mate], plans, [], "pack_two_mate", 3_000_000_000)[0]
    for di in others:
        note(("two x", di), on_row(two_x, di), contents["two x", di])
    note("two y", from_layer(two_y, 2), contents["two y"])
    early_mates = ["mate far"] + [("mate x", di) for di in others]
    note("two m", from_layer(two_m, 1), contents["two m"])

    buffers["geos"] = geos
    names = ["two y", "geos"] + [("two x", di) for di in others]
    place = {name: i for i, name in enumerate(names)}
    gather = [(place["geos"], 0, 3 * GEO)] + [(place["two x", di], 2 * picks + size, 3 * GEO) for di in others]
    xs = [place["two x", di] for di in others]
    plans = [
        [(0, 0, picks)],
        [(x, picks, picks) for x in xs],
        [(x, 0, 2 * picks + size) for x in xs] + [(0, 0, lengths["two y"])] + gather,
        gather,
    ]
    three_x, three_y, three_m, geos = pack([buffers[name] for name in names], plans, [buffers[name] for name in early_mates] + [two_m, info], "pack_three")
    for di in others:
        note(("three x", di), on_row(three_x, di), contents["three x", di])
    note("three y", from_layer(three_y, 2), contents["three y"])
    note("three m", from_layer(three_m, 1), contents["three m"])
    third_geos = from_layer(geos, 3)

    spread, own_basis = pl.pallas_call(
        functools.partial(spread_kernel, axes),
        out_shape=(
            jax.ShapeDtypeStruct((LANES, full), jnp.bfloat16),
            jax.ShapeDtypeStruct((16, size), jnp.bfloat16),
        ),
        in_specs=[HBM, VMEM, ANY],
        out_specs=(VMEM, VMEM),
        scratch_shapes=[pltpu.SMEM((slots, atoms), jnp.int32), pltpu.SemaphoreType.DMA((1,))],
        compiler_params=pltpu.CompilerParams(vmem_limit_bytes=(2 << 20) + atoms * 16384),
        cost_estimate=pl.CostEstimate(flops=1000, bytes_accessed=1000, transcendentals=0),
        name="spread_basis",
    )(listings, basis_proj.transpose(1, 0, 2).reshape(SHELLS * atoms, size), three_x)

    early_values = [buffers[name] for name in early_order]
    gram = pl.pallas_call(
        functools.partial(gram_kernel, len(early_values)),
        out_shape=jax.ShapeDtypeStruct((full, full), jnp.bfloat16),
        in_specs=[SMEM] + [VMEM] * len(early_values) + [ANY],
        out_specs=VMEM,
        scratch_shapes=[pltpu.VMEM((late_from, LANES), jnp.bfloat16)],
        compiler_params=pltpu.CompilerParams(vmem_limit_bytes=(6 << 20) + 2 * late_from * LANES * 2),
        cost_estimate=pl.CostEstimate(flops=1000, bytes_accessed=1000, transcendentals=0),
        name="gram_early",
    )(early_table, *early_values, three_x)

    thirds = [buffers["three x", di] for di in others] + [buffers["three y"]]
    four = pack(thirds, [[(i, 0, value.shape[0]) for i, value in enumerate(thirds)]], [gram, third_geos, own_basis], "pack_four")[0]
    note("four", from_layer(four, 1), contents["four"])

    column_steps = (0, 1, -1)
    tile_steps = [(dr, dc) for dr in steps for dc in column_steps]
    tiles = len(tile_steps)
    periods = (float(BX * n_row), float(BY * n_col), float(BZ * n_lay))
    plane, line = pl.pallas_call(
        functools.partial(profile_kernel, periods, tile_steps, at["geos"][1]),
        out_shape=(
            jax.ShapeDtypeStruct((tiles, SHELLS, BX * BY, LANES), jnp.bfloat16),
            jax.ShapeDtypeStruct((tiles, SHELLS, LANES, BZ), jnp.bfloat16),
        ),
        in_specs=[ANY] * 3,
        out_specs=(VMEM, VMEM),
        scratch_shapes=[
            pltpu.VMEM((3, tiles * GEO, LANES), jnp.bfloat16),
            pltpu.SemaphoreType.DMA((3,)),
        ],
        compiler_params=pltpu.CompilerParams(vmem_limit_bytes=10 << 20),
        cost_estimate=pl.CostEstimate(flops=1000, bytes_accessed=1000, transcendentals=0),
        name="profiles",
    )(geos, buffers["three m"], third_geos)

    late_values = [buffers[name] for name in late_order]
    sign_next, coef = pl.pallas_call(
        functools.partial(step_kernel, len(late_values)),
        out_shape=(
            jax.ShapeDtypeStruct((slots, size, size), jnp.bfloat16),
            jax.ShapeDtypeStruct((8, LANES), jnp.float32),
        ),
        in_specs=[SMEM, SMEM, VMEM, VMEM, VMEM, VMEM] + [VMEM] * len(late_values),
        out_specs=(VMEM, VMEM),
        scratch_shapes=[
            pltpu.VMEM((total - late_from, LANES), jnp.bfloat16),
            pltpu.VMEM((full, full), jnp.bfloat16),
            pltpu.VMEM((size, full), jnp.bfloat16),
            pltpu.VMEM((size, full), jnp.bfloat16),
        ],
        compiler_params=pltpu.CompilerParams(vmem_limit_bytes=(15 << 20) + 2 * (total - late_from) * LANES * 2),
        cost_estimate=pl.CostEstimate(flops=1_300_000_000, bytes_accessed=8_000_000, transcendentals=0),
        name="square_cube_coefficients",
    )(late_table, info, own_basis, spread, own, gram, *late_values)

    mate_coef = from_layer(coef, 1)
    third_coef = from_layer(coef, 3)
    odd = lax.axis_index("layer") % 2 == 1
    below = jnp.where(odd, mate_coef, third_coef)
    above = jnp.where(odd, third_coef, mate_coef)
    merged = jnp.concatenate(
        [
            coef[:, : 4 * SPAN],
            below[:, SPAN : 3 * SPAN],
            above[:, 3 * SPAN : 4 * SPAN],
            jnp.zeros((8, LANES - 7 * SPAN), jnp.float32),
        ],
        axis=1,
    )
    stacked = jnp.concatenate([merged] + [on_row(merged, di) for di in others], axis=0)
    far_side = from_column(stacked, 1)
    received = [stacked, far_side, from_column(stacked, 0)]

    density = pl.pallas_call(
        functools.partial(density_kernel, len(column_steps)),
        out_shape=jax.ShapeDtypeStruct((BX * BY, BZ), jnp.float32),
        in_specs=[VMEM] * (len(received) + 2),
        out_specs=VMEM,
        scratch_shapes=[pltpu.VMEM((BX * BY, tiles * SHELLS * LANES), jnp.bfloat16)],
        compiler_params=pltpu.CompilerParams(vmem_limit_bytes=16 << 20),
        cost_estimate=pl.CostEstimate(flops=310_000_000, bytes_accessed=4_000_000, transcendentals=0),
        name="density",
    )(*received, plane, line.reshape(tiles * SHELLS * LANES, BZ))
    return sign_next[None], density.reshape(BX, BY, BZ)


def solution(mesh):
    rows = P(("row", "col", "layer"), None, None, None)
    in_specs = (rows, P(), P(), P(), P(("row", "col", "layer"), None), P(), P(), P())
    out_specs = (rows, P("row", "col", "layer"))
    return jax.shard_map(local, mesh=mesh, in_specs=in_specs, out_specs=out_specs, check_vma=False)
```

```python
import functools

import jax
import jax.numpy as jnp
from jax import lax
from jax.experimental import pallas as pl
from jax.experimental.pallas import tpu as pltpu
from jax.sharding import PartitionSpec as P

BX = 16
BY = 16
BZ = 128
LANES = 128
UNROLL = 4
SHELLS = 6
SPAN = 3 * SHELLS
GEO = 16
VMEM = pl.BlockSpec(memory_space=pltpu.VMEM)
SMEM = pl.BlockSpec(memory_space=pltpu.SMEM)
ANY = pl.BlockSpec(memory_space=pl.ANY)
HBM = pl.BlockSpec(memory_space=pltpu.HBM)


def from_offset(x, axis, step):
    count = lax.axis_size(axis)
    return lax.ppermute(x, axis, [((i + step) % count, i) for i in range(count)])


def from_column(x, side):
    count = lax.axis_size("col")
    step = [1 if (i + side) % 2 == 0 else -1 for i in range(count)]
    return lax.ppermute(x, "col", [((i + step[i]) % count, i) for i in range(count)])


def from_layer(x, flip):
    count = lax.axis_size("layer")
    return lax.ppermute(x, "layer", [(i ^ flip, i) for i in range(count)])


def column_targets(n_row):
    return 5 if n_row == 2 else 7


def target_place(n_row, step_row, step_lay, row):
    same = jnp.where(step_lay < 3, step_lay, -1)
    if n_row == 2:
        lead = step_lay - row
        across = jnp.where((lead >= 0) & (lead < 2), 3 + lead, -1)
    else:
        across = 3 + step_lay
    return jnp.where(step_row == 0, same, jnp.where(step_row == 1, across, -1))


class Places:
    def __init__(self, n_row, n_col, n_lay):
        self.n_row, self.n_col, self.n_lay = n_row, n_col, n_lay
        self.lay_bits = n_lay.bit_length() - 1
        self.col_bits = n_col.bit_length() - 1
        self.row = lax.axis_index("row")
        self.col = lax.axis_index("col")
        self.lay = lax.axis_index("layer")
        self.me = (((self.row << self.col_bits) + self.col) << self.lay_bits) + self.lay

    def split(self, atom):
        return (
            atom >> (self.lay_bits + self.col_bits),
            (atom >> self.lay_bits) & (self.n_col - 1),
            atom & (self.n_lay - 1),
        )


def load(sources, targets, sems):
    copies = [pltpu.make_async_copy(a, b, sems.at[i]) for i, (a, b) in enumerate(zip(sources, targets))]
    for copy in copies:
        copy.start()
    for copy in copies:
        copy.wait()


def own_ranks(at, neighbors_ref):
    seen = [jnp.int32(0)] * at.n_lay
    listed = []
    for w in range(neighbors_ref.shape[0]):
        atom = neighbors_ref[w, at.me]
        step_lay = (atom - at.lay) & (at.n_lay - 1)
        rank = jnp.int32(0)
        for k in range(at.n_lay):
            rank = jnp.where(step_lay == k, 3 * k + seen[k], rank)
            seen[k] = seen[k] + (step_lay == k).astype(jnp.int32)
        listed.append((atom, rank))
    return listed


def pick_kernel(axes, *refs):
    sign_ref, out_ref, neighbors_ref, extent_ref, x_ref, y_ref, z_ref, place_ref, loads, sems = refs[5:]
    at = Places(*axes)
    slots = sign_ref.shape[0]
    n_pick = place_ref.shape[0] - 1
    size = sign_ref.shape[1]
    for i in range(n_pick + 1):
        place_ref[i] = 0
    load(refs[:5], (neighbors_ref, extent_ref, x_ref, y_ref, z_ref), loads)
    ranks = own_ranks(at, neighbors_ref)
    for w, (atom, _) in enumerate(ranks):
        row, col, lay = at.split(atom)
        place = target_place(at.n_row, (row - at.row) & (at.n_row - 1), (lay - at.lay) & (at.n_lay - 1), at.row)
        place_ref[jnp.where((col == at.col) & (place >= 0), place, n_pick)] = w
    copies = []
    for i in range(n_pick):
        copy = pltpu.make_async_copy(sign_ref.at[place_ref[i]], out_ref.at[pl.ds(i * size, size)], sems.at[i])
        copy.start()
        copies.append(copy)
    sub = lax.broadcasted_iota(jnp.int32, (GEO, LANES), 0)
    lane_pair = lax.broadcasted_iota(jnp.int32, (GEO, LANES), 1) // SHELLS
    geo = jnp.zeros((GEO, LANES), jnp.int32)
    for w, (atom, rank) in enumerate(ranks):
        row, col, lay = at.split(atom)
        go_row = ((row - at.row + 1) & (at.n_row - 1)) - 1
        go_col = ((col - at.col + 1) & (at.n_col - 1)) - 1
        go_lay = jnp.minimum(((lay - at.lay + 1) & (at.n_lay - 1)) - 1, 1)
        twice_x = x_ref[at.me] + x_ref[atom] + BX * go_row
        twice_y = y_ref[at.me] + y_ref[atom] + BY * go_col
        twice_z = z_ref[at.me] + z_ref[atom] + BZ * go_lay - BZ
        extent = extent_ref[0, w]
        values = jnp.where(sub == 0, twice_x, jnp.where(sub == 1, twice_y, jnp.where(sub == 2, twice_z, extent)))
        geo = jnp.where(lane_pair == rank, values, geo)
    out_ref[n_pick * size :] = geo.astype(jnp.float32).astype(out_ref.dtype)
    for copy in copies:
        copy.wait()


def spread_kernel(axes, *refs):
    basis_ref, info_ref, sign_ref = refs[1:4]
    spread_ref, own_basis_ref, own_ref, seen_ref, neighbors_ref, loads = refs[-6:]
    at = Places(*axes)
    load(refs[:1], (neighbors_ref,), loads)
    slots, atoms = neighbors_ref.shape
    bits = atoms.bit_length() - 1

    def hot(rows, atom, first):
        sub = lax.broadcasted_iota(jnp.int32, (rows, SHELLS * atoms), 0)
        lane = lax.broadcasted_iota(jnp.int32, (rows, SHELLS * atoms), 1)
        return ((lane & (atoms - 1)) == atom) & (sub == first + (lane >> bits))

    def rows_of(chosen):
        picked = jnp.where(chosen, 1.0, 0.0).astype(jnp.bfloat16)
        return jnp.dot(picked, basis_ref[...], preferred_element_type=jnp.float32).astype(jnp.bfloat16)

    for w, (atom, rank) in enumerate(own_ranks(at, neighbors_ref)):
        spread_ref[:, w * LANES : (w + 1) * LANES] = rows_of(hot(LANES, atom, rank * SHELLS))
    own_basis = rows_of(hot(16, at.me, 0))
    own_basis_ref[...] = own_basis
    size = sign_ref.shape[1]
    rows = lax.broadcasted_iota(jnp.int32, (size, size), 0)
    lanes = lax.broadcasted_iota(jnp.int32, (size, size), 1)
    for w in range(slots):
        kept = (rows < info_ref[slots]) & (lanes < info_ref[w])
        block = jnp.where(kept, sign_ref[w].astype(jnp.float32), 0.0).astype(own_ref.dtype)
        own_ref[:, w * size : (w + 1) * size] = block
        seen_ref[:, w * size : (w + 1) * size] = jnp.dot(own_basis, block, preferred_element_type=jnp.float32)


def prepare_kernel(axes, count, layout, late_from, *refs):
    early_ref, late_ref, info_ref, neighbors_ref, size_ref, known, inverse, layout_ref, loads = refs[-9:]
    at = Places(*axes)
    load(refs[:2], (neighbors_ref, size_ref), loads)
    slots = neighbors_ref.shape[0]
    lines = count * at.n_lay
    for i, value in enumerate(layout):
        layout_ref[i] = value
    self_slot = jnp.int32(0)
    for w in range(slots):
        atom = neighbors_ref[w, at.me]
        row, col, lay = at.split(atom)
        step_row = (row - at.row) & (at.n_row - 1)
        self_slot = jnp.where(atom == at.me, w, self_slot)
        info_ref[w] = size_ref[atom]
        known[0, w] = atom
        known[1, w] = jnp.where(col == at.col, 0, jnp.where(col == (at.col ^ 1), 1, 2))
        known[2, w] = jnp.where(step_row == 0, 0, jnp.where(step_row == 1, 1, 2)) * at.n_lay + (lay ^ at.lay)
        inverse[atom] = -1
    info_ref[slots] = size_ref[at.me]
    info_ref[slots + 1] = self_slot

    def row_of_pairs(v, totals):
        early, late = totals
        atom = known[0, v]
        side = known[1, v]
        line = known[2, v]
        for u in range(slots):
            inverse[neighbors_ref[u, atom]] = v * 16 + u

        def from_row(totals):
            total, late = totals
            for w in range(slots):
                mark = inverse[known[0, w]]
                chosen = ((mark >> 4) == v) & ((known[1, w] != 0) | (v <= w))
                where = layout_ref[line * slots + (mark & 15)]
                is_late = where >= late_from
                entry = v + 16 * w
                early_ref[total + 1] = entry + 256 * where
                late_ref[late + 1] = entry + 256 * (where - late_from)
                total = total + (chosen & ~is_late).astype(jnp.int32)
                late = late + (chosen & is_late).astype(jnp.int32)
            return total, late

        def from_column(totals):
            early, late = totals
            row, _, lay = at.split(atom)
            beside = layout_ref[lines * slots + (side - 1) * lines + line]
            for w in range(slots):
                other = known[0, w]
                mark = inverse[other]
                o_row, _, o_lay = at.split(other)
                d_row = (o_row - row) & (at.n_row - 1)
                d_lay = (o_lay - lay) & (at.n_lay - 1)
                there = target_place(at.n_row, d_row, d_lay, row)
                back = target_place(at.n_row, -d_row & (at.n_row - 1), -d_lay & (at.n_lay - 1), o_row)
                chosen = ((mark >> 4) == v) & (side == known[1, w]) & (there >= 0) & ((back < 0) | (v <= w))
                where = beside + there * LANES
                is_late = where >= late_from
                entry = v + 16 * w
                early_ref[early + 1] = entry + 256 * where
                late_ref[late + 1] = entry + 256 * (where - late_from)
                early = early + (chosen & ~is_late).astype(jnp.int32)
                late = late + (chosen & is_late).astype(jnp.int32)
            return early, late

        return lax.cond(side == 0, from_row, from_column, (early, late))

    totals = lax.fori_loop(0, slots, row_of_pairs, (jnp.int32(0), jnp.int32(0)))
    for ref, total in zip((early_ref, late_ref), totals):
        ref[0] = (total + UNROLL - 1) // UNROLL
        for i in range(UNROLL - 1):
            ref[total + i + 1] = ref[jnp.maximum(total, 1)]


def pack_kernel(moves, inputs, *refs):
    for source, start, rows, target, place in moves:
        refs[inputs + target][place : place + rows] = refs[source][start : start + rows]


def pack(values, plans, extra, name, cost=0):
    moves, shapes = [], []
    for target, plan in enumerate(plans):
        place = 0
        for source, start, rows in plan:
            moves.append((source, start, rows, target, place))
            place += rows
        shapes.append(jax.ShapeDtypeStruct((place, LANES), values[0].dtype))
    inputs = len(values) + len(extra)
    return pl.pallas_call(
        functools.partial(pack_kernel, tuple(moves), inputs),
        out_shape=tuple(shapes),
        in_specs=[VMEM] * len(values) + [ANY] * len(extra),
        out_specs=tuple([VMEM] * len(plans)),
        compiler_params=pltpu.CompilerParams(
            vmem_limit_bytes=(1 << 20) + 256 * sum(x.shape[0] for x in list(values) + shapes)
        ),
        cost_estimate=pl.CostEstimate(flops=cost, bytes_accessed=1000, transcendentals=0),
        name=name,
    )(*values, *extra)


def fill(piece_refs, pool):
    place = 0
    for piece in piece_refs:
        rows = piece.shape[0]
        pool[place : place + rows] = piece[...]
        place += rows


def place_pairs(table_ref, pool, gram, size):
    def place(i, carry):
        for k in range(UNROLL):
            entry = table_ref[i * UNROLL + k + 1]
            p = pl.multiple_of((entry & 15) * size, size)
            q = pl.multiple_of(((entry >> 4) & 15) * size, size)
            block = pool[pl.ds(pl.multiple_of(entry >> 8, 16), size)]
            gram[pl.ds(p, size), pl.ds(q, size)] = block
            gram[pl.ds(q, size), pl.ds(p, size)] = block.T
        return carry

    lax.fori_loop(0, table_ref[0], place, 0)


def gram_kernel(pieces, *refs):
    table_ref = refs[0]
    piece_refs = refs[1 : 1 + pieces]
    gram, pool = refs[-2:]
    size = LANES
    fill(piece_refs, pool)
    for v in range(gram.shape[0] // size):
        gram[v * size : (v + 1) * size] = jnp.zeros((size, gram.shape[1]), gram.dtype)
    place_pairs(table_ref, pool, gram, size)


def step_kernel(pieces, *refs):
    table_ref, info_ref, basis_ref, spread_ref, own, seen_ref, early_ref = refs[:7]
    piece_refs = refs[7 : 7 + pieces]
    next_ref, coef_ref, pool, gram, square = refs[-5:]
    slots, size = next_ref.shape[0], next_ref.shape[1]
    shells = basis_ref.shape[0]
    fill(piece_refs, pool)
    for v in range(slots):
        gram[v * size : (v + 1) * size] = early_ref[v * size : (v + 1) * size]
    place_pairs(table_ref, pool, gram, size)
    own_size = info_ref[slots]
    self_slot = info_ref[slots + 1]
    wide = 2 * size

    def column_kept(n, rows):
        lanes = lax.broadcasted_iota(jnp.int32, (rows, wide), 1)
        return (lanes < info_ref[2 * n]) | ((lanes >= size) & (lanes < size + info_ref[2 * n + 1]))

    for n in range(slots // 2):
        span = slice(n * wide, (n + 1) * wide)
        part = jnp.dot(own[...], gram[:, span], preferred_element_type=jnp.float32)
        part = jnp.where(column_kept(n, size), part, 0.0).astype(square.dtype)
        square[:size, span] = part
        seen = jnp.dot(basis_ref[...], part, preferred_element_type=jnp.float32)
        high = seen.astype(square.dtype)
        square[size : size + shells, span] = high
        square[size + shells :, span] = (seen - high.astype(jnp.float32)).astype(square.dtype)
    coef = jnp.zeros((2 * shells, LANES), jnp.float32)
    across = (((1,), (1,)), ((), ()))
    wide_lanes = lax.broadcasted_iota(jnp.int32, (shells, wide), 1)
    basis = basis_ref[...].astype(jnp.float32)
    basis = jnp.concatenate([basis, basis], axis=1)
    for n in range(slots // 2):
        span = slice(n * wide, (n + 1) * wide)
        part = jnp.dot(square[...], gram[:, span], preferred_element_type=jnp.float32)
        cube = jnp.where(column_kept(n, size), part[:size], 0.0)
        full = 1.5 * own[:, span].astype(jnp.float32) - 0.5 * cube
        next_ref[2 * n] = full[:, :size].astype(next_ref.dtype)
        next_ref[2 * n + 1] = full[:, size:].astype(next_ref.dtype)
        seen = part[size : size + shells] + part[size + shells :]
        seen = jnp.where(column_kept(n, shells), seen, 0.0)
        first = (self_slot - 2 * n) * size
        is_self = (self_slot >= 2 * n) & (self_slot < 2 * n + 2)
        diag = (wide_lanes >= first) & (wide_lanes < first + own_size) & is_self
        half = 0.5 * (jnp.where(diag, basis, 0.0) - (1.5 * seen_ref[:, span] - 0.5 * seen))
        half_high = half.astype(jnp.bfloat16)
        half_low = (half - half_high.astype(jnp.float32)).astype(jnp.bfloat16)
        coef = coef + lax.dot_general(
            jnp.concatenate([half_high, half_low], axis=0),
            spread_ref[:, span],
            across,
            preferred_element_type=jnp.float32,
        )
    coef = coef[:shells] + coef[shells:]
    coef_ref[...] = coef[: coef_ref.shape[0]]


def profile_kernel(periods, steps, mate_from, *refs):
    own_ref, mate_ref, third_ref = refs[:3]
    plane_ref, line_ref, geos, sems = refs[-4:]
    odd = (lax.axis_index("layer") & 1) == 1
    rows = len(steps) * GEO
    copies = []
    for k, source in enumerate((own_ref, mate_ref.at[pl.ds(mate_from, rows)], third_ref)):
        copy = pltpu.make_async_copy(source, geos.at[k], sems.at[k])
        copy.start()
        copies.append(copy)
    steps_x = lax.broadcasted_iota(jnp.int32, (BX, LANES), 0).astype(jnp.float32)
    steps_y = lax.broadcasted_iota(jnp.int32, (BY, LANES), 0).astype(jnp.float32)
    grid_z = lax.broadcasted_iota(jnp.int32, (LANES, BZ), 1).astype(jnp.float32)
    lane = lax.broadcasted_iota(jnp.int32, (1, LANES), 1)
    shell = (lane % SHELLS + 1).astype(jnp.float32)
    valid = lane < 7 * SPAN
    from_own = lane < 4 * SPAN
    from_below = lane < 6 * SPAN
    lift = jnp.where(from_own, 0.0, jnp.where(from_below, -float(BZ), float(BZ))) + 0.5 * BZ

    def nearest(offset, period):
        return offset - period * jnp.floor(offset * (1.0 / period) + 0.5)

    for copy in copies:
        copy.wait()
    ahead = 1.0 - 2.0 * (lax.axis_index("col") & 1).astype(jnp.float32)
    for o, (step_row, side) in enumerate(steps):
        own, first, third = (geos[k, o * GEO : (o + 1) * GEO].astype(jnp.float32) for k in range(3))
        below = jnp.where(odd, first, third)
        above = jnp.where(odd, third, first)
        moved = jnp.where(from_below, pltpu.roll(below, 3 * SPAN, axis=1), pltpu.roll(above, 3 * SPAN, axis=1))
        geo = jnp.where(from_own, own, moved)
        extent = jnp.where(valid, geo[3:4], 1.0)
        inverse = (SHELLS / extent) * (SHELLS / extent)
        reach = jnp.where(valid, extent, -1.0)
        rate_t = inverse / (shell * shell)
        packed = jnp.concatenate(
            [0.5 * geo[2:3] + lift, reach, rate_t, inverse, jnp.zeros((4, LANES), jnp.float32)], axis=0
        )
        sub = packed.T
        d_x = nearest(steps_x - (0.5 * geo[0:1] + float(BX * step_row)), periods[0])
        d_y = nearest(steps_y - (0.5 * geo[1:2] + float(BY * side) * ahead), periods[1])
        inside_x = jnp.abs(d_x) <= reach
        inside_y = jnp.abs(d_y) <= reach
        squared_x = d_x * d_x
        squared_y = d_y * d_y
        d_z = nearest(grid_z - sub[:, 0:1], periods[2])
        inside_z = jnp.abs(d_z) <= sub[:, 1:2]
        squared_z = d_z * d_z
        for s in range(SHELLS):
            part = 1.0 / ((s + 1) * (s + 1))
            rate = inverse * part + rate_t
            along_x = jnp.where(inside_x, jnp.exp(-rate * squared_x), 0.0)
            along_y = jnp.where(inside_y, jnp.exp(-rate * squared_y), 0.0)
            for x in range(BX):
                plane_ref[o, s, x * BY : (x + 1) * BY] = (along_x[x : x + 1] * along_y).astype(plane_ref.dtype)
            rate_z = sub[:, 3:4] * part + sub[:, 2:3]
            line_ref[o, s] = jnp.where(inside_z, jnp.exp(-rate_z * squared_z), 0.0).astype(line_ref.dtype)


def density_kernel(column_steps, *refs):
    coef_refs = refs[:column_steps]
    plane_ref, line_ref, out_ref, terms = refs[column_steps:]
    for o in range(plane_ref.shape[0]):
        coef = coef_refs[-o % column_steps]
        first = 8 * (o // column_steps)
        for s in range(SHELLS):
            scaled = plane_ref[o, s].astype(jnp.float32) * coef[first + s : first + s + 1, :]
            at = (o * SHELLS + s) * LANES
            terms[:, at : at + LANES] = scaled.astype(terms.dtype)
    out_ref[...] = jnp.dot(terms[...], line_ref[...], preferred_element_type=jnp.float32)


def local(sign_start, neighbors, atom_size, basis_proj, pair_extent, atom_x, atom_y, atom_z):
    n_row = lax.axis_size("row")
    n_col = lax.axis_size("col")
    n_lay = lax.axis_size("layer")
    assert n_lay == 4 and n_col >= 4 and (n_row == 2 or n_row >= 4)
    assert n_row & (n_row - 1) == 0 and n_col & (n_col - 1) == 0
    axes = (n_row, n_col, n_lay)
    atoms, slots = neighbors.shape
    size = sign_start.shape[2]
    steps = [0, 1] if n_row == 2 else [0, 1, -1]
    count = len(steps)
    others = range(1, count)
    own = sign_start[0]
    flat = own.reshape(slots * size, size)
    listings = neighbors.T
    full = slots * size
    half = full // 2
    most = half - size
    n_pick = column_targets(n_row)
    picks = n_pick * size
    part = picks + GEO

    def on_row(value, di):
        return from_offset(value, "row", steps[di])

    x_row = {di: on_row(flat, di) for di in others}
    y_row = from_layer(flat, 2)
    m_row = from_layer(flat, 1)
    picked = pl.pallas_call(
        functools.partial(pick_kernel, axes),
        out_shape=jax.ShapeDtypeStruct((part, size), own.dtype),
        in_specs=[HBM] * 6,
        out_specs=VMEM,
        scratch_shapes=[
            pltpu.SMEM((slots, atoms), jnp.int32),
            pltpu.SMEM((1, slots), jnp.int32),
            pltpu.SMEM((atoms,), jnp.int32),
            pltpu.SMEM((atoms,), jnp.int32),
            pltpu.SMEM((atoms,), jnp.int32),
            pltpu.SMEM((n_pick + 1,), jnp.int32),
            pltpu.SemaphoreType.DMA((5,)),
            pltpu.SemaphoreType.DMA((n_pick,)),
        ],
        compiler_params=pltpu.CompilerParams(vmem_limit_bytes=60 << 20),
        name="pick_column_blocks",
    )(listings, pair_extent, atom_x, atom_y, atom_z, own)
    down = from_column(picked, 1)
    up = from_column(picked, 0)

    halves = pack(
        [y_row] + [x_row[di] for di in others] + [picked],
        [[(0, half, most)]] + [[(di, 0, most)] for di in others] + [[(count, picks, GEO)]],
        [],
        "pack_halves",
    )
    ends = {di: on_row(halves[0], di) for di in others}
    tops = {di: from_layer(halves[di], 2) for di in others}

    at = {}
    buffers = {}

    def note(name, value, contents):
        buffers[name] = value
        start = 0
        for what, rows in contents:
            if what is not None:
                at[what] = (name, start)
            start += rows

    def row_of(di, flip, start=0, stop=slots):
        return [(("row", slot, di, flip), size) for slot in range(start, stop)]

    halfway = slots // 2

    def side_of(kind, di, flip):
        return [((kind, di, flip), picks)]

    note("own", flat, row_of(0, 0))
    note("mate", m_row, row_of(0, 1))
    note("far", y_row, row_of(0, 2))
    note("up", up, side_of("up", 0, 0) + [(("up geo", 0, 0), GEO)])
    note("down", down, side_of("down", 0, 0) + [(("down geo", 0, 0), GEO)])
    note("geo", halves[count], [(("geo", 0, 0), GEO)])
    for di in others:
        note(("x", di), x_row[di], row_of(di, 0))
        note(("end", di), ends[di], row_of(di, 2, halfway, slots - 1))
        note(("top", di), tops[di], row_of(di, 2, 0, halfway - 1))

    corners = [("end", di) for di in others] + [("top", di) for di in others]
    names = ["down", "up", "geo", "far"] + [("x", di) for di in others]
    plans = [
        [(1, 0, picks), (0, 0, picks), (3, full - size, size), (2, 0, GEO), (1, picks, GEO), (0, picks, GEO)],
        [(1, 0, picks), (0, 0, picks)] + [(di + 3, most, size) for di in others] + [(2, 0, GEO), (1, picks, GEO), (0, picks, GEO)],
        [(2, 0, GEO), (1, picks, GEO), (0, picks, GEO)],
    ]
    two_x, two_y, geos = pack([buffers[name] for name in names], plans, [m_row], "pack_two")
    to_mate = corners + ["up", "down"]
    for di in others:
        note(("mate x", di), from_layer(x_row[di], 1), row_of(di, 1))
    note("mate far", from_layer(y_row, 1), row_of(0, 3))

    early_order = ["own", "mate", "far", "up", "down", "geo"] + [("x", di) for di in others]
    early_order += [("mate x", di) for di in others] + ["mate far"]
    early_order += corners + [("two x", di) for di in others] + ["two y", "two m"]
    late_order = [("three x", di) for di in others] + ["three y", "three m"]
    late_order += ["four"]

    contents = {}
    for di in others:
        contents["two x", di] = side_of("up", di, 0) + side_of("down", di, 0)
        contents["two x", di] += row_of(di, 2, slots - 1, slots) + [(("geo", di, 0), GEO)]
        contents["two x", di] += [(("up geo", di, 0), GEO), (("down geo", di, 0), GEO)]
    contents["two y"] = side_of("up", 0, 2) + side_of("down", 0, 2)
    contents["two y"] += sum([row_of(di, 2, halfway - 1, halfway) for di in others], []) + [(None, 3 * GEO)]
    contents["two m"] = sum([row_of(di, 3, halfway, slots - 1) for di in others], [])
    contents["two m"] += sum([row_of(di, 3, 0, halfway - 1) for di in others], [])
    contents["two m"] += side_of("up", 0, 1) + side_of("down", 0, 1)
    for di in others:
        contents["three x", di] = side_of("up", di, 2)
    contents["three y"] = sum([side_of("down", di, 2) for di in others], [])
    contents["three m"] = []
    for di in others:
        contents["three m"] += side_of("up", di, 1) + side_of("down", di, 1) + row_of(di, 3, slots - 1, slots)
    contents["three m"] += side_of("up", 0, 3) + side_of("down", 0, 3)
    contents["three m"] += sum([row_of(di, 3, halfway - 1, halfway) for di in others], []) + [(None, 3 * GEO)]
    contents["three m"] += [("geos", count * 3 * GEO)]
    contents["four"] = sum([side_of("up", di, 3) for di in others], [])
    contents["four"] += sum([side_of("down", di, 3) for di in others], [])
    lengths = {name: sum(rows for _, rows in content) for name, content in contents.items()}
    for name in early_order:
        if name in buffers:
            lengths[name] = buffers[name].shape[0]
    base = {}
    total = 0
    for name in early_order + late_order:
        base[name] = total
        total += lengths[name]
        if name == early_order[-1]:
            late_from = total
    located = dict(at)
    for name, content in contents.items():
        start = 0
        for what, rows in content:
            located[what] = (name, start)
            start += rows
    layout = [
        base[located["row", slot, di, flip][0]] + located["row", slot, di, flip][1]
        for di in range(count)
        for flip in range(n_lay)
        for slot in range(slots)
    ]
    layout += [
        base[located[kind, di, flip][0]] + located[kind, di, flip][1]
        for kind in ("up", "down")
        for di in range(count)
        for flip in range(n_lay)
    ]
    pairs = slots * (slots + 1) // 2
    entries = pairs + UNROLL + 1
    early_table, late_table, info = pl.pallas_call(
        functools.partial(prepare_kernel, axes, count, tuple(layout), late_from),
        out_shape=(
            jax.ShapeDtypeStruct((entries,), jnp.int32),
            jax.ShapeDtypeStruct((entries,), jnp.int32),
            jax.ShapeDtypeStruct((slots + 2,), jnp.int32),
        ),
        in_specs=[HBM, HBM, ANY],
        out_specs=(SMEM, SMEM, SMEM),
        scratch_shapes=[
            pltpu.SMEM((slots, atoms), jnp.int32),
            pltpu.SMEM((atoms,), jnp.int32),
            pltpu.SMEM((3, slots), jnp.int32),
            pltpu.SMEM((atoms,), jnp.int32),
            pltpu.SMEM((len(layout),), jnp.int32),
            pltpu.SemaphoreType.DMA((2,)),
        ],
        compiler_params=pltpu.CompilerParams(vmem_limit_bytes=1 << 20),
        cost_estimate=pl.CostEstimate(flops=1000, bytes_accessed=1000, transcendentals=0),
        name="prepare",
    )(listings, atom_size, two_x)

    plans = [[(i, 0, picks if name in ("up", "down") else most) for i, name in enumerate(to_mate)]]
    two_m = pack([buffers[name] for name in to_mate], plans, [], "pack_two_mate", 3_000_000_000)[0]
    for di in others:
        note(("two x", di), on_row(two_x, di), contents["two x", di])
    note("two y", from_layer(two_y, 2), contents["two y"])
    early_mates = ["mate far"] + [("mate x", di) for di in others]
    note("two m", from_layer(two_m, 1), contents["two m"])

    buffers["geos"] = geos
    names = ["two y", "geos"] + [("two x", di) for di in others]
    place = {name: i for i, name in enumerate(names)}
    gather = [(place["geos"], 0, 3 * GEO)] + [(place["two x", di], 2 * picks + size, 3 * GEO) for di in others]
    xs = [place["two x", di] for di in others]
    plans = [
        [(0, 0, picks)],
        [(x, picks, picks) for x in xs],
        [(x, 0, 2 * picks + size) for x in xs] + [(0, 0, lengths["two y"])] + gather,
        gather,
    ]
    three_x, three_y, three_m, geos = pack([buffers[name] for name in names], plans, [buffers[name] for name in early_mates] + [two_m, info], "pack_three")
    for di in others:
        note(("three x", di), on_row(three_x, di), contents["three x", di])
    note("three y", from_layer(three_y, 2), contents["three y"])
    note("three m", from_layer(three_m, 1), contents["three m"])
    third_geos = from_layer(geos, 3)

    spread, own_basis, own_kept, seen = pl.pallas_call(
        functools.partial(spread_kernel, axes),
        out_shape=(
            jax.ShapeDtypeStruct((LANES, full), jnp.bfloat16),
            jax.ShapeDtypeStruct((16, size), jnp.bfloat16),
            jax.ShapeDtypeStruct((size, full), jnp.bfloat16),
            jax.ShapeDtypeStruct((16, full), jnp.float32),
        ),
        in_specs=[HBM, VMEM, SMEM, VMEM, ANY],
        out_specs=(VMEM, VMEM, VMEM, VMEM),
        scratch_shapes=[pltpu.SMEM((slots, atoms), jnp.int32), pltpu.SemaphoreType.DMA((1,))],
        compiler_params=pltpu.CompilerParams(vmem_limit_bytes=(2 << 20) + atoms * 16384),
        cost_estimate=pl.CostEstimate(flops=1000, bytes_accessed=1000, transcendentals=0),
        name="spread_basis",
    )(listings, basis_proj.transpose(1, 0, 2).reshape(SHELLS * atoms, size), info, own, three_x)

    early_values = [buffers[name] for name in early_order]
    gram = pl.pallas_call(
        functools.partial(gram_kernel, len(early_values)),
        out_shape=jax.ShapeDtypeStruct((full, full), jnp.bfloat16),
        in_specs=[SMEM] + [VMEM] * len(early_values) + [ANY],
        out_specs=VMEM,
        scratch_shapes=[pltpu.VMEM((late_from, LANES), jnp.bfloat16)],
        compiler_params=pltpu.CompilerParams(vmem_limit_bytes=(6 << 20) + 2 * late_from * LANES * 2),
        cost_estimate=pl.CostEstimate(flops=1000, bytes_accessed=1000, transcendentals=0),
        name="gram_early",
    )(early_table, *early_values, three_x)

    thirds = [buffers["three x", di] for di in others] + [buffers["three y"]]
    four = pack(thirds, [[(i, 0, value.shape[0]) for i, value in enumerate(thirds)]], [gram, third_geos, own_basis], "pack_four")[0]
    note("four", from_layer(four, 1), contents["four"])

    column_steps = (0, 1, -1)
    tile_steps = [(dr, dc) for dr in steps for dc in column_steps]
    tiles = len(tile_steps)
    periods = (float(BX * n_row), float(BY * n_col), float(BZ * n_lay))
    plane, line = pl.pallas_call(
        functools.partial(profile_kernel, periods, tile_steps, at["geos"][1]),
        out_shape=(
            jax.ShapeDtypeStruct((tiles, SHELLS, BX * BY, LANES), jnp.bfloat16),
            jax.ShapeDtypeStruct((tiles, SHELLS, LANES, BZ), jnp.bfloat16),
        ),
        in_specs=[ANY] * 3,
        out_specs=(VMEM, VMEM),
        scratch_shapes=[
            pltpu.VMEM((3, tiles * GEO, LANES), jnp.bfloat16),
            pltpu.SemaphoreType.DMA((3,)),
        ],
        compiler_params=pltpu.CompilerParams(vmem_limit_bytes=10 << 20),
        cost_estimate=pl.CostEstimate(flops=1000, bytes_accessed=1000, transcendentals=0),
        name="profiles",
    )(geos, buffers["three m"], third_geos)

    late_values = [buffers[name] for name in late_order]
    sign_next, coef = pl.pallas_call(
        functools.partial(step_kernel, len(late_values)),
        out_shape=(
            jax.ShapeDtypeStruct((slots, size, size), jnp.bfloat16),
            jax.ShapeDtypeStruct((8, LANES), jnp.float32),
        ),
        in_specs=[SMEM, SMEM] + [VMEM] * (5 + len(late_values)),
        out_specs=(VMEM, VMEM),
        scratch_shapes=[
            pltpu.VMEM((total - late_from, LANES), jnp.bfloat16),
            pltpu.VMEM((full, full), jnp.bfloat16),
            pltpu.VMEM((size + 32, full), jnp.bfloat16),
        ],
        compiler_params=pltpu.CompilerParams(vmem_limit_bytes=(15 << 20) + 2 * (total - late_from) * LANES * 2),
        cost_estimate=pl.CostEstimate(flops=1_300_000_000, bytes_accessed=8_000_000, transcendentals=0),
        name="square_cube_coefficients",
    )(late_table, info, own_basis, spread, own_kept, seen, gram, *late_values)

    mate_coef = from_layer(coef, 1)
    third_coef = from_layer(coef, 3)
    odd = lax.axis_index("layer") % 2 == 1
    below = jnp.where(odd, mate_coef, third_coef)
    above = jnp.where(odd, third_coef, mate_coef)
    merged = jnp.concatenate(
        [
            coef[:, : 4 * SPAN],
            below[:, SPAN : 3 * SPAN],
            above[:, 3 * SPAN : 4 * SPAN],
            jnp.zeros((8, LANES - 7 * SPAN), jnp.float32),
        ],
        axis=1,
    )
    stacked = jnp.concatenate([merged] + [on_row(merged, di) for di in others], axis=0)
    far_side = from_column(stacked, 1)
    received = [stacked, far_side, from_column(stacked, 0)]

    density = pl.pallas_call(
        functools.partial(density_kernel, len(column_steps)),
        out_shape=jax.ShapeDtypeStruct((BX * BY, BZ), jnp.float32),
        in_specs=[VMEM] * (len(received) + 2),
        out_specs=VMEM,
        scratch_shapes=[pltpu.VMEM((BX * BY, tiles * SHELLS * LANES), jnp.bfloat16)],
        compiler_params=pltpu.CompilerParams(vmem_limit_bytes=16 << 20),
        cost_estimate=pl.CostEstimate(flops=310_000_000, bytes_accessed=4_000_000, transcendentals=0),
        name="density",
    )(*received, plane, line.reshape(tiles * SHELLS * LANES, BZ))
    return sign_next[None], density.reshape(BX, BY, BZ)


def solution(mesh):
    rows = P(("row", "col", "layer"), None, None, None)
    in_specs = (rows, P(), P(), P(), P(("row", "col", "layer"), None), P(), P(), P())
    out_specs = (rows, P("row", "col", "layer"))
    return jax.shard_map(local, mesh=mesh, in_specs=in_specs, out_specs=out_specs, check_vma=False)
```

```python
import functools

import jax
import jax.numpy as jnp
from jax import lax
from jax.experimental import pallas as pl
from jax.experimental.pallas import tpu as pltpu
from jax.sharding import PartitionSpec as P

BX = 16
BY = 16
BZ = 128
LANES = 128
UNROLL = 4
SHELLS = 6
SPAN = 3 * SHELLS
GEO = 16
VMEM = pl.BlockSpec(memory_space=pltpu.VMEM)
SMEM = pl.BlockSpec(memory_space=pltpu.SMEM)
ANY = pl.BlockSpec(memory_space=pl.ANY)
HBM = pl.BlockSpec(memory_space=pltpu.HBM)


def from_offset(x, axis, step):
    count = lax.axis_size(axis)
    return lax.ppermute(x, axis, [((i + step) % count, i) for i in range(count)])


def from_column(x, side):
    count = lax.axis_size("col")
    step = [1 if (i + side) % 2 == 0 else -1 for i in range(count)]
    return lax.ppermute(x, "col", [((i + step[i]) % count, i) for i in range(count)])


def from_layer(x, flip):
    count = lax.axis_size("layer")
    return lax.ppermute(x, "layer", [(i ^ flip, i) for i in range(count)])


def column_targets(n_row):
    return 5 if n_row == 2 else 7


def target_place(n_row, step_row, step_lay, row):
    same = jnp.where(step_lay < 3, step_lay, -1)
    if n_row == 2:
        lead = step_lay - row
        across = jnp.where((lead >= 0) & (lead < 2), 3 + lead, -1)
    else:
        across = 3 + step_lay
    return jnp.where(step_row == 0, same, jnp.where(step_row == 1, across, -1))


class Places:
    def __init__(self, n_row, n_col, n_lay):
        self.n_row, self.n_col, self.n_lay = n_row, n_col, n_lay
        self.lay_bits = n_lay.bit_length() - 1
        self.col_bits = n_col.bit_length() - 1
        self.row = lax.axis_index("row")
        self.col = lax.axis_index("col")
        self.lay = lax.axis_index("layer")
        self.me = (((self.row << self.col_bits) + self.col) << self.lay_bits) + self.lay

    def split(self, atom):
        return (
            atom >> (self.lay_bits + self.col_bits),
            (atom >> self.lay_bits) & (self.n_col - 1),
            atom & (self.n_lay - 1),
        )


def load(sources, targets, sems):
    copies = [pltpu.make_async_copy(a, b, sems.at[i]) for i, (a, b) in enumerate(zip(sources, targets))]
    for copy in copies:
        copy.start()
    for copy in copies:
        copy.wait()


def own_ranks(at, neighbors_ref):
    seen = [jnp.int32(0)] * at.n_lay
    listed = []
    for w in range(neighbors_ref.shape[0]):
        atom = neighbors_ref[w, at.me]
        step_lay = (atom - at.lay) & (at.n_lay - 1)
        rank = jnp.int32(0)
        for k in range(at.n_lay):
            rank = jnp.where(step_lay == k, 3 * k + seen[k], rank)
            seen[k] = seen[k] + (step_lay == k).astype(jnp.int32)
        listed.append((atom, rank))
    return listed


def pick_kernel(axes, *refs):
    sign_ref, out_ref, geo_ref, neighbors_ref, extent_ref, x_ref, y_ref, z_ref, place_ref, tile, loads, sems = refs[5:]
    at = Places(*axes)
    slots = sign_ref.shape[0]
    n_pick = place_ref.shape[0] - 1
    size = sign_ref.shape[1]
    for i in range(n_pick + 1):
        place_ref[i] = 0
    load(refs[:5], (neighbors_ref, extent_ref, x_ref, y_ref, z_ref), loads)
    ranks = own_ranks(at, neighbors_ref)
    for w, (atom, _) in enumerate(ranks):
        row, col, lay = at.split(atom)
        place = target_place(at.n_row, (row - at.row) & (at.n_row - 1), (lay - at.lay) & (at.n_lay - 1), at.row)
        place_ref[jnp.where((col == at.col) & (place >= 0), place, n_pick)] = w
    copies = []
    for i in range(n_pick):
        copy = pltpu.make_async_copy(sign_ref.at[place_ref[i]], out_ref.at[pl.ds(i * size, size)], sems.at[i])
        copy.start()
        copies.append(copy)
    sub = lax.broadcasted_iota(jnp.int32, (GEO, LANES), 0)
    lane_pair = lax.broadcasted_iota(jnp.int32, (GEO, LANES), 1) // SHELLS
    geo = jnp.zeros((GEO, LANES), jnp.int32)
    for w, (atom, rank) in enumerate(ranks):
        row, col, lay = at.split(atom)
        go_row = ((row - at.row + 1) & (at.n_row - 1)) - 1
        go_col = ((col - at.col + 1) & (at.n_col - 1)) - 1
        go_lay = jnp.minimum(((lay - at.lay + 1) & (at.n_lay - 1)) - 1, 1)
        twice_x = x_ref[at.me] + x_ref[atom] + BX * go_row
        twice_y = y_ref[at.me] + y_ref[atom] + BY * go_col
        twice_z = z_ref[at.me] + z_ref[atom] + BZ * go_lay - BZ
        extent = extent_ref[0, w]
        values = jnp.where(sub == 0, twice_x, jnp.where(sub == 1, twice_y, jnp.where(sub == 2, twice_z, extent)))
        geo = jnp.where(lane_pair == rank, values, geo)
    geo = geo.astype(jnp.float32).astype(out_ref.dtype)
    geo_ref[...] = geo
    tile[...] = geo
    copy = pltpu.make_async_copy(tile, out_ref.at[pl.ds(n_pick * size, GEO)], sems.at[n_pick])
    copy.start()
    copies.append(copy)
    for copy in copies:
        copy.wait()


def spread_kernel(axes, *refs):
    basis_ref, info_ref, sign_ref = refs[1:4]
    spread_ref, own_basis_ref, own_ref, neighbors_ref, loads = refs[-5:]
    at = Places(*axes)
    load(refs[:1], (neighbors_ref,), loads)
    slots, atoms = neighbors_ref.shape
    bits = atoms.bit_length() - 1

    def hot(rows, atom, first):
        sub = lax.broadcasted_iota(jnp.int32, (rows, SHELLS * atoms), 0)
        lane = lax.broadcasted_iota(jnp.int32, (rows, SHELLS * atoms), 1)
        return ((lane & (atoms - 1)) == atom) & (sub == first + (lane >> bits))

    def rows_of(chosen):
        picked = jnp.where(chosen, 1.0, 0.0).astype(jnp.bfloat16)
        return jnp.dot(picked, basis_ref[...], preferred_element_type=jnp.float32).astype(jnp.bfloat16)

    for w, (atom, rank) in enumerate(own_ranks(at, neighbors_ref)):
        spread_ref[:, w * LANES : (w + 1) * LANES] = rows_of(hot(LANES, atom, rank * SHELLS))
    own_basis_ref[...] = rows_of(hot(16, at.me, 0))
    size = sign_ref.shape[1]
    rows = lax.broadcasted_iota(jnp.int32, (size, size), 0)
    lanes = lax.broadcasted_iota(jnp.int32, (size, size), 1)
    for w in range(slots):
        kept = (rows < info_ref[slots]) & (lanes < info_ref[w])
        block = jnp.where(kept, sign_ref[w].astype(jnp.float32), 0.0)
        own_ref[:, w * size : (w + 1) * size] = block.astype(own_ref.dtype)


def prepare_kernel(axes, count, layout, late_from, *refs):
    early_ref, late_ref, info_ref, neighbors_ref, size_ref, known, inverse, layout_ref, loads = refs[-9:]
    at = Places(*axes)
    load(refs[:2], (neighbors_ref, size_ref), loads)
    slots = neighbors_ref.shape[0]
    lines = count * at.n_lay
    for i, value in enumerate(layout):
        layout_ref[i] = value
    self_slot = jnp.int32(0)
    for w in range(slots):
        atom = neighbors_ref[w, at.me]
        row, col, lay = at.split(atom)
        step_row = (row - at.row) & (at.n_row - 1)
        self_slot = jnp.where(atom == at.me, w, self_slot)
        info_ref[w] = size_ref[atom]
        known[0, w] = atom
        known[1, w] = jnp.where(col == at.col, 0, jnp.where(col == (at.col ^ 1), 1, 2))
        known[2, w] = jnp.where(step_row == 0, 0, jnp.where(step_row == 1, 1, 2)) * at.n_lay + (lay ^ at.lay)
        inverse[atom] = -1
    info_ref[slots] = size_ref[at.me]
    info_ref[slots + 1] = self_slot

    def row_of_pairs(v, totals):
        early, late = totals
        atom = known[0, v]
        side = known[1, v]
        line = known[2, v]
        for u in range(slots):
            inverse[neighbors_ref[u, atom]] = v * 16 + u

        def from_row(totals):
            total, late = totals
            for w in range(slots):
                mark = inverse[known[0, w]]
                chosen = ((mark >> 4) == v) & ((known[1, w] != 0) | (v <= w))
                where = layout_ref[line * slots + (mark & 15)]
                is_late = where >= late_from
                entry = v + 16 * w
                early_ref[total + 1] = entry + 256 * where
                late_ref[late + 1] = entry + 256 * (where - late_from)
                total = total + (chosen & ~is_late).astype(jnp.int32)
                late = late + (chosen & is_late).astype(jnp.int32)
            return total, late

        def from_column(totals):
            early, late = totals
            row, _, lay = at.split(atom)
            beside = layout_ref[lines * slots + (side - 1) * lines + line]
            for w in range(slots):
                other = known[0, w]
                mark = inverse[other]
                o_row, _, o_lay = at.split(other)
                d_row = (o_row - row) & (at.n_row - 1)
                d_lay = (o_lay - lay) & (at.n_lay - 1)
                there = target_place(at.n_row, d_row, d_lay, row)
                back = target_place(at.n_row, -d_row & (at.n_row - 1), -d_lay & (at.n_lay - 1), o_row)
                chosen = ((mark >> 4) == v) & (side == known[1, w]) & (there >= 0) & ((back < 0) | (v <= w))
                where = beside + there * LANES
                is_late = where >= late_from
                entry = v + 16 * w
                early_ref[early + 1] = entry + 256 * where
                late_ref[late + 1] = entry + 256 * (where - late_from)
                early = early + (chosen & ~is_late).astype(jnp.int32)
                late = late + (chosen & is_late).astype(jnp.int32)
            return early, late

        return lax.cond(side == 0, from_row, from_column, (early, late))

    totals = lax.fori_loop(0, slots, row_of_pairs, (jnp.int32(0), jnp.int32(0)))
    for ref, total in zip((early_ref, late_ref), totals):
        ref[0] = (total + UNROLL - 1) // UNROLL
        for i in range(UNROLL - 1):
            ref[total + i + 1] = ref[jnp.maximum(total, 1)]


def pack_kernel(moves, inputs, *refs):
    for source, start, rows, target, place in moves:
        refs[inputs + target][place : place + rows] = refs[source][start : start + rows]


def pack(values, plans, extra, name, cost=0):
    moves, shapes = [], []
    for target, plan in enumerate(plans):
        place = 0
        for source, start, rows in plan:
            moves.append((source, start, rows, target, place))
            place += rows
        shapes.append(jax.ShapeDtypeStruct((place, LANES), values[0].dtype))
    inputs = len(values) + len(extra)
    return pl.pallas_call(
        functools.partial(pack_kernel, tuple(moves), inputs),
        out_shape=tuple(shapes),
        in_specs=[VMEM] * len(values) + [ANY] * len(extra),
        out_specs=tuple([VMEM] * len(plans)),
        compiler_params=pltpu.CompilerParams(
            vmem_limit_bytes=(1 << 20) + 256 * sum(x.shape[0] for x in list(values) + shapes)
        ),
        cost_estimate=pl.CostEstimate(flops=cost, bytes_accessed=1000, transcendentals=0),
        name=name,
    )(*values, *extra)


def fill(piece_refs, pool):
    place = 0
    for piece in piece_refs:
        rows = piece.shape[0]
        pool[place : place + rows] = piece[...]
        place += rows


def place_pairs(table_ref, pool, gram, size):
    def place(i, carry):
        for k in range(UNROLL):
            entry = table_ref[i * UNROLL + k + 1]
            p = pl.multiple_of((entry & 15) * size, size)
            q = pl.multiple_of(((entry >> 4) & 15) * size, size)
            block = pool[pl.ds(pl.multiple_of(entry >> 8, 16), size)]
            gram[pl.ds(p, size), pl.ds(q, size)] = block
            gram[pl.ds(q, size), pl.ds(p, size)] = block.T
        return carry

    lax.fori_loop(0, table_ref[0], place, 0)


def gram_kernel(pieces, *refs):
    table_ref = refs[0]
    piece_refs = refs[1 : 1 + pieces]
    gram, pool = refs[-2:]
    size = LANES
    fill(piece_refs, pool)
    for v in range(gram.shape[0] // size):
        gram[v * size : (v + 1) * size] = jnp.zeros((size, gram.shape[1]), gram.dtype)
    place_pairs(table_ref, pool, gram, size)


def step_kernel(pieces, *refs):
    table_ref, info_ref, basis_ref, spread_ref, own, early_ref = refs[:6]
    piece_refs = refs[6 : 6 + pieces]
    next_ref, coef_ref, pool, gram, square = refs[-5:]
    slots, size = next_ref.shape[0], next_ref.shape[1]
    fill(piece_refs, pool)
    for v in range(slots):
        gram[v * size : (v + 1) * size] = early_ref[v * size : (v + 1) * size]
    own_size = info_ref[slots]
    self_slot = info_ref[slots + 1]
    place_pairs(table_ref, pool, gram, size)
    wide = 2 * size
    wide_lanes = lax.broadcasted_iota(jnp.int32, (size, wide), 1)
    wide_rows = lax.broadcasted_iota(jnp.int32, (size, wide), 0)

    def column_kept(n):
        first = info_ref[2 * n]
        second = info_ref[2 * n + 1]
        return (wide_lanes < first) | ((wide_lanes >= size) & (wide_lanes < size + second))

    for n in range(slots // 2):
        part = jnp.dot(own[...], gram[:, n * wide : (n + 1) * wide], preferred_element_type=jnp.float32)
        square[:, n * wide : (n + 1) * wide] = jnp.where(column_kept(n), part, 0.0).astype(square.dtype)
    basis = jnp.concatenate([basis_ref[...], basis_ref[...]], axis=1)
    coef = jnp.zeros((2 * basis_ref.shape[0], LANES), jnp.float32)
    across = (((1,), (1,)), ((), ()))
    for n in range(slots // 2):
        part = jnp.dot(square[...], gram[:, n * wide : (n + 1) * wide], preferred_element_type=jnp.float32)
        cube = jnp.where(column_kept(n), part, 0.0)
        full = 1.5 * own[:, n * wide : (n + 1) * wide].astype(jnp.float32) - 0.5 * cube
        next_ref[2 * n] = full[:, :size].astype(next_ref.dtype)
        next_ref[2 * n + 1] = full[:, size:].astype(next_ref.dtype)
        shift = (self_slot - 2 * n) * size
        is_self = (self_slot >= 2 * n) & (self_slot < 2 * n + 2)
        diag = (wide_lanes == wide_rows + shift) & (wide_rows < own_size) & is_self
        dmat = 0.5 * (jnp.where(diag, 1.0, 0.0) - full)
        high = dmat.astype(jnp.bfloat16)
        low = (dmat - high.astype(jnp.float32)).astype(jnp.bfloat16)
        half = jnp.dot(basis, jnp.concatenate([high, low], axis=0), preferred_element_type=jnp.float32)
        half_high = half.astype(jnp.bfloat16)
        half_low = (half - half_high.astype(jnp.float32)).astype(jnp.bfloat16)
        coef = coef + lax.dot_general(
            jnp.concatenate([half_high, half_low], axis=0),
            spread_ref[:, n * wide : (n + 1) * wide],
            across,
            preferred_element_type=jnp.float32,
        )
    coef = coef[: basis_ref.shape[0]] + coef[basis_ref.shape[0] :]
    coef_ref[...] = coef[: coef_ref.shape[0]]


def profile_kernel(periods, steps, mate_from, *refs):
    own_ref, mate_ref, third_ref = refs[:3]
    plane_ref, line_ref, geos, sems = refs[-4:]
    odd = (lax.axis_index("layer") & 1) == 1
    rows = len(steps) * GEO
    copies = []
    for k, source in enumerate((own_ref, mate_ref.at[pl.ds(mate_from, rows)], third_ref)):
        copy = pltpu.make_async_copy(source, geos.at[k], sems.at[k])
        copy.start()
        copies.append(copy)
    steps_x = lax.broadcasted_iota(jnp.int32, (BX, LANES), 0).astype(jnp.float32)
    steps_y = lax.broadcasted_iota(jnp.int32, (BY, LANES), 0).astype(jnp.float32)
    grid_z = lax.broadcasted_iota(jnp.int32, (LANES, BZ), 1).astype(jnp.float32)
    lane = lax.broadcasted_iota(jnp.int32, (1, LANES), 1)
    shell = (lane % SHELLS + 1).astype(jnp.float32)
    valid = lane < 7 * SPAN
    from_own = lane < 4 * SPAN
    from_below = lane < 6 * SPAN
    lift = jnp.where(from_own, 0.0, jnp.where(from_below, -float(BZ), float(BZ))) + 0.5 * BZ

    def nearest(offset, period):
        return offset - period * jnp.floor(offset * (1.0 / period) + 0.5)

    for copy in copies:
        copy.wait()
    ahead = 1.0 - 2.0 * (lax.axis_index("col") & 1).astype(jnp.float32)
    for o, (step_row, side) in enumerate(steps):
        own, first, third = (geos[k, o * GEO : (o + 1) * GEO].astype(jnp.float32) for k in range(3))
        below = jnp.where(odd, first, third)
        above = jnp.where(odd, third, first)
        moved = jnp.where(from_below, pltpu.roll(below, 3 * SPAN, axis=1), pltpu.roll(above, 3 * SPAN, axis=1))
        geo = jnp.where(from_own, own, moved)
        extent = jnp.where(valid, geo[3:4], 1.0)
        inverse = (SHELLS / extent) * (SHELLS / extent)
        reach = jnp.where(valid, extent, -1.0)
        rate_t = inverse / (shell * shell)
        packed = jnp.concatenate(
            [0.5 * geo[2:3] + lift, reach, rate_t, inverse, jnp.zeros((4, LANES), jnp.float32)], axis=0
        )
        sub = packed.T
        d_x = nearest(steps_x - (0.5 * geo[0:1] + float(BX * step_row)), periods[0])
        d_y = nearest(steps_y - (0.5 * geo[1:2] + float(BY * side) * ahead), periods[1])
        inside_x = jnp.abs(d_x) <= reach
        inside_y = jnp.abs(d_y) <= reach
        squared_x = d_x * d_x
        squared_y = d_y * d_y
        d_z = nearest(grid_z - sub[:, 0:1], periods[2])
        inside_z = jnp.abs(d_z) <= sub[:, 1:2]
        squared_z = d_z * d_z
        for s in range(SHELLS):
            part = 1.0 / ((s + 1) * (s + 1))
            rate = inverse * part + rate_t
            along_x = jnp.where(inside_x, jnp.exp(-rate * squared_x), 0.0)
            along_y = jnp.where(inside_y, jnp.exp(-rate * squared_y), 0.0)
            for x in range(BX):
                plane_ref[o, s, x * BY : (x + 1) * BY] = (along_x[x : x + 1] * along_y).astype(plane_ref.dtype)
            rate_z = sub[:, 3:4] * part + sub[:, 2:3]
            line_ref[o, s] = jnp.where(inside_z, jnp.exp(-rate_z * squared_z), 0.0).astype(line_ref.dtype)


def density_kernel(column_steps, *refs):
    coef_refs = refs[:column_steps]
    plane_ref, line_ref, out_ref, terms = refs[column_steps:]
    for o in range(plane_ref.shape[0]):
        coef = coef_refs[-o % column_steps]
        first = 8 * (o // column_steps)
        for s in range(SHELLS):
            scaled = plane_ref[o, s].astype(jnp.float32) * coef[first + s : first + s + 1, :]
            at = (o * SHELLS + s) * LANES
            terms[:, at : at + LANES] = scaled.astype(terms.dtype)
    out_ref[...] = jnp.dot(terms[...], line_ref[...], preferred_element_type=jnp.float32)


def local(sign_start, neighbors, atom_size, basis_proj, pair_extent, atom_x, atom_y, atom_z):
    n_row = lax.axis_size("row")
    n_col = lax.axis_size("col")
    n_lay = lax.axis_size("layer")
    assert n_lay == 4 and n_col >= 4 and (n_row == 2 or n_row >= 4)
    assert n_row & (n_row - 1) == 0 and n_col & (n_col - 1) == 0
    axes = (n_row, n_col, n_lay)
    atoms, slots = neighbors.shape
    size = sign_start.shape[2]
    steps = [0, 1] if n_row == 2 else [0, 1, -1]
    count = len(steps)
    others = range(1, count)
    own = sign_start[0]
    flat = own.reshape(slots * size, size)
    listings = neighbors.T
    full = slots * size
    half = full // 2
    most = half - size
    n_pick = column_targets(n_row)
    picks = n_pick * size
    part = picks + GEO

    def on_row(value, di):
        return from_offset(value, "row", steps[di])

    x_row = {di: on_row(flat, di) for di in others}
    y_row = from_layer(flat, 2)
    m_row = from_layer(flat, 1)
    picked, geo = pl.pallas_call(
        functools.partial(pick_kernel, axes),
        out_shape=(
            jax.ShapeDtypeStruct((part, size), own.dtype),
            jax.ShapeDtypeStruct((GEO, LANES), own.dtype),
        ),
        in_specs=[HBM] * 6,
        out_specs=(HBM, VMEM),
        scratch_shapes=[
            pltpu.SMEM((slots, atoms), jnp.int32),
            pltpu.SMEM((1, slots), jnp.int32),
            pltpu.SMEM((atoms,), jnp.int32),
            pltpu.SMEM((atoms,), jnp.int32),
            pltpu.SMEM((atoms,), jnp.int32),
            pltpu.SMEM((n_pick + 1,), jnp.int32),
            pltpu.VMEM((GEO, LANES), jnp.bfloat16),
            pltpu.SemaphoreType.DMA((5,)),
            pltpu.SemaphoreType.DMA((n_pick + 1,)),
        ],
        compiler_params=pltpu.CompilerParams(vmem_limit_bytes=60 << 20),
        name="pick_column_blocks",
    )(listings, pair_extent, atom_x, atom_y, atom_z, own)
    down = from_column(picked, 1)
    up = from_column(picked, 0)

    halves = pack(
        [y_row] + [x_row[di] for di in others],
        [[(0, half, most)]] + [[(di, 0, most)] for di in others],
        [],
        "pack_halves",
    )
    ends = {di: on_row(halves[0], di) for di in others}
    tops = {di: from_layer(halves[di], 2) for di in others}

    at = {}
    buffers = {}

    def note(name, value, contents):
        buffers[name] = value
        start = 0
        for what, rows in contents:
            if what is not None:
                at[what] = (name, start)
            start += rows

    def row_of(di, flip, start=0, stop=slots):
        return [(("row", slot, di, flip), size) for slot in range(start, stop)]

    halfway = slots // 2

    def side_of(kind, di, flip):
        return [((kind, di, flip), picks)]

    note("own", flat, row_of(0, 0))
    note("mate", m_row, row_of(0, 1))
    note("far", y_row, row_of(0, 2))
    note("up", up, side_of("up", 0, 0) + [(("up geo", 0, 0), GEO)])
    note("down", down, side_of("down", 0, 0) + [(("down geo", 0, 0), GEO)])
    buffers["geo"] = geo
    for di in others:
        note(("x", di), x_row[di], row_of(di, 0))
        note(("end", di), ends[di], row_of(di, 2, halfway, slots - 1))
        note(("top", di), tops[di], row_of(di, 2, 0, halfway - 1))

    corners = [("end", di) for di in others] + [("top", di) for di in others]
    names = ["down", "up", "geo", "far"] + [("x", di) for di in others]
    plans = [
        [(1, 0, picks), (0, 0, picks), (3, full - size, size), (2, 0, GEO), (1, picks, GEO), (0, picks, GEO)],
        [(1, 0, picks), (0, 0, picks)] + [(di + 3, most, size) for di in others] + [(2, 0, GEO), (1, picks, GEO), (0, picks, GEO)],
        [(2, 0, GEO), (1, picks, GEO), (0, picks, GEO)],
    ]
    two_x, two_y, geos = pack([buffers[name] for name in names], plans, [m_row], "pack_two")
    sides = pack([up, down], [[(0, 0, picks), (1, 0, picks)]], [], "pack_mate_sides")[0]
    for di in others:
        note(("mate x", di), from_layer(x_row[di], 1), row_of(di, 1))
    note("mate far", from_layer(y_row, 1), row_of(0, 3))

    early_order = ["own", "mate", "far", "up", "down"] + [("x", di) for di in others]
    early_order += [("mate x", di) for di in others] + ["mate far"]
    early_order += corners + [("two x", di) for di in others] + ["two y", "two m", "mate sides"]
    late_order = [("three x", di) for di in others] + ["three y", "three m"]
    late_order += ["four"]

    contents = {}
    for di in others:
        contents["two x", di] = side_of("up", di, 0) + side_of("down", di, 0)
        contents["two x", di] += row_of(di, 2, slots - 1, slots) + [(("geo", di, 0), GEO)]
        contents["two x", di] += [(("up geo", di, 0), GEO), (("down geo", di, 0), GEO)]
    contents["two y"] = side_of("up", 0, 2) + side_of("down", 0, 2)
    contents["two y"] += sum([row_of(di, 2, halfway - 1, halfway) for di in others], []) + [(None, 3 * GEO)]
    contents["two m"] = sum([row_of(di, 3, halfway, slots - 1) for di in others], [])
    contents["two m"] += sum([row_of(di, 3, 0, halfway - 1) for di in others], [])
    contents["mate sides"] = side_of("up", 0, 1) + side_of("down", 0, 1)
    for di in others:
        contents["three x", di] = side_of("up", di, 2)
    contents["three y"] = sum([side_of("down", di, 2) for di in others], [])
    contents["three m"] = []
    for di in others:
        contents["three m"] += side_of("up", di, 1) + side_of("down", di, 1) + row_of(di, 3, slots - 1, slots)
    contents["three m"] += side_of("up", 0, 3) + side_of("down", 0, 3)
    contents["three m"] += sum([row_of(di, 3, halfway - 1, halfway) for di in others], []) + [(None, 3 * GEO)]
    contents["three m"] += [("geos", count * 3 * GEO)]
    contents["four"] = sum([side_of("up", di, 3) for di in others], [])
    contents["four"] += sum([side_of("down", di, 3) for di in others], [])
    lengths = {name: sum(rows for _, rows in content) for name, content in contents.items()}
    for name in early_order:
        if name in buffers:
            lengths[name] = buffers[name].shape[0]
    base = {}
    total = 0
    for name in early_order + late_order:
        base[name] = total
        total += lengths[name]
        if name == early_order[-1]:
            late_from = total
    located = dict(at)
    for name, content in contents.items():
        start = 0
        for what, rows in content:
            located[what] = (name, start)
            start += rows
    layout = [
        base[located["row", slot, di, flip][0]] + located["row", slot, di, flip][1]
        for di in range(count)
        for flip in range(n_lay)
        for slot in range(slots)
    ]
    layout += [
        base[located[kind, di, flip][0]] + located[kind, di, flip][1]
        for kind in ("up", "down")
        for di in range(count)
        for flip in range(n_lay)
    ]
    pairs = slots * (slots + 1) // 2
    entries = pairs + UNROLL + 1
    early_table, late_table, info = pl.pallas_call(
        functools.partial(prepare_kernel, axes, count, tuple(layout), late_from),
        out_shape=(
            jax.ShapeDtypeStruct((entries,), jnp.int32),
            jax.ShapeDtypeStruct((entries,), jnp.int32),
            jax.ShapeDtypeStruct((slots + 2,), jnp.int32),
        ),
        in_specs=[HBM, HBM, ANY],
        out_specs=(SMEM, SMEM, SMEM),
        scratch_shapes=[
            pltpu.SMEM((slots, atoms), jnp.int32),
            pltpu.SMEM((atoms,), jnp.int32),
            pltpu.SMEM((3, slots), jnp.int32),
            pltpu.SMEM((atoms,), jnp.int32),
            pltpu.SMEM((len(layout),), jnp.int32),
            pltpu.SemaphoreType.DMA((2,)),
        ],
        compiler_params=pltpu.CompilerParams(vmem_limit_bytes=1 << 20),
        cost_estimate=pl.CostEstimate(flops=1000, bytes_accessed=1000, transcendentals=0),
        name="prepare",
    )(listings, atom_size, two_x)

    plans = [[(i, 0, most) for i in range(len(corners))]]
    two_m = pack([buffers[name] for name in corners], plans, [], "pack_two_mate", 3_000_000_000)[0]
    for di in others:
        note(("two x", di), on_row(two_x, di), contents["two x", di])
    note("two y", from_layer(two_y, 2), contents["two y"])
    early_mates = ["two m", "mate sides", "mate far"] + [("mate x", di) for di in others]
    note("two m", from_layer(two_m, 1), contents["two m"])
    note("mate sides", from_layer(sides, 1), contents["mate sides"])

    buffers["geos"] = geos
    names = ["two y", "geos"] + [("two x", di) for di in others]
    place = {name: i for i, name in enumerate(names)}
    gather = [(place["geos"], 0, 3 * GEO)] + [(place["two x", di], 2 * picks + size, 3 * GEO) for di in others]
    xs = [place["two x", di] for di in others]
    plans = [
        [(0, 0, picks)],
        [(x, picks, picks) for x in xs],
        [(x, 0, 2 * picks + size) for x in xs] + [(0, 0, lengths["two y"])] + gather,
        gather,
    ]
    three_x, three_y, three_m, geos = pack([buffers[name] for name in names], plans, [buffers[name] for name in early_mates] + [info], "pack_three")
    for di in others:
        note(("three x", di), on_row(three_x, di), contents["three x", di])
    note("three y", from_layer(three_y, 2), contents["three y"])
    note("three m", from_layer(three_m, 1), contents["three m"])
    third_geos = from_layer(geos, 3)

    spread, own_basis, own_kept = pl.pallas_call(
        functools.partial(spread_kernel, axes),
        out_shape=(
            jax.ShapeDtypeStruct((LANES, full), jnp.bfloat16),
            jax.ShapeDtypeStruct((16, size), jnp.bfloat16),
            jax.ShapeDtypeStruct((size, full), jnp.bfloat16),
        ),
        in_specs=[HBM, VMEM, SMEM, VMEM, ANY],
        out_specs=(VMEM, VMEM, VMEM),
        scratch_shapes=[pltpu.SMEM((slots, atoms), jnp.int32), pltpu.SemaphoreType.DMA((1,))],
        compiler_params=pltpu.CompilerParams(vmem_limit_bytes=(2 << 20) + atoms * 16384),
        cost_estimate=pl.CostEstimate(flops=1000, bytes_accessed=1000, transcendentals=0),
        name="spread_basis",
    )(listings, basis_proj.transpose(1, 0, 2).reshape(SHELLS * atoms, size), info, own, three_x)

    early_values = [buffers[name] for name in early_order]
    gram = pl.pallas_call(
        functools.partial(gram_kernel, len(early_values)),
        out_shape=jax.ShapeDtypeStruct((full, full), jnp.bfloat16),
        in_specs=[SMEM] + [VMEM] * len(early_values) + [ANY],
        out_specs=VMEM,
        scratch_shapes=[pltpu.VMEM((late_from, LANES), jnp.bfloat16)],
        compiler_params=pltpu.CompilerParams(vmem_limit_bytes=(6 << 20) + 2 * late_from * LANES * 2),
        cost_estimate=pl.CostEstimate(flops=1000, bytes_accessed=1000, transcendentals=0),
        name="gram_early",
    )(early_table, *early_values, three_x)

    thirds = [buffers["three x", di] for di in others] + [buffers["three y"]]
    four = pack(thirds, [[(i, 0, value.shape[0]) for i, value in enumerate(thirds)]], [gram, third_geos, own_basis], "pack_four")[0]
    note("four", from_layer(four, 1), contents["four"])

    column_steps = (0, 1, -1)
    tile_steps = [(dr, dc) for dr in steps for dc in column_steps]
    tiles = len(tile_steps)
    periods = (float(BX * n_row), float(BY * n_col), float(BZ * n_lay))
    plane, line = pl.pallas_call(
        functools.partial(profile_kernel, periods, tile_steps, at["geos"][1]),
        out_shape=(
            jax.ShapeDtypeStruct((tiles, SHELLS, BX * BY, LANES), jnp.bfloat16),
            jax.ShapeDtypeStruct((tiles, SHELLS, LANES, BZ), jnp.bfloat16),
        ),
        in_specs=[ANY] * 3,
        out_specs=(VMEM, VMEM),
        scratch_shapes=[
            pltpu.VMEM((3, tiles * GEO, LANES), jnp.bfloat16),
            pltpu.SemaphoreType.DMA((3,)),
        ],
        compiler_params=pltpu.CompilerParams(vmem_limit_bytes=10 << 20),
        cost_estimate=pl.CostEstimate(flops=1000, bytes_accessed=1000, transcendentals=0),
        name="profiles",
    )(geos, buffers["three m"], third_geos)

    late_values = [buffers[name] for name in late_order]
    sign_next, coef = pl.pallas_call(
        functools.partial(step_kernel, len(late_values)),
        out_shape=(
            jax.ShapeDtypeStruct((slots, size, size), jnp.bfloat16),
            jax.ShapeDtypeStruct((8, LANES), jnp.float32),
        ),
        in_specs=[SMEM, SMEM, VMEM, VMEM, VMEM, VMEM] + [VMEM] * len(late_values),
        out_specs=(VMEM, VMEM),
        scratch_shapes=[
            pltpu.VMEM((total - late_from, LANES), jnp.bfloat16),
            pltpu.VMEM((full, full), jnp.bfloat16),
            pltpu.VMEM((size, full), jnp.bfloat16),
        ],
        compiler_params=pltpu.CompilerParams(vmem_limit_bytes=(15 << 20) + 2 * (total - late_from) * LANES * 2),
        cost_estimate=pl.CostEstimate(flops=1_300_000_000, bytes_accessed=8_000_000, transcendentals=0),
        name="square_cube_coefficients",
    )(late_table, info, own_basis, spread, own_kept, gram, *late_values)

    mate_coef = from_layer(coef, 1)
    third_coef = from_layer(coef, 3)
    odd = lax.axis_index("layer") % 2 == 1
    below = jnp.where(odd, mate_coef, third_coef)
    above = jnp.where(odd, third_coef, mate_coef)
    merged = jnp.concatenate(
        [
            coef[:, : 4 * SPAN],
            below[:, SPAN : 3 * SPAN],
            above[:, 3 * SPAN : 4 * SPAN],
            jnp.zeros((8, LANES - 7 * SPAN), jnp.float32),
        ],
        axis=1,
    )
    stacked = jnp.concatenate([merged] + [on_row(merged, di) for di in others], axis=0)
    far_side = from_column(stacked, 1)
    received = [stacked, far_side, from_column(stacked, 0)]

    density = pl.pallas_call(
        functools.partial(density_kernel, len(column_steps)),
        out_shape=jax.ShapeDtypeStruct((BX * BY, BZ), jnp.float32),
        in_specs=[VMEM] * (len(received) + 2),
        out_specs=VMEM,
        scratch_shapes=[pltpu.VMEM((BX * BY, tiles * SHELLS * LANES), jnp.bfloat16)],
        compiler_params=pltpu.CompilerParams(vmem_limit_bytes=16 << 20),
        cost_estimate=pl.CostEstimate(flops=310_000_000, bytes_accessed=4_000_000, transcendentals=0),
        name="density",
    )(*received, plane, line.reshape(tiles * SHELLS * LANES, BZ))
    return sign_next[None], density.reshape(BX, BY, BZ)


def solution(mesh):
    rows = P(("row", "col", "layer"), None, None, None)
    in_specs = (rows, P(), P(), P(), P(("row", "col", "layer"), None), P(), P(), P())
    out_specs = (rows, P("row", "col", "layer"))
    return jax.shard_map(local, mesh=mesh, in_specs=in_specs, out_specs=out_specs, check_vma=False)
```

```python
import functools

import jax
import jax.numpy as jnp
from jax import lax
from jax.experimental import pallas as pl
from jax.experimental.pallas import tpu as pltpu
from jax.sharding import PartitionSpec as P

BX = 16
BY = 16
BZ = 128
LANES = 128
UNROLL = 4
SHELLS = 6
SPAN = 3 * SHELLS
GEO = 16
VMEM = pl.BlockSpec(memory_space=pltpu.VMEM)
SMEM = pl.BlockSpec(memory_space=pltpu.SMEM)
ANY = pl.BlockSpec(memory_space=pl.ANY)
HBM = pl.BlockSpec(memory_space=pltpu.HBM)


def from_offset(x, axis, step):
    count = lax.axis_size(axis)
    return lax.ppermute(x, axis, [((i + step) % count, i) for i in range(count)])


def from_column(x, side):
    count = lax.axis_size("col")
    step = [1 if (i + side) % 2 == 0 else -1 for i in range(count)]
    return lax.ppermute(x, "col", [((i + step[i]) % count, i) for i in range(count)])


def from_layer(x, flip):
    count = lax.axis_size("layer")
    return lax.ppermute(x, "layer", [(i ^ flip, i) for i in range(count)])


def column_targets(n_row):
    return 5 if n_row == 2 else 7


def target_place(n_row, step_row, step_lay, row):
    same = jnp.where(step_lay < 3, step_lay, -1)
    if n_row == 2:
        lead = step_lay - row
        across = jnp.where((lead >= 0) & (lead < 2), 3 + lead, -1)
    else:
        across = 3 + step_lay
    return jnp.where(step_row == 0, same, jnp.where(step_row == 1, across, -1))


class Places:
    def __init__(self, n_row, n_col, n_lay):
        self.n_row, self.n_col, self.n_lay = n_row, n_col, n_lay
        self.lay_bits = n_lay.bit_length() - 1
        self.col_bits = n_col.bit_length() - 1
        self.row = lax.axis_index("row")
        self.col = lax.axis_index("col")
        self.lay = lax.axis_index("layer")
        self.me = (((self.row << self.col_bits) + self.col) << self.lay_bits) + self.lay

    def split(self, atom):
        return (
            atom >> (self.lay_bits + self.col_bits),
            (atom >> self.lay_bits) & (self.n_col - 1),
            atom & (self.n_lay - 1),
        )


def load(sources, targets, sems):
    copies = [pltpu.make_async_copy(a, b, sems.at[i]) for i, (a, b) in enumerate(zip(sources, targets))]
    for copy in copies:
        copy.start()
    for copy in copies:
        copy.wait()


def own_ranks(at, neighbors_ref):
    seen = [jnp.int32(0)] * at.n_lay
    listed = []
    for w in range(neighbors_ref.shape[0]):
        atom = neighbors_ref[w, at.me]
        step_lay = (atom - at.lay) & (at.n_lay - 1)
        rank = jnp.int32(0)
        for k in range(at.n_lay):
            rank = jnp.where(step_lay == k, 3 * k + seen[k], rank)
            seen[k] = seen[k] + (step_lay == k).astype(jnp.int32)
        listed.append((atom, rank))
    return listed


def pick_kernel(axes, *refs):
    sign_ref, out_ref, geo_ref, neighbors_ref, extent_ref, x_ref, y_ref, z_ref, place_ref, loads, sems = refs[5:]
    at = Places(*axes)
    slots = sign_ref.shape[0]
    n_pick = place_ref.shape[0] - 1
    size = sign_ref.shape[1]
    for i in range(n_pick + 1):
        place_ref[i] = 0
    load(refs[:5], (neighbors_ref, extent_ref, x_ref, y_ref, z_ref), loads)
    ranks = own_ranks(at, neighbors_ref)
    for w, (atom, _) in enumerate(ranks):
        row, col, lay = at.split(atom)
        place = target_place(at.n_row, (row - at.row) & (at.n_row - 1), (lay - at.lay) & (at.n_lay - 1), at.row)
        place_ref[jnp.where((col == at.col) & (place >= 0), place, n_pick)] = w
    copies = []
    for i in range(n_pick):
        copy = pltpu.make_async_copy(sign_ref.at[place_ref[i]], out_ref.at[pl.ds(i * size, size)], sems.at[i])
        copy.start()
        copies.append(copy)
    sub = lax.broadcasted_iota(jnp.int32, (GEO, LANES), 0)
    lane_pair = lax.broadcasted_iota(jnp.int32, (GEO, LANES), 1) // SHELLS
    geo = jnp.zeros((GEO, LANES), jnp.int32)
    for w, (atom, rank) in enumerate(ranks):
        row, col, lay = at.split(atom)
        go_row = ((row - at.row + 1) & (at.n_row - 1)) - 1
        go_col = ((col - at.col + 1) & (at.n_col - 1)) - 1
        go_lay = jnp.minimum(((lay - at.lay + 1) & (at.n_lay - 1)) - 1, 1)
        twice_x = x_ref[at.me] + x_ref[atom] + BX * go_row
        twice_y = y_ref[at.me] + y_ref[atom] + BY * go_col
        twice_z = z_ref[at.me] + z_ref[atom] + BZ * go_lay - BZ
        extent = extent_ref[0, w]
        values = jnp.where(sub == 0, twice_x, jnp.where(sub == 1, twice_y, jnp.where(sub == 2, twice_z, extent)))
        geo = jnp.where(lane_pair == rank, values, geo)
    geo = geo.astype(jnp.float32).astype(out_ref.dtype)
    geo_ref[...] = geo
    out_ref[n_pick * size :] = geo
    for copy in copies:
        copy.wait()


def spread_kernel(axes, *refs):
    basis_ref, info_ref, sign_ref = refs[1:4]
    spread_ref, own_basis_ref, own_ref, neighbors_ref, loads = refs[-5:]
    at = Places(*axes)
    load(refs[:1], (neighbors_ref,), loads)
    slots, atoms = neighbors_ref.shape
    bits = atoms.bit_length() - 1

    def hot(rows, atom, first):
        sub = lax.broadcasted_iota(jnp.int32, (rows, SHELLS * atoms), 0)
        lane = lax.broadcasted_iota(jnp.int32, (rows, SHELLS * atoms), 1)
        return ((lane & (atoms - 1)) == atom) & (sub == first + (lane >> bits))

    def rows_of(chosen):
        picked = jnp.where(chosen, 1.0, 0.0).astype(jnp.bfloat16)
        return jnp.dot(picked, basis_ref[...], preferred_element_type=jnp.float32).astype(jnp.bfloat16)

    for w, (atom, rank) in enumerate(own_ranks(at, neighbors_ref)):
        spread_ref[:, w * LANES : (w + 1) * LANES] = rows_of(hot(LANES, atom, rank * SHELLS))
    own_basis_ref[...] = rows_of(hot(16, at.me, 0))
    size = sign_ref.shape[1]
    rows = lax.broadcasted_iota(jnp.int32, (size, size), 0)
    lanes = lax.broadcasted_iota(jnp.int32, (size, size), 1)
    for w in range(slots):
        kept = (rows < info_ref[slots]) & (lanes < info_ref[w])
        block = jnp.where(kept, sign_ref[w].astype(jnp.float32), 0.0)
        own_ref[:, w * size : (w + 1) * size] = block.astype(own_ref.dtype)


def prepare_kernel(axes, count, layout, late_from, *refs):
    early_ref, late_ref, info_ref, neighbors_ref, size_ref, known, inverse, layout_ref, loads = refs[-9:]
    at = Places(*axes)
    load(refs[:2], (neighbors_ref, size_ref), loads)
    slots = neighbors_ref.shape[0]
    lines = count * at.n_lay
    for i, value in enumerate(layout):
        layout_ref[i] = value
    self_slot = jnp.int32(0)
    for w in range(slots):
        atom = neighbors_ref[w, at.me]
        row, col, lay = at.split(atom)
        step_row = (row - at.row) & (at.n_row - 1)
        self_slot = jnp.where(atom == at.me, w, self_slot)
        info_ref[w] = size_ref[atom]
        known[0, w] = atom
        known[1, w] = jnp.where(col == at.col, 0, jnp.where(col == (at.col ^ 1), 1, 2))
        known[2, w] = jnp.where(step_row == 0, 0, jnp.where(step_row == 1, 1, 2)) * at.n_lay + (lay ^ at.lay)
        inverse[atom] = -1
    info_ref[slots] = size_ref[at.me]
    info_ref[slots + 1] = self_slot

    def row_of_pairs(v, totals):
        early, late = totals
        atom = known[0, v]
        side = known[1, v]
        line = known[2, v]
        for u in range(slots):
            inverse[neighbors_ref[u, atom]] = v * 16 + u

        def from_row(totals):
            total, late = totals
            for w in range(slots):
                mark = inverse[known[0, w]]
                chosen = ((mark >> 4) == v) & ((known[1, w] != 0) | (v <= w))
                where = layout_ref[line * slots + (mark & 15)]
                is_late = where >= late_from
                entry = v + 16 * w
                early_ref[total + 1] = entry + 256 * where
                late_ref[late + 1] = entry + 256 * (where - late_from)
                total = total + (chosen & ~is_late).astype(jnp.int32)
                late = late + (chosen & is_late).astype(jnp.int32)
            return total, late

        def from_column(totals):
            early, late = totals
            row, _, lay = at.split(atom)
            beside = layout_ref[lines * slots + (side - 1) * lines + line]
            for w in range(slots):
                other = known[0, w]
                mark = inverse[other]
                o_row, _, o_lay = at.split(other)
                d_row = (o_row - row) & (at.n_row - 1)
                d_lay = (o_lay - lay) & (at.n_lay - 1)
                there = target_place(at.n_row, d_row, d_lay, row)
                back = target_place(at.n_row, -d_row & (at.n_row - 1), -d_lay & (at.n_lay - 1), o_row)
                chosen = ((mark >> 4) == v) & (side == known[1, w]) & (there >= 0) & ((back < 0) | (v <= w))
                where = beside + there * LANES
                is_late = where >= late_from
                entry = v + 16 * w
                early_ref[early + 1] = entry + 256 * where
                late_ref[late + 1] = entry + 256 * (where - late_from)
                early = early + (chosen & ~is_late).astype(jnp.int32)
                late = late + (chosen & is_late).astype(jnp.int32)
            return early, late

        return lax.cond(side == 0, from_row, from_column, (early, late))

    totals = lax.fori_loop(0, slots, row_of_pairs, (jnp.int32(0), jnp.int32(0)))
    for ref, total in zip((early_ref, late_ref), totals):
        ref[0] = (total + UNROLL - 1) // UNROLL
        for i in range(UNROLL - 1):
            ref[total + i + 1] = ref[jnp.maximum(total, 1)]


def pack_kernel(moves, inputs, *refs):
    for source, start, rows, target, place in moves:
        refs[inputs + target][place : place + rows] = refs[source][start : start + rows]


def pack(values, plans, extra, name, cost=0):
    moves, shapes = [], []
    for target, plan in enumerate(plans):
        place = 0
        for source, start, rows in plan:
            moves.append((source, start, rows, target, place))
            place += rows
        shapes.append(jax.ShapeDtypeStruct((place, LANES), values[0].dtype))
    inputs = len(values) + len(extra)
    return pl.pallas_call(
        functools.partial(pack_kernel, tuple(moves), inputs),
        out_shape=tuple(shapes),
        in_specs=[VMEM] * len(values) + [ANY] * len(extra),
        out_specs=tuple([VMEM] * len(plans)),
        compiler_params=pltpu.CompilerParams(
            vmem_limit_bytes=(1 << 20) + 256 * sum(x.shape[0] for x in list(values) + shapes)
        ),
        cost_estimate=pl.CostEstimate(flops=cost, bytes_accessed=1000, transcendentals=0),
        name=name,
    )(*values, *extra)


def fill(piece_refs, pool):
    place = 0
    for piece in piece_refs:
        rows = piece.shape[0]
        pool[place : place + rows] = piece[...]
        place += rows


def place_pairs(table_ref, pool, gram, size):
    def place(i, carry):
        for k in range(UNROLL):
            entry = table_ref[i * UNROLL + k + 1]
            p = pl.multiple_of((entry & 15) * size, size)
            q = pl.multiple_of(((entry >> 4) & 15) * size, size)
            block = pool[pl.ds(pl.multiple_of(entry >> 8, 16), size)]
            gram[pl.ds(p, size), pl.ds(q, size)] = block
            gram[pl.ds(q, size), pl.ds(p, size)] = block.T
        return carry

    lax.fori_loop(0, table_ref[0], place, 0)


def gram_kernel(pieces, *refs):
    table_ref = refs[0]
    piece_refs = refs[1 : 1 + pieces]
    gram, pool = refs[-2:]
    size = LANES
    fill(piece_refs, pool)
    for v in range(gram.shape[0] // size):
        gram[v * size : (v + 1) * size] = jnp.zeros((size, gram.shape[1]), gram.dtype)
    place_pairs(table_ref, pool, gram, size)


def step_kernel(pieces, *refs):
    table_ref, info_ref, basis_ref, spread_ref, own, early_ref = refs[:6]
    piece_refs = refs[6 : 6 + pieces]
    next_ref, coef_ref, pool, gram, square = refs[-5:]
    slots, size = next_ref.shape[0], next_ref.shape[1]
    fill(piece_refs, pool)
    for v in range(slots):
        gram[v * size : (v + 1) * size] = early_ref[v * size : (v + 1) * size]
    own_size = info_ref[slots]
    self_slot = info_ref[slots + 1]
    place_pairs(table_ref, pool, gram, size)
    wide = 2 * size
    wide_lanes = lax.broadcasted_iota(jnp.int32, (size, wide), 1)
    wide_rows = lax.broadcasted_iota(jnp.int32, (size, wide), 0)

    def column_kept(n):
        first = info_ref[2 * n]
        second = info_ref[2 * n + 1]
        return (wide_lanes < first) | ((wide_lanes >= size) & (wide_lanes < size + second))

    for n in range(slots // 2):
        part = jnp.dot(own[...], gram[:, n * wide : (n + 1) * wide], preferred_element_type=jnp.float32)
        square[:, n * wide : (n + 1) * wide] = jnp.where(column_kept(n), part, 0.0).astype(square.dtype)
    basis = jnp.concatenate([basis_ref[...], basis_ref[...]], axis=1)
    coef = jnp.zeros((2 * basis_ref.shape[0], LANES), jnp.float32)
    across = (((1,), (1,)), ((), ()))
    for n in range(slots // 2):
        part = jnp.dot(square[...], gram[:, n * wide : (n + 1) * wide], preferred_element_type=jnp.float32)
        cube = jnp.where(column_kept(n), part, 0.0)
        full = 1.5 * own[:, n * wide : (n + 1) * wide].astype(jnp.float32) - 0.5 * cube
        next_ref[2 * n] = full[:, :size].astype(next_ref.dtype)
        next_ref[2 * n + 1] = full[:, size:].astype(next_ref.dtype)
        shift = (self_slot - 2 * n) * size
        is_self = (self_slot >= 2 * n) & (self_slot < 2 * n + 2)
        diag = (wide_lanes == wide_rows + shift) & (wide_rows < own_size) & is_self
        dmat = 0.5 * (jnp.where(diag, 1.0, 0.0) - full)
        high = dmat.astype(jnp.bfloat16)
        low = (dmat - high.astype(jnp.float32)).astype(jnp.bfloat16)
        half = jnp.dot(basis, jnp.concatenate([high, low], axis=0), preferred_element_type=jnp.float32)
        half_high = half.astype(jnp.bfloat16)
        half_low = (half - half_high.astype(jnp.float32)).astype(jnp.bfloat16)
        coef = coef + lax.dot_general(
            jnp.concatenate([half_high, half_low], axis=0),
            spread_ref[:, n * wide : (n + 1) * wide],
            across,
            preferred_element_type=jnp.float32,
        )
    coef = coef[: basis_ref.shape[0]] + coef[basis_ref.shape[0] :]
    coef_ref[...] = coef[: coef_ref.shape[0]]


def profile_kernel(periods, steps, mate_from, *refs):
    own_ref, mate_ref, third_ref = refs[:3]
    plane_ref, line_ref, geos, sems = refs[-4:]
    odd = (lax.axis_index("layer") & 1) == 1
    rows = len(steps) * GEO
    copies = []
    for k, source in enumerate((own_ref, mate_ref.at[pl.ds(mate_from, rows)], third_ref)):
        copy = pltpu.make_async_copy(source, geos.at[k], sems.at[k])
        copy.start()
        copies.append(copy)
    steps_x = lax.broadcasted_iota(jnp.int32, (BX, LANES), 0).astype(jnp.float32)
    steps_y = lax.broadcasted_iota(jnp.int32, (BY, LANES), 0).astype(jnp.float32)
    grid_z = lax.broadcasted_iota(jnp.int32, (LANES, BZ), 1).astype(jnp.float32)
    lane = lax.broadcasted_iota(jnp.int32, (1, LANES), 1)
    shell = (lane % SHELLS + 1).astype(jnp.float32)
    valid = lane < 7 * SPAN
    from_own = lane < 4 * SPAN
    from_below = lane < 6 * SPAN
    lift = jnp.where(from_own, 0.0, jnp.where(from_below, -float(BZ), float(BZ))) + 0.5 * BZ

    def nearest(offset, period):
        return offset - period * jnp.floor(offset * (1.0 / period) + 0.5)

    for copy in copies:
        copy.wait()
    ahead = 1.0 - 2.0 * (lax.axis_index("col") & 1).astype(jnp.float32)
    for o, (step_row, side) in enumerate(steps):
        own, first, third = (geos[k, o * GEO : (o + 1) * GEO].astype(jnp.float32) for k in range(3))
        below = jnp.where(odd, first, third)
        above = jnp.where(odd, third, first)
        moved = jnp.where(from_below, pltpu.roll(below, 3 * SPAN, axis=1), pltpu.roll(above, 3 * SPAN, axis=1))
        geo = jnp.where(from_own, own, moved)
        extent = jnp.where(valid, geo[3:4], 1.0)
        inverse = (SHELLS / extent) * (SHELLS / extent)
        reach = jnp.where(valid, extent, -1.0)
        rate_t = inverse / (shell * shell)
        packed = jnp.concatenate(
            [0.5 * geo[2:3] + lift, reach, rate_t, inverse, jnp.zeros((4, LANES), jnp.float32)], axis=0
        )
        sub = packed.T
        d_x = nearest(steps_x - (0.5 * geo[0:1] + float(BX * step_row)), periods[0])
        d_y = nearest(steps_y - (0.5 * geo[1:2] + float(BY * side) * ahead), periods[1])
        inside_x = jnp.abs(d_x) <= reach
        inside_y = jnp.abs(d_y) <= reach
        squared_x = d_x * d_x
        squared_y = d_y * d_y
        d_z = nearest(grid_z - sub[:, 0:1], periods[2])
        inside_z = jnp.abs(d_z) <= sub[:, 1:2]
        squared_z = d_z * d_z
        for s in range(SHELLS):
            part = 1.0 / ((s + 1) * (s + 1))
            rate = inverse * part + rate_t
            along_x = jnp.where(inside_x, jnp.exp(-rate * squared_x), 0.0)
            along_y = jnp.where(inside_y, jnp.exp(-rate * squared_y), 0.0)
            for x in range(BX):
                plane_ref[o, s, x * BY : (x + 1) * BY] = (along_x[x : x + 1] * along_y).astype(plane_ref.dtype)
            rate_z = sub[:, 3:4] * part + sub[:, 2:3]
            line_ref[o, s] = jnp.where(inside_z, jnp.exp(-rate_z * squared_z), 0.0).astype(line_ref.dtype)


def density_kernel(column_steps, *refs):
    coef_refs = refs[:column_steps]
    plane_ref, line_ref, out_ref, terms = refs[column_steps:]
    for o in range(plane_ref.shape[0]):
        coef = coef_refs[-o % column_steps]
        first = 8 * (o // column_steps)
        for s in range(SHELLS):
            scaled = plane_ref[o, s].astype(jnp.float32) * coef[first + s : first + s + 1, :]
            at = (o * SHELLS + s) * LANES
            terms[:, at : at + LANES] = scaled.astype(terms.dtype)
    out_ref[...] = jnp.dot(terms[...], line_ref[...], preferred_element_type=jnp.float32)


def local(sign_start, neighbors, atom_size, basis_proj, pair_extent, atom_x, atom_y, atom_z):
    n_row = lax.axis_size("row")
    n_col = lax.axis_size("col")
    n_lay = lax.axis_size("layer")
    assert n_lay == 4 and n_col >= 4 and (n_row == 2 or n_row >= 4)
    assert n_row & (n_row - 1) == 0 and n_col & (n_col - 1) == 0
    axes = (n_row, n_col, n_lay)
    atoms, slots = neighbors.shape
    size = sign_start.shape[2]
    steps = [0, 1] if n_row == 2 else [0, 1, -1]
    count = len(steps)
    others = range(1, count)
    own = sign_start[0]
    flat = own.reshape(slots * size, size)
    listings = neighbors.T
    full = slots * size
    half = full // 2
    most = half - size
    n_pick = column_targets(n_row)
    picks = n_pick * size
    part = picks + GEO

    def on_row(value, di):
        return from_offset(value, "row", steps[di])

    x_row = {di: on_row(flat, di) for di in others}
    y_row = from_layer(flat, 2)
    m_row = from_layer(flat, 1)
    picked, geo = pl.pallas_call(
        functools.partial(pick_kernel, axes),
        out_shape=(
            jax.ShapeDtypeStruct((part, size), own.dtype),
            jax.ShapeDtypeStruct((GEO, LANES), own.dtype),
        ),
        in_specs=[HBM] * 6,
        out_specs=(VMEM, VMEM),
        scratch_shapes=[
            pltpu.SMEM((slots, atoms), jnp.int32),
            pltpu.SMEM((1, slots), jnp.int32),
            pltpu.SMEM((atoms,), jnp.int32),
            pltpu.SMEM((atoms,), jnp.int32),
            pltpu.SMEM((atoms,), jnp.int32),
            pltpu.SMEM((n_pick + 1,), jnp.int32),
            pltpu.SemaphoreType.DMA((5,)),
            pltpu.SemaphoreType.DMA((n_pick,)),
        ],
        compiler_params=pltpu.CompilerParams(vmem_limit_bytes=60 << 20),
        name="pick_column_blocks",
    )(listings, pair_extent, atom_x, atom_y, atom_z, own)
    down = from_column(picked, 1)
    up = from_column(picked, 0)

    halves = pack(
        [y_row] + [x_row[di] for di in others],
        [[(0, half, most)]] + [[(di, 0, most)] for di in others],
        [],
        "pack_halves",
    )
    ends = {di: on_row(halves[0], di) for di in others}
    tops = {di: from_layer(halves[di], 2) for di in others}

    at = {}
    buffers = {}

    def note(name, value, contents):
        buffers[name] = value
        start = 0
        for what, rows in contents:
            if what is not None:
                at[what] = (name, start)
            start += rows

    def row_of(di, flip, start=0, stop=slots):
        return [(("row", slot, di, flip), size) for slot in range(start, stop)]

    halfway = slots // 2

    def side_of(kind, di, flip):
        return [((kind, di, flip), picks)]

    note("own", flat, row_of(0, 0))
    note("mate", m_row, row_of(0, 1))
    note("far", y_row, row_of(0, 2))
    note("up", up, side_of("up", 0, 0) + [(("up geo", 0, 0), GEO)])
    note("down", down, side_of("down", 0, 0) + [(("down geo", 0, 0), GEO)])
    buffers["geo"] = geo
    for di in others:
        note(("x", di), x_row[di], row_of(di, 0))
        note(("end", di), ends[di], row_of(di, 2, halfway, slots - 1))
        note(("top", di), tops[di], row_of(di, 2, 0, halfway - 1))

    corners = [("end", di) for di in others] + [("top", di) for di in others]
    names = ["down", "up", "geo", "far"] + [("x", di) for di in others]
    plans = [
        [(1, 0, picks), (0, 0, picks), (3, full - size, size), (2, 0, GEO), (1, picks, GEO), (0, picks, GEO)],
        [(1, 0, picks), (0, 0, picks)] + [(di + 3, most, size) for di in others] + [(2, 0, GEO), (1, picks, GEO), (0, picks, GEO)],
        [(2, 0, GEO), (1, picks, GEO), (0, picks, GEO)],
    ]
    two_x, two_y, geos = pack([buffers[name] for name in names], plans, [m_row], "pack_two")
    sides = pack([up, down], [[(0, 0, picks), (1, 0, picks)]], [], "pack_mate_sides")[0]
    for di in others:
        note(("mate x", di), from_layer(x_row[di], 1), row_of(di, 1))
    note("mate far", from_layer(y_row, 1), row_of(0, 3))

    early_order = ["own", "mate", "far", "up", "down"] + [("x", di) for di in others]
    early_order += [("mate x", di) for di in others] + ["mate far"]
    early_order += corners + [("two x", di) for di in others] + ["two y", "two m", "mate sides"]
    late_order = [("three x", di) for di in others] + ["three y", "three m"]
    late_order += ["four"]

    contents = {}
    for di in others:
        contents["two x", di] = side_of("up", di, 0) + side_of("down", di, 0)
        contents["two x", di] += row_of(di, 2, slots - 1, slots) + [(("geo", di, 0), GEO)]
        contents["two x", di] += [(("up geo", di, 0), GEO), (("down geo", di, 0), GEO)]
    contents["two y"] = side_of("up", 0, 2) + side_of("down", 0, 2)
    contents["two y"] += sum([row_of(di, 2, halfway - 1, halfway) for di in others], []) + [(None, 3 * GEO)]
    contents["two m"] = sum([row_of(di, 3, halfway, slots - 1) for di in others], [])
    contents["two m"] += sum([row_of(di, 3, 0, halfway - 1) for di in others], [])
    contents["mate sides"] = side_of("up", 0, 1) + side_of("down", 0, 1)
    for di in others:
        contents["three x", di] = side_of("up", di, 2)
    contents["three y"] = sum([side_of("down", di, 2) for di in others], [])
    contents["three m"] = []
    for di in others:
        contents["three m"] += side_of("up", di, 1) + side_of("down", di, 1) + row_of(di, 3, slots - 1, slots)
    contents["three m"] += side_of("up", 0, 3) + side_of("down", 0, 3)
    contents["three m"] += sum([row_of(di, 3, halfway - 1, halfway) for di in others], []) + [(None, 3 * GEO)]
    contents["three m"] += [("geos", count * 3 * GEO)]
    contents["four"] = sum([side_of("up", di, 3) for di in others], [])
    contents["four"] += sum([side_of("down", di, 3) for di in others], [])
    lengths = {name: sum(rows for _, rows in content) for name, content in contents.items()}
    for name in early_order:
        if name in buffers:
            lengths[name] = buffers[name].shape[0]
    base = {}
    total = 0
    for name in early_order + late_order:
        base[name] = total
        total += lengths[name]
        if name == early_order[-1]:
            late_from = total
    located = dict(at)
    for name, content in contents.items():
        start = 0
        for what, rows in content:
            located[what] = (name, start)
            start += rows
    layout = [
        base[located["row", slot, di, flip][0]] + located["row", slot, di, flip][1]
        for di in range(count)
        for flip in range(n_lay)
        for slot in range(slots)
    ]
    layout += [
        base[located[kind, di, flip][0]] + located[kind, di, flip][1]
        for kind in ("up", "down")
        for di in range(count)
        for flip in range(n_lay)
    ]
    pairs = slots * (slots + 1) // 2
    entries = pairs + UNROLL + 1
    early_table, late_table, info = pl.pallas_call(
        functools.partial(prepare_kernel, axes, count, tuple(layout), late_from),
        out_shape=(
            jax.ShapeDtypeStruct((entries,), jnp.int32),
            jax.ShapeDtypeStruct((entries,), jnp.int32),
            jax.ShapeDtypeStruct((slots + 2,), jnp.int32),
        ),
        in_specs=[HBM, HBM, ANY],
        out_specs=(SMEM, SMEM, SMEM),
        scratch_shapes=[
            pltpu.SMEM((slots, atoms), jnp.int32),
            pltpu.SMEM((atoms,), jnp.int32),
            pltpu.SMEM((3, slots), jnp.int32),
            pltpu.SMEM((atoms,), jnp.int32),
            pltpu.SMEM((len(layout),), jnp.int32),
            pltpu.SemaphoreType.DMA((2,)),
        ],
        compiler_params=pltpu.CompilerParams(vmem_limit_bytes=1 << 20),
        cost_estimate=pl.CostEstimate(flops=1000, bytes_accessed=1000, transcendentals=0),
        name="prepare",
    )(listings, atom_size, two_x)

    plans = [[(i, 0, most) for i in range(len(corners))]]
    two_m = pack([buffers[name] for name in corners], plans, [], "pack_two_mate", 3_000_000_000)[0]
    for di in others:
        note(("two x", di), on_row(two_x, di), contents["two x", di])
    note("two y", from_layer(two_y, 2), contents["two y"])
    early_mates = ["two m", "mate sides", "mate far"] + [("mate x", di) for di in others]
    note("two m", from_layer(two_m, 1), contents["two m"])
    note("mate sides", from_layer(sides, 1), contents["mate sides"])

    buffers["geos"] = geos
    names = ["two y", "geos"] + [("two x", di) for di in others]
    place = {name: i for i, name in enumerate(names)}
    gather = [(place["geos"], 0, 3 * GEO)] + [(place["two x", di], 2 * picks + size, 3 * GEO) for di in others]
    xs = [place["two x", di] for di in others]
    plans = [
        [(0, 0, picks)],
        [(x, picks, picks) for x in xs],
        [(x, 0, 2 * picks + size) for x in xs] + [(0, 0, lengths["two y"])] + gather,
        gather,
    ]
    three_x, three_y, three_m, geos = pack([buffers[name] for name in names], plans, [buffers[name] for name in early_mates] + [info], "pack_three")
    for di in others:
        note(("three x", di), on_row(three_x, di), contents["three x", di])
    note("three y", from_layer(three_y, 2), contents["three y"])
    note("three m", from_layer(three_m, 1), contents["three m"])
    third_geos = from_layer(geos, 3)

    spread, own_basis, own_kept = pl.pallas_call(
        functools.partial(spread_kernel, axes),
        out_shape=(
            jax.ShapeDtypeStruct((LANES, full), jnp.bfloat16),
            jax.ShapeDtypeStruct((16, size), jnp.bfloat16),
            jax.ShapeDtypeStruct((size, full), jnp.bfloat16),
        ),
        in_specs=[HBM, VMEM, SMEM, VMEM, ANY],
        out_specs=(VMEM, VMEM, VMEM),
        scratch_shapes=[pltpu.SMEM((slots, atoms), jnp.int32), pltpu.SemaphoreType.DMA((1,))],
        compiler_params=pltpu.CompilerParams(vmem_limit_bytes=(2 << 20) + atoms * 16384),
        cost_estimate=pl.CostEstimate(flops=1000, bytes_accessed=1000, transcendentals=0),
        name="spread_basis",
    )(listings, basis_proj.transpose(1, 0, 2).reshape(SHELLS * atoms, size), info, own, three_x)

    early_values = [buffers[name] for name in early_order]
    gram = pl.pallas_call(
        functools.partial(gram_kernel, len(early_values)),
        out_shape=jax.ShapeDtypeStruct((full, full), jnp.bfloat16),
        in_specs=[SMEM] + [VMEM] * len(early_values) + [ANY],
        out_specs=VMEM,
        scratch_shapes=[pltpu.VMEM((late_from, LANES), jnp.bfloat16)],
        compiler_params=pltpu.CompilerParams(vmem_limit_bytes=(6 << 20) + 2 * late_from * LANES * 2),
        cost_estimate=pl.CostEstimate(flops=1000, bytes_accessed=1000, transcendentals=0),
        name="gram_early",
    )(early_table, *early_values, three_x)

    thirds = [buffers["three x", di] for di in others] + [buffers["three y"]]
    four = pack(thirds, [[(i, 0, value.shape[0]) for i, value in enumerate(thirds)]], [gram, third_geos, own_basis], "pack_four")[0]
    note("four", from_layer(four, 1), contents["four"])

    column_steps = (0, 1, -1)
    tile_steps = [(dr, dc) for dr in steps for dc in column_steps]
    tiles = len(tile_steps)
    periods = (float(BX * n_row), float(BY * n_col), float(BZ * n_lay))
    plane, line = pl.pallas_call(
        functools.partial(profile_kernel, periods, tile_steps, at["geos"][1]),
        out_shape=(
            jax.ShapeDtypeStruct((tiles, SHELLS, BX * BY, LANES), jnp.bfloat16),
            jax.ShapeDtypeStruct((tiles, SHELLS, LANES, BZ), jnp.bfloat16),
        ),
        in_specs=[ANY] * 3,
        out_specs=(VMEM, VMEM),
        scratch_shapes=[
            pltpu.VMEM((3, tiles * GEO, LANES), jnp.bfloat16),
            pltpu.SemaphoreType.DMA((3,)),
        ],
        compiler_params=pltpu.CompilerParams(vmem_limit_bytes=10 << 20),
        cost_estimate=pl.CostEstimate(flops=1000, bytes_accessed=1000, transcendentals=0),
        name="profiles",
    )(geos, buffers["three m"], third_geos)

    late_values = [buffers[name] for name in late_order]
    sign_next, coef = pl.pallas_call(
        functools.partial(step_kernel, len(late_values)),
        out_shape=(
            jax.ShapeDtypeStruct((slots, size, size), jnp.bfloat16),
            jax.ShapeDtypeStruct((8, LANES), jnp.float32),
        ),
        in_specs=[SMEM, SMEM, VMEM, VMEM, VMEM, VMEM] + [VMEM] * len(late_values),
        out_specs=(VMEM, VMEM),
        scratch_shapes=[
            pltpu.VMEM((total - late_from, LANES), jnp.bfloat16),
            pltpu.VMEM((full, full), jnp.bfloat16),
            pltpu.VMEM((size, full), jnp.bfloat16),
        ],
        compiler_params=pltpu.CompilerParams(vmem_limit_bytes=(15 << 20) + 2 * (total - late_from) * LANES * 2),
        cost_estimate=pl.CostEstimate(flops=1_300_000_000, bytes_accessed=8_000_000, transcendentals=0),
        name="square_cube_coefficients",
    )(late_table, info, own_basis, spread, own_kept, gram, *late_values)

    mate_coef = from_layer(coef, 1)
    third_coef = from_layer(coef, 3)
    odd = lax.axis_index("layer") % 2 == 1
    below = jnp.where(odd, mate_coef, third_coef)
    above = jnp.where(odd, third_coef, mate_coef)
    merged = jnp.concatenate(
        [
            coef[:, : 4 * SPAN],
            below[:, SPAN : 3 * SPAN],
            above[:, 3 * SPAN : 4 * SPAN],
            jnp.zeros((8, LANES - 7 * SPAN), jnp.float32),
        ],
        axis=1,
    )
    stacked = jnp.concatenate([merged] + [on_row(merged, di) for di in others], axis=0)
    far_side = from_column(stacked, 1)
    received = [stacked, far_side, from_column(stacked, 0)]

    density = pl.pallas_call(
        functools.partial(density_kernel, len(column_steps)),
        out_shape=jax.ShapeDtypeStruct((BX * BY, BZ), jnp.float32),
        in_specs=[VMEM] * (len(received) + 2),
        out_specs=VMEM,
        scratch_shapes=[pltpu.VMEM((BX * BY, tiles * SHELLS * LANES), jnp.bfloat16)],
        compiler_params=pltpu.CompilerParams(vmem_limit_bytes=16 << 20),
        cost_estimate=pl.CostEstimate(flops=310_000_000, bytes_accessed=4_000_000, transcendentals=0),
        name="density",
    )(*received, plane, line.reshape(tiles * SHELLS * LANES, BZ))
    return sign_next[None], density.reshape(BX, BY, BZ)


def solution(mesh):
    rows = P(("row", "col", "layer"), None, None, None)
    in_specs = (rows, P(), P(), P(), P(("row", "col", "layer"), None), P(), P(), P())
    out_specs = (rows, P("row", "col", "layer"))
    return jax.shard_map(local, mesh=mesh, in_specs=in_specs, out_specs=out_specs, check_vma=False)
```

```python
import functools

import jax
import jax.numpy as jnp
from jax import lax
from jax.experimental import pallas as pl
from jax.experimental.pallas import tpu as pltpu
from jax.sharding import PartitionSpec as P

BX = 16
BY = 16
BZ = 128
LANES = 128
UNROLL = 4
SHELLS = 6
SPAN = 3 * SHELLS
GEO = 16
VMEM = pl.BlockSpec(memory_space=pltpu.VMEM)
SMEM = pl.BlockSpec(memory_space=pltpu.SMEM)
ANY = pl.BlockSpec(memory_space=pl.ANY)
HBM = pl.BlockSpec(memory_space=pltpu.HBM)


def from_offset(x, axis, step):
    count = lax.axis_size(axis)
    return lax.ppermute(x, axis, [((i + step) % count, i) for i in range(count)])


def from_column(x, side):
    count = lax.axis_size("col")
    step = [1 if (i + side) % 2 == 0 else -1 for i in range(count)]
    return lax.ppermute(x, "col", [((i + step[i]) % count, i) for i in range(count)])


def from_layer(x, flip):
    count = lax.axis_size("layer")
    return lax.ppermute(x, "layer", [(i ^ flip, i) for i in range(count)])


def column_targets(n_row):
    return 5 if n_row == 2 else 7


def target_place(n_row, step_row, step_lay, row):
    same = jnp.where(step_lay < 3, step_lay, -1)
    if n_row == 2:
        lead = step_lay - row
        across = jnp.where((lead >= 0) & (lead < 2), 3 + lead, -1)
    else:
        across = 3 + step_lay
    return jnp.where(step_row == 0, same, jnp.where(step_row == 1, across, -1))


class Places:
    def __init__(self, n_row, n_col, n_lay):
        self.n_row, self.n_col, self.n_lay = n_row, n_col, n_lay
        self.lay_bits = n_lay.bit_length() - 1
        self.col_bits = n_col.bit_length() - 1
        self.row = lax.axis_index("row")
        self.col = lax.axis_index("col")
        self.lay = lax.axis_index("layer")
        self.me = (((self.row << self.col_bits) + self.col) << self.lay_bits) + self.lay

    def split(self, atom):
        return (
            atom >> (self.lay_bits + self.col_bits),
            (atom >> self.lay_bits) & (self.n_col - 1),
            atom & (self.n_lay - 1),
        )


def load(sources, targets, sems):
    copies = [pltpu.make_async_copy(a, b, sems.at[i]) for i, (a, b) in enumerate(zip(sources, targets))]
    for copy in copies:
        copy.start()
    for copy in copies:
        copy.wait()


def own_ranks(at, neighbors_ref):
    seen = [jnp.int32(0)] * at.n_lay
    listed = []
    for w in range(neighbors_ref.shape[0]):
        atom = neighbors_ref[w, at.me]
        step_lay = (atom - at.lay) & (at.n_lay - 1)
        rank = jnp.int32(0)
        for k in range(at.n_lay):
            rank = jnp.where(step_lay == k, 3 * k + seen[k], rank)
            seen[k] = seen[k] + (step_lay == k).astype(jnp.int32)
        listed.append((atom, rank))
    return listed


def pick_kernel(axes, *refs):
    sign_ref, out_ref, neighbors_ref, extent_ref, x_ref, y_ref, z_ref, place_ref, loads, sems = refs[5:]
    at = Places(*axes)
    slots = sign_ref.shape[0]
    n_pick = place_ref.shape[0] - 1
    size = sign_ref.shape[1]
    for i in range(n_pick + 1):
        place_ref[i] = 0
    load(refs[:5], (neighbors_ref, extent_ref, x_ref, y_ref, z_ref), loads)
    for w in range(slots):
        row, col, lay = at.split(neighbors_ref[w, at.me])
        place = target_place(at.n_row, (row - at.row) & (at.n_row - 1), (lay - at.lay) & (at.n_lay - 1), at.row)
        place_ref[jnp.where((col == at.col) & (place >= 0), place, n_pick)] = w
    copies = []
    for i in range(n_pick):
        copy = pltpu.make_async_copy(sign_ref.at[place_ref[i]], out_ref.at[pl.ds(i * size, size)], sems.at[i])
        copy.start()
        copies.append(copy)
    ranks = own_ranks(at, neighbors_ref)
    sub = lax.broadcasted_iota(jnp.int32, (GEO, LANES), 0)
    lane_pair = lax.broadcasted_iota(jnp.int32, (GEO, LANES), 1) // SHELLS
    geo = jnp.zeros((GEO, LANES), jnp.int32)
    for w, (atom, rank) in enumerate(ranks):
        row, col, lay = at.split(atom)
        go_row = ((row - at.row + 1) & (at.n_row - 1)) - 1
        go_col = ((col - at.col + 1) & (at.n_col - 1)) - 1
        go_lay = jnp.minimum(((lay - at.lay + 1) & (at.n_lay - 1)) - 1, 1)
        twice_x = x_ref[at.me] + x_ref[atom] + BX * go_row
        twice_y = y_ref[at.me] + y_ref[atom] + BY * go_col
        twice_z = z_ref[at.me] + z_ref[atom] + BZ * go_lay - BZ
        extent = extent_ref[0, w]
        values = jnp.where(sub == 0, twice_x, jnp.where(sub == 1, twice_y, jnp.where(sub == 2, twice_z, extent)))
        geo = jnp.where(lane_pair == rank, values, geo)
    out_ref[n_pick * size :] = geo.astype(jnp.float32).astype(out_ref.dtype)
    for copy in copies:
        copy.wait()


def spread_kernel(axes, *refs):
    basis_ref = refs[1]
    spread_ref, own_basis_ref, neighbors_ref, loads = refs[-4:]
    at = Places(*axes)
    load(refs[:1], (neighbors_ref,), loads)
    slots, atoms = neighbors_ref.shape
    bits = atoms.bit_length() - 1

    def hot(rows, atom, first):
        sub = lax.broadcasted_iota(jnp.int32, (rows, SHELLS * atoms), 0)
        lane = lax.broadcasted_iota(jnp.int32, (rows, SHELLS * atoms), 1)
        return ((lane & (atoms - 1)) == atom) & (sub == first + (lane >> bits))

    def rows_of(chosen):
        picked = jnp.where(chosen, 1.0, 0.0).astype(jnp.bfloat16)
        return jnp.dot(picked, basis_ref[...], preferred_element_type=jnp.float32).astype(jnp.bfloat16)

    for w, (atom, rank) in enumerate(own_ranks(at, neighbors_ref)):
        spread_ref[:, w * LANES : (w + 1) * LANES] = rows_of(hot(LANES, atom, rank * SHELLS))
    own_basis_ref[...] = rows_of(hot(16, at.me, 0))


def prepare_kernel(axes, count, layout, late_from, *refs):
    early_ref, late_ref, info_ref, neighbors_ref, size_ref, known, inverse, layout_ref, loads = refs[-9:]
    at = Places(*axes)
    load(refs[:2], (neighbors_ref, size_ref), loads)
    slots = neighbors_ref.shape[0]
    lines = count * at.n_lay
    for i, value in enumerate(layout):
        layout_ref[i] = value
    self_slot = jnp.int32(0)
    for w in range(slots):
        atom = neighbors_ref[w, at.me]
        row, col, lay = at.split(atom)
        step_row = (row - at.row) & (at.n_row - 1)
        self_slot = jnp.where(atom == at.me, w, self_slot)
        info_ref[w] = size_ref[atom]
        known[0, w] = atom
        known[1, w] = jnp.where(col == at.col, 0, jnp.where(col == (at.col ^ 1), 1, 2))
        known[2, w] = jnp.where(step_row == 0, 0, jnp.where(step_row == 1, 1, 2)) * at.n_lay + (lay ^ at.lay)
        inverse[atom] = -1
    info_ref[slots] = size_ref[at.me]
    info_ref[slots + 1] = self_slot

    def row_of_pairs(v, totals):
        early, late = totals
        atom = known[0, v]
        side = known[1, v]
        line = known[2, v]
        for u in range(slots):
            inverse[neighbors_ref[u, atom]] = v * 16 + u

        def from_row(totals):
            total, late = totals
            for w in range(slots):
                mark = inverse[known[0, w]]
                chosen = ((mark >> 4) == v) & ((known[1, w] != 0) | (v <= w))
                where = layout_ref[line * slots + (mark & 15)]
                is_late = where >= late_from
                entry = v + 16 * w
                early_ref[total + 1] = entry + 256 * where
                late_ref[late + 1] = entry + 256 * (where - late_from)
                total = total + (chosen & ~is_late).astype(jnp.int32)
                late = late + (chosen & is_late).astype(jnp.int32)
            return total, late

        def from_column(totals):
            early, late = totals
            row, _, lay = at.split(atom)
            beside = layout_ref[lines * slots + (side - 1) * lines + line]
            for w in range(slots):
                other = known[0, w]
                mark = inverse[other]
                o_row, _, o_lay = at.split(other)
                d_row = (o_row - row) & (at.n_row - 1)
                d_lay = (o_lay - lay) & (at.n_lay - 1)
                there = target_place(at.n_row, d_row, d_lay, row)
                back = target_place(at.n_row, -d_row & (at.n_row - 1), -d_lay & (at.n_lay - 1), o_row)
                chosen = ((mark >> 4) == v) & (side == known[1, w]) & (there >= 0) & ((back < 0) | (v <= w))
                where = beside + there * LANES
                is_late = where >= late_from
                entry = v + 16 * w
                early_ref[early + 1] = entry + 256 * where
                late_ref[late + 1] = entry + 256 * (where - late_from)
                early = early + (chosen & ~is_late).astype(jnp.int32)
                late = late + (chosen & is_late).astype(jnp.int32)
            return early, late

        return lax.cond(side == 0, from_row, from_column, (early, late))

    totals = lax.fori_loop(0, slots, row_of_pairs, (jnp.int32(0), jnp.int32(0)))
    for ref, total in zip((early_ref, late_ref), totals):
        ref[0] = (total + UNROLL - 1) // UNROLL
        for i in range(UNROLL - 1):
            ref[total + i + 1] = ref[jnp.maximum(total, 1)]


def pack_kernel(moves, inputs, *refs):
    for source, start, rows, target, place in moves:
        refs[inputs + target][place : place + rows] = refs[source][start : start + rows]


def pack(values, plans, extra, name, cost=0):
    moves, shapes = [], []
    for target, plan in enumerate(plans):
        place = 0
        for source, start, rows in plan:
            moves.append((source, start, rows, target, place))
            place += rows
        shapes.append(jax.ShapeDtypeStruct((place, LANES), values[0].dtype))
    inputs = len(values) + len(extra)
    return pl.pallas_call(
        functools.partial(pack_kernel, tuple(moves), inputs),
        out_shape=tuple(shapes),
        in_specs=[VMEM] * len(values) + [ANY] * len(extra),
        out_specs=tuple([VMEM] * len(plans)),
        compiler_params=pltpu.CompilerParams(
            vmem_limit_bytes=(1 << 20) + 256 * sum(x.shape[0] for x in list(values) + shapes)
        ),
        cost_estimate=pl.CostEstimate(flops=cost, bytes_accessed=1000, transcendentals=0),
        name=name,
    )(*values, *extra)


def fill(piece_refs, pool):
    place = 0
    for piece in piece_refs:
        rows = piece.shape[0]
        pool[place : place + rows] = piece[...]
        place += rows


def place_pairs(table_ref, pool, gram, size):
    def place(i, carry):
        for k in range(UNROLL):
            entry = table_ref[i * UNROLL + k + 1]
            p = pl.multiple_of((entry & 15) * size, size)
            q = pl.multiple_of(((entry >> 4) & 15) * size, size)
            block = pool[pl.ds(pl.multiple_of(entry >> 8, 16), size)]
            gram[pl.ds(p, size), pl.ds(q, size)] = block
            gram[pl.ds(q, size), pl.ds(p, size)] = block.T
        return carry

    lax.fori_loop(0, table_ref[0], place, 0)


def gram_kernel(pieces, *refs):
    table_ref = refs[0]
    piece_refs = refs[1 : 1 + pieces]
    gram, pool = refs[-2:]
    size = LANES
    fill(piece_refs, pool)
    for v in range(gram.shape[0] // size):
        gram[v * size : (v + 1) * size] = jnp.zeros((size, gram.shape[1]), gram.dtype)
    place_pairs(table_ref, pool, gram, size)


def step_kernel(pieces, *refs):
    table_ref, info_ref, basis_ref, spread_ref, sign_ref, early_ref = refs[:6]
    piece_refs = refs[6 : 6 + pieces]
    next_ref, coef_ref, pool, gram, own, square = refs[-6:]
    slots, size = sign_ref.shape[0], sign_ref.shape[1]
    fill(piece_refs, pool)
    for v in range(slots):
        gram[v * size : (v + 1) * size] = early_ref[v * size : (v + 1) * size]
    rows = lax.broadcasted_iota(jnp.int32, (size, size), 0)
    lanes = lax.broadcasted_iota(jnp.int32, (size, size), 1)
    own_size = info_ref[slots]
    self_slot = info_ref[slots + 1]
    for w in range(slots):
        kept = (rows < own_size) & (lanes < info_ref[w])
        block = jnp.where(kept, sign_ref[w].astype(jnp.float32), 0.0)
        own[:, w * size : (w + 1) * size] = block.astype(own.dtype)
    place_pairs(table_ref, pool, gram, size)
    wide = 2 * size
    wide_lanes = lax.broadcasted_iota(jnp.int32, (size, wide), 1)
    wide_rows = lax.broadcasted_iota(jnp.int32, (size, wide), 0)

    def column_kept(n):
        first = info_ref[2 * n]
        second = info_ref[2 * n + 1]
        return (wide_lanes < first) | ((wide_lanes >= size) & (wide_lanes < size + second))

    for n in range(slots // 2):
        part = jnp.dot(own[...], gram[:, n * wide : (n + 1) * wide], preferred_element_type=jnp.float32)
        square[:, n * wide : (n + 1) * wide] = jnp.where(column_kept(n), part, 0.0).astype(square.dtype)
    basis = jnp.concatenate([basis_ref[...], basis_ref[...]], axis=1)
    coef = jnp.zeros((2 * basis_ref.shape[0], LANES), jnp.float32)
    across = (((1,), (1,)), ((), ()))
    for n in range(slots // 2):
        part = jnp.dot(square[...], gram[:, n * wide : (n + 1) * wide], preferred_element_type=jnp.float32)
        cube = jnp.where(column_kept(n), part, 0.0)
        full = 1.5 * own[:, n * wide : (n + 1) * wide].astype(jnp.float32) - 0.5 * cube
        next_ref[2 * n] = full[:, :size].astype(next_ref.dtype)
        next_ref[2 * n + 1] = full[:, size:].astype(next_ref.dtype)
        shift = (self_slot - 2 * n) * size
        is_self = (self_slot >= 2 * n) & (self_slot < 2 * n + 2)
        diag = (wide_lanes == wide_rows + shift) & (wide_rows < own_size) & is_self
        dmat = 0.5 * (jnp.where(diag, 1.0, 0.0) - full)
        high = dmat.astype(jnp.bfloat16)
        low = (dmat - high.astype(jnp.float32)).astype(jnp.bfloat16)
        half = jnp.dot(basis, jnp.concatenate([high, low], axis=0), preferred_element_type=jnp.float32)
        half_high = half.astype(jnp.bfloat16)
        half_low = (half - half_high.astype(jnp.float32)).astype(jnp.bfloat16)
        coef = coef + lax.dot_general(
            jnp.concatenate([half_high, half_low], axis=0),
            spread_ref[:, n * wide : (n + 1) * wide],
            across,
            preferred_element_type=jnp.float32,
        )
    coef = coef[: basis_ref.shape[0]] + coef[basis_ref.shape[0] :]
    coef_ref[...] = coef[: coef_ref.shape[0]]


def profile_kernel(periods, steps, mate_from, *refs):
    own_ref, mate_ref, third_ref = refs[:3]
    plane_ref, line_ref, geos, sems = refs[-4:]
    odd = (lax.axis_index("layer") & 1) == 1
    rows = len(steps) * GEO
    copies = []
    for k, source in enumerate((own_ref, mate_ref.at[pl.ds(mate_from, rows)], third_ref)):
        copy = pltpu.make_async_copy(source, geos.at[k], sems.at[k])
        copy.start()
        copies.append(copy)
    steps_x = lax.broadcasted_iota(jnp.int32, (BX, LANES), 0).astype(jnp.float32)
    steps_y = lax.broadcasted_iota(jnp.int32, (BY, LANES), 0).astype(jnp.float32)
    grid_z = lax.broadcasted_iota(jnp.int32, (LANES, BZ), 1).astype(jnp.float32)
    lane = lax.broadcasted_iota(jnp.int32, (1, LANES), 1)
    shell = (lane % SHELLS + 1).astype(jnp.float32)
    valid = lane < 7 * SPAN
    from_own = lane < 4 * SPAN
    from_below = lane < 6 * SPAN
    lift = jnp.where(from_own, 0.0, jnp.where(from_below, -float(BZ), float(BZ))) + 0.5 * BZ

    def nearest(offset, period):
        return offset - period * jnp.floor(offset * (1.0 / period) + 0.5)

    for copy in copies:
        copy.wait()
    ahead = 1.0 - 2.0 * (lax.axis_index("col") & 1).astype(jnp.float32)
    for o, (step_row, side) in enumerate(steps):
        own, first, third = (geos[k, o * GEO : (o + 1) * GEO].astype(jnp.float32) for k in range(3))
        below = jnp.where(odd, first, third)
        above = jnp.where(odd, third, first)
        moved = jnp.where(from_below, pltpu.roll(below, 3 * SPAN, axis=1), pltpu.roll(above, 3 * SPAN, axis=1))
        geo = jnp.where(from_own, own, moved)
        extent = jnp.where(valid, geo[3:4], 1.0)
        inverse = (SHELLS / extent) * (SHELLS / extent)
        reach = jnp.where(valid, extent, -1.0)
        rate_t = inverse / (shell * shell)
        packed = jnp.concatenate(
            [0.5 * geo[2:3] + lift, reach, rate_t, inverse, jnp.zeros((4, LANES), jnp.float32)], axis=0
        )
        sub = packed.T
        d_x = nearest(steps_x - (0.5 * geo[0:1] + float(BX * step_row)), periods[0])
        d_y = nearest(steps_y - (0.5 * geo[1:2] + float(BY * side) * ahead), periods[1])
        inside_x = jnp.abs(d_x) <= reach
        inside_y = jnp.abs(d_y) <= reach
        squared_x = d_x * d_x
        squared_y = d_y * d_y
        d_z = nearest(grid_z - sub[:, 0:1], periods[2])
        inside_z = jnp.abs(d_z) <= sub[:, 1:2]
        squared_z = d_z * d_z
        for s in range(SHELLS):
            part = 1.0 / ((s + 1) * (s + 1))
            rate = inverse * part + rate_t
            along_x = jnp.where(inside_x, jnp.exp(-rate * squared_x), 0.0)
            along_y = jnp.where(inside_y, jnp.exp(-rate * squared_y), 0.0)
            for x in range(BX):
                plane_ref[o, s, x * BY : (x + 1) * BY] = (along_x[x : x + 1] * along_y).astype(plane_ref.dtype)
            rate_z = sub[:, 3:4] * part + sub[:, 2:3]
            line_ref[o, s] = jnp.where(inside_z, jnp.exp(-rate_z * squared_z), 0.0).astype(line_ref.dtype)


def density_kernel(column_steps, *refs):
    coef_refs = refs[:column_steps]
    plane_ref, line_ref = refs[column_steps : column_steps + 2]
    out_ref, terms = refs[-2:]
    for o in range(plane_ref.shape[0]):
        coef = coef_refs[-o % column_steps]
        first = 8 * (o // column_steps)
        for s in range(SHELLS):
            scaled = plane_ref[o, s].astype(jnp.float32) * coef[first + s : first + s + 1, :]
            at = (o * SHELLS + s) * LANES
            terms[:, at : at + LANES] = scaled.astype(terms.dtype)
    out_ref[...] = jnp.dot(terms[...], line_ref[...], preferred_element_type=jnp.float32)


def local(sign_start, neighbors, atom_size, basis_proj, pair_extent, atom_x, atom_y, atom_z):
    n_row = lax.axis_size("row")
    n_col = lax.axis_size("col")
    n_lay = lax.axis_size("layer")
    assert n_lay == 4 and n_col >= 4 and (n_row == 2 or n_row >= 4)
    assert n_row & (n_row - 1) == 0 and n_col & (n_col - 1) == 0
    axes = (n_row, n_col, n_lay)
    atoms, slots = neighbors.shape
    size = sign_start.shape[2]
    steps = [0, 1] if n_row == 2 else [0, 1, -1]
    count = len(steps)
    others = range(1, count)
    own = sign_start[0]
    flat = own.reshape(slots * size, size)
    listings = neighbors.T
    full = slots * size
    half = full // 2
    most = half - size
    n_pick = column_targets(n_row)
    picks = n_pick * size
    part = picks + GEO

    def on_row(value, di):
        return from_offset(value, "row", steps[di])

    x_row = {di: on_row(flat, di) for di in others}
    y_row = from_layer(flat, 2)
    m_row = from_layer(flat, 1)
    picked = pl.pallas_call(
        functools.partial(pick_kernel, axes),
        out_shape=jax.ShapeDtypeStruct((part, size), own.dtype),
        in_specs=[HBM] * 6,
        out_specs=VMEM,
        scratch_shapes=[
            pltpu.SMEM((slots, atoms), jnp.int32),
            pltpu.SMEM((1, slots), jnp.int32),
            pltpu.SMEM((atoms,), jnp.int32),
            pltpu.SMEM((atoms,), jnp.int32),
            pltpu.SMEM((atoms,), jnp.int32),
            pltpu.SMEM((n_pick + 1,), jnp.int32),
            pltpu.SemaphoreType.DMA((5,)),
            pltpu.SemaphoreType.DMA((n_pick,)),
        ],
        compiler_params=pltpu.CompilerParams(vmem_limit_bytes=60 << 20),
        name="pick_column_blocks",
    )(listings, pair_extent, atom_x, atom_y, atom_z, own)
    down = from_column(picked, 1)
    up = from_column(picked, 0)

    halves = pack(
        [y_row] + [x_row[di] for di in others] + [picked],
        [[(0, half, most)]] + [[(di, 0, most)] for di in others] + [[(count, picks, GEO)]],
        [],
        "pack_halves",
    )
    ends = {di: on_row(halves[0], di) for di in others}
    tops = {di: from_layer(halves[di], 2) for di in others}

    at = {}
    buffers = {}

    def note(name, value, contents):
        buffers[name] = value
        start = 0
        for what, rows in contents:
            if what is not None:
                at[what] = (name, start)
            start += rows

    def row_of(di, flip, start=0, stop=slots):
        return [(("row", slot, di, flip), size) for slot in range(start, stop)]

    halfway = slots // 2

    def side_of(kind, di, flip):
        return [((kind, di, flip), picks)]

    note("own", flat, row_of(0, 0))
    note("mate", m_row, row_of(0, 1))
    note("far", y_row, row_of(0, 2))
    note("up", up, side_of("up", 0, 0) + [(("up geo", 0, 0), GEO)])
    note("down", down, side_of("down", 0, 0) + [(("down geo", 0, 0), GEO)])
    note("geo", halves[count], [(("geo", 0, 0), GEO)])
    for di in others:
        note(("x", di), x_row[di], row_of(di, 0))
        note(("end", di), ends[di], row_of(di, 2, halfway, slots - 1))
        note(("top", di), tops[di], row_of(di, 2, 0, halfway - 1))

    corners = [("end", di) for di in others] + [("top", di) for di in others]
    names = ["down", "up", "geo", "far"] + [("x", di) for di in others]
    plans = [
        [(1, 0, picks), (0, 0, picks), (3, full - size, size), (2, 0, GEO), (1, picks, GEO), (0, picks, GEO)],
        [(1, 0, picks), (0, 0, picks)] + [(di + 3, most, size) for di in others] + [(2, 0, GEO), (1, picks, GEO), (0, picks, GEO)],
        [(2, 0, GEO), (1, picks, GEO), (0, picks, GEO)],
    ]
    two_x, two_y, geos = pack([buffers[name] for name in names], plans, [m_row], "pack_two")
    to_mate = corners + ["up", "down"]
    for di in others:
        note(("mate x", di), from_layer(x_row[di], 1), row_of(di, 1))
    note("mate far", from_layer(y_row, 1), row_of(0, 3))

    early_order = ["own", "mate", "far", "up", "down", "geo"] + [("x", di) for di in others]
    early_order += [("mate x", di) for di in others] + ["mate far"]
    early_order += corners + [("two x", di) for di in others] + ["two y", "two m"]
    late_order = [("three x", di) for di in others] + ["three y", "three m"]
    late_order += ["four"]

    contents = {}
    for di in others:
        contents["two x", di] = side_of("up", di, 0) + side_of("down", di, 0)
        contents["two x", di] += row_of(di, 2, slots - 1, slots) + [(("geo", di, 0), GEO)]
        contents["two x", di] += [(("up geo", di, 0), GEO), (("down geo", di, 0), GEO)]
    contents["two y"] = side_of("up", 0, 2) + side_of("down", 0, 2)
    contents["two y"] += sum([row_of(di, 2, halfway - 1, halfway) for di in others], []) + [(None, 3 * GEO)]
    contents["two m"] = sum([row_of(di, 3, halfway, slots - 1) for di in others], [])
    contents["two m"] += sum([row_of(di, 3, 0, halfway - 1) for di in others], [])
    contents["two m"] += side_of("up", 0, 1) + side_of("down", 0, 1)
    for di in others:
        contents["three x", di] = side_of("up", di, 2)
    contents["three y"] = sum([side_of("down", di, 2) for di in others], [])
    contents["three m"] = []
    for di in others:
        contents["three m"] += side_of("up", di, 1) + side_of("down", di, 1) + row_of(di, 3, slots - 1, slots)
    contents["three m"] += side_of("up", 0, 3) + side_of("down", 0, 3)
    contents["three m"] += sum([row_of(di, 3, halfway - 1, halfway) for di in others], []) + [(None, 3 * GEO)]
    contents["three m"] += [("geos", count * 3 * GEO)]
    contents["four"] = sum([side_of("up", di, 3) for di in others], [])
    contents["four"] += sum([side_of("down", di, 3) for di in others], [])
    lengths = {name: sum(rows for _, rows in content) for name, content in contents.items()}
    for name in early_order:
        if name in buffers:
            lengths[name] = buffers[name].shape[0]
    base = {}
    total = 0
    for name in early_order + late_order:
        base[name] = total
        total += lengths[name]
        if name == early_order[-1]:
            late_from = total
    located = dict(at)
    for name, content in contents.items():
        start = 0
        for what, rows in content:
            located[what] = (name, start)
            start += rows
    layout = [
        base[located["row", slot, di, flip][0]] + located["row", slot, di, flip][1]
        for di in range(count)
        for flip in range(n_lay)
        for slot in range(slots)
    ]
    layout += [
        base[located[kind, di, flip][0]] + located[kind, di, flip][1]
        for kind in ("up", "down")
        for di in range(count)
        for flip in range(n_lay)
    ]
    pairs = slots * (slots + 1) // 2
    entries = pairs + UNROLL + 1
    early_table, late_table, info = pl.pallas_call(
        functools.partial(prepare_kernel, axes, count, tuple(layout), late_from),
        out_shape=(
            jax.ShapeDtypeStruct((entries,), jnp.int32),
            jax.ShapeDtypeStruct((entries,), jnp.int32),
            jax.ShapeDtypeStruct((slots + 2,), jnp.int32),
        ),
        in_specs=[HBM, HBM, ANY],
        out_specs=(SMEM, SMEM, SMEM),
        scratch_shapes=[
            pltpu.SMEM((slots, atoms), jnp.int32),
            pltpu.SMEM((atoms,), jnp.int32),
            pltpu.SMEM((3, slots), jnp.int32),
            pltpu.SMEM((atoms,), jnp.int32),
            pltpu.SMEM((len(layout),), jnp.int32),
            pltpu.SemaphoreType.DMA((2,)),
        ],
        compiler_params=pltpu.CompilerParams(vmem_limit_bytes=1 << 20),
        cost_estimate=pl.CostEstimate(flops=1000, bytes_accessed=1000, transcendentals=0),
        name="prepare",
    )(listings, atom_size, two_x)

    plans = [[(i, 0, picks if name in ("up", "down") else most) for i, name in enumerate(to_mate)]]
    two_m = pack([buffers[name] for name in to_mate], plans, [], "pack_two_mate", 3_000_000_000)[0]
    for di in others:
        note(("two x", di), on_row(two_x, di), contents["two x", di])
    note("two y", from_layer(two_y, 2), contents["two y"])
    early_mates = ["mate far"] + [("mate x", di) for di in others]
    note("two m", from_layer(two_m, 1), contents["two m"])

    buffers["geos"] = geos
    names = ["two y", "geos"] + [("two x", di) for di in others]
    place = {name: i for i, name in enumerate(names)}
    gather = [(place["geos"], 0, 3 * GEO)] + [(place["two x", di], 2 * picks + size, 3 * GEO) for di in others]
    xs = [place["two x", di] for di in others]
    plans = [
        [(0, 0, picks)],
        [(x, picks, picks) for x in xs],
        [(x, 0, 2 * picks + size) for x in xs] + [(0, 0, lengths["two y"])] + gather,
        gather,
    ]
    three_x, three_y, three_m, geos = pack([buffers[name] for name in names], plans, [buffers[name] for name in early_mates] + [two_m, info], "pack_three")
    for di in others:
        note(("three x", di), on_row(three_x, di), contents["three x", di])
    note("three y", from_layer(three_y, 2), contents["three y"])
    note("three m", from_layer(three_m, 1), contents["three m"])
    third_geos = from_layer(geos, 3)

    spread, own_basis = pl.pallas_call(
        functools.partial(spread_kernel, axes),
        out_shape=(
            jax.ShapeDtypeStruct((LANES, full), jnp.bfloat16),
            jax.ShapeDtypeStruct((16, size), jnp.bfloat16),
        ),
        in_specs=[HBM, VMEM, ANY],
        out_specs=(VMEM, VMEM),
        scratch_shapes=[pltpu.SMEM((slots, atoms), jnp.int32), pltpu.SemaphoreType.DMA((1,))],
        compiler_params=pltpu.CompilerParams(vmem_limit_bytes=(2 << 20) + atoms * 16384),
        cost_estimate=pl.CostEstimate(flops=1000, bytes_accessed=1000, transcendentals=0),
        name="spread_basis",
    )(listings, basis_proj.transpose(1, 0, 2).reshape(SHELLS * atoms, size), three_x)

    early_values = [buffers[name] for name in early_order]
    gram = pl.pallas_call(
        functools.partial(gram_kernel, len(early_values)),
        out_shape=jax.ShapeDtypeStruct((full, full), jnp.bfloat16),
        in_specs=[SMEM] + [VMEM] * len(early_values) + [ANY],
        out_specs=VMEM,
        scratch_shapes=[pltpu.VMEM((late_from, LANES), jnp.bfloat16)],
        compiler_params=pltpu.CompilerParams(vmem_limit_bytes=(6 << 20) + 2 * late_from * LANES * 2),
        cost_estimate=pl.CostEstimate(flops=1000, bytes_accessed=1000, transcendentals=0),
        name="gram_early",
    )(early_table, *early_values, three_x)

    thirds = [buffers["three x", di] for di in others] + [buffers["three y"]]
    four = pack(thirds, [[(i, 0, value.shape[0]) for i, value in enumerate(thirds)]], [gram, third_geos, own_basis], "pack_four")[0]
    note("four", from_layer(four, 1), contents["four"])

    column_steps = (0, 1, -1)
    tile_steps = [(dr, dc) for dr in steps for dc in column_steps]
    tiles = len(tile_steps)
    periods = (float(BX * n_row), float(BY * n_col), float(BZ * n_lay))
    plane, line = pl.pallas_call(
        functools.partial(profile_kernel, periods, tile_steps, at["geos"][1]),
        out_shape=(
            jax.ShapeDtypeStruct((tiles, SHELLS, BX * BY, LANES), jnp.bfloat16),
            jax.ShapeDtypeStruct((tiles, SHELLS, LANES, BZ), jnp.bfloat16),
        ),
        in_specs=[ANY] * 3,
        out_specs=(VMEM, VMEM),
        scratch_shapes=[
            pltpu.VMEM((3, tiles * GEO, LANES), jnp.bfloat16),
            pltpu.SemaphoreType.DMA((3,)),
        ],
        compiler_params=pltpu.CompilerParams(vmem_limit_bytes=10 << 20),
        cost_estimate=pl.CostEstimate(flops=1000, bytes_accessed=1000, transcendentals=0),
        name="profiles",
    )(geos, buffers["three m"], third_geos)

    late_values = [buffers[name] for name in late_order]
    sign_next, coef = pl.pallas_call(
        functools.partial(step_kernel, len(late_values)),
        out_shape=(
            jax.ShapeDtypeStruct((slots, size, size), jnp.bfloat16),
            jax.ShapeDtypeStruct((8, LANES), jnp.float32),
        ),
        in_specs=[SMEM, SMEM, VMEM, VMEM, VMEM, VMEM] + [VMEM] * len(late_values),
        out_specs=(VMEM, VMEM),
        scratch_shapes=[
            pltpu.VMEM((total - late_from, LANES), jnp.bfloat16),
            pltpu.VMEM((full, full), jnp.bfloat16),
            pltpu.VMEM((size, full), jnp.bfloat16),
            pltpu.VMEM((size, full), jnp.bfloat16),
        ],
        compiler_params=pltpu.CompilerParams(vmem_limit_bytes=(15 << 20) + 2 * (total - late_from) * LANES * 2),
        cost_estimate=pl.CostEstimate(flops=1_300_000_000, bytes_accessed=8_000_000, transcendentals=0),
        name="square_cube_coefficients",
    )(late_table, info, own_basis, spread, own, gram, *late_values)

    mate_coef = from_layer(coef, 1)
    third_coef = from_layer(coef, 3)
    odd = lax.axis_index("layer") % 2 == 1
    below = jnp.where(odd, mate_coef, third_coef)
    above = jnp.where(odd, third_coef, mate_coef)
    merged = jnp.concatenate(
        [
            coef[:, : 4 * SPAN],
            below[:, SPAN : 3 * SPAN],
            above[:, 3 * SPAN : 4 * SPAN],
            jnp.zeros((8, LANES - 7 * SPAN), jnp.float32),
        ],
        axis=1,
    )
    stacked = jnp.concatenate([merged] + [on_row(merged, di) for di in others], axis=0)
    far_side = from_column(stacked, 1)
    received = [stacked, far_side, from_column(stacked, 0)]

    given = pack([sign_next.reshape(full, size)], [[(0, 0, full)]], [], "give_sign")[0]
    density = pl.pallas_call(
        functools.partial(density_kernel, len(column_steps)),
        out_shape=jax.ShapeDtypeStruct((BX * BY, BZ), jnp.float32),
        in_specs=[VMEM] * (len(received) + 2) + [ANY],
        out_specs=VMEM,
        scratch_shapes=[pltpu.VMEM((BX * BY, tiles * SHELLS * LANES), jnp.bfloat16)],
        compiler_params=pltpu.CompilerParams(vmem_limit_bytes=16 << 20),
        cost_estimate=pl.CostEstimate(flops=310_000_000, bytes_accessed=4_000_000, transcendentals=0),
        name="density",
    )(*received, plane, line.reshape(tiles * SHELLS * LANES, BZ), given)
    return given.reshape(1, slots, size, size), density.reshape(BX, BY, BZ)


def solution(mesh):
    rows = P(("row", "col", "layer"), None, None, None)
    in_specs = (rows, P(), P(), P(), P(("row", "col", "layer"), None), P(), P(), P())
    out_specs = (rows, P("row", "col", "layer"))
    return jax.shard_map(local, mesh=mesh, in_specs=in_specs, out_specs=out_specs, check_vma=False)
```

```python
import functools

import jax
import jax.numpy as jnp
from jax import lax
from jax.experimental import pallas as pl
from jax.experimental.pallas import tpu as pltpu
from jax.sharding import PartitionSpec as P

BX = 16
BY = 16
BZ = 128
LANES = 128
UNROLL = 4
SHELLS = 6
SPAN = 3 * SHELLS
GEO = 16
VMEM = pl.BlockSpec(memory_space=pltpu.VMEM)
SMEM = pl.BlockSpec(memory_space=pltpu.SMEM)
ANY = pl.BlockSpec(memory_space=pl.ANY)
HBM = pl.BlockSpec(memory_space=pltpu.HBM)


def from_offset(x, axis, step):
    count = lax.axis_size(axis)
    return lax.ppermute(x, axis, [((i + step) % count, i) for i in range(count)])


def from_column(x, side):
    count = lax.axis_size("col")
    step = [1 if (i + side) % 2 == 0 else -1 for i in range(count)]
    return lax.ppermute(x, "col", [((i + step[i]) % count, i) for i in range(count)])


def from_layer(x, flip):
    count = lax.axis_size("layer")
    return lax.ppermute(x, "layer", [(i ^ flip, i) for i in range(count)])


def column_targets(n_row):
    return 5 if n_row == 2 else 7


def target_place(n_row, step_row, step_lay, row):
    same = jnp.where(step_lay < 3, step_lay, -1)
    if n_row == 2:
        lead = step_lay - row
        across = jnp.where((lead >= 0) & (lead < 2), 3 + lead, -1)
    else:
        across = 3 + step_lay
    return jnp.where(step_row == 0, same, jnp.where(step_row == 1, across, -1))


class Places:
    def __init__(self, n_row, n_col, n_lay):
        self.n_row, self.n_col, self.n_lay = n_row, n_col, n_lay
        self.lay_bits = n_lay.bit_length() - 1
        self.col_bits = n_col.bit_length() - 1
        self.row = lax.axis_index("row")
        self.col = lax.axis_index("col")
        self.lay = lax.axis_index("layer")
        self.me = (((self.row << self.col_bits) + self.col) << self.lay_bits) + self.lay

    def split(self, atom):
        return (
            atom >> (self.lay_bits + self.col_bits),
            (atom >> self.lay_bits) & (self.n_col - 1),
            atom & (self.n_lay - 1),
        )


def load(sources, targets, sems):
    copies = [pltpu.make_async_copy(a, b, sems.at[i]) for i, (a, b) in enumerate(zip(sources, targets))]
    for copy in copies:
        copy.start()
    for copy in copies:
        copy.wait()


def own_ranks(at, neighbors_ref):
    seen = [jnp.int32(0)] * at.n_lay
    listed = []
    for w in range(neighbors_ref.shape[0]):
        atom = neighbors_ref[w, at.me]
        step_lay = (atom - at.lay) & (at.n_lay - 1)
        rank = jnp.int32(0)
        for k in range(at.n_lay):
            rank = jnp.where(step_lay == k, 3 * k + seen[k], rank)
            seen[k] = seen[k] + (step_lay == k).astype(jnp.int32)
        listed.append((atom, rank))
    return listed


def pick_kernel(axes, *refs):
    sign_ref, out_ref, neighbors_ref, extent_ref, x_ref, y_ref, z_ref, place_ref, loads, sems = refs[5:]
    at = Places(*axes)
    slots = sign_ref.shape[0]
    n_pick = place_ref.shape[0] - 1
    size = sign_ref.shape[1]
    for i in range(n_pick + 1):
        place_ref[i] = 0
    load(refs[:5], (neighbors_ref, extent_ref, x_ref, y_ref, z_ref), loads)
    for w in range(slots):
        row, col, lay = at.split(neighbors_ref[w, at.me])
        place = target_place(at.n_row, (row - at.row) & (at.n_row - 1), (lay - at.lay) & (at.n_lay - 1), at.row)
        place_ref[jnp.where((col == at.col) & (place >= 0), place, n_pick)] = w
    copies = []
    for i in range(n_pick):
        copy = pltpu.make_async_copy(sign_ref.at[place_ref[i]], out_ref.at[pl.ds(i * size, size)], sems.at[i])
        copy.start()
        copies.append(copy)
    ranks = own_ranks(at, neighbors_ref)
    sub = lax.broadcasted_iota(jnp.int32, (GEO, LANES), 0)
    lane_pair = lax.broadcasted_iota(jnp.int32, (GEO, LANES), 1) // SHELLS
    geo = jnp.zeros((GEO, LANES), jnp.int32)
    for w, (atom, rank) in enumerate(ranks):
        row, col, lay = at.split(atom)
        go_row = ((row - at.row + 1) & (at.n_row - 1)) - 1
        go_col = ((col - at.col + 1) & (at.n_col - 1)) - 1
        go_lay = jnp.minimum(((lay - at.lay + 1) & (at.n_lay - 1)) - 1, 1)
        twice_x = x_ref[at.me] + x_ref[atom] + BX * go_row
        twice_y = y_ref[at.me] + y_ref[atom] + BY * go_col
        twice_z = z_ref[at.me] + z_ref[atom] + BZ * go_lay - BZ
        extent = extent_ref[0, w]
        values = jnp.where(sub == 0, twice_x, jnp.where(sub == 1, twice_y, jnp.where(sub == 2, twice_z, extent)))
        geo = jnp.where(lane_pair == rank, values, geo)
    out_ref[n_pick * size :] = geo.astype(jnp.float32).astype(out_ref.dtype)
    for copy in copies:
        copy.wait()


def spread_kernel(axes, *refs):
    basis_ref = refs[1]
    spread_ref, own_basis_ref, neighbors_ref, loads = refs[-4:]
    at = Places(*axes)
    load(refs[:1], (neighbors_ref,), loads)
    slots, atoms = neighbors_ref.shape
    bits = atoms.bit_length() - 1

    def hot(rows, atom, first):
        sub = lax.broadcasted_iota(jnp.int32, (rows, SHELLS * atoms), 0)
        lane = lax.broadcasted_iota(jnp.int32, (rows, SHELLS * atoms), 1)
        return ((lane & (atoms - 1)) == atom) & (sub == first + (lane >> bits))

    def rows_of(chosen):
        picked = jnp.where(chosen, 1.0, 0.0).astype(jnp.bfloat16)
        return jnp.dot(picked, basis_ref[...], preferred_element_type=jnp.float32).astype(jnp.bfloat16)

    for w, (atom, rank) in enumerate(own_ranks(at, neighbors_ref)):
        spread_ref[:, w * LANES : (w + 1) * LANES] = rows_of(hot(LANES, atom, rank * SHELLS))
    own_basis_ref[...] = rows_of(hot(16, at.me, 0))


def prepare_kernel(axes, count, layout, late_from, *refs):
    early_ref, late_ref, info_ref, neighbors_ref, size_ref, known, inverse, layout_ref, loads = refs[-9:]
    at = Places(*axes)
    load(refs[:2], (neighbors_ref, size_ref), loads)
    slots = neighbors_ref.shape[0]
    lines = count * at.n_lay
    for i, value in enumerate(layout):
        layout_ref[i] = value
    self_slot = jnp.int32(0)
    for w in range(slots):
        atom = neighbors_ref[w, at.me]
        row, col, lay = at.split(atom)
        step_row = (row - at.row) & (at.n_row - 1)
        self_slot = jnp.where(atom == at.me, w, self_slot)
        info_ref[w] = size_ref[atom]
        known[0, w] = atom
        known[1, w] = jnp.where(col == at.col, 0, jnp.where(col == (at.col ^ 1), 1, 2))
        known[2, w] = jnp.where(step_row == 0, 0, jnp.where(step_row == 1, 1, 2)) * at.n_lay + (lay ^ at.lay)
        inverse[atom] = -1
    info_ref[slots] = size_ref[at.me]
    info_ref[slots + 1] = self_slot

    def row_of_pairs(v, totals):
        early, late = totals
        atom = known[0, v]
        side = known[1, v]
        line = known[2, v]
        for u in range(slots):
            inverse[neighbors_ref[u, atom]] = v * 16 + u

        def from_row(totals):
            total, late = totals
            for w in range(slots):
                mark = inverse[known[0, w]]
                chosen = ((mark >> 4) == v) & ((known[1, w] != 0) | (v <= w))
                where = layout_ref[line * slots + (mark & 15)]
                is_late = where >= late_from
                entry = v + 16 * w
                early_ref[total + 1] = entry + 256 * where
                late_ref[late + 1] = entry + 256 * (where - late_from)
                total = total + (chosen & ~is_late).astype(jnp.int32)
                late = late + (chosen & is_late).astype(jnp.int32)
            return total, late

        def from_column(totals):
            early, late = totals
            row, _, lay = at.split(atom)
            beside = layout_ref[lines * slots + (side - 1) * lines + line]
            for w in range(slots):
                other = known[0, w]
                mark = inverse[other]
                o_row, _, o_lay = at.split(other)
                d_row = (o_row - row) & (at.n_row - 1)
                d_lay = (o_lay - lay) & (at.n_lay - 1)
                there = target_place(at.n_row, d_row, d_lay, row)
                back = target_place(at.n_row, -d_row & (at.n_row - 1), -d_lay & (at.n_lay - 1), o_row)
                chosen = ((mark >> 4) == v) & (side == known[1, w]) & (there >= 0) & ((back < 0) | (v <= w))
                where = beside + there * LANES
                is_late = where >= late_from
                entry = v + 16 * w
                early_ref[early + 1] = entry + 256 * where
                late_ref[late + 1] = entry + 256 * (where - late_from)
                early = early + (chosen & ~is_late).astype(jnp.int32)
                late = late + (chosen & is_late).astype(jnp.int32)
            return early, late

        return lax.cond(side == 0, from_row, from_column, (early, late))

    totals = lax.fori_loop(0, slots, row_of_pairs, (jnp.int32(0), jnp.int32(0)))
    for ref, total in zip((early_ref, late_ref), totals):
        ref[0] = (total + UNROLL - 1) // UNROLL
        for i in range(UNROLL - 1):
            ref[total + i + 1] = ref[jnp.maximum(total, 1)]


def pack_kernel(moves, inputs, *refs):
    for source, start, rows, target, place in moves:
        refs[inputs + target][place : place + rows] = refs[source][start : start + rows]


def pack(values, plans, extra, name, cost=0):
    moves, shapes = [], []
    for target, plan in enumerate(plans):
        place = 0
        for source, start, rows in plan:
            moves.append((source, start, rows, target, place))
            place += rows
        shapes.append(jax.ShapeDtypeStruct((place, LANES), values[0].dtype))
    inputs = len(values) + len(extra)
    return pl.pallas_call(
        functools.partial(pack_kernel, tuple(moves), inputs),
        out_shape=tuple(shapes),
        in_specs=[VMEM] * len(values) + [ANY] * len(extra),
        out_specs=tuple([VMEM] * len(plans)),
        compiler_params=pltpu.CompilerParams(
            vmem_limit_bytes=(1 << 20) + 256 * sum(x.shape[0] for x in list(values) + shapes)
        ),
        cost_estimate=pl.CostEstimate(flops=cost, bytes_accessed=1000, transcendentals=0),
        name=name,
    )(*values, *extra)


def fill(piece_refs, pool):
    place = 0
    for piece in piece_refs:
        rows = piece.shape[0]
        pool[place : place + rows] = piece[...]
        place += rows


def place_pairs(table_ref, pool, gram, size):
    def place(i, carry):
        for k in range(UNROLL):
            entry = table_ref[i * UNROLL + k + 1]
            p = pl.multiple_of((entry & 15) * size, size)
            q = pl.multiple_of(((entry >> 4) & 15) * size, size)
            block = pool[pl.ds(pl.multiple_of(entry >> 8, 16), size)]
            gram[pl.ds(p, size), pl.ds(q, size)] = block
            gram[pl.ds(q, size), pl.ds(p, size)] = block.T
        return carry

    lax.fori_loop(0, table_ref[0], place, 0)


def gram_kernel(pieces, *refs):
    table_ref = refs[0]
    piece_refs = refs[1 : 1 + pieces]
    gram, pool = refs[-2:]
    size = LANES
    fill(piece_refs, pool)
    for v in range(gram.shape[0] // size):
        gram[v * size : (v + 1) * size] = jnp.zeros((size, gram.shape[1]), gram.dtype)
    place_pairs(table_ref, pool, gram, size)


def step_kernel(pieces, *refs):
    table_ref, info_ref, basis_ref, spread_ref, sign_ref, early_ref = refs[:6]
    piece_refs = refs[6 : 6 + pieces]
    next_ref, coef_ref, pool, gram, own, square = refs[-6:]
    slots, size = sign_ref.shape[0], sign_ref.shape[1]
    fill(piece_refs, pool)
    for v in range(slots):
        gram[v * size : (v + 1) * size] = early_ref[v * size : (v + 1) * size]
    rows = lax.broadcasted_iota(jnp.int32, (size, size), 0)
    lanes = lax.broadcasted_iota(jnp.int32, (size, size), 1)
    own_size = info_ref[slots]
    self_slot = info_ref[slots + 1]
    for w in range(slots):
        kept = (rows < own_size) & (lanes < info_ref[w])
        block = jnp.where(kept, sign_ref[w].astype(jnp.float32), 0.0)
        own[:, w * size : (w + 1) * size] = block.astype(own.dtype)
    place_pairs(table_ref, pool, gram, size)
    wide = 2 * size
    wide_lanes = lax.broadcasted_iota(jnp.int32, (size, wide), 1)
    wide_rows = lax.broadcasted_iota(jnp.int32, (size, wide), 0)

    def column_kept(n):
        first = info_ref[2 * n]
        second = info_ref[2 * n + 1]
        return (wide_lanes < first) | ((wide_lanes >= size) & (wide_lanes < size + second))

    for n in range(slots // 2):
        part = jnp.dot(own[...], gram[:, n * wide : (n + 1) * wide], preferred_element_type=jnp.float32)
        square[:, n * wide : (n + 1) * wide] = jnp.where(column_kept(n), part, 0.0).astype(square.dtype)
    basis = jnp.concatenate([basis_ref[...], basis_ref[...]], axis=1)
    coef = jnp.zeros((2 * basis_ref.shape[0], LANES), jnp.float32)
    across = (((1,), (1,)), ((), ()))
    for n in range(slots // 2):
        part = jnp.dot(square[...], gram[:, n * wide : (n + 1) * wide], preferred_element_type=jnp.float32)
        cube = jnp.where(column_kept(n), part, 0.0)
        full = 1.5 * own[:, n * wide : (n + 1) * wide].astype(jnp.float32) - 0.5 * cube
        next_ref[2 * n] = full[:, :size].astype(next_ref.dtype)
        next_ref[2 * n + 1] = full[:, size:].astype(next_ref.dtype)
        shift = (self_slot - 2 * n) * size
        is_self = (self_slot >= 2 * n) & (self_slot < 2 * n + 2)
        diag = (wide_lanes == wide_rows + shift) & (wide_rows < own_size) & is_self
        dmat = 0.5 * (jnp.where(diag, 1.0, 0.0) - full)
        high = dmat.astype(jnp.bfloat16)
        low = (dmat - high.astype(jnp.float32)).astype(jnp.bfloat16)
        half = jnp.dot(basis, jnp.concatenate([high, low], axis=0), preferred_element_type=jnp.float32)
        half_high = half.astype(jnp.bfloat16)
        half_low = (half - half_high.astype(jnp.float32)).astype(jnp.bfloat16)
        coef = coef + lax.dot_general(
            jnp.concatenate([half_high, half_low], axis=0),
            spread_ref[:, n * wide : (n + 1) * wide],
            across,
            preferred_element_type=jnp.float32,
        )
    coef = coef[: basis_ref.shape[0]] + coef[basis_ref.shape[0] :]
    coef_ref[...] = coef[: coef_ref.shape[0]]


def profile_kernel(periods, steps, mate_from, *refs):
    own_ref, mate_ref, third_ref = refs[:3]
    plane_ref, line_ref, geos, sems = refs[-4:]
    odd = (lax.axis_index("layer") & 1) == 1
    rows = len(steps) * GEO
    copies = []
    for k, source in enumerate((own_ref, mate_ref.at[pl.ds(mate_from, rows)], third_ref)):
        copy = pltpu.make_async_copy(source, geos.at[k], sems.at[k])
        copy.start()
        copies.append(copy)
    steps_x = lax.broadcasted_iota(jnp.int32, (BX, LANES), 0).astype(jnp.float32)
    steps_y = lax.broadcasted_iota(jnp.int32, (BY, LANES), 0).astype(jnp.float32)
    grid_z = lax.broadcasted_iota(jnp.int32, (LANES, BZ), 1).astype(jnp.float32)
    lane = lax.broadcasted_iota(jnp.int32, (1, LANES), 1)
    shell = (lane % SHELLS + 1).astype(jnp.float32)
    valid = lane < 7 * SPAN
    from_own = lane < 4 * SPAN
    from_below = lane < 6 * SPAN
    lift = jnp.where(from_own, 0.0, jnp.where(from_below, -float(BZ), float(BZ))) + 0.5 * BZ

    def nearest(offset, period):
        return offset - period * jnp.floor(offset * (1.0 / period) + 0.5)

    for copy in copies:
        copy.wait()
    ahead = 1.0 - 2.0 * (lax.axis_index("col") & 1).astype(jnp.float32)
    for o, (step_row, side) in enumerate(steps):
        own, first, third = (geos[k, o * GEO : (o + 1) * GEO].astype(jnp.float32) for k in range(3))
        below = jnp.where(odd, first, third)
        above = jnp.where(odd, third, first)
        moved = jnp.where(from_below, pltpu.roll(below, 3 * SPAN, axis=1), pltpu.roll(above, 3 * SPAN, axis=1))
        geo = jnp.where(from_own, own, moved)
        extent = jnp.where(valid, geo[3:4], 1.0)
        inverse = (SHELLS / extent) * (SHELLS / extent)
        reach = jnp.where(valid, extent, -1.0)
        rate_t = inverse / (shell * shell)
        packed = jnp.concatenate(
            [0.5 * geo[2:3] + lift, reach, rate_t, inverse, jnp.zeros((4, LANES), jnp.float32)], axis=0
        )
        sub = packed.T
        d_x = nearest(steps_x - (0.5 * geo[0:1] + float(BX * step_row)), periods[0])
        d_y = nearest(steps_y - (0.5 * geo[1:2] + float(BY * side) * ahead), periods[1])
        inside_x = jnp.abs(d_x) <= reach
        inside_y = jnp.abs(d_y) <= reach
        squared_x = d_x * d_x
        squared_y = d_y * d_y
        d_z = nearest(grid_z - sub[:, 0:1], periods[2])
        inside_z = jnp.abs(d_z) <= sub[:, 1:2]
        squared_z = d_z * d_z
        for s in range(SHELLS):
            part = 1.0 / ((s + 1) * (s + 1))
            rate = inverse * part + rate_t
            along_x = jnp.where(inside_x, jnp.exp(-rate * squared_x), 0.0)
            along_y = jnp.where(inside_y, jnp.exp(-rate * squared_y), 0.0)
            for x in range(BX):
                plane_ref[o, s, x * BY : (x + 1) * BY] = (along_x[x : x + 1] * along_y).astype(plane_ref.dtype)
            rate_z = sub[:, 3:4] * part + sub[:, 2:3]
            line_ref[o, s] = jnp.where(inside_z, jnp.exp(-rate_z * squared_z), 0.0).astype(line_ref.dtype)


def density_kernel(column_steps, *refs):
    coef_refs = refs[:column_steps]
    plane_ref, line_ref = refs[column_steps : column_steps + 2]
    out_ref, terms = refs[-2:]
    for o in range(plane_ref.shape[0]):
        coef = coef_refs[-o % column_steps]
        first = 8 * (o // column_steps)
        for s in range(SHELLS):
            scaled = plane_ref[o, s].astype(jnp.float32) * coef[first + s : first + s + 1, :]
            at = (o * SHELLS + s) * LANES
            terms[:, at : at + LANES] = scaled.astype(terms.dtype)
    out_ref[...] = jnp.dot(terms[...], line_ref[...], preferred_element_type=jnp.float32)


def local(sign_start, neighbors, atom_size, basis_proj, pair_extent, atom_x, atom_y, atom_z):
    n_row = lax.axis_size("row")
    n_col = lax.axis_size("col")
    n_lay = lax.axis_size("layer")
    assert n_lay == 4 and n_col >= 4 and (n_row == 2 or n_row >= 4)
    assert n_row & (n_row - 1) == 0 and n_col & (n_col - 1) == 0
    axes = (n_row, n_col, n_lay)
    atoms, slots = neighbors.shape
    size = sign_start.shape[2]
    steps = [0, 1] if n_row == 2 else [0, 1, -1]
    count = len(steps)
    others = range(1, count)
    own = sign_start[0]
    flat = own.reshape(slots * size, size)
    listings = neighbors.T
    full = slots * size
    half = full // 2
    most = half - size
    n_pick = column_targets(n_row)
    picks = n_pick * size
    part = picks + GEO

    def on_row(value, di):
        return from_offset(value, "row", steps[di])

    x_row = {di: on_row(flat, di) for di in others}
    y_row = from_layer(flat, 2)
    m_row = from_layer(flat, 1)
    picked = pl.pallas_call(
        functools.partial(pick_kernel, axes),
        out_shape=jax.ShapeDtypeStruct((part, size), own.dtype),
        in_specs=[HBM] * 6,
        out_specs=VMEM,
        scratch_shapes=[
            pltpu.SMEM((slots, atoms), jnp.int32),
            pltpu.SMEM((1, slots), jnp.int32),
            pltpu.SMEM((atoms,), jnp.int32),
            pltpu.SMEM((atoms,), jnp.int32),
            pltpu.SMEM((atoms,), jnp.int32),
            pltpu.SMEM((n_pick + 1,), jnp.int32),
            pltpu.SemaphoreType.DMA((5,)),
            pltpu.SemaphoreType.DMA((n_pick,)),
        ],
        compiler_params=pltpu.CompilerParams(vmem_limit_bytes=60 << 20),
        name="pick_column_blocks",
    )(listings, pair_extent, atom_x, atom_y, atom_z, own)
    down = from_column(picked, 1)
    up = from_column(picked, 0)

    halves = pack(
        [y_row] + [x_row[di] for di in others] + [picked],
        [[(0, half, most)]] + [[(di, 0, most)] for di in others] + [[(count, picks, GEO)]],
        [],
        "pack_halves",
    )
    ends = {di: on_row(halves[0], di) for di in others}
    tops = {di: from_layer(halves[di], 2) for di in others}

    at = {}
    buffers = {}

    def note(name, value, contents):
        buffers[name] = value
        start = 0
        for what, rows in contents:
            if what is not None:
                at[what] = (name, start)
            start += rows

    def row_of(di, flip, start=0, stop=slots):
        return [(("row", slot, di, flip), size) for slot in range(start, stop)]

    halfway = slots // 2

    def side_of(kind, di, flip):
        return [((kind, di, flip), picks)]

    note("own", flat, row_of(0, 0))
    note("mate", m_row, row_of(0, 1))
    note("far", y_row, row_of(0, 2))
    note("up", up, side_of("up", 0, 0) + [(("up geo", 0, 0), GEO)])
    note("down", down, side_of("down", 0, 0) + [(("down geo", 0, 0), GEO)])
    note("geo", halves[count], [(("geo", 0, 0), GEO)])
    for di in others:
        note(("x", di), x_row[di], row_of(di, 0))
        note(("end", di), ends[di], row_of(di, 2, halfway, slots - 1))
        note(("top", di), tops[di], row_of(di, 2, 0, halfway - 1))

    corners = [("end", di) for di in others] + [("top", di) for di in others]
    names = ["down", "up", "geo", "far"] + [("x", di) for di in others]
    plans = [
        [(1, 0, picks), (0, 0, picks), (3, full - size, size), (2, 0, GEO), (1, picks, GEO), (0, picks, GEO)],
        [(1, 0, picks), (0, 0, picks)] + [(di + 3, most, size) for di in others] + [(2, 0, GEO), (1, picks, GEO), (0, picks, GEO)],
        [(2, 0, GEO), (1, picks, GEO), (0, picks, GEO)],
    ]
    two_x, two_y, geos = pack([buffers[name] for name in names], plans, [m_row], "pack_two")
    to_mate = corners + ["up", "down"]
    for di in others:
        note(("mate x", di), from_layer(x_row[di], 1), row_of(di, 1))
    note("mate far", from_layer(y_row, 1), row_of(0, 3))

    early_order = ["own", "mate", "far", "up", "down", "geo"] + [("x", di) for di in others]
    early_order += [("mate x", di) for di in others] + ["mate far"]
    early_order += corners + [("two x", di) for di in others] + ["two y", "two m"]
    late_order = [("three x", di) for di in others] + ["three y", "three m"]
    late_order += ["four"]

    contents = {}
    for di in others:
        contents["two x", di] = side_of("up", di, 0) + side_of("down", di, 0)
        contents["two x", di] += row_of(di, 2, slots - 1, slots) + [(("geo", di, 0), GEO)]
        contents["two x", di] += [(("up geo", di, 0), GEO), (("down geo", di, 0), GEO)]
    contents["two y"] = side_of("up", 0, 2) + side_of("down", 0, 2)
    contents["two y"] += sum([row_of(di, 2, halfway - 1, halfway) for di in others], []) + [(None, 3 * GEO)]
    contents["two m"] = sum([row_of(di, 3, halfway, slots - 1) for di in others], [])
    contents["two m"] += sum([row_of(di, 3, 0, halfway - 1) for di in others], [])
    contents["two m"] += side_of("up", 0, 1) + side_of("down", 0, 1)
    for di in others:
        contents["three x", di] = side_of("up", di, 2)
    contents["three y"] = sum([side_of("down", di, 2) for di in others], [])
    contents["three m"] = []
    for di in others:
        contents["three m"] += side_of("up", di, 1) + side_of("down", di, 1) + row_of(di, 3, slots - 1, slots)
    contents["three m"] += side_of("up", 0, 3) + side_of("down", 0, 3)
    contents["three m"] += sum([row_of(di, 3, halfway - 1, halfway) for di in others], []) + [(None, 3 * GEO)]
    contents["three m"] += [("geos", count * 3 * GEO)]
    contents["four"] = sum([side_of("up", di, 3) for di in others], [])
    contents["four"] += sum([side_of("down", di, 3) for di in others], [])
    lengths = {name: sum(rows for _, rows in content) for name, content in contents.items()}
    for name in early_order:
        if name in buffers:
            lengths[name] = buffers[name].shape[0]
    base = {}
    total = 0
    for name in early_order + late_order:
        base[name] = total
        total += lengths[name]
        if name == early_order[-1]:
            late_from = total
    located = dict(at)
    for name, content in contents.items():
        start = 0
        for what, rows in content:
            located[what] = (name, start)
            start += rows
    layout = [
        base[located["row", slot, di, flip][0]] + located["row", slot, di, flip][1]
        for di in range(count)
        for flip in range(n_lay)
        for slot in range(slots)
    ]
    layout += [
        base[located[kind, di, flip][0]] + located[kind, di, flip][1]
        for kind in ("up", "down")
        for di in range(count)
        for flip in range(n_lay)
    ]
    pairs = slots * (slots + 1) // 2
    entries = pairs + UNROLL + 1
    early_table, late_table, info = pl.pallas_call(
        functools.partial(prepare_kernel, axes, count, tuple(layout), late_from),
        out_shape=(
            jax.ShapeDtypeStruct((entries,), jnp.int32),
            jax.ShapeDtypeStruct((entries,), jnp.int32),
            jax.ShapeDtypeStruct((slots + 2,), jnp.int32),
        ),
        in_specs=[HBM, HBM, ANY],
        out_specs=(SMEM, SMEM, SMEM),
        scratch_shapes=[
            pltpu.SMEM((slots, atoms), jnp.int32),
            pltpu.SMEM((atoms,), jnp.int32),
            pltpu.SMEM((3, slots), jnp.int32),
            pltpu.SMEM((atoms,), jnp.int32),
            pltpu.SMEM((len(layout),), jnp.int32),
            pltpu.SemaphoreType.DMA((2,)),
        ],
        compiler_params=pltpu.CompilerParams(vmem_limit_bytes=1 << 20),
        cost_estimate=pl.CostEstimate(flops=1000, bytes_accessed=1000, transcendentals=0),
        name="prepare",
    )(listings, atom_size, two_x)

    plans = [[(i, 0, picks if name in ("up", "down") else most) for i, name in enumerate(to_mate)]]
    two_m = pack([buffers[name] for name in to_mate], plans, [], "pack_two_mate", 3_000_000_000)[0]
    for di in others:
        note(("two x", di), on_row(two_x, di), contents["two x", di])
    note("two y", from_layer(two_y, 2), contents["two y"])
    early_mates = ["mate far"] + [("mate x", di) for di in others]
    note("two m", from_layer(two_m, 1), contents["two m"])

    buffers["geos"] = geos
    names = ["two y", "geos"] + [("two x", di) for di in others]
    place = {name: i for i, name in enumerate(names)}
    gather = [(place["geos"], 0, 3 * GEO)] + [(place["two x", di], 2 * picks + size, 3 * GEO) for di in others]
    xs = [place["two x", di] for di in others]
    plans = [
        [(0, 0, picks)],
        [(x, picks, picks) for x in xs],
        [(x, 0, 2 * picks + size) for x in xs] + [(0, 0, lengths["two y"])] + gather,
        gather,
    ]
    three_x, three_y, three_m, geos = pack([buffers[name] for name in names], plans, [buffers[name] for name in early_mates] + [two_m, info], "pack_three")
    for di in others:
        note(("three x", di), on_row(three_x, di), contents["three x", di])
    note("three y", from_layer(three_y, 2), contents["three y"])
    note("three m", from_layer(three_m, 1), contents["three m"])
    third_geos = from_layer(geos, 3)

    spread, own_basis = pl.pallas_call(
        functools.partial(spread_kernel, axes),
        out_shape=(
            jax.ShapeDtypeStruct((LANES, full), jnp.bfloat16),
            jax.ShapeDtypeStruct((16, size), jnp.bfloat16),
        ),
        in_specs=[HBM, VMEM, ANY],
        out_specs=(VMEM, VMEM),
        scratch_shapes=[pltpu.SMEM((slots, atoms), jnp.int32), pltpu.SemaphoreType.DMA((1,))],
        compiler_params=pltpu.CompilerParams(vmem_limit_bytes=(2 << 20) + atoms * 16384),
        cost_estimate=pl.CostEstimate(flops=1000, bytes_accessed=1000, transcendentals=0),
        name="spread_basis",
    )(listings, basis_proj.transpose(1, 0, 2).reshape(SHELLS * atoms, size), three_x)

    early_values = [buffers[name] for name in early_order]
    gram = pl.pallas_call(
        functools.partial(gram_kernel, len(early_values)),
        out_shape=jax.ShapeDtypeStruct((full, full), jnp.bfloat16),
        in_specs=[SMEM] + [VMEM] * len(early_values) + [ANY],
        out_specs=VMEM,
        scratch_shapes=[pltpu.VMEM((late_from, LANES), jnp.bfloat16)],
        compiler_params=pltpu.CompilerParams(vmem_limit_bytes=(6 << 20) + 2 * late_from * LANES * 2),
        cost_estimate=pl.CostEstimate(flops=1000, bytes_accessed=1000, transcendentals=0),
        name="gram_early",
    )(early_table, *early_values, three_x)

    thirds = [buffers["three x", di] for di in others] + [buffers["three y"]]
    four = pack(thirds, [[(i, 0, value.shape[0]) for i, value in enumerate(thirds)]], [gram, third_geos, own_basis], "pack_four")[0]
    note("four", from_layer(four, 1), contents["four"])

    column_steps = (0, 1, -1)
    tile_steps = [(dr, dc) for dr in steps for dc in column_steps]
    tiles = len(tile_steps)
    periods = (float(BX * n_row), float(BY * n_col), float(BZ * n_lay))
    plane, line = pl.pallas_call(
        functools.partial(profile_kernel, periods, tile_steps, at["geos"][1]),
        out_shape=(
            jax.ShapeDtypeStruct((tiles, SHELLS, BX * BY, LANES), jnp.bfloat16),
            jax.ShapeDtypeStruct((tiles, SHELLS, LANES, BZ), jnp.bfloat16),
        ),
        in_specs=[ANY] * 3,
        out_specs=(VMEM, VMEM),
        scratch_shapes=[
            pltpu.VMEM((3, tiles * GEO, LANES), jnp.bfloat16),
            pltpu.SemaphoreType.DMA((3,)),
        ],
        compiler_params=pltpu.CompilerParams(vmem_limit_bytes=10 << 20),
        cost_estimate=pl.CostEstimate(flops=1000, bytes_accessed=1000, transcendentals=0),
        name="profiles",
    )(geos, buffers["three m"], third_geos)

    late_values = [buffers[name] for name in late_order]
    sign_next, coef = pl.pallas_call(
        functools.partial(step_kernel, len(late_values)),
        out_shape=(
            jax.ShapeDtypeStruct((slots, size, size), jnp.bfloat16),
            jax.ShapeDtypeStruct((8, LANES), jnp.float32),
        ),
        in_specs=[SMEM, SMEM, VMEM, VMEM, VMEM, VMEM] + [VMEM] * len(late_values),
        out_specs=(VMEM, VMEM),
        scratch_shapes=[
            pltpu.VMEM((total - late_from, LANES), jnp.bfloat16),
            pltpu.VMEM((full, full), jnp.bfloat16),
            pltpu.VMEM((size, full), jnp.bfloat16),
            pltpu.VMEM((size, full), jnp.bfloat16),
        ],
        compiler_params=pltpu.CompilerParams(vmem_limit_bytes=(15 << 20) + 2 * (total - late_from) * LANES * 2),
        cost_estimate=pl.CostEstimate(flops=1_300_000_000, bytes_accessed=8_000_000, transcendentals=0),
        name="square_cube_coefficients",
    )(late_table, info, own_basis, spread, own, gram, *late_values)

    mate_coef = from_layer(coef, 1)
    third_coef = from_layer(coef, 3)
    odd = lax.axis_index("layer") % 2 == 1
    below = jnp.where(odd, mate_coef, third_coef)
    above = jnp.where(odd, third_coef, mate_coef)
    merged = jnp.concatenate(
        [
            coef[:, : 4 * SPAN],
            below[:, SPAN : 3 * SPAN],
            above[:, 3 * SPAN : 4 * SPAN],
            jnp.zeros((8, LANES - 7 * SPAN), jnp.float32),
        ],
        axis=1,
    )
    given, token = pack([sign_next.reshape(full, size)], [[(0, 0, full)], [(0, 0, GEO)]], [], "give_sign")
    parts = [merged] + [on_row(merged, di) for di in others]
    stacked = pack(parts, [[(i, 0, 8) for i in range(count)]], [token], "stack_tiles")[0]
    far_side = from_column(stacked, 1)
    received = [stacked, far_side, from_column(stacked, 0)]

    density = pl.pallas_call(
        functools.partial(density_kernel, len(column_steps)),
        out_shape=jax.ShapeDtypeStruct((BX * BY, BZ), jnp.float32),
        in_specs=[VMEM] * (len(received) + 2),
        out_specs=VMEM,
        scratch_shapes=[pltpu.VMEM((BX * BY, tiles * SHELLS * LANES), jnp.bfloat16)],
        compiler_params=pltpu.CompilerParams(vmem_limit_bytes=16 << 20),
        cost_estimate=pl.CostEstimate(flops=310_000_000, bytes_accessed=4_000_000, transcendentals=0),
        name="density",
    )(*received, plane, line.reshape(tiles * SHELLS * LANES, BZ))
    return given.reshape(1, slots, size, size), density.reshape(BX, BY, BZ)


def solution(mesh):
    rows = P(("row", "col", "layer"), None, None, None)
    in_specs = (rows, P(), P(), P(), P(("row", "col", "layer"), None), P(), P(), P())
    out_specs = (rows, P("row", "col", "layer"))
    return jax.shard_map(local, mesh=mesh, in_specs=in_specs, out_specs=out_specs, check_vma=False)
```

```python
import functools

import jax
import jax.numpy as jnp
from jax import lax
from jax.experimental import pallas as pl
from jax.experimental.pallas import tpu as pltpu
from jax.sharding import PartitionSpec as P

BX = 16
BY = 16
BZ = 128
LANES = 128
UNROLL = 4
SHELLS = 6
SPAN = 3 * SHELLS
GEO = 16
VMEM = pl.BlockSpec(memory_space=pltpu.VMEM)
SMEM = pl.BlockSpec(memory_space=pltpu.SMEM)
ANY = pl.BlockSpec(memory_space=pl.ANY)
HBM = pl.BlockSpec(memory_space=pltpu.HBM)


def from_offset(x, axis, step):
    count = lax.axis_size(axis)
    return lax.ppermute(x, axis, [((i + step) % count, i) for i in range(count)])


def from_column(x, side):
    count = lax.axis_size("col")
    step = [1 if (i + side) % 2 == 0 else -1 for i in range(count)]
    return lax.ppermute(x, "col", [((i + step[i]) % count, i) for i in range(count)])


def from_layer(x, flip):
    count = lax.axis_size("layer")
    return lax.ppermute(x, "layer", [(i ^ flip, i) for i in range(count)])


def column_targets(n_row):
    return 5 if n_row == 2 else 7


def target_place(n_row, step_row, step_lay, row):
    same = jnp.where(step_lay < 3, step_lay, -1)
    if n_row == 2:
        lead = step_lay - row
        across = jnp.where((lead >= 0) & (lead < 2), 3 + lead, -1)
    else:
        across = 3 + step_lay
    return jnp.where(step_row == 0, same, jnp.where(step_row == 1, across, -1))


class Places:
    def __init__(self, n_row, n_col, n_lay):
        self.n_row, self.n_col, self.n_lay = n_row, n_col, n_lay
        self.lay_bits = n_lay.bit_length() - 1
        self.col_bits = n_col.bit_length() - 1
        self.row = lax.axis_index("row")
        self.col = lax.axis_index("col")
        self.lay = lax.axis_index("layer")
        self.me = (((self.row << self.col_bits) + self.col) << self.lay_bits) + self.lay

    def split(self, atom):
        return (
            atom >> (self.lay_bits + self.col_bits),
            (atom >> self.lay_bits) & (self.n_col - 1),
            atom & (self.n_lay - 1),
        )


def load(sources, targets, sems):
    copies = [pltpu.make_async_copy(a, b, sems.at[i]) for i, (a, b) in enumerate(zip(sources, targets))]
    for copy in copies:
        copy.start()
    for copy in copies:
        copy.wait()


def own_ranks(at, neighbors_ref):
    seen = [jnp.int32(0)] * at.n_lay
    listed = []
    for w in range(neighbors_ref.shape[0]):
        atom = neighbors_ref[w, at.me]
        step_lay = (atom - at.lay) & (at.n_lay - 1)
        rank = jnp.int32(0)
        for k in range(at.n_lay):
            rank = jnp.where(step_lay == k, 3 * k + seen[k], rank)
            seen[k] = seen[k] + (step_lay == k).astype(jnp.int32)
        listed.append((atom, rank))
    return listed


def pick_kernel(axes, *refs):
    sign_ref, out_ref, neighbors_ref, extent_ref, x_ref, y_ref, z_ref, place_ref, loads, sems = refs[5:]
    at = Places(*axes)
    slots = sign_ref.shape[0]
    n_pick = place_ref.shape[0] - 1
    size = sign_ref.shape[1]
    for i in range(n_pick + 1):
        place_ref[i] = 0
    load(refs[:5], (neighbors_ref, extent_ref, x_ref, y_ref, z_ref), loads)
    for w in range(slots):
        row, col, lay = at.split(neighbors_ref[w, at.me])
        place = target_place(at.n_row, (row - at.row) & (at.n_row - 1), (lay - at.lay) & (at.n_lay - 1), at.row)
        place_ref[jnp.where((col == at.col) & (place >= 0), place, n_pick)] = w
    copies = []
    for i in range(n_pick):
        copy = pltpu.make_async_copy(sign_ref.at[place_ref[i]], out_ref.at[pl.ds(i * size, size)], sems.at[i])
        copy.start()
        copies.append(copy)
    ranks = own_ranks(at, neighbors_ref)
    sub = lax.broadcasted_iota(jnp.int32, (GEO, LANES), 0)
    lane_pair = lax.broadcasted_iota(jnp.int32, (GEO, LANES), 1) // SHELLS
    geo = jnp.zeros((GEO, LANES), jnp.int32)
    for w, (atom, rank) in enumerate(ranks):
        row, col, lay = at.split(atom)
        go_row = ((row - at.row + 1) & (at.n_row - 1)) - 1
        go_col = ((col - at.col + 1) & (at.n_col - 1)) - 1
        go_lay = jnp.minimum(((lay - at.lay + 1) & (at.n_lay - 1)) - 1, 1)
        twice_x = x_ref[at.me] + x_ref[atom] + BX * go_row
        twice_y = y_ref[at.me] + y_ref[atom] + BY * go_col
        twice_z = z_ref[at.me] + z_ref[atom] + BZ * go_lay - BZ
        extent = extent_ref[0, w]
        values = jnp.where(sub == 0, twice_x, jnp.where(sub == 1, twice_y, jnp.where(sub == 2, twice_z, extent)))
        geo = jnp.where(lane_pair == rank, values, geo)
    out_ref[n_pick * size :] = geo.astype(jnp.float32).astype(out_ref.dtype)
    for copy in copies:
        copy.wait()


def spread_kernel(axes, *refs):
    basis_ref = refs[1]
    spread_ref, own_basis_ref, neighbors_ref, loads = refs[-4:]
    at = Places(*axes)
    load(refs[:1], (neighbors_ref,), loads)
    slots, atoms = neighbors_ref.shape
    bits = atoms.bit_length() - 1

    def hot(rows, atom, first):
        sub = lax.broadcasted_iota(jnp.int32, (rows, SHELLS * atoms), 0)
        lane = lax.broadcasted_iota(jnp.int32, (rows, SHELLS * atoms), 1)
        return ((lane & (atoms - 1)) == atom) & (sub == first + (lane >> bits))

    def rows_of(chosen):
        picked = jnp.where(chosen, 1.0, 0.0).astype(jnp.bfloat16)
        return jnp.dot(picked, basis_ref[...], preferred_element_type=jnp.float32).astype(jnp.bfloat16)

    for w, (atom, rank) in enumerate(own_ranks(at, neighbors_ref)):
        spread_ref[:, w * LANES : (w + 1) * LANES] = rows_of(hot(LANES, atom, rank * SHELLS))
    own_basis_ref[...] = rows_of(hot(16, at.me, 0))


def prepare_kernel(axes, count, layout, late_from, *refs):
    early_ref, late_ref, info_ref, neighbors_ref, size_ref, known, inverse, layout_ref, loads = refs[-9:]
    at = Places(*axes)
    load(refs[:2], (neighbors_ref, size_ref), loads)
    slots = neighbors_ref.shape[0]
    lines = count * at.n_lay
    for i, value in enumerate(layout):
        layout_ref[i] = value
    self_slot = jnp.int32(0)
    for w in range(slots):
        atom = neighbors_ref[w, at.me]
        row, col, lay = at.split(atom)
        step_row = (row - at.row) & (at.n_row - 1)
        self_slot = jnp.where(atom == at.me, w, self_slot)
        info_ref[w] = size_ref[atom]
        known[0, w] = atom
        known[1, w] = jnp.where(col == at.col, 0, jnp.where(col == (at.col ^ 1), 1, 2))
        known[2, w] = jnp.where(step_row == 0, 0, jnp.where(step_row == 1, 1, 2)) * at.n_lay + (lay ^ at.lay)
        inverse[atom] = -1
    info_ref[slots] = size_ref[at.me]
    info_ref[slots + 1] = self_slot

    def row_of_pairs(v, totals):
        early, late = totals
        atom = known[0, v]
        side = known[1, v]
        line = known[2, v]
        for u in range(slots):
            inverse[neighbors_ref[u, atom]] = v * 16 + u

        def from_row(totals):
            total, late = totals
            for w in range(slots):
                mark = inverse[known[0, w]]
                chosen = ((mark >> 4) == v) & ((known[1, w] != 0) | (v <= w))
                where = layout_ref[line * slots + (mark & 15)]
                is_late = where >= late_from
                entry = v + 16 * w
                early_ref[total + 1] = entry + 256 * where
                late_ref[late + 1] = entry + 256 * (where - late_from)
                total = total + (chosen & ~is_late).astype(jnp.int32)
                late = late + (chosen & is_late).astype(jnp.int32)
            return total, late

        def from_column(totals):
            early, late = totals
            row, _, lay = at.split(atom)
            beside = layout_ref[lines * slots + (side - 1) * lines + line]
            for w in range(slots):
                other = known[0, w]
                mark = inverse[other]
                o_row, _, o_lay = at.split(other)
                d_row = (o_row - row) & (at.n_row - 1)
                d_lay = (o_lay - lay) & (at.n_lay - 1)
                there = target_place(at.n_row, d_row, d_lay, row)
                back = target_place(at.n_row, -d_row & (at.n_row - 1), -d_lay & (at.n_lay - 1), o_row)
                chosen = ((mark >> 4) == v) & (side == known[1, w]) & (there >= 0) & ((back < 0) | (v <= w))
                where = beside + there * LANES
                is_late = where >= late_from
                entry = v + 16 * w
                early_ref[early + 1] = entry + 256 * where
                late_ref[late + 1] = entry + 256 * (where - late_from)
                early = early + (chosen & ~is_late).astype(jnp.int32)
                late = late + (chosen & is_late).astype(jnp.int32)
            return early, late

        return lax.cond(side == 0, from_row, from_column, (early, late))

    totals = lax.fori_loop(0, slots, row_of_pairs, (jnp.int32(0), jnp.int32(0)))
    for ref, total in zip((early_ref, late_ref), totals):
        ref[0] = (total + UNROLL - 1) // UNROLL
        for i in range(UNROLL - 1):
            ref[total + i + 1] = ref[jnp.maximum(total, 1)]


def pack_kernel(moves, inputs, *refs):
    for source, start, rows, target, place in moves:
        refs[inputs + target][place : place + rows] = refs[source][start : start + rows]


def pack(values, plans, extra, name, cost=0):
    moves, shapes = [], []
    for target, plan in enumerate(plans):
        place = 0
        for source, start, rows in plan:
            moves.append((source, start, rows, target, place))
            place += rows
        shapes.append(jax.ShapeDtypeStruct((place, LANES), values[0].dtype))
    inputs = len(values) + len(extra)
    return pl.pallas_call(
        functools.partial(pack_kernel, tuple(moves), inputs),
        out_shape=tuple(shapes),
        in_specs=[VMEM] * len(values) + [ANY] * len(extra),
        out_specs=tuple([VMEM] * len(plans)),
        compiler_params=pltpu.CompilerParams(
            vmem_limit_bytes=(1 << 20) + 256 * sum(x.shape[0] for x in list(values) + shapes)
        ),
        cost_estimate=pl.CostEstimate(flops=cost, bytes_accessed=1000, transcendentals=0),
        name=name,
    )(*values, *extra)


def fill(piece_refs, pool):
    place = 0
    for piece in piece_refs:
        rows = piece.shape[0]
        pool[place : place + rows] = piece[...]
        place += rows


def place_pairs(table_ref, pool, gram, size):
    def place(i, carry):
        for k in range(UNROLL):
            entry = table_ref[i * UNROLL + k + 1]
            p = pl.multiple_of((entry & 15) * size, size)
            q = pl.multiple_of(((entry >> 4) & 15) * size, size)
            block = pool[pl.ds(pl.multiple_of(entry >> 8, 16), size)]
            gram[pl.ds(p, size), pl.ds(q, size)] = block
            gram[pl.ds(q, size), pl.ds(p, size)] = block.T
        return carry

    lax.fori_loop(0, table_ref[0], place, 0)


def gram_kernel(pieces, *refs):
    table_ref = refs[0]
    piece_refs = refs[1 : 1 + pieces]
    gram, pool = refs[-2:]
    size = LANES
    fill(piece_refs, pool)
    for v in range(gram.shape[0] // size):
        gram[v * size : (v + 1) * size] = jnp.zeros((size, gram.shape[1]), gram.dtype)
    place_pairs(table_ref, pool, gram, size)


def step_kernel(pieces, *refs):
    table_ref, info_ref, basis_ref, spread_ref, sign_ref, early_ref = refs[:6]
    piece_refs = refs[6 : 6 + pieces]
    next_ref, coef_ref, pool, gram, own, square = refs[-6:]
    slots, size = sign_ref.shape[0], sign_ref.shape[1]
    fill(piece_refs, pool)
    for v in range(slots):
        gram[v * size : (v + 1) * size] = early_ref[v * size : (v + 1) * size]
    rows = lax.broadcasted_iota(jnp.int32, (size, size), 0)
    lanes = lax.broadcasted_iota(jnp.int32, (size, size), 1)
    own_size = info_ref[slots]
    self_slot = info_ref[slots + 1]
    for w in range(slots):
        kept = (rows < own_size) & (lanes < info_ref[w])
        block = jnp.where(kept, sign_ref[w].astype(jnp.float32), 0.0)
        own[:, w * size : (w + 1) * size] = block.astype(own.dtype)
    place_pairs(table_ref, pool, gram, size)
    wide = 2 * size
    wide_lanes = lax.broadcasted_iota(jnp.int32, (size, wide), 1)
    wide_rows = lax.broadcasted_iota(jnp.int32, (size, wide), 0)

    def column_kept(n):
        first = info_ref[2 * n]
        second = info_ref[2 * n + 1]
        return (wide_lanes < first) | ((wide_lanes >= size) & (wide_lanes < size + second))

    for n in range(slots // 2):
        part = jnp.dot(own[...], gram[:, n * wide : (n + 1) * wide], preferred_element_type=jnp.float32)
        square[:, n * wide : (n + 1) * wide] = jnp.where(column_kept(n), part, 0.0).astype(square.dtype)
    basis = jnp.concatenate([basis_ref[...], basis_ref[...]], axis=1)
    coef = jnp.zeros((2 * basis_ref.shape[0], LANES), jnp.float32)
    across = (((1,), (1,)), ((), ()))
    for n in range(slots // 2):
        part = jnp.dot(square[...], gram[:, n * wide : (n + 1) * wide], preferred_element_type=jnp.float32)
        cube = jnp.where(column_kept(n), part, 0.0)
        full = 1.5 * own[:, n * wide : (n + 1) * wide].astype(jnp.float32) - 0.5 * cube
        next_ref[2 * n] = full[:, :size].astype(next_ref.dtype)
        next_ref[2 * n + 1] = full[:, size:].astype(next_ref.dtype)
        shift = (self_slot - 2 * n) * size
        is_self = (self_slot >= 2 * n) & (self_slot < 2 * n + 2)
        diag = (wide_lanes == wide_rows + shift) & (wide_rows < own_size) & is_self
        dmat = 0.5 * (jnp.where(diag, 1.0, 0.0) - full)
        high = dmat.astype(jnp.bfloat16)
        low = (dmat - high.astype(jnp.float32)).astype(jnp.bfloat16)
        half = jnp.dot(basis, jnp.concatenate([high, low], axis=0), preferred_element_type=jnp.float32)
        half_high = half.astype(jnp.bfloat16)
        half_low = (half - half_high.astype(jnp.float32)).astype(jnp.bfloat16)
        coef = coef + lax.dot_general(
            jnp.concatenate([half_high, half_low], axis=0),
            spread_ref[:, n * wide : (n + 1) * wide],
            across,
            preferred_element_type=jnp.float32,
        )
    coef = coef[: basis_ref.shape[0]] + coef[basis_ref.shape[0] :]
    coef_ref[...] = coef[: coef_ref.shape[0]]


def profile_kernel(periods, steps, mate_from, *refs):
    own_ref, mate_ref, third_ref = refs[:3]
    plane_ref, line_ref, geos, sems = refs[-4:]
    odd = (lax.axis_index("layer") & 1) == 1
    rows = len(steps) * GEO
    copies = []
    for k, source in enumerate((own_ref, mate_ref.at[pl.ds(mate_from, rows)], third_ref)):
        copy = pltpu.make_async_copy(source, geos.at[k], sems.at[k])
        copy.start()
        copies.append(copy)
    steps_x = lax.broadcasted_iota(jnp.int32, (BX, LANES), 0).astype(jnp.float32)
    steps_y = lax.broadcasted_iota(jnp.int32, (BY, LANES), 0).astype(jnp.float32)
    grid_z = lax.broadcasted_iota(jnp.int32, (LANES, BZ), 1).astype(jnp.float32)
    lane = lax.broadcasted_iota(jnp.int32, (1, LANES), 1)
    shell = (lane % SHELLS + 1).astype(jnp.float32)
    valid = lane < 7 * SPAN
    from_own = lane < 4 * SPAN
    from_below = lane < 6 * SPAN
    lift = jnp.where(from_own, 0.0, jnp.where(from_below, -float(BZ), float(BZ))) + 0.5 * BZ

    def nearest(offset, period):
        return offset - period * jnp.floor(offset * (1.0 / period) + 0.5)

    for copy in copies:
        copy.wait()
    ahead = 1.0 - 2.0 * (lax.axis_index("col") & 1).astype(jnp.float32)
    for o, (step_row, side) in enumerate(steps):
        own, first, third = (geos[k, o * GEO : (o + 1) * GEO].astype(jnp.float32) for k in range(3))
        below = jnp.where(odd, first, third)
        above = jnp.where(odd, third, first)
        moved = jnp.where(from_below, pltpu.roll(below, 3 * SPAN, axis=1), pltpu.roll(above, 3 * SPAN, axis=1))
        geo = jnp.where(from_own, own, moved)
        extent = jnp.where(valid, geo[3:4], 1.0)
        inverse = (SHELLS / extent) * (SHELLS / extent)
        reach = jnp.where(valid, extent, -1.0)
        rate_t = inverse / (shell * shell)
        packed = jnp.concatenate(
            [0.5 * geo[2:3] + lift, reach, rate_t, inverse, jnp.zeros((4, LANES), jnp.float32)], axis=0
        )
        sub = packed.T
        d_x = nearest(steps_x - (0.5 * geo[0:1] + float(BX * step_row)), periods[0])
        d_y = nearest(steps_y - (0.5 * geo[1:2] + float(BY * side) * ahead), periods[1])
        inside_x = jnp.abs(d_x) <= reach
        inside_y = jnp.abs(d_y) <= reach
        squared_x = d_x * d_x
        squared_y = d_y * d_y
        d_z = nearest(grid_z - sub[:, 0:1], periods[2])
        inside_z = jnp.abs(d_z) <= sub[:, 1:2]
        squared_z = d_z * d_z
        for s in range(SHELLS):
            part = 1.0 / ((s + 1) * (s + 1))
            rate = inverse * part + rate_t
            along_x = jnp.where(inside_x, jnp.exp(-rate * squared_x), 0.0)
            along_y = jnp.where(inside_y, jnp.exp(-rate * squared_y), 0.0)
            for x in range(BX):
                plane_ref[o, s, x * BY : (x + 1) * BY] = (along_x[x : x + 1] * along_y).astype(plane_ref.dtype)
            rate_z = sub[:, 3:4] * part + sub[:, 2:3]
            line_ref[o, s] = jnp.where(inside_z, jnp.exp(-rate_z * squared_z), 0.0).astype(line_ref.dtype)


def density_kernel(column_steps, *refs):
    coef_refs = refs[:column_steps]
    plane_ref, line_ref, out_ref = refs[column_steps:]
    total = jnp.zeros(out_ref.shape, jnp.float32)
    wide = SHELLS * LANES
    for o in range(plane_ref.shape[0]):
        coef = coef_refs[-o % column_steps]
        first = 8 * (o // column_steps)
        terms = [
            (plane_ref[o, s].astype(jnp.float32) * coef[first + s : first + s + 1, :]).astype(line_ref.dtype)
            for s in range(SHELLS)
        ]
        total = total + jnp.dot(
            jnp.concatenate(terms, axis=1),
            line_ref[o * wide : (o + 1) * wide],
            preferred_element_type=jnp.float32,
        )
    out_ref[...] = total


def local(sign_start, neighbors, atom_size, basis_proj, pair_extent, atom_x, atom_y, atom_z):
    n_row = lax.axis_size("row")
    n_col = lax.axis_size("col")
    n_lay = lax.axis_size("layer")
    assert n_lay == 4 and n_col >= 4 and (n_row == 2 or n_row >= 4)
    assert n_row & (n_row - 1) == 0 and n_col & (n_col - 1) == 0
    axes = (n_row, n_col, n_lay)
    atoms, slots = neighbors.shape
    size = sign_start.shape[2]
    steps = [0, 1] if n_row == 2 else [0, 1, -1]
    count = len(steps)
    others = range(1, count)
    own = sign_start[0]
    flat = own.reshape(slots * size, size)
    listings = neighbors.T
    full = slots * size
    half = full // 2
    most = half - size
    n_pick = column_targets(n_row)
    picks = n_pick * size
    part = picks + GEO

    def on_row(value, di):
        return from_offset(value, "row", steps[di])

    x_row = {di: on_row(flat, di) for di in others}
    y_row = from_layer(flat, 2)
    m_row = from_layer(flat, 1)
    picked = pl.pallas_call(
        functools.partial(pick_kernel, axes),
        out_shape=jax.ShapeDtypeStruct((part, size), own.dtype),
        in_specs=[HBM] * 6,
        out_specs=VMEM,
        scratch_shapes=[
            pltpu.SMEM((slots, atoms), jnp.int32),
            pltpu.SMEM((1, slots), jnp.int32),
            pltpu.SMEM((atoms,), jnp.int32),
            pltpu.SMEM((atoms,), jnp.int32),
            pltpu.SMEM((atoms,), jnp.int32),
            pltpu.SMEM((n_pick + 1,), jnp.int32),
            pltpu.SemaphoreType.DMA((5,)),
            pltpu.SemaphoreType.DMA((n_pick,)),
        ],
        compiler_params=pltpu.CompilerParams(vmem_limit_bytes=60 << 20),
        name="pick_column_blocks",
    )(listings, pair_extent, atom_x, atom_y, atom_z, own)
    down = from_column(picked, 1)
    up = from_column(picked, 0)

    halves = pack(
        [y_row] + [x_row[di] for di in others] + [picked],
        [[(0, half, most)]] + [[(di, 0, most)] for di in others] + [[(count, picks, GEO)]],
        [],
        "pack_halves",
    )
    ends = {di: on_row(halves[0], di) for di in others}
    tops = {di: from_layer(halves[di], 2) for di in others}

    at = {}
    buffers = {}

    def note(name, value, contents):
        buffers[name] = value
        start = 0
        for what, rows in contents:
            if what is not None:
                at[what] = (name, start)
            start += rows

    def row_of(di, flip, start=0, stop=slots):
        return [(("row", slot, di, flip), size) for slot in range(start, stop)]

    halfway = slots // 2

    def side_of(kind, di, flip):
        return [((kind, di, flip), picks)]

    note("own", flat, row_of(0, 0))
    note("mate", m_row, row_of(0, 1))
    note("far", y_row, row_of(0, 2))
    note("up", up, side_of("up", 0, 0) + [(("up geo", 0, 0), GEO)])
    note("down", down, side_of("down", 0, 0) + [(("down geo", 0, 0), GEO)])
    note("geo", halves[count], [(("geo", 0, 0), GEO)])
    for di in others:
        note(("x", di), x_row[di], row_of(di, 0))
        note(("end", di), ends[di], row_of(di, 2, halfway, slots - 1))
        note(("top", di), tops[di], row_of(di, 2, 0, halfway - 1))

    corners = [("end", di) for di in others] + [("top", di) for di in others]
    names = ["down", "up", "geo", "far"] + [("x", di) for di in others]
    plans = [
        [(1, 0, picks), (0, 0, picks), (3, full - size, size), (2, 0, GEO), (1, picks, GEO), (0, picks, GEO)],
        [(1, 0, picks), (0, 0, picks)] + [(di + 3, most, size) for di in others] + [(2, 0, GEO), (1, picks, GEO), (0, picks, GEO)],
        [(2, 0, GEO), (1, picks, GEO), (0, picks, GEO)],
    ]
    two_x, two_y, geos = pack([buffers[name] for name in names], plans, [m_row], "pack_two")
    to_mate = corners + ["up", "down"]
    for di in others:
        note(("mate x", di), from_layer(x_row[di], 1), row_of(di, 1))
    note("mate far", from_layer(y_row, 1), row_of(0, 3))

    early_order = ["own", "mate", "far", "up", "down", "geo"] + [("x", di) for di in others]
    early_order += [("mate x", di) for di in others] + ["mate far"]
    early_order += corners + [("two x", di) for di in others] + ["two y", "two m"]
    late_order = [("three x", di) for di in others] + ["three y", "three m"]
    late_order += ["four"]

    contents = {}
    for di in others:
        contents["two x", di] = side_of("up", di, 0) + side_of("down", di, 0)
        contents["two x", di] += row_of(di, 2, slots - 1, slots) + [(("geo", di, 0), GEO)]
        contents["two x", di] += [(("up geo", di, 0), GEO), (("down geo", di, 0), GEO)]
    contents["two y"] = side_of("up", 0, 2) + side_of("down", 0, 2)
    contents["two y"] += sum([row_of(di, 2, halfway - 1, halfway) for di in others], []) + [(None, 3 * GEO)]
    contents["two m"] = sum([row_of(di, 3, halfway, slots - 1) for di in others], [])
    contents["two m"] += sum([row_of(di, 3, 0, halfway - 1) for di in others], [])
    contents["two m"] += side_of("up", 0, 1) + side_of("down", 0, 1)
    for di in others:
        contents["three x", di] = side_of("up", di, 2)
    contents["three y"] = sum([side_of("down", di, 2) for di in others], [])
    contents["three m"] = []
    for di in others:
        contents["three m"] += side_of("up", di, 1) + side_of("down", di, 1) + row_of(di, 3, slots - 1, slots)
    contents["three m"] += side_of("up", 0, 3) + side_of("down", 0, 3)
    contents["three m"] += sum([row_of(di, 3, halfway - 1, halfway) for di in others], []) + [(None, 3 * GEO)]
    contents["three m"] += [("geos", count * 3 * GEO)]
    contents["four"] = sum([side_of("up", di, 3) for di in others], [])
    contents["four"] += sum([side_of("down", di, 3) for di in others], [])
    lengths = {name: sum(rows for _, rows in content) for name, content in contents.items()}
    for name in early_order:
        if name in buffers:
            lengths[name] = buffers[name].shape[0]
    base = {}
    total = 0
    for name in early_order + late_order:
        base[name] = total
        total += lengths[name]
        if name == early_order[-1]:
            late_from = total
    located = dict(at)
    for name, content in contents.items():
        start = 0
        for what, rows in content:
            located[what] = (name, start)
            start += rows
    layout = [
        base[located["row", slot, di, flip][0]] + located["row", slot, di, flip][1]
        for di in range(count)
        for flip in range(n_lay)
        for slot in range(slots)
    ]
    layout += [
        base[located[kind, di, flip][0]] + located[kind, di, flip][1]
        for kind in ("up", "down")
        for di in range(count)
        for flip in range(n_lay)
    ]
    pairs = slots * (slots + 1) // 2
    entries = pairs + UNROLL + 1
    early_table, late_table, info = pl.pallas_call(
        functools.partial(prepare_kernel, axes, count, tuple(layout), late_from),
        out_shape=(
            jax.ShapeDtypeStruct((entries,), jnp.int32),
            jax.ShapeDtypeStruct((entries,), jnp.int32),
            jax.ShapeDtypeStruct((slots + 2,), jnp.int32),
        ),
        in_specs=[HBM, HBM, ANY],
        out_specs=(SMEM, SMEM, SMEM),
        scratch_shapes=[
            pltpu.SMEM((slots, atoms), jnp.int32),
            pltpu.SMEM((atoms,), jnp.int32),
            pltpu.SMEM((3, slots), jnp.int32),
            pltpu.SMEM((atoms,), jnp.int32),
            pltpu.SMEM((len(layout),), jnp.int32),
            pltpu.SemaphoreType.DMA((2,)),
        ],
        compiler_params=pltpu.CompilerParams(vmem_limit_bytes=1 << 20),
        cost_estimate=pl.CostEstimate(flops=1000, bytes_accessed=1000, transcendentals=0),
        name="prepare",
    )(listings, atom_size, two_x)

    plans = [[(i, 0, picks if name in ("up", "down") else most) for i, name in enumerate(to_mate)]]
    two_m = pack([buffers[name] for name in to_mate], plans, [], "pack_two_mate", 3_000_000_000)[0]
    for di in others:
        note(("two x", di), on_row(two_x, di), contents["two x", di])
    note("two y", from_layer(two_y, 2), contents["two y"])
    early_mates = ["mate far"] + [("mate x", di) for di in others]
    note("two m", from_layer(two_m, 1), contents["two m"])

    buffers["geos"] = geos
    names = ["two y", "geos"] + [("two x", di) for di in others]
    place = {name: i for i, name in enumerate(names)}
    gather = [(place["geos"], 0, 3 * GEO)] + [(place["two x", di], 2 * picks + size, 3 * GEO) for di in others]
    xs = [place["two x", di] for di in others]
    plans = [
        [(0, 0, picks)],
        [(x, picks, picks) for x in xs],
        [(x, 0, 2 * picks + size) for x in xs] + [(0, 0, lengths["two y"])] + gather,
        gather,
    ]
    three_x, three_y, three_m, geos = pack([buffers[name] for name in names], plans, [buffers[name] for name in early_mates] + [two_m, info], "pack_three")
    for di in others:
        note(("three x", di), on_row(three_x, di), contents["three x", di])
    note("three y", from_layer(three_y, 2), contents["three y"])
    note("three m", from_layer(three_m, 1), contents["three m"])
    third_geos = from_layer(geos, 3)

    spread, own_basis = pl.pallas_call(
        functools.partial(spread_kernel, axes),
        out_shape=(
            jax.ShapeDtypeStruct((LANES, full), jnp.bfloat16),
            jax.ShapeDtypeStruct((16, size), jnp.bfloat16),
        ),
        in_specs=[HBM, VMEM, ANY],
        out_specs=(VMEM, VMEM),
        scratch_shapes=[pltpu.SMEM((slots, atoms), jnp.int32), pltpu.SemaphoreType.DMA((1,))],
        compiler_params=pltpu.CompilerParams(vmem_limit_bytes=(2 << 20) + atoms * 16384),
        cost_estimate=pl.CostEstimate(flops=1000, bytes_accessed=1000, transcendentals=0),
        name="spread_basis",
    )(listings, basis_proj.transpose(1, 0, 2).reshape(SHELLS * atoms, size), three_x)

    early_values = [buffers[name] for name in early_order]
    gram = pl.pallas_call(
        functools.partial(gram_kernel, len(early_values)),
        out_shape=jax.ShapeDtypeStruct((full, full), jnp.bfloat16),
        in_specs=[SMEM] + [VMEM] * len(early_values) + [ANY],
        out_specs=VMEM,
        scratch_shapes=[pltpu.VMEM((late_from, LANES), jnp.bfloat16)],
        compiler_params=pltpu.CompilerParams(vmem_limit_bytes=(6 << 20) + 2 * late_from * LANES * 2),
        cost_estimate=pl.CostEstimate(flops=1000, bytes_accessed=1000, transcendentals=0),
        name="gram_early",
    )(early_table, *early_values, three_x)

    thirds = [buffers["three x", di] for di in others] + [buffers["three y"]]
    four = pack(thirds, [[(i, 0, value.shape[0]) for i, value in enumerate(thirds)]], [gram, third_geos, own_basis], "pack_four")[0]
    note("four", from_layer(four, 1), contents["four"])

    column_steps = (0, 1, -1)
    tile_steps = [(dr, dc) for dr in steps for dc in column_steps]
    tiles = len(tile_steps)
    periods = (float(BX * n_row), float(BY * n_col), float(BZ * n_lay))
    plane, line = pl.pallas_call(
        functools.partial(profile_kernel, periods, tile_steps, at["geos"][1]),
        out_shape=(
            jax.ShapeDtypeStruct((tiles, SHELLS, BX * BY, LANES), jnp.bfloat16),
            jax.ShapeDtypeStruct((tiles, SHELLS, LANES, BZ), jnp.bfloat16),
        ),
        in_specs=[ANY] * 3,
        out_specs=(VMEM, VMEM),
        scratch_shapes=[
            pltpu.VMEM((3, tiles * GEO, LANES), jnp.bfloat16),
            pltpu.SemaphoreType.DMA((3,)),
        ],
        compiler_params=pltpu.CompilerParams(vmem_limit_bytes=10 << 20),
        cost_estimate=pl.CostEstimate(flops=1000, bytes_accessed=1000, transcendentals=0),
        name="profiles",
    )(geos, buffers["three m"], third_geos)

    late_values = [buffers[name] for name in late_order]
    sign_next, coef = pl.pallas_call(
        functools.partial(step_kernel, len(late_values)),
        out_shape=(
            jax.ShapeDtypeStruct((slots, size, size), jnp.bfloat16),
            jax.ShapeDtypeStruct((8, LANES), jnp.float32),
        ),
        in_specs=[SMEM, SMEM, VMEM, VMEM, VMEM, VMEM] + [VMEM] * len(late_values),
        out_specs=(VMEM, VMEM),
        scratch_shapes=[
            pltpu.VMEM((total - late_from, LANES), jnp.bfloat16),
            pltpu.VMEM((full, full), jnp.bfloat16),
            pltpu.VMEM((size, full), jnp.bfloat16),
            pltpu.VMEM((size, full), jnp.bfloat16),
        ],
        compiler_params=pltpu.CompilerParams(vmem_limit_bytes=(15 << 20) + 2 * (total - late_from) * LANES * 2),
        cost_estimate=pl.CostEstimate(flops=1_300_000_000, bytes_accessed=8_000_000, transcendentals=0),
        name="square_cube_coefficients",
    )(late_table, info, own_basis, spread, own, gram, *late_values)

    mate_coef = from_layer(coef, 1)
    third_coef = from_layer(coef, 3)
    odd = lax.axis_index("layer") % 2 == 1
    below = jnp.where(odd, mate_coef, third_coef)
    above = jnp.where(odd, third_coef, mate_coef)
    merged = jnp.concatenate(
        [
            coef[:, : 4 * SPAN],
            below[:, SPAN : 3 * SPAN],
            above[:, 3 * SPAN : 4 * SPAN],
            jnp.zeros((8, LANES - 7 * SPAN), jnp.float32),
        ],
        axis=1,
    )
    given, token = pack([sign_next.reshape(full, size)], [[(0, 0, full)], [(0, 0, GEO)]], [], "give_sign")
    parts = [merged] + [on_row(merged, di) for di in others]
    stacked = pack(parts, [[(i, 0, 8) for i in range(count)]], [token], "stack_tiles")[0]
    far_side = from_column(stacked, 1)
    received = [stacked, far_side, from_column(stacked, 0)]

    density = pl.pallas_call(
        functools.partial(density_kernel, len(column_steps)),
        out_shape=jax.ShapeDtypeStruct((BX * BY, BZ), jnp.float32),
        in_specs=[VMEM] * (len(received) + 2),
        out_specs=VMEM,
        compiler_params=pltpu.CompilerParams(vmem_limit_bytes=16 << 20),
        cost_estimate=pl.CostEstimate(flops=310_000_000, bytes_accessed=4_000_000, transcendentals=0),
        name="density",
    )(*received, plane, line.reshape(tiles * SHELLS * LANES, BZ))
    return given.reshape(1, slots, size, size), density.reshape(BX, BY, BZ)


def solution(mesh):
    rows = P(("row", "col", "layer"), None, None, None)
    in_specs = (rows, P(), P(), P(), P(("row", "col", "layer"), None), P(), P(), P())
    out_specs = (rows, P("row", "col", "layer"))
    return jax.shard_map(local, mesh=mesh, in_specs=in_specs, out_specs=out_specs, check_vma=False)
```

```python
import functools

import jax
import jax.numpy as jnp
from jax import lax
from jax.experimental import pallas as pl
from jax.experimental.pallas import tpu as pltpu
from jax.sharding import PartitionSpec as P

BX = 16
BY = 16
BZ = 128
LANES = 128
UNROLL = 4
SHELLS = 6
SPAN = 3 * SHELLS
GEO = 16
VMEM = pl.BlockSpec(memory_space=pltpu.VMEM)
SMEM = pl.BlockSpec(memory_space=pltpu.SMEM)
ANY = pl.BlockSpec(memory_space=pl.ANY)
HBM = pl.BlockSpec(memory_space=pltpu.HBM)


def from_offset(x, axis, step):
    count = lax.axis_size(axis)
    return lax.ppermute(x, axis, [((i + step) % count, i) for i in range(count)])


def from_column(x, side):
    count = lax.axis_size("col")
    step = [1 if (i + side) % 2 == 0 else -1 for i in range(count)]
    return lax.ppermute(x, "col", [((i + step[i]) % count, i) for i in range(count)])


def from_layer(x, flip):
    count = lax.axis_size("layer")
    return lax.ppermute(x, "layer", [(i ^ flip, i) for i in range(count)])


def column_targets(n_row):
    return 5 if n_row == 2 else 7


def target_place(n_row, step_row, step_lay, row):
    same = jnp.where(step_lay < 3, step_lay, -1)
    if n_row == 2:
        lead = step_lay - row
        across = jnp.where((lead >= 0) & (lead < 2), 3 + lead, -1)
    else:
        across = 3 + step_lay
    return jnp.where(step_row == 0, same, jnp.where(step_row == 1, across, -1))


class Places:
    def __init__(self, n_row, n_col, n_lay):
        self.n_row, self.n_col, self.n_lay = n_row, n_col, n_lay
        self.lay_bits = n_lay.bit_length() - 1
        self.col_bits = n_col.bit_length() - 1
        self.row = lax.axis_index("row")
        self.col = lax.axis_index("col")
        self.lay = lax.axis_index("layer")
        self.me = (((self.row << self.col_bits) + self.col) << self.lay_bits) + self.lay

    def split(self, atom):
        return (
            atom >> (self.lay_bits + self.col_bits),
            (atom >> self.lay_bits) & (self.n_col - 1),
            atom & (self.n_lay - 1),
        )


def load(sources, targets, sems):
    copies = [pltpu.make_async_copy(a, b, sems.at[i]) for i, (a, b) in enumerate(zip(sources, targets))]
    for copy in copies:
        copy.start()
    for copy in copies:
        copy.wait()


def own_ranks(at, neighbors_ref):
    seen = [jnp.int32(0)] * at.n_lay
    listed = []
    for w in range(neighbors_ref.shape[0]):
        atom = neighbors_ref[w, at.me]
        step_lay = (atom - at.lay) & (at.n_lay - 1)
        rank = jnp.int32(0)
        for k in range(at.n_lay):
            rank = jnp.where(step_lay == k, 3 * k + seen[k], rank)
            seen[k] = seen[k] + (step_lay == k).astype(jnp.int32)
        listed.append((atom, rank))
    return listed


def pick_kernel(axes, *refs):
    sign_ref, out_ref, neighbors_ref, extent_ref, x_ref, y_ref, z_ref, place_ref, loads, sems = refs[5:]
    at = Places(*axes)
    slots = sign_ref.shape[0]
    n_pick = place_ref.shape[0] - 1
    size = sign_ref.shape[1]
    for i in range(n_pick + 1):
        place_ref[i] = 0
    load(refs[:5], (neighbors_ref, extent_ref, x_ref, y_ref, z_ref), loads)
    for w in range(slots):
        row, col, lay = at.split(neighbors_ref[w, at.me])
        place = target_place(at.n_row, (row - at.row) & (at.n_row - 1), (lay - at.lay) & (at.n_lay - 1), at.row)
        place_ref[jnp.where((col == at.col) & (place >= 0), place, n_pick)] = w
    copies = []
    for i in range(n_pick):
        copy = pltpu.make_async_copy(sign_ref.at[place_ref[i]], out_ref.at[pl.ds(i * size, size)], sems.at[i])
        copy.start()
        copies.append(copy)
    ranks = own_ranks(at, neighbors_ref)
    sub = lax.broadcasted_iota(jnp.int32, (GEO, LANES), 0)
    lane_pair = lax.broadcasted_iota(jnp.int32, (GEO, LANES), 1) // SHELLS
    geo = jnp.zeros((GEO, LANES), jnp.int32)
    for w, (atom, rank) in enumerate(ranks):
        row, col, lay = at.split(atom)
        go_row = ((row - at.row + 1) & (at.n_row - 1)) - 1
        go_col = ((col - at.col + 1) & (at.n_col - 1)) - 1
        go_lay = jnp.minimum(((lay - at.lay + 1) & (at.n_lay - 1)) - 1, 1)
        twice_x = x_ref[at.me] + x_ref[atom] + BX * go_row
        twice_y = y_ref[at.me] + y_ref[atom] + BY * go_col
        twice_z = z_ref[at.me] + z_ref[atom] + BZ * go_lay - BZ
        extent = extent_ref[0, w]
        values = jnp.where(sub == 0, twice_x, jnp.where(sub == 1, twice_y, jnp.where(sub == 2, twice_z, extent)))
        geo = jnp.where(lane_pair == rank, values, geo)
    out_ref[n_pick * size :] = geo.astype(jnp.float32).astype(out_ref.dtype)
    for copy in copies:
        copy.wait()


def spread_kernel(axes, *refs):
    basis_ref = refs[1]
    spread_ref, own_basis_ref, neighbors_ref, loads = refs[-4:]
    at = Places(*axes)
    load(refs[:1], (neighbors_ref,), loads)
    slots, atoms = neighbors_ref.shape
    bits = atoms.bit_length() - 1

    def hot(rows, atom, first):
        sub = lax.broadcasted_iota(jnp.int32, (rows, SHELLS * atoms), 0)
        lane = lax.broadcasted_iota(jnp.int32, (rows, SHELLS * atoms), 1)
        return ((lane & (atoms - 1)) == atom) & (sub == first + (lane >> bits))

    def rows_of(chosen):
        picked = jnp.where(chosen, 1.0, 0.0).astype(jnp.bfloat16)
        return jnp.dot(picked, basis_ref[...], preferred_element_type=jnp.float32).astype(jnp.bfloat16)

    for w, (atom, rank) in enumerate(own_ranks(at, neighbors_ref)):
        spread_ref[:, w * LANES : (w + 1) * LANES] = rows_of(hot(LANES, atom, rank * SHELLS))
    own_basis_ref[...] = rows_of(hot(16, at.me, 0))


def prepare_kernel(axes, count, layout, late_from, last_from, *refs):
    early_ref, late_ref, last_ref, info_ref, neighbors_ref, size_ref, known, inverse, layout_ref, loads = refs[-10:]
    at = Places(*axes)
    load(refs[:2], (neighbors_ref, size_ref), loads)
    slots = neighbors_ref.shape[0]
    lines = count * at.n_lay
    for i, value in enumerate(layout):
        layout_ref[i] = value
    self_slot = jnp.int32(0)
    for w in range(slots):
        atom = neighbors_ref[w, at.me]
        row, col, lay = at.split(atom)
        step_row = (row - at.row) & (at.n_row - 1)
        self_slot = jnp.where(atom == at.me, w, self_slot)
        info_ref[w] = size_ref[atom]
        known[0, w] = atom
        known[1, w] = jnp.where(col == at.col, 0, jnp.where(col == (at.col ^ 1), 1, 2))
        known[2, w] = jnp.where(step_row == 0, 0, jnp.where(step_row == 1, 1, 2)) * at.n_lay + (lay ^ at.lay)
        inverse[atom] = -1
    info_ref[slots] = size_ref[at.me]
    info_ref[slots + 1] = self_slot

    def row_of_pairs(v, totals):
        early, late, last = totals
        atom = known[0, v]
        side = known[1, v]
        line = known[2, v]
        for u in range(slots):
            inverse[neighbors_ref[u, atom]] = v * 16 + u

        def from_row(totals):
            total, late, last = totals
            for w in range(slots):
                mark = inverse[known[0, w]]
                chosen = ((mark >> 4) == v) & ((known[1, w] != 0) | (v <= w))
                where = layout_ref[line * slots + (mark & 15)]
                is_late = where >= late_from
                entry = v + 16 * w
                early_ref[total + 1] = entry + 256 * where
                late_ref[late + 1] = entry + 256 * (where - late_from)
                total = total + (chosen & ~is_late).astype(jnp.int32)
                late = late + (chosen & is_late).astype(jnp.int32)
            return total, late, last

        def from_column(totals):
            early, late, last = totals
            row, _, lay = at.split(atom)
            beside = layout_ref[lines * slots + (side - 1) * lines + line]
            for w in range(slots):
                other = known[0, w]
                mark = inverse[other]
                o_row, _, o_lay = at.split(other)
                d_row = (o_row - row) & (at.n_row - 1)
                d_lay = (o_lay - lay) & (at.n_lay - 1)
                there = target_place(at.n_row, d_row, d_lay, row)
                back = target_place(at.n_row, -d_row & (at.n_row - 1), -d_lay & (at.n_lay - 1), o_row)
                chosen = ((mark >> 4) == v) & (side == known[1, w]) & (there >= 0) & ((back < 0) | (v <= w))
                where = beside + there * LANES
                is_late = where >= late_from
                is_last = where >= last_from
                entry = v + 16 * w
                early_ref[early + 1] = entry + 256 * where
                late_ref[late + 1] = entry + 256 * (where - late_from)
                last_ref[last + 1] = entry + 256 * (where - last_from)
                early = early + (chosen & ~is_late).astype(jnp.int32)
                late = late + (chosen & is_late & ~is_last).astype(jnp.int32)
                last = last + (chosen & is_last).astype(jnp.int32)
            return early, late, last

        return lax.cond(side == 0, from_row, from_column, (early, late, last))

    totals = lax.fori_loop(0, slots, row_of_pairs, (jnp.int32(0),) * 3)
    for ref, total in zip((early_ref, late_ref, last_ref), totals):
        ref[0] = (total + UNROLL - 1) // UNROLL
        for i in range(UNROLL - 1):
            ref[total + i + 1] = ref[jnp.maximum(total, 1)]


def pack_kernel(moves, inputs, *refs):
    for source, start, rows, target, place in moves:
        refs[inputs + target][place : place + rows] = refs[source][start : start + rows]


def pack(values, plans, extra, name, cost=0):
    moves, shapes = [], []
    for target, plan in enumerate(plans):
        place = 0
        for source, start, rows in plan:
            moves.append((source, start, rows, target, place))
            place += rows
        shapes.append(jax.ShapeDtypeStruct((place, LANES), values[0].dtype))
    inputs = len(values) + len(extra)
    return pl.pallas_call(
        functools.partial(pack_kernel, tuple(moves), inputs),
        out_shape=tuple(shapes),
        in_specs=[VMEM] * len(values) + [ANY] * len(extra),
        out_specs=tuple([VMEM] * len(plans)),
        compiler_params=pltpu.CompilerParams(
            vmem_limit_bytes=(1 << 20) + 256 * sum(x.shape[0] for x in list(values) + shapes)
        ),
        cost_estimate=pl.CostEstimate(flops=cost, bytes_accessed=1000, transcendentals=0),
        name=name,
    )(*values, *extra)


def fill(piece_refs, pool):
    place = 0
    for piece in piece_refs:
        rows = piece.shape[0]
        pool[place : place + rows] = piece[...]
        place += rows


def place_pairs(table_ref, pool, gram, size):
    def place(i, carry):
        for k in range(UNROLL):
            entry = table_ref[i * UNROLL + k + 1]
            p = pl.multiple_of((entry & 15) * size, size)
            q = pl.multiple_of(((entry >> 4) & 15) * size, size)
            block = pool[pl.ds(pl.multiple_of(entry >> 8, 16), size)]
            gram[pl.ds(p, size), pl.ds(q, size)] = block
            gram[pl.ds(q, size), pl.ds(p, size)] = block.T
        return carry

    lax.fori_loop(0, table_ref[0], place, 0)


def gram_kernel(pieces, *refs):
    table_ref = refs[0]
    piece_refs = refs[1 : 1 + pieces]
    gram, pool = refs[-2:]
    size = LANES
    fill(piece_refs, pool)
    for v in range(gram.shape[0] // size):
        gram[v * size : (v + 1) * size] = jnp.zeros((size, gram.shape[1]), gram.dtype)
    place_pairs(table_ref, pool, gram, size)


def middle_kernel(pieces, *refs):
    table_ref, info_ref, sign_ref, early_ref = refs[:4]
    piece_refs = refs[4 : 4 + pieces]
    gram, own, pool = refs[-3:]
    slots, size = sign_ref.shape[0], sign_ref.shape[1]
    fill(piece_refs, pool)
    for v in range(slots):
        gram[v * size : (v + 1) * size] = early_ref[v * size : (v + 1) * size]
    place_pairs(table_ref, pool, gram, size)
    rows = lax.broadcasted_iota(jnp.int32, (size, size), 0)
    lanes = lax.broadcasted_iota(jnp.int32, (size, size), 1)
    for w in range(slots):
        kept = (rows < info_ref[slots]) & (lanes < info_ref[w])
        block = jnp.where(kept, sign_ref[w].astype(jnp.float32), 0.0)
        own[:, w * size : (w + 1) * size] = block.astype(own.dtype)


def step_kernel(pieces, *refs):
    table_ref, info_ref, basis_ref, spread_ref, own, early_ref = refs[:6]
    piece_refs = refs[6 : 6 + pieces]
    next_ref, coef_ref, pool, gram, square = refs[-5:]
    slots, size = next_ref.shape[0], next_ref.shape[1]
    fill(piece_refs, pool)
    for v in range(slots):
        gram[v * size : (v + 1) * size] = early_ref[v * size : (v + 1) * size]
    own_size = info_ref[slots]
    self_slot = info_ref[slots + 1]
    place_pairs(table_ref, pool, gram, size)
    wide = 2 * size
    wide_lanes = lax.broadcasted_iota(jnp.int32, (size, wide), 1)
    wide_rows = lax.broadcasted_iota(jnp.int32, (size, wide), 0)

    def column_kept(n):
        first = info_ref[2 * n]
        second = info_ref[2 * n + 1]
        return (wide_lanes < first) | ((wide_lanes >= size) & (wide_lanes < size + second))

    for n in range(slots // 2):
        part = jnp.dot(own[...], gram[:, n * wide : (n + 1) * wide], preferred_element_type=jnp.float32)
        square[:, n * wide : (n + 1) * wide] = jnp.where(column_kept(n), part, 0.0).astype(square.dtype)
    basis = jnp.concatenate([basis_ref[...], basis_ref[...]], axis=1)
    coef = jnp.zeros((2 * basis_ref.shape[0], LANES), jnp.float32)
    across = (((1,), (1,)), ((), ()))
    for n in range(slots // 2):
        part = jnp.dot(square[...], gram[:, n * wide : (n + 1) * wide], preferred_element_type=jnp.float32)
        cube = jnp.where(column_kept(n), part, 0.0)
        full = 1.5 * own[:, n * wide : (n + 1) * wide].astype(jnp.float32) - 0.5 * cube
        next_ref[2 * n] = full[:, :size].astype(next_ref.dtype)
        next_ref[2 * n + 1] = full[:, size:].astype(next_ref.dtype)
        shift = (self_slot - 2 * n) * size
        is_self = (self_slot >= 2 * n) & (self_slot < 2 * n + 2)
        diag = (wide_lanes == wide_rows + shift) & (wide_rows < own_size) & is_self
        dmat = 0.5 * (jnp.where(diag, 1.0, 0.0) - full)
        high = dmat.astype(jnp.bfloat16)
        low = (dmat - high.astype(jnp.float32)).astype(jnp.bfloat16)
        half = jnp.dot(basis, jnp.concatenate([high, low], axis=0), preferred_element_type=jnp.float32)
        half_high = half.astype(jnp.bfloat16)
        half_low = (half - half_high.astype(jnp.float32)).astype(jnp.bfloat16)
        coef = coef + lax.dot_general(
            jnp.concatenate([half_high, half_low], axis=0),
            spread_ref[:, n * wide : (n + 1) * wide],
            across,
            preferred_element_type=jnp.float32,
        )
    coef = coef[: basis_ref.shape[0]] + coef[basis_ref.shape[0] :]
    coef_ref[...] = coef[: coef_ref.shape[0]]


def profile_kernel(periods, steps, mate_from, *refs):
    own_ref, mate_ref, third_ref = refs[:3]
    plane_ref, line_ref, geos, sems = refs[-4:]
    odd = (lax.axis_index("layer") & 1) == 1
    rows = len(steps) * GEO
    copies = []
    for k, source in enumerate((own_ref, mate_ref.at[pl.ds(mate_from, rows)], third_ref)):
        copy = pltpu.make_async_copy(source, geos.at[k], sems.at[k])
        copy.start()
        copies.append(copy)
    steps_x = lax.broadcasted_iota(jnp.int32, (BX, LANES), 0).astype(jnp.float32)
    steps_y = lax.broadcasted_iota(jnp.int32, (BY, LANES), 0).astype(jnp.float32)
    grid_z = lax.broadcasted_iota(jnp.int32, (LANES, BZ), 1).astype(jnp.float32)
    lane = lax.broadcasted_iota(jnp.int32, (1, LANES), 1)
    shell = (lane % SHELLS + 1).astype(jnp.float32)
    valid = lane < 7 * SPAN
    from_own = lane < 4 * SPAN
    from_below = lane < 6 * SPAN
    lift = jnp.where(from_own, 0.0, jnp.where(from_below, -float(BZ), float(BZ))) + 0.5 * BZ

    def nearest(offset, period):
        return offset - period * jnp.floor(offset * (1.0 / period) + 0.5)

    for copy in copies:
        copy.wait()
    ahead = 1.0 - 2.0 * (lax.axis_index("col") & 1).astype(jnp.float32)
    for o, (step_row, side) in enumerate(steps):
        own, first, third = (geos[k, o * GEO : (o + 1) * GEO].astype(jnp.float32) for k in range(3))
        below = jnp.where(odd, first, third)
        above = jnp.where(odd, third, first)
        moved = jnp.where(from_below, pltpu.roll(below, 3 * SPAN, axis=1), pltpu.roll(above, 3 * SPAN, axis=1))
        geo = jnp.where(from_own, own, moved)
        extent = jnp.where(valid, geo[3:4], 1.0)
        inverse = (SHELLS / extent) * (SHELLS / extent)
        reach = jnp.where(valid, extent, -1.0)
        rate_t = inverse / (shell * shell)
        packed = jnp.concatenate(
            [0.5 * geo[2:3] + lift, reach, rate_t, inverse, jnp.zeros((4, LANES), jnp.float32)], axis=0
        )
        sub = packed.T
        d_x = nearest(steps_x - (0.5 * geo[0:1] + float(BX * step_row)), periods[0])
        d_y = nearest(steps_y - (0.5 * geo[1:2] + float(BY * side) * ahead), periods[1])
        inside_x = jnp.abs(d_x) <= reach
        inside_y = jnp.abs(d_y) <= reach
        squared_x = d_x * d_x
        squared_y = d_y * d_y
        d_z = nearest(grid_z - sub[:, 0:1], periods[2])
        inside_z = jnp.abs(d_z) <= sub[:, 1:2]
        squared_z = d_z * d_z
        for s in range(SHELLS):
            part = 1.0 / ((s + 1) * (s + 1))
            rate = inverse * part + rate_t
            along_x = jnp.where(inside_x, jnp.exp(-rate * squared_x), 0.0)
            along_y = jnp.where(inside_y, jnp.exp(-rate * squared_y), 0.0)
            for x in range(BX):
                plane_ref[o, s, x * BY : (x + 1) * BY] = (along_x[x : x + 1] * along_y).astype(plane_ref.dtype)
            rate_z = sub[:, 3:4] * part + sub[:, 2:3]
            line_ref[o, s] = jnp.where(inside_z, jnp.exp(-rate_z * squared_z), 0.0).astype(line_ref.dtype)


def density_kernel(column_steps, *refs):
    coef_refs = refs[:column_steps]
    plane_ref, line_ref, out_ref = refs[column_steps:]
    total = jnp.zeros(out_ref.shape, jnp.float32)
    wide = SHELLS * LANES
    for o in range(plane_ref.shape[0]):
        coef = coef_refs[-o % column_steps]
        first = 8 * (o // column_steps)
        terms = [
            (plane_ref[o, s].astype(jnp.float32) * coef[first + s : first + s + 1, :]).astype(line_ref.dtype)
            for s in range(SHELLS)
        ]
        total = total + jnp.dot(
            jnp.concatenate(terms, axis=1),
            line_ref[o * wide : (o + 1) * wide],
            preferred_element_type=jnp.float32,
        )
    out_ref[...] = total


def local(sign_start, neighbors, atom_size, basis_proj, pair_extent, atom_x, atom_y, atom_z):
    n_row = lax.axis_size("row")
    n_col = lax.axis_size("col")
    n_lay = lax.axis_size("layer")
    assert n_lay == 4 and n_col >= 4 and (n_row == 2 or n_row >= 4)
    assert n_row & (n_row - 1) == 0 and n_col & (n_col - 1) == 0
    axes = (n_row, n_col, n_lay)
    atoms, slots = neighbors.shape
    size = sign_start.shape[2]
    steps = [0, 1] if n_row == 2 else [0, 1, -1]
    count = len(steps)
    others = range(1, count)
    own = sign_start[0]
    flat = own.reshape(slots * size, size)
    listings = neighbors.T
    full = slots * size
    half = full // 2
    most = half - size
    n_pick = column_targets(n_row)
    picks = n_pick * size
    part = picks + GEO

    def on_row(value, di):
        return from_offset(value, "row", steps[di])

    x_row = {di: on_row(flat, di) for di in others}
    y_row = from_layer(flat, 2)
    m_row = from_layer(flat, 1)
    picked = pl.pallas_call(
        functools.partial(pick_kernel, axes),
        out_shape=jax.ShapeDtypeStruct((part, size), own.dtype),
        in_specs=[HBM] * 6,
        out_specs=VMEM,
        scratch_shapes=[
            pltpu.SMEM((slots, atoms), jnp.int32),
            pltpu.SMEM((1, slots), jnp.int32),
            pltpu.SMEM((atoms,), jnp.int32),
            pltpu.SMEM((atoms,), jnp.int32),
            pltpu.SMEM((atoms,), jnp.int32),
            pltpu.SMEM((n_pick + 1,), jnp.int32),
            pltpu.SemaphoreType.DMA((5,)),
            pltpu.SemaphoreType.DMA((n_pick,)),
        ],
        compiler_params=pltpu.CompilerParams(vmem_limit_bytes=60 << 20),
        name="pick_column_blocks",
    )(listings, pair_extent, atom_x, atom_y, atom_z, own)
    down = from_column(picked, 1)
    up = from_column(picked, 0)

    halves = pack(
        [y_row] + [x_row[di] for di in others] + [picked],
        [[(0, half, most)]] + [[(di, 0, most)] for di in others] + [[(count, picks, GEO)]],
        [],
        "pack_halves",
    )
    ends = {di: on_row(halves[0], di) for di in others}
    tops = {di: from_layer(halves[di], 2) for di in others}

    at = {}
    buffers = {}

    def note(name, value, contents):
        buffers[name] = value
        start = 0
        for what, rows in contents:
            if what is not None:
                at[what] = (name, start)
            start += rows

    def row_of(di, flip, start=0, stop=slots):
        return [(("row", slot, di, flip), size) for slot in range(start, stop)]

    halfway = slots // 2

    def side_of(kind, di, flip):
        return [((kind, di, flip), picks)]

    note("own", flat, row_of(0, 0))
    note("mate", m_row, row_of(0, 1))
    note("far", y_row, row_of(0, 2))
    note("up", up, side_of("up", 0, 0) + [(("up geo", 0, 0), GEO)])
    note("down", down, side_of("down", 0, 0) + [(("down geo", 0, 0), GEO)])
    note("geo", halves[count], [(("geo", 0, 0), GEO)])
    for di in others:
        note(("x", di), x_row[di], row_of(di, 0))
        note(("end", di), ends[di], row_of(di, 2, halfway, slots - 1))
        note(("top", di), tops[di], row_of(di, 2, 0, halfway - 1))

    corners = [("end", di) for di in others] + [("top", di) for di in others]
    names = ["down", "up", "geo", "far"] + [("x", di) for di in others]
    plans = [
        [(1, 0, picks), (0, 0, picks), (3, full - size, size), (2, 0, GEO), (1, picks, GEO), (0, picks, GEO)],
        [(1, 0, picks), (0, 0, picks)] + [(di + 3, most, size) for di in others] + [(2, 0, GEO), (1, picks, GEO), (0, picks, GEO)],
        [(2, 0, GEO), (1, picks, GEO), (0, picks, GEO)],
    ]
    two_x, two_y, geos = pack([buffers[name] for name in names], plans, [m_row], "pack_two")
    to_mate = corners + ["up", "down"]
    for di in others:
        note(("mate x", di), from_layer(x_row[di], 1), row_of(di, 1))
    note("mate far", from_layer(y_row, 1), row_of(0, 3))

    early_order = ["own", "mate", "far", "up", "down", "geo"] + [("x", di) for di in others]
    early_order += [("mate x", di) for di in others] + ["mate far"]
    early_order += corners + [("two x", di) for di in others] + ["two y", "two m"]
    late_order = [("three x", di) for di in others] + ["three y", "three m"]
    late_order += ["four"]

    contents = {}
    for di in others:
        contents["two x", di] = side_of("up", di, 0) + side_of("down", di, 0)
        contents["two x", di] += row_of(di, 2, slots - 1, slots) + [(("geo", di, 0), GEO)]
        contents["two x", di] += [(("up geo", di, 0), GEO), (("down geo", di, 0), GEO)]
    contents["two y"] = side_of("up", 0, 2) + side_of("down", 0, 2)
    contents["two y"] += sum([row_of(di, 2, halfway - 1, halfway) for di in others], []) + [(None, 3 * GEO)]
    contents["two m"] = sum([row_of(di, 3, halfway, slots - 1) for di in others], [])
    contents["two m"] += sum([row_of(di, 3, 0, halfway - 1) for di in others], [])
    contents["two m"] += side_of("up", 0, 1) + side_of("down", 0, 1)
    for di in others:
        contents["three x", di] = side_of("up", di, 2)
    contents["three y"] = sum([side_of("down", di, 2) for di in others], [])
    contents["three m"] = []
    for di in others:
        contents["three m"] += side_of("up", di, 1) + side_of("down", di, 1) + row_of(di, 3, slots - 1, slots)
    contents["three m"] += side_of("up", 0, 3) + side_of("down", 0, 3)
    contents["three m"] += sum([row_of(di, 3, halfway - 1, halfway) for di in others], []) + [(None, 3 * GEO)]
    contents["three m"] += [("geos", count * 3 * GEO)]
    contents["four"] = sum([side_of("up", di, 3) for di in others], [])
    contents["four"] += sum([side_of("down", di, 3) for di in others], [])
    lengths = {name: sum(rows for _, rows in content) for name, content in contents.items()}
    for name in early_order:
        if name in buffers:
            lengths[name] = buffers[name].shape[0]
    base = {}
    total = 0
    for name in early_order + late_order:
        base[name] = total
        total += lengths[name]
        if name == early_order[-1]:
            late_from = total
    located = dict(at)
    for name, content in contents.items():
        start = 0
        for what, rows in content:
            located[what] = (name, start)
            start += rows
    layout = [
        base[located["row", slot, di, flip][0]] + located["row", slot, di, flip][1]
        for di in range(count)
        for flip in range(n_lay)
        for slot in range(slots)
    ]
    layout += [
        base[located[kind, di, flip][0]] + located[kind, di, flip][1]
        for kind in ("up", "down")
        for di in range(count)
        for flip in range(n_lay)
    ]
    pairs = slots * (slots + 1) // 2
    entries = pairs + UNROLL + 1
    early_table, late_table, last_table, info = pl.pallas_call(
        functools.partial(prepare_kernel, axes, count, tuple(layout), late_from, base["four"]),
        out_shape=(
            jax.ShapeDtypeStruct((entries,), jnp.int32),
            jax.ShapeDtypeStruct((entries,), jnp.int32),
            jax.ShapeDtypeStruct((entries,), jnp.int32),
            jax.ShapeDtypeStruct((slots + 2,), jnp.int32),
        ),
        in_specs=[HBM, HBM, ANY],
        out_specs=(SMEM, SMEM, SMEM, SMEM),
        scratch_shapes=[
            pltpu.SMEM((slots, atoms), jnp.int32),
            pltpu.SMEM((atoms,), jnp.int32),
            pltpu.SMEM((3, slots), jnp.int32),
            pltpu.SMEM((atoms,), jnp.int32),
            pltpu.SMEM((len(layout),), jnp.int32),
            pltpu.SemaphoreType.DMA((2,)),
        ],
        compiler_params=pltpu.CompilerParams(vmem_limit_bytes=1 << 20),
        cost_estimate=pl.CostEstimate(flops=1000, bytes_accessed=1000, transcendentals=0),
        name="prepare",
    )(listings, atom_size, two_x)

    plans = [[(i, 0, picks if name in ("up", "down") else most) for i, name in enumerate(to_mate)]]
    two_m = pack([buffers[name] for name in to_mate], plans, [], "pack_two_mate", 3_000_000_000)[0]
    for di in others:
        note(("two x", di), on_row(two_x, di), contents["two x", di])
    note("two y", from_layer(two_y, 2), contents["two y"])
    early_mates = ["mate far"] + [("mate x", di) for di in others]
    note("two m", from_layer(two_m, 1), contents["two m"])

    buffers["geos"] = geos
    names = ["two y", "geos"] + [("two x", di) for di in others]
    place = {name: i for i, name in enumerate(names)}
    gather = [(place["geos"], 0, 3 * GEO)] + [(place["two x", di], 2 * picks + size, 3 * GEO) for di in others]
    xs = [place["two x", di] for di in others]
    plans = [
        [(0, 0, picks)],
        [(x, picks, picks) for x in xs],
        [(x, 0, 2 * picks + size) for x in xs] + [(0, 0, lengths["two y"])] + gather,
        gather,
    ]
    three_x, three_y, three_m, geos = pack([buffers[name] for name in names], plans, [buffers[name] for name in early_mates] + [two_m, info], "pack_three")
    for di in others:
        note(("three x", di), on_row(three_x, di), contents["three x", di])
    note("three y", from_layer(three_y, 2), contents["three y"])
    note("three m", from_layer(three_m, 1), contents["three m"])
    third_geos = from_layer(geos, 3)

    spread, own_basis = pl.pallas_call(
        functools.partial(spread_kernel, axes),
        out_shape=(
            jax.ShapeDtypeStruct((LANES, full), jnp.bfloat16),
            jax.ShapeDtypeStruct((16, size), jnp.bfloat16),
        ),
        in_specs=[HBM, VMEM, ANY],
        out_specs=(VMEM, VMEM),
        scratch_shapes=[pltpu.SMEM((slots, atoms), jnp.int32), pltpu.SemaphoreType.DMA((1,))],
        compiler_params=pltpu.CompilerParams(vmem_limit_bytes=(2 << 20) + atoms * 16384),
        cost_estimate=pl.CostEstimate(flops=1000, bytes_accessed=1000, transcendentals=0),
        name="spread_basis",
    )(listings, basis_proj.transpose(1, 0, 2).reshape(SHELLS * atoms, size), three_x)

    early_values = [buffers[name] for name in early_order]
    gram = pl.pallas_call(
        functools.partial(gram_kernel, len(early_values)),
        out_shape=jax.ShapeDtypeStruct((full, full), jnp.bfloat16),
        in_specs=[SMEM] + [VMEM] * len(early_values) + [ANY],
        out_specs=VMEM,
        scratch_shapes=[pltpu.VMEM((late_from, LANES), jnp.bfloat16)],
        compiler_params=pltpu.CompilerParams(vmem_limit_bytes=(6 << 20) + 2 * late_from * LANES * 2),
        cost_estimate=pl.CostEstimate(flops=1000, bytes_accessed=1000, transcendentals=0),
        name="gram_early",
    )(early_table, *early_values, three_x)

    thirds = [buffers["three x", di] for di in others] + [buffers["three y"]]
    four = pack(thirds, [[(i, 0, value.shape[0]) for i, value in enumerate(thirds)]], [gram, third_geos, own_basis], "pack_four")[0]
    note("four", from_layer(four, 1), contents["four"])

    column_steps = (0, 1, -1)
    tile_steps = [(dr, dc) for dr in steps for dc in column_steps]
    tiles = len(tile_steps)
    periods = (float(BX * n_row), float(BY * n_col), float(BZ * n_lay))
    plane, line = pl.pallas_call(
        functools.partial(profile_kernel, periods, tile_steps, at["geos"][1]),
        out_shape=(
            jax.ShapeDtypeStruct((tiles, SHELLS, BX * BY, LANES), jnp.bfloat16),
            jax.ShapeDtypeStruct((tiles, SHELLS, LANES, BZ), jnp.bfloat16),
        ),
        in_specs=[ANY] * 3,
        out_specs=(VMEM, VMEM),
        scratch_shapes=[
            pltpu.VMEM((3, tiles * GEO, LANES), jnp.bfloat16),
            pltpu.SemaphoreType.DMA((3,)),
        ],
        compiler_params=pltpu.CompilerParams(vmem_limit_bytes=10 << 20),
        cost_estimate=pl.CostEstimate(flops=1000, bytes_accessed=1000, transcendentals=0),
        name="profiles",
    )(geos, buffers["three m"], third_geos)

    late_values = [buffers[name] for name in late_order[:-1]]
    middle, own_kept = pl.pallas_call(
        functools.partial(middle_kernel, len(late_values)),
        out_shape=(
            jax.ShapeDtypeStruct((full, full), jnp.bfloat16),
            jax.ShapeDtypeStruct((size, full), jnp.bfloat16),
        ),
        in_specs=[SMEM, SMEM] + [VMEM] * (2 + len(late_values)) + [ANY],
        out_specs=(VMEM, VMEM),
        scratch_shapes=[pltpu.VMEM((base["four"] - late_from, LANES), jnp.bfloat16)],
        compiler_params=pltpu.CompilerParams(
            vmem_limit_bytes=(13 << 20) + 2 * (base["four"] - late_from) * LANES * 2
        ),
        cost_estimate=pl.CostEstimate(flops=1000, bytes_accessed=1000, transcendentals=0),
        name="gram_middle",
    )(late_table, info, own, gram, *late_values, four)

    late_values = [buffers["four"]]
    sign_next, coef = pl.pallas_call(
        functools.partial(step_kernel, len(late_values)),
        out_shape=(
            jax.ShapeDtypeStruct((slots, size, size), jnp.bfloat16),
            jax.ShapeDtypeStruct((8, LANES), jnp.float32),
        ),
        in_specs=[SMEM, SMEM, VMEM, VMEM, VMEM, VMEM] + [VMEM] * len(late_values),
        out_specs=(VMEM, VMEM),
        scratch_shapes=[
            pltpu.VMEM((total - base["four"], LANES), jnp.bfloat16),
            pltpu.VMEM((full, full), jnp.bfloat16),
            pltpu.VMEM((size, full), jnp.bfloat16),
        ],
        compiler_params=pltpu.CompilerParams(vmem_limit_bytes=(15 << 20) + 2 * (total - late_from) * LANES * 2),
        cost_estimate=pl.CostEstimate(flops=1_300_000_000, bytes_accessed=8_000_000, transcendentals=0),
        name="square_cube_coefficients",
    )(last_table, info, own_basis, spread, own_kept, middle, *late_values)

    mate_coef = from_layer(coef, 1)
    third_coef = from_layer(coef, 3)
    odd = lax.axis_index("layer") % 2 == 1
    below = jnp.where(odd, mate_coef, third_coef)
    above = jnp.where(odd, third_coef, mate_coef)
    merged = jnp.concatenate(
        [
            coef[:, : 4 * SPAN],
            below[:, SPAN : 3 * SPAN],
            above[:, 3 * SPAN : 4 * SPAN],
            jnp.zeros((8, LANES - 7 * SPAN), jnp.float32),
        ],
        axis=1,
    )
    given, token = pack([sign_next.reshape(full, size)], [[(0, 0, full)], [(0, 0, GEO)]], [], "give_sign")
    parts = [merged] + [on_row(merged, di) for di in others]
    stacked = pack(parts, [[(i, 0, 8) for i in range(count)]], [token], "stack_tiles")[0]
    far_side = from_column(stacked, 1)
    received = [stacked, far_side, from_column(stacked, 0)]

    density = pl.pallas_call(
        functools.partial(density_kernel, len(column_steps)),
        out_shape=jax.ShapeDtypeStruct((BX * BY, BZ), jnp.float32),
        in_specs=[VMEM] * (len(received) + 2),
        out_specs=VMEM,
        compiler_params=pltpu.CompilerParams(vmem_limit_bytes=16 << 20),
        cost_estimate=pl.CostEstimate(flops=310_000_000, bytes_accessed=4_000_000, transcendentals=0),
        name="density",
    )(*received, plane, line.reshape(tiles * SHELLS * LANES, BZ))
    return given.reshape(1, slots, size, size), density.reshape(BX, BY, BZ)


def solution(mesh):
    rows = P(("row", "col", "layer"), None, None, None)
    in_specs = (rows, P(), P(), P(), P(("row", "col", "layer"), None), P(), P(), P())
    out_specs = (rows, P("row", "col", "layer"))
    return jax.shard_map(local, mesh=mesh, in_specs=in_specs, out_specs=out_specs, check_vma=False)
```

```python
import functools

import jax
import jax.numpy as jnp
from jax import lax
from jax.experimental import pallas as pl
from jax.experimental.pallas import tpu as pltpu
from jax.sharding import PartitionSpec as P

BX = 16
BY = 16
BZ = 128
LANES = 128
UNROLL = 4
SHELLS = 6
SPAN = 3 * SHELLS
GEO = 16
VMEM = pl.BlockSpec(memory_space=pltpu.VMEM)
SMEM = pl.BlockSpec(memory_space=pltpu.SMEM)
ANY = pl.BlockSpec(memory_space=pl.ANY)
HBM = pl.BlockSpec(memory_space=pltpu.HBM)


def from_offset(x, axis, step):
    count = lax.axis_size(axis)
    return lax.ppermute(x, axis, [((i + step) % count, i) for i in range(count)])


def from_column(x, side):
    count = lax.axis_size("col")
    step = [1 if (i + side) % 2 == 0 else -1 for i in range(count)]
    return lax.ppermute(x, "col", [((i + step[i]) % count, i) for i in range(count)])


def from_layer(x, flip):
    count = lax.axis_size("layer")
    return lax.ppermute(x, "layer", [(i ^ flip, i) for i in range(count)])


def column_targets(n_row):
    return 5 if n_row == 2 else 7


def target_place(n_row, step_row, step_lay, row):
    same = jnp.where(step_lay < 3, step_lay, -1)
    if n_row == 2:
        lead = step_lay - row
        across = jnp.where((lead >= 0) & (lead < 2), 3 + lead, -1)
    else:
        across = 3 + step_lay
    return jnp.where(step_row == 0, same, jnp.where(step_row == 1, across, -1))


class Places:
    def __init__(self, n_row, n_col, n_lay):
        self.n_row, self.n_col, self.n_lay = n_row, n_col, n_lay
        self.lay_bits = n_lay.bit_length() - 1
        self.col_bits = n_col.bit_length() - 1
        self.row = lax.axis_index("row")
        self.col = lax.axis_index("col")
        self.lay = lax.axis_index("layer")
        self.me = (((self.row << self.col_bits) + self.col) << self.lay_bits) + self.lay

    def split(self, atom):
        return (
            atom >> (self.lay_bits + self.col_bits),
            (atom >> self.lay_bits) & (self.n_col - 1),
            atom & (self.n_lay - 1),
        )


def load(sources, targets, sems):
    copies = [pltpu.make_async_copy(a, b, sems.at[i]) for i, (a, b) in enumerate(zip(sources, targets))]
    for copy in copies:
        copy.start()
    for copy in copies:
        copy.wait()


def own_ranks(at, neighbors_ref):
    seen = [jnp.int32(0)] * at.n_lay
    listed = []
    for w in range(neighbors_ref.shape[0]):
        atom = neighbors_ref[w, at.me]
        step_lay = (atom - at.lay) & (at.n_lay - 1)
        rank = jnp.int32(0)
        for k in range(at.n_lay):
            rank = jnp.where(step_lay == k, 3 * k + seen[k], rank)
            seen[k] = seen[k] + (step_lay == k).astype(jnp.int32)
        listed.append((atom, rank))
    return listed


def pick_kernel(axes, *refs):
    sign_ref, out_ref, geo_ref, neighbors_ref, extent_ref, x_ref, y_ref, z_ref, place_ref, loads, sems = refs[5:]
    at = Places(*axes)
    slots = sign_ref.shape[0]
    n_pick = place_ref.shape[0] - 1
    size = sign_ref.shape[1]
    for i in range(n_pick + 1):
        place_ref[i] = 0
    load(refs[:5], (neighbors_ref, extent_ref, x_ref, y_ref, z_ref), loads)
    for w in range(slots):
        row, col, lay = at.split(neighbors_ref[w, at.me])
        place = target_place(at.n_row, (row - at.row) & (at.n_row - 1), (lay - at.lay) & (at.n_lay - 1), at.row)
        place_ref[jnp.where((col == at.col) & (place >= 0), place, n_pick)] = w
    copies = []
    for i in range(n_pick):
        copy = pltpu.make_async_copy(sign_ref.at[place_ref[i]], out_ref.at[pl.ds(i * size, size)], sems.at[i])
        copy.start()
        copies.append(copy)
    ranks = own_ranks(at, neighbors_ref)
    sub = lax.broadcasted_iota(jnp.int32, (GEO, LANES), 0)
    lane_pair = lax.broadcasted_iota(jnp.int32, (GEO, LANES), 1) // SHELLS
    geo = jnp.zeros((GEO, LANES), jnp.int32)
    for w, (atom, rank) in enumerate(ranks):
        row, col, lay = at.split(atom)
        go_row = ((row - at.row + 1) & (at.n_row - 1)) - 1
        go_col = ((col - at.col + 1) & (at.n_col - 1)) - 1
        go_lay = jnp.minimum(((lay - at.lay + 1) & (at.n_lay - 1)) - 1, 1)
        twice_x = x_ref[at.me] + x_ref[atom] + BX * go_row
        twice_y = y_ref[at.me] + y_ref[atom] + BY * go_col
        twice_z = z_ref[at.me] + z_ref[atom] + BZ * go_lay - BZ
        extent = extent_ref[0, w]
        values = jnp.where(sub == 0, twice_x, jnp.where(sub == 1, twice_y, jnp.where(sub == 2, twice_z, extent)))
        geo = jnp.where(lane_pair == rank, values, geo)
    geo = geo.astype(jnp.float32).astype(out_ref.dtype)
    geo_ref[...] = geo
    out_ref[n_pick * size :] = geo
    for copy in copies:
        copy.wait()


def spread_kernel(axes, *refs):
    basis_ref = refs[1]
    spread_ref, own_basis_ref, neighbors_ref, loads = refs[-4:]
    at = Places(*axes)
    load(refs[:1], (neighbors_ref,), loads)
    slots, atoms = neighbors_ref.shape
    bits = atoms.bit_length() - 1

    def hot(rows, atom, first):
        sub = lax.broadcasted_iota(jnp.int32, (rows, SHELLS * atoms), 0)
        lane = lax.broadcasted_iota(jnp.int32, (rows, SHELLS * atoms), 1)
        return ((lane & (atoms - 1)) == atom) & (sub == first + (lane >> bits))

    def rows_of(chosen):
        picked = jnp.where(chosen, 1.0, 0.0).astype(jnp.bfloat16)
        return jnp.dot(picked, basis_ref[...], preferred_element_type=jnp.float32).astype(jnp.bfloat16)

    for w, (atom, rank) in enumerate(own_ranks(at, neighbors_ref)):
        spread_ref[:, w * LANES : (w + 1) * LANES] = rows_of(hot(LANES, atom, rank * SHELLS))
    own_basis_ref[...] = rows_of(hot(16, at.me, 0))


def prepare_kernel(axes, count, layout, late_from, last_from, *refs):
    early_ref, late_ref, last_ref, info_ref, neighbors_ref, size_ref, known, inverse, layout_ref, loads = refs[-10:]
    at = Places(*axes)
    load(refs[:2], (neighbors_ref, size_ref), loads)
    slots = neighbors_ref.shape[0]
    lines = count * at.n_lay
    for i, value in enumerate(layout):
        layout_ref[i] = value
    self_slot = jnp.int32(0)
    for w in range(slots):
        atom = neighbors_ref[w, at.me]
        row, col, lay = at.split(atom)
        step_row = (row - at.row) & (at.n_row - 1)
        self_slot = jnp.where(atom == at.me, w, self_slot)
        info_ref[w] = size_ref[atom]
        known[0, w] = atom
        known[1, w] = jnp.where(col == at.col, 0, jnp.where(col == (at.col ^ 1), 1, 2))
        known[2, w] = jnp.where(step_row == 0, 0, jnp.where(step_row == 1, 1, 2)) * at.n_lay + (lay ^ at.lay)
        inverse[atom] = -1
    info_ref[slots] = size_ref[at.me]
    info_ref[slots + 1] = self_slot

    def row_of_pairs(v, totals):
        early, late, last = totals
        atom = known[0, v]
        side = known[1, v]
        line = known[2, v]
        for u in range(slots):
            inverse[neighbors_ref[u, atom]] = v * 16 + u

        def from_row(totals):
            total, late, last = totals
            for w in range(slots):
                mark = inverse[known[0, w]]
                chosen = ((mark >> 4) == v) & ((known[1, w] != 0) | (v <= w))
                where = layout_ref[line * slots + (mark & 15)]
                is_late = where >= late_from
                entry = v + 16 * w
                early_ref[total + 1] = entry + 256 * where
                late_ref[late + 1] = entry + 256 * (where - late_from)
                total = total + (chosen & ~is_late).astype(jnp.int32)
                late = late + (chosen & is_late).astype(jnp.int32)
            return total, late, last

        def from_column(totals):
            early, late, last = totals
            row, _, lay = at.split(atom)
            beside = layout_ref[lines * slots + (side - 1) * lines + line]
            for w in range(slots):
                other = known[0, w]
                mark = inverse[other]
                o_row, _, o_lay = at.split(other)
                d_row = (o_row - row) & (at.n_row - 1)
                d_lay = (o_lay - lay) & (at.n_lay - 1)
                there = target_place(at.n_row, d_row, d_lay, row)
                back = target_place(at.n_row, -d_row & (at.n_row - 1), -d_lay & (at.n_lay - 1), o_row)
                chosen = ((mark >> 4) == v) & (side == known[1, w]) & (there >= 0) & ((back < 0) | (v <= w))
                where = beside + there * LANES
                is_late = where >= late_from
                is_last = where >= last_from
                entry = v + 16 * w
                early_ref[early + 1] = entry + 256 * where
                late_ref[late + 1] = entry + 256 * (where - late_from)
                last_ref[last + 1] = entry + 256 * (where - last_from)
                early = early + (chosen & ~is_late).astype(jnp.int32)
                late = late + (chosen & is_late & ~is_last).astype(jnp.int32)
                last = last + (chosen & is_last).astype(jnp.int32)
            return early, late, last

        return lax.cond(side == 0, from_row, from_column, (early, late, last))

    totals = lax.fori_loop(0, slots, row_of_pairs, (jnp.int32(0),) * 3)
    for ref, total in zip((early_ref, late_ref, last_ref), totals):
        ref[0] = (total + UNROLL - 1) // UNROLL
        for i in range(UNROLL - 1):
            ref[total + i + 1] = ref[jnp.maximum(total, 1)]


def pack_kernel(moves, inputs, *refs):
    for source, start, rows, target, place in moves:
        refs[inputs + target][place : place + rows] = refs[source][start : start + rows]


def pack(values, plans, extra, name, cost=0):
    moves, shapes = [], []
    for target, plan in enumerate(plans):
        place = 0
        for source, start, rows in plan:
            moves.append((source, start, rows, target, place))
            place += rows
        shapes.append(jax.ShapeDtypeStruct((place, LANES), values[0].dtype))
    inputs = len(values) + len(extra)
    return pl.pallas_call(
        functools.partial(pack_kernel, tuple(moves), inputs),
        out_shape=tuple(shapes),
        in_specs=[VMEM] * len(values) + [ANY] * len(extra),
        out_specs=tuple([VMEM] * len(plans)),
        compiler_params=pltpu.CompilerParams(
            vmem_limit_bytes=(1 << 20) + 256 * sum(x.shape[0] for x in list(values) + shapes)
        ),
        cost_estimate=pl.CostEstimate(flops=cost, bytes_accessed=1000, transcendentals=0),
        name=name,
    )(*values, *extra)


def fill(piece_refs, pool):
    place = 0
    for piece in piece_refs:
        rows = piece.shape[0]
        pool[place : place + rows] = piece[...]
        place += rows


def place_pairs(table_ref, pool, gram, size):
    def place(i, carry):
        for k in range(UNROLL):
            entry = table_ref[i * UNROLL + k + 1]
            p = pl.multiple_of((entry & 15) * size, size)
            q = pl.multiple_of(((entry >> 4) & 15) * size, size)
            block = pool[pl.ds(pl.multiple_of(entry >> 8, 16), size)]
            gram[pl.ds(p, size), pl.ds(q, size)] = block
            gram[pl.ds(q, size), pl.ds(p, size)] = block.T
        return carry

    lax.fori_loop(0, table_ref[0], place, 0)


def gram_kernel(pieces, *refs):
    table_ref = refs[0]
    piece_refs = refs[1 : 1 + pieces]
    gram, pool = refs[-2:]
    size = LANES
    fill(piece_refs, pool)
    for v in range(gram.shape[0] // size):
        gram[v * size : (v + 1) * size] = jnp.zeros((size, gram.shape[1]), gram.dtype)
    place_pairs(table_ref, pool, gram, size)


def middle_kernel(pieces, *refs):
    table_ref, info_ref, sign_ref, early_ref = refs[:4]
    piece_refs = refs[4 : 4 + pieces]
    gram, own, pool = refs[-3:]
    slots, size = sign_ref.shape[0], sign_ref.shape[1]
    fill(piece_refs, pool)
    for v in range(slots):
        gram[v * size : (v + 1) * size] = early_ref[v * size : (v + 1) * size]
    place_pairs(table_ref, pool, gram, size)
    rows = lax.broadcasted_iota(jnp.int32, (size, size), 0)
    lanes = lax.broadcasted_iota(jnp.int32, (size, size), 1)
    for w in range(slots):
        kept = (rows < info_ref[slots]) & (lanes < info_ref[w])
        block = jnp.where(kept, sign_ref[w].astype(jnp.float32), 0.0)
        own[:, w * size : (w + 1) * size] = block.astype(own.dtype)


def step_kernel(pieces, *refs):
    table_ref, info_ref, basis_ref, spread_ref, own, early_ref = refs[:6]
    piece_refs = refs[6 : 6 + pieces]
    next_ref, coef_ref, pool, gram, square = refs[-5:]
    slots, size = next_ref.shape[0], next_ref.shape[1]
    fill(piece_refs, pool)
    for v in range(slots):
        gram[v * size : (v + 1) * size] = early_ref[v * size : (v + 1) * size]
    own_size = info_ref[slots]
    self_slot = info_ref[slots + 1]
    place_pairs(table_ref, pool, gram, size)
    wide = 2 * size
    wide_lanes = lax.broadcasted_iota(jnp.int32, (size, wide), 1)
    wide_rows = lax.broadcasted_iota(jnp.int32, (size, wide), 0)

    def column_kept(n):
        first = info_ref[2 * n]
        second = info_ref[2 * n + 1]
        return (wide_lanes < first) | ((wide_lanes >= size) & (wide_lanes < size + second))

    for n in range(slots // 2):
        part = jnp.dot(own[...], gram[:, n * wide : (n + 1) * wide], preferred_element_type=jnp.float32)
        square[:, n * wide : (n + 1) * wide] = jnp.where(column_kept(n), part, 0.0).astype(square.dtype)
    basis = jnp.concatenate([basis_ref[...], basis_ref[...]], axis=1)
    coef = jnp.zeros((2 * basis_ref.shape[0], LANES), jnp.float32)
    across = (((1,), (1,)), ((), ()))
    for n in range(slots // 2):
        part = jnp.dot(square[...], gram[:, n * wide : (n + 1) * wide], preferred_element_type=jnp.float32)
        cube = jnp.where(column_kept(n), part, 0.0)
        full = 1.5 * own[:, n * wide : (n + 1) * wide].astype(jnp.float32) - 0.5 * cube
        next_ref[2 * n] = full[:, :size].astype(next_ref.dtype)
        next_ref[2 * n + 1] = full[:, size:].astype(next_ref.dtype)
        shift = (self_slot - 2 * n) * size
        is_self = (self_slot >= 2 * n) & (self_slot < 2 * n + 2)
        diag = (wide_lanes == wide_rows + shift) & (wide_rows < own_size) & is_self
        dmat = 0.5 * (jnp.where(diag, 1.0, 0.0) - full)
        high = dmat.astype(jnp.bfloat16)
        low = (dmat - high.astype(jnp.float32)).astype(jnp.bfloat16)
        half = jnp.dot(basis, jnp.concatenate([high, low], axis=0), preferred_element_type=jnp.float32)
        half_high = half.astype(jnp.bfloat16)
        half_low = (half - half_high.astype(jnp.float32)).astype(jnp.bfloat16)
        coef = coef + lax.dot_general(
            jnp.concatenate([half_high, half_low], axis=0),
            spread_ref[:, n * wide : (n + 1) * wide],
            across,
            preferred_element_type=jnp.float32,
        )
    coef = coef[: basis_ref.shape[0]] + coef[basis_ref.shape[0] :]
    coef_ref[...] = coef[: coef_ref.shape[0]]


def profile_kernel(periods, steps, mate_from, *refs):
    own_ref, mate_ref, third_ref = refs[:3]
    plane_ref, line_ref, geos, sems = refs[-4:]
    odd = (lax.axis_index("layer") & 1) == 1
    rows = len(steps) * GEO
    copies = []
    for k, source in enumerate((own_ref, mate_ref.at[pl.ds(mate_from, rows)], third_ref)):
        copy = pltpu.make_async_copy(source, geos.at[k], sems.at[k])
        copy.start()
        copies.append(copy)
    steps_x = lax.broadcasted_iota(jnp.int32, (BX, LANES), 0).astype(jnp.float32)
    steps_y = lax.broadcasted_iota(jnp.int32, (BY, LANES), 0).astype(jnp.float32)
    grid_z = lax.broadcasted_iota(jnp.int32, (LANES, BZ), 1).astype(jnp.float32)
    lane = lax.broadcasted_iota(jnp.int32, (1, LANES), 1)
    shell = (lane % SHELLS + 1).astype(jnp.float32)
    valid = lane < 7 * SPAN
    from_own = lane < 4 * SPAN
    from_below = lane < 6 * SPAN
    lift = jnp.where(from_own, 0.0, jnp.where(from_below, -float(BZ), float(BZ))) + 0.5 * BZ

    def nearest(offset, period):
        return offset - period * jnp.floor(offset * (1.0 / period) + 0.5)

    for copy in copies:
        copy.wait()
    ahead = 1.0 - 2.0 * (lax.axis_index("col") & 1).astype(jnp.float32)
    for o, (step_row, side) in enumerate(steps):
        own, first, third = (geos[k, o * GEO : (o + 1) * GEO].astype(jnp.float32) for k in range(3))
        below = jnp.where(odd, first, third)
        above = jnp.where(odd, third, first)
        moved = jnp.where(from_below, pltpu.roll(below, 3 * SPAN, axis=1), pltpu.roll(above, 3 * SPAN, axis=1))
        geo = jnp.where(from_own, own, moved)
        extent = jnp.where(valid, geo[3:4], 1.0)
        inverse = (SHELLS / extent) * (SHELLS / extent)
        reach = jnp.where(valid, extent, -1.0)
        rate_t = inverse / (shell * shell)
        packed = jnp.concatenate(
            [0.5 * geo[2:3] + lift, reach, rate_t, inverse, jnp.zeros((4, LANES), jnp.float32)], axis=0
        )
        sub = packed.T
        d_x = nearest(steps_x - (0.5 * geo[0:1] + float(BX * step_row)), periods[0])
        d_y = nearest(steps_y - (0.5 * geo[1:2] + float(BY * side) * ahead), periods[1])
        inside_x = jnp.abs(d_x) <= reach
        inside_y = jnp.abs(d_y) <= reach
        squared_x = d_x * d_x
        squared_y = d_y * d_y
        d_z = nearest(grid_z - sub[:, 0:1], periods[2])
        inside_z = jnp.abs(d_z) <= sub[:, 1:2]
        squared_z = d_z * d_z
        for s in range(SHELLS):
            part = 1.0 / ((s + 1) * (s + 1))
            rate = inverse * part + rate_t
            along_x = jnp.where(inside_x, jnp.exp(-rate * squared_x), 0.0)
            along_y = jnp.where(inside_y, jnp.exp(-rate * squared_y), 0.0)
            for x in range(BX):
                plane_ref[o, s, x * BY : (x + 1) * BY] = (along_x[x : x + 1] * along_y).astype(plane_ref.dtype)
            rate_z = sub[:, 3:4] * part + sub[:, 2:3]
            line_ref[o, s] = jnp.where(inside_z, jnp.exp(-rate_z * squared_z), 0.0).astype(line_ref.dtype)


def merge_kernel(own_ref, mate_ref, third_ref, out_ref):
    odd = (lax.axis_index("layer") & 1) == 1
    lane = lax.broadcasted_iota(jnp.int32, out_ref.shape, 1)
    below = jnp.where(odd, mate_ref[...], third_ref[...])
    above = jnp.where(odd, third_ref[...], mate_ref[...])
    moved = jnp.where(lane < 6 * SPAN, pltpu.roll(below, 3 * SPAN, axis=1), pltpu.roll(above, 3 * SPAN, axis=1))
    out_ref[...] = jnp.where(lane < 4 * SPAN, own_ref[...], jnp.where(lane < 7 * SPAN, moved, 0.0))


def density_kernel(column_steps, *refs):
    coef_refs = refs[:column_steps]
    plane_ref, line_ref, out_ref = refs[column_steps:]
    total = jnp.zeros(out_ref.shape, jnp.float32)
    wide = SHELLS * LANES
    for o in range(plane_ref.shape[0]):
        coef = coef_refs[-o % column_steps]
        first = 8 * (o // column_steps)
        terms = [
            (plane_ref[o, s].astype(jnp.float32) * coef[first + s : first + s + 1, :]).astype(line_ref.dtype)
            for s in range(SHELLS)
        ]
        total = total + jnp.dot(
            jnp.concatenate(terms, axis=1),
            line_ref[o * wide : (o + 1) * wide],
            preferred_element_type=jnp.float32,
        )
    out_ref[...] = total


def local(sign_start, neighbors, atom_size, basis_proj, pair_extent, atom_x, atom_y, atom_z):
    n_row = lax.axis_size("row")
    n_col = lax.axis_size("col")
    n_lay = lax.axis_size("layer")
    assert n_lay == 4 and n_col >= 4 and (n_row == 2 or n_row >= 4)
    assert n_row & (n_row - 1) == 0 and n_col & (n_col - 1) == 0
    axes = (n_row, n_col, n_lay)
    atoms, slots = neighbors.shape
    size = sign_start.shape[2]
    steps = [0, 1] if n_row == 2 else [0, 1, -1]
    count = len(steps)
    others = range(1, count)
    own = sign_start[0]
    flat = own.reshape(slots * size, size)
    listings = neighbors.T
    full = slots * size
    half = full // 2
    most = half - size
    n_pick = column_targets(n_row)
    picks = n_pick * size
    part = picks + GEO

    def on_row(value, di):
        return from_offset(value, "row", steps[di])

    x_row = {di: on_row(flat, di) for di in others}
    y_row = from_layer(flat, 2)
    m_row = from_layer(flat, 1)
    picked, geo = pl.pallas_call(
        functools.partial(pick_kernel, axes),
        out_shape=(
            jax.ShapeDtypeStruct((part, size), own.dtype),
            jax.ShapeDtypeStruct((GEO, LANES), own.dtype),
        ),
        in_specs=[HBM] * 6,
        out_specs=(VMEM, VMEM),
        scratch_shapes=[
            pltpu.SMEM((slots, atoms), jnp.int32),
            pltpu.SMEM((1, slots), jnp.int32),
            pltpu.SMEM((atoms,), jnp.int32),
            pltpu.SMEM((atoms,), jnp.int32),
            pltpu.SMEM((atoms,), jnp.int32),
            pltpu.SMEM((n_pick + 1,), jnp.int32),
            pltpu.SemaphoreType.DMA((5,)),
            pltpu.SemaphoreType.DMA((n_pick,)),
        ],
        compiler_params=pltpu.CompilerParams(vmem_limit_bytes=60 << 20),
        name="pick_column_blocks",
    )(listings, pair_extent, atom_x, atom_y, atom_z, own)
    down = from_column(picked, 1)
    up = from_column(picked, 0)

    halves = pack(
        [y_row] + [x_row[di] for di in others] + [geo],
        [[(0, half, most)]] + [[(di, 0, most)] for di in others] + [[(count, 0, GEO)]],
        [],
        "pack_halves",
    )
    ends = {di: on_row(halves[0], di) for di in others}
    tops = {di: from_layer(halves[di], 2) for di in others}

    at = {}
    buffers = {}

    def note(name, value, contents):
        buffers[name] = value
        start = 0
        for what, rows in contents:
            if what is not None:
                at[what] = (name, start)
            start += rows

    def row_of(di, flip, start=0, stop=slots):
        return [(("row", slot, di, flip), size) for slot in range(start, stop)]

    halfway = slots // 2

    def side_of(kind, di, flip):
        return [((kind, di, flip), picks)]

    note("own", flat, row_of(0, 0))
    note("mate", m_row, row_of(0, 1))
    note("far", y_row, row_of(0, 2))
    note("up", up, side_of("up", 0, 0) + [(("up geo", 0, 0), GEO)])
    note("down", down, side_of("down", 0, 0) + [(("down geo", 0, 0), GEO)])
    note("geo", halves[count], [(("geo", 0, 0), GEO)])
    for di in others:
        note(("x", di), x_row[di], row_of(di, 0))
        note(("end", di), ends[di], row_of(di, 2, halfway, slots - 1))
        note(("top", di), tops[di], row_of(di, 2, 0, halfway - 1))

    corners = [("end", di) for di in others] + [("top", di) for di in others]
    names = ["down", "up", "geo", "far"] + [("x", di) for di in others]
    plans = [
        [(1, 0, picks), (0, 0, picks), (3, full - size, size), (2, 0, GEO), (1, picks, GEO), (0, picks, GEO)],
        [(1, 0, picks), (0, 0, picks)] + [(di + 3, most, size) for di in others] + [(2, 0, GEO), (1, picks, GEO), (0, picks, GEO)],
        [(2, 0, GEO), (1, picks, GEO), (0, picks, GEO)],
    ]
    two_x, two_y, geos = pack([buffers[name] for name in names], plans, [m_row], "pack_two")
    to_mate = corners + ["up", "down"]
    for di in others:
        note(("mate x", di), from_layer(x_row[di], 1), row_of(di, 1))
    note("mate far", from_layer(y_row, 1), row_of(0, 3))

    early_order = ["own", "mate", "far", "up", "down", "geo"] + [("x", di) for di in others]
    early_order += [("mate x", di) for di in others] + ["mate far"]
    early_order += corners + [("two x", di) for di in others] + ["two y", "two m"]
    late_order = [("three x", di) for di in others] + ["three y", "three m"]
    late_order += ["four"]

    contents = {}
    for di in others:
        contents["two x", di] = side_of("up", di, 0) + side_of("down", di, 0)
        contents["two x", di] += row_of(di, 2, slots - 1, slots) + [(("geo", di, 0), GEO)]
        contents["two x", di] += [(("up geo", di, 0), GEO), (("down geo", di, 0), GEO)]
    contents["two y"] = side_of("up", 0, 2) + side_of("down", 0, 2)
    contents["two y"] += sum([row_of(di, 2, halfway - 1, halfway) for di in others], []) + [(None, 3 * GEO)]
    contents["two m"] = sum([row_of(di, 3, halfway, slots - 1) for di in others], [])
    contents["two m"] += sum([row_of(di, 3, 0, halfway - 1) for di in others], [])
    contents["two m"] += side_of("up", 0, 1) + side_of("down", 0, 1)
    for di in others:
        contents["three x", di] = side_of("up", di, 2)
    contents["three y"] = sum([side_of("down", di, 2) for di in others], [])
    contents["three m"] = []
    for di in others:
        contents["three m"] += side_of("up", di, 1) + side_of("down", di, 1) + row_of(di, 3, slots - 1, slots)
    contents["three m"] += side_of("up", 0, 3) + side_of("down", 0, 3)
    contents["three m"] += sum([row_of(di, 3, halfway - 1, halfway) for di in others], []) + [(None, 3 * GEO)]
    contents["three m"] += [("geos", count * 3 * GEO)]
    contents["four"] = sum([side_of("up", di, 3) for di in others], [])
    contents["four"] += sum([side_of("down", di, 3) for di in others], [])
    lengths = {name: sum(rows for _, rows in content) for name, content in contents.items()}
    for name in early_order:
        if name in buffers:
            lengths[name] = buffers[name].shape[0]
    base = {}
    total = 0
    for name in early_order + late_order:
        base[name] = total
        total += lengths[name]
        if name == early_order[-1]:
            late_from = total
    located = dict(at)
    for name, content in contents.items():
        start = 0
        for what, rows in content:
            located[what] = (name, start)
            start += rows
    layout = [
        base[located["row", slot, di, flip][0]] + located["row", slot, di, flip][1]
        for di in range(count)
        for flip in range(n_lay)
        for slot in range(slots)
    ]
    layout += [
        base[located[kind, di, flip][0]] + located[kind, di, flip][1]
        for kind in ("up", "down")
        for di in range(count)
        for flip in range(n_lay)
    ]
    pairs = slots * (slots + 1) // 2
    entries = pairs + UNROLL + 1
    early_table, late_table, last_table, info = pl.pallas_call(
        functools.partial(prepare_kernel, axes, count, tuple(layout), late_from, base["four"]),
        out_shape=(
            jax.ShapeDtypeStruct((entries,), jnp.int32),
            jax.ShapeDtypeStruct((entries,), jnp.int32),
            jax.ShapeDtypeStruct((entries,), jnp.int32),
            jax.ShapeDtypeStruct((slots + 2,), jnp.int32),
        ),
        in_specs=[HBM, HBM, ANY],
        out_specs=(SMEM, SMEM, SMEM, SMEM),
        scratch_shapes=[
            pltpu.SMEM((slots, atoms), jnp.int32),
            pltpu.SMEM((atoms,), jnp.int32),
            pltpu.SMEM((3, slots), jnp.int32),
            pltpu.SMEM((atoms,), jnp.int32),
            pltpu.SMEM((len(layout),), jnp.int32),
            pltpu.SemaphoreType.DMA((2,)),
        ],
        compiler_params=pltpu.CompilerParams(vmem_limit_bytes=1 << 20),
        cost_estimate=pl.CostEstimate(flops=1000, bytes_accessed=1000, transcendentals=0),
        name="prepare",
    )(listings, atom_size, two_x)

    plans = [[(i, 0, picks if name in ("up", "down") else most) for i, name in enumerate(to_mate)]]
    two_m = pack([buffers[name] for name in to_mate], plans, [], "pack_two_mate", 3_000_000_000)[0]
    for di in others:
        note(("two x", di), on_row(two_x, di), contents["two x", di])
    note("two y", from_layer(two_y, 2), contents["two y"])
    early_mates = ["mate far"] + [("mate x", di) for di in others]
    note("two m", from_layer(two_m, 1), contents["two m"])

    buffers["geos"] = geos
    names = ["two y", "geos"] + [("two x", di) for di in others]
    place = {name: i for i, name in enumerate(names)}
    gather = [(place["geos"], 0, 3 * GEO)] + [(place["two x", di], 2 * picks + size, 3 * GEO) for di in others]
    xs = [place["two x", di] for di in others]
    plans = [
        [(0, 0, picks)],
        [(x, picks, picks) for x in xs],
        [(x, 0, 2 * picks + size) for x in xs] + [(0, 0, lengths["two y"])] + gather,
        gather,
    ]
    three_x, three_y, three_m, geos = pack([buffers[name] for name in names], plans, [buffers[name] for name in early_mates] + [two_m, info], "pack_three")
    for di in others:
        note(("three x", di), on_row(three_x, di), contents["three x", di])
    note("three y", from_layer(three_y, 2), contents["three y"])
    note("three m", from_layer(three_m, 1), contents["three m"])
    third_geos = from_layer(geos, 3)

    spread, own_basis = pl.pallas_call(
        functools.partial(spread_kernel, axes),
        out_shape=(
            jax.ShapeDtypeStruct((LANES, full), jnp.bfloat16),
            jax.ShapeDtypeStruct((16, size), jnp.bfloat16),
        ),
        in_specs=[HBM, VMEM, ANY],
        out_specs=(VMEM, VMEM),
        scratch_shapes=[pltpu.SMEM((slots, atoms), jnp.int32), pltpu.SemaphoreType.DMA((1,))],
        compiler_params=pltpu.CompilerParams(vmem_limit_bytes=(2 << 20) + atoms * 16384),
        cost_estimate=pl.CostEstimate(flops=1000, bytes_accessed=1000, transcendentals=0),
        name="spread_basis",
    )(listings, basis_proj.transpose(1, 0, 2).reshape(SHELLS * atoms, size), three_x)

    early_values = [buffers[name] for name in early_order]
    gram = pl.pallas_call(
        functools.partial(gram_kernel, len(early_values)),
        out_shape=jax.ShapeDtypeStruct((full, full), jnp.bfloat16),
        in_specs=[SMEM] + [VMEM] * len(early_values) + [ANY],
        out_specs=VMEM,
        scratch_shapes=[pltpu.VMEM((late_from, LANES), jnp.bfloat16)],
        compiler_params=pltpu.CompilerParams(vmem_limit_bytes=(6 << 20) + 2 * late_from * LANES * 2),
        cost_estimate=pl.CostEstimate(flops=1000, bytes_accessed=1000, transcendentals=0),
        name="gram_early",
    )(early_table, *early_values, three_x)

    thirds = [buffers["three x", di] for di in others] + [buffers["three y"]]
    four = pack(thirds, [[(i, 0, value.shape[0]) for i, value in enumerate(thirds)]], [gram, third_geos, own_basis], "pack_four")[0]
    note("four", from_layer(four, 1), contents["four"])

    column_steps = (0, 1, -1)
    tile_steps = [(dr, dc) for dr in steps for dc in column_steps]
    tiles = len(tile_steps)
    periods = (float(BX * n_row), float(BY * n_col), float(BZ * n_lay))
    plane, line = pl.pallas_call(
        functools.partial(profile_kernel, periods, tile_steps, at["geos"][1]),
        out_shape=(
            jax.ShapeDtypeStruct((tiles, SHELLS, BX * BY, LANES), jnp.bfloat16),
            jax.ShapeDtypeStruct((tiles, SHELLS, LANES, BZ), jnp.bfloat16),
        ),
        in_specs=[ANY] * 3,
        out_specs=(VMEM, VMEM),
        scratch_shapes=[
            pltpu.VMEM((3, tiles * GEO, LANES), jnp.bfloat16),
            pltpu.SemaphoreType.DMA((3,)),
        ],
        compiler_params=pltpu.CompilerParams(vmem_limit_bytes=10 << 20),
        cost_estimate=pl.CostEstimate(flops=1000, bytes_accessed=1000, transcendentals=0),
        name="profiles",
    )(geos, buffers["three m"], third_geos)

    late_values = [buffers[name] for name in late_order[:-1]]
    middle, own_kept = pl.pallas_call(
        functools.partial(middle_kernel, len(late_values)),
        out_shape=(
            jax.ShapeDtypeStruct((full, full), jnp.bfloat16),
            jax.ShapeDtypeStruct((size, full), jnp.bfloat16),
        ),
        in_specs=[SMEM, SMEM] + [VMEM] * (2 + len(late_values)) + [ANY],
        out_specs=(VMEM, VMEM),
        scratch_shapes=[pltpu.VMEM((base["four"] - late_from, LANES), jnp.bfloat16)],
        compiler_params=pltpu.CompilerParams(
            vmem_limit_bytes=(13 << 20) + 2 * (base["four"] - late_from) * LANES * 2
        ),
        cost_estimate=pl.CostEstimate(flops=1000, bytes_accessed=1000, transcendentals=0),
        name="gram_middle",
    )(late_table, info, own, gram, *late_values, four)

    late_values = [buffers["four"]]
    sign_next, coef = pl.pallas_call(
        functools.partial(step_kernel, len(late_values)),
        out_shape=(
            jax.ShapeDtypeStruct((slots, size, size), jnp.bfloat16),
            jax.ShapeDtypeStruct((8, LANES), jnp.float32),
        ),
        in_specs=[SMEM, SMEM, VMEM, VMEM, VMEM, VMEM] + [VMEM] * len(late_values),
        out_specs=(VMEM, VMEM),
        scratch_shapes=[
            pltpu.VMEM((total - base["four"], LANES), jnp.bfloat16),
            pltpu.VMEM((full, full), jnp.bfloat16),
            pltpu.VMEM((size, full), jnp.bfloat16),
        ],
        compiler_params=pltpu.CompilerParams(vmem_limit_bytes=(15 << 20) + 2 * (total - late_from) * LANES * 2),
        cost_estimate=pl.CostEstimate(flops=1_300_000_000, bytes_accessed=8_000_000, transcendentals=0),
        name="square_cube_coefficients",
    )(last_table, info, own_basis, spread, own_kept, middle, *late_values)

    mate_coef = from_layer(coef, 1)
    third_coef = from_layer(coef, 3)
    merged = pl.pallas_call(
        merge_kernel,
        out_shape=jax.ShapeDtypeStruct((8, LANES), jnp.float32),
        in_specs=[VMEM] * 3,
        out_specs=VMEM,
        compiler_params=pltpu.CompilerParams(vmem_limit_bytes=1 << 20),
        cost_estimate=pl.CostEstimate(flops=1000, bytes_accessed=1000, transcendentals=0),
        name="merge_layers",
    )(coef, mate_coef, third_coef)
    given, token = pack([sign_next.reshape(full, size)], [[(0, 0, full)], [(0, 0, GEO)]], [], "give_sign")
    parts = [merged] + [on_row(merged, di) for di in others]
    stacked = pack(parts, [[(i, 0, 8) for i in range(count)]], [token], "stack_tiles")[0]
    far_side = from_column(stacked, 1)
    received = [stacked, far_side, from_column(stacked, 0)]

    density = pl.pallas_call(
        functools.partial(density_kernel, len(column_steps)),
        out_shape=jax.ShapeDtypeStruct((BX * BY, BZ), jnp.float32),
        in_specs=[VMEM] * (len(received) + 2),
        out_specs=VMEM,
        compiler_params=pltpu.CompilerParams(vmem_limit_bytes=16 << 20),
        cost_estimate=pl.CostEstimate(flops=310_000_000, bytes_accessed=4_000_000, transcendentals=0),
        name="density",
    )(*received, plane, line.reshape(tiles * SHELLS * LANES, BZ))
    return given.reshape(1, slots, size, size), density.reshape(BX, BY, BZ)


def solution(mesh):
    rows = P(("row", "col", "layer"), None, None, None)
    in_specs = (rows, P(), P(), P(), P(("row", "col", "layer"), None), P(), P(), P())
    out_specs = (rows, P("row", "col", "layer"))
    return jax.shard_map(local, mesh=mesh, in_specs=in_specs, out_specs=out_specs, check_vma=False)
```

```python
import functools

import jax
import jax.numpy as jnp
from jax import lax
from jax.experimental import pallas as pl
from jax.experimental.pallas import tpu as pltpu
from jax.sharding import PartitionSpec as P

BX = 16
BY = 16
BZ = 128
LANES = 128
UNROLL = 4
SHELLS = 6
SPAN = 3 * SHELLS
GEO = 16
VMEM = pl.BlockSpec(memory_space=pltpu.VMEM)
SMEM = pl.BlockSpec(memory_space=pltpu.SMEM)
ANY = pl.BlockSpec(memory_space=pl.ANY)
HBM = pl.BlockSpec(memory_space=pltpu.HBM)


def from_offset(x, axis, step):
    count = lax.axis_size(axis)
    return lax.ppermute(x, axis, [((i + step) % count, i) for i in range(count)])


def from_column(x, side):
    count = lax.axis_size("col")
    step = [1 if (i + side) % 2 == 0 else -1 for i in range(count)]
    return lax.ppermute(x, "col", [((i + step[i]) % count, i) for i in range(count)])


def from_layer(x, flip):
    count = lax.axis_size("layer")
    return lax.ppermute(x, "layer", [(i ^ flip, i) for i in range(count)])


def column_targets(n_row):
    return 5 if n_row == 2 else 7


def target_place(n_row, step_row, step_lay, row):
    same = jnp.where(step_lay < 3, step_lay, -1)
    if n_row == 2:
        lead = step_lay - row
        across = jnp.where((lead >= 0) & (lead < 2), 3 + lead, -1)
    else:
        across = 3 + step_lay
    return jnp.where(step_row == 0, same, jnp.where(step_row == 1, across, -1))


class Places:
    def __init__(self, n_row, n_col, n_lay):
        self.n_row, self.n_col, self.n_lay = n_row, n_col, n_lay
        self.lay_bits = n_lay.bit_length() - 1
        self.col_bits = n_col.bit_length() - 1
        self.row = lax.axis_index("row")
        self.col = lax.axis_index("col")
        self.lay = lax.axis_index("layer")
        self.me = (((self.row << self.col_bits) + self.col) << self.lay_bits) + self.lay

    def split(self, atom):
        return (
            atom >> (self.lay_bits + self.col_bits),
            (atom >> self.lay_bits) & (self.n_col - 1),
            atom & (self.n_lay - 1),
        )


def load(sources, targets, sems):
    copies = [pltpu.make_async_copy(a, b, sems.at[i]) for i, (a, b) in enumerate(zip(sources, targets))]
    for copy in copies:
        copy.start()
    for copy in copies:
        copy.wait()


def own_ranks(at, neighbors_ref):
    seen = [jnp.int32(0)] * at.n_lay
    listed = []
    for w in range(neighbors_ref.shape[0]):
        atom = neighbors_ref[w, at.me]
        step_lay = (atom - at.lay) & (at.n_lay - 1)
        rank = jnp.int32(0)
        for k in range(at.n_lay):
            rank = jnp.where(step_lay == k, 3 * k + seen[k], rank)
            seen[k] = seen[k] + (step_lay == k).astype(jnp.int32)
        listed.append((atom, rank))
    return listed


def pick_kernel(axes, *refs):
    sign_ref, out_ref, geo_ref, neighbors_ref, extent_ref, x_ref, y_ref, z_ref, place_ref, loads, sems = refs[5:]
    at = Places(*axes)
    slots = sign_ref.shape[0]
    n_pick = place_ref.shape[0] - 1
    size = sign_ref.shape[1]
    for i in range(n_pick + 1):
        place_ref[i] = 0
    scalars = (neighbors_ref, extent_ref, x_ref, y_ref, z_ref)
    loading = [pltpu.make_async_copy(refs[i], target, loads.at[i]) for i, target in enumerate(scalars)]
    for copy in loading:
        copy.start()
    loading[0].wait()
    for w in range(slots):
        row, col, lay = at.split(neighbors_ref[w, at.me])
        place = target_place(at.n_row, (row - at.row) & (at.n_row - 1), (lay - at.lay) & (at.n_lay - 1), at.row)
        place_ref[jnp.where((col == at.col) & (place >= 0), place, n_pick)] = w
    copies = []
    for i in range(n_pick):
        copy = pltpu.make_async_copy(sign_ref.at[place_ref[i]], out_ref.at[pl.ds(i * size, size)], sems.at[i])
        copy.start()
        copies.append(copy)
    ranks = own_ranks(at, neighbors_ref)
    for copy in loading[1:]:
        copy.wait()
    sub = lax.broadcasted_iota(jnp.int32, (GEO, LANES), 0)
    lane_pair = lax.broadcasted_iota(jnp.int32, (GEO, LANES), 1) // SHELLS
    geo = jnp.zeros((GEO, LANES), jnp.int32)
    for w, (atom, rank) in enumerate(ranks):
        row, col, lay = at.split(atom)
        go_row = ((row - at.row + 1) & (at.n_row - 1)) - 1
        go_col = ((col - at.col + 1) & (at.n_col - 1)) - 1
        go_lay = jnp.minimum(((lay - at.lay + 1) & (at.n_lay - 1)) - 1, 1)
        twice_x = x_ref[at.me] + x_ref[atom] + BX * go_row
        twice_y = y_ref[at.me] + y_ref[atom] + BY * go_col
        twice_z = z_ref[at.me] + z_ref[atom] + BZ * go_lay - BZ
        extent = extent_ref[0, w]
        values = jnp.where(sub == 0, twice_x, jnp.where(sub == 1, twice_y, jnp.where(sub == 2, twice_z, extent)))
        geo = jnp.where(lane_pair == rank, values, geo)
    geo = geo.astype(jnp.float32).astype(out_ref.dtype)
    geo_ref[...] = geo
    out_ref[n_pick * size :] = geo
    for copy in copies:
        copy.wait()


def spread_kernel(axes, *refs):
    basis_ref = refs[1]
    spread_ref, own_basis_ref, neighbors_ref, loads = refs[-4:]
    at = Places(*axes)
    load(refs[:1], (neighbors_ref,), loads)
    slots, atoms = neighbors_ref.shape
    bits = atoms.bit_length() - 1

    def hot(rows, atom, first):
        sub = lax.broadcasted_iota(jnp.int32, (rows, SHELLS * atoms), 0)
        lane = lax.broadcasted_iota(jnp.int32, (rows, SHELLS * atoms), 1)
        return ((lane & (atoms - 1)) == atom) & (sub == first + (lane >> bits))

    def rows_of(chosen):
        picked = jnp.where(chosen, 1.0, 0.0).astype(jnp.bfloat16)
        return jnp.dot(picked, basis_ref[...], preferred_element_type=jnp.float32).astype(jnp.bfloat16)

    for w, (atom, rank) in enumerate(own_ranks(at, neighbors_ref)):
        spread_ref[:, w * LANES : (w + 1) * LANES] = rows_of(hot(LANES, atom, rank * SHELLS))
    own_basis_ref[...] = rows_of(hot(16, at.me, 0))


def prepare_kernel(axes, count, layout, late_from, last_from, *refs):
    early_ref, late_ref, last_ref, info_ref, neighbors_ref, size_ref, known, inverse, layout_ref, loads = refs[-10:]
    at = Places(*axes)
    load(refs[:2], (neighbors_ref, size_ref), loads)
    slots = neighbors_ref.shape[0]
    lines = count * at.n_lay
    for i, value in enumerate(layout):
        layout_ref[i] = value
    self_slot = jnp.int32(0)
    for w in range(slots):
        atom = neighbors_ref[w, at.me]
        row, col, lay = at.split(atom)
        step_row = (row - at.row) & (at.n_row - 1)
        self_slot = jnp.where(atom == at.me, w, self_slot)
        info_ref[w] = size_ref[atom]
        known[0, w] = atom
        known[1, w] = jnp.where(col == at.col, 0, jnp.where(col == (at.col ^ 1), 1, 2))
        known[2, w] = jnp.where(step_row == 0, 0, jnp.where(step_row == 1, 1, 2)) * at.n_lay + (lay ^ at.lay)
        inverse[atom] = -1
    info_ref[slots] = size_ref[at.me]
    info_ref[slots + 1] = self_slot

    def row_of_pairs(v, totals):
        early, late, last = totals
        atom = known[0, v]
        side = known[1, v]
        line = known[2, v]
        for u in range(slots):
            inverse[neighbors_ref[u, atom]] = v * 16 + u

        def from_row(totals):
            total, late, last = totals
            for w in range(slots):
                mark = inverse[known[0, w]]
                chosen = ((mark >> 4) == v) & ((known[1, w] != 0) | (v <= w))
                where = layout_ref[line * slots + (mark & 15)]
                is_late = where >= late_from
                entry = v + 16 * w
                early_ref[total + 1] = entry + 256 * where
                late_ref[late + 1] = entry + 256 * (where - late_from)
                total = total + (chosen & ~is_late).astype(jnp.int32)
                late = late + (chosen & is_late).astype(jnp.int32)
            return total, late, last

        def from_column(totals):
            early, late, last = totals
            row, _, lay = at.split(atom)
            beside = layout_ref[lines * slots + (side - 1) * lines + line]
            for w in range(slots):
                other = known[0, w]
                mark = inverse[other]
                o_row, _, o_lay = at.split(other)
                d_row = (o_row - row) & (at.n_row - 1)
                d_lay = (o_lay - lay) & (at.n_lay - 1)
                there = target_place(at.n_row, d_row, d_lay, row)
                back = target_place(at.n_row, -d_row & (at.n_row - 1), -d_lay & (at.n_lay - 1), o_row)
                chosen = ((mark >> 4) == v) & (side == known[1, w]) & (there >= 0) & ((back < 0) | (v <= w))
                where = beside + there * LANES
                is_late = where >= late_from
                is_last = where >= last_from
                entry = v + 16 * w
                early_ref[early + 1] = entry + 256 * where
                late_ref[late + 1] = entry + 256 * (where - late_from)
                last_ref[last + 1] = entry + 256 * (where - last_from)
                early = early + (chosen & ~is_late).astype(jnp.int32)
                late = late + (chosen & is_late & ~is_last).astype(jnp.int32)
                last = last + (chosen & is_last).astype(jnp.int32)
            return early, late, last

        return lax.cond(side == 0, from_row, from_column, (early, late, last))

    totals = lax.fori_loop(0, slots, row_of_pairs, (jnp.int32(0),) * 3)
    for ref, total in zip((early_ref, late_ref, last_ref), totals):
        ref[0] = (total + UNROLL - 1) // UNROLL
        for i in range(UNROLL - 1):
            ref[total + i + 1] = ref[jnp.maximum(total, 1)]


def pack_kernel(moves, inputs, *refs):
    for source, start, rows, target, place in moves:
        refs[inputs + target][place : place + rows] = refs[source][start : start + rows]


def pack(values, plans, extra, name, cost=0):
    moves, shapes = [], []
    for target, plan in enumerate(plans):
        place = 0
        for source, start, rows in plan:
            moves.append((source, start, rows, target, place))
            place += rows
        shapes.append(jax.ShapeDtypeStruct((place, LANES), values[0].dtype))
    inputs = len(values) + len(extra)
    return pl.pallas_call(
        functools.partial(pack_kernel, tuple(moves), inputs),
        out_shape=tuple(shapes),
        in_specs=[VMEM] * len(values) + [ANY] * len(extra),
        out_specs=tuple([VMEM] * len(plans)),
        compiler_params=pltpu.CompilerParams(
            vmem_limit_bytes=(1 << 20) + 256 * sum(x.shape[0] for x in list(values) + shapes)
        ),
        cost_estimate=pl.CostEstimate(flops=cost, bytes_accessed=1000, transcendentals=0),
        name=name,
    )(*values, *extra)


def fill(piece_refs, pool):
    place = 0
    for piece in piece_refs:
        rows = piece.shape[0]
        pool[place : place + rows] = piece[...]
        place += rows


def place_pairs(table_ref, pool, gram, size):
    def place(i, carry):
        for k in range(UNROLL):
            entry = table_ref[i * UNROLL + k + 1]
            p = pl.multiple_of((entry & 15) * size, size)
            q = pl.multiple_of(((entry >> 4) & 15) * size, size)
            block = pool[pl.ds(pl.multiple_of(entry >> 8, 16), size)]
            gram[pl.ds(p, size), pl.ds(q, size)] = block
            gram[pl.ds(q, size), pl.ds(p, size)] = block.T
        return carry

    lax.fori_loop(0, table_ref[0], place, 0)


def gram_kernel(pieces, *refs):
    table_ref = refs[0]
    piece_refs = refs[1 : 1 + pieces]
    gram, pool = refs[-2:]
    size = LANES
    fill(piece_refs, pool)
    for v in range(gram.shape[0] // size):
        gram[v * size : (v + 1) * size] = jnp.zeros((size, gram.shape[1]), gram.dtype)
    place_pairs(table_ref, pool, gram, size)


def middle_kernel(pieces, *refs):
    table_ref, info_ref, sign_ref, early_ref = refs[:4]
    piece_refs = refs[4 : 4 + pieces]
    gram, own, pool = refs[-3:]
    slots, size = sign_ref.shape[0], sign_ref.shape[1]
    fill(piece_refs, pool)
    for v in range(slots):
        gram[v * size : (v + 1) * size] = early_ref[v * size : (v + 1) * size]
    place_pairs(table_ref, pool, gram, size)
    rows = lax.broadcasted_iota(jnp.int32, (size, size), 0)
    lanes = lax.broadcasted_iota(jnp.int32, (size, size), 1)
    for w in range(slots):
        kept = (rows < info_ref[slots]) & (lanes < info_ref[w])
        block = jnp.where(kept, sign_ref[w].astype(jnp.float32), 0.0)
        own[:, w * size : (w + 1) * size] = block.astype(own.dtype)


def step_kernel(pieces, *refs):
    table_ref, info_ref, basis_ref, spread_ref, own, early_ref = refs[:6]
    piece_refs = refs[6 : 6 + pieces]
    next_ref, coef_ref, pool, gram, square = refs[-5:]
    slots, size = next_ref.shape[0], next_ref.shape[1]
    fill(piece_refs, pool)
    for v in range(slots):
        gram[v * size : (v + 1) * size] = early_ref[v * size : (v + 1) * size]
    own_size = info_ref[slots]
    self_slot = info_ref[slots + 1]
    place_pairs(table_ref, pool, gram, size)
    wide = 2 * size
    wide_lanes = lax.broadcasted_iota(jnp.int32, (size, wide), 1)
    wide_rows = lax.broadcasted_iota(jnp.int32, (size, wide), 0)

    def column_kept(n):
        first = info_ref[2 * n]
        second = info_ref[2 * n + 1]
        return (wide_lanes < first) | ((wide_lanes >= size) & (wide_lanes < size + second))

    for n in range(slots // 2):
        part = jnp.dot(own[...], gram[:, n * wide : (n + 1) * wide], preferred_element_type=jnp.float32)
        square[:, n * wide : (n + 1) * wide] = jnp.where(column_kept(n), part, 0.0).astype(square.dtype)
    basis = jnp.concatenate([basis_ref[...], basis_ref[...]], axis=1)
    coef = jnp.zeros((2 * basis_ref.shape[0], LANES), jnp.float32)
    across = (((1,), (1,)), ((), ()))
    for n in range(slots // 2):
        part = jnp.dot(square[...], gram[:, n * wide : (n + 1) * wide], preferred_element_type=jnp.float32)
        cube = jnp.where(column_kept(n), part, 0.0)
        full = 1.5 * own[:, n * wide : (n + 1) * wide].astype(jnp.float32) - 0.5 * cube
        next_ref[2 * n] = full[:, :size].astype(next_ref.dtype)
        next_ref[2 * n + 1] = full[:, size:].astype(next_ref.dtype)
        shift = (self_slot - 2 * n) * size
        is_self = (self_slot >= 2 * n) & (self_slot < 2 * n + 2)
        diag = (wide_lanes == wide_rows + shift) & (wide_rows < own_size) & is_self
        dmat = 0.5 * (jnp.where(diag, 1.0, 0.0) - full)
        high = dmat.astype(jnp.bfloat16)
        low = (dmat - high.astype(jnp.float32)).astype(jnp.bfloat16)
        half = jnp.dot(basis, jnp.concatenate([high, low], axis=0), preferred_element_type=jnp.float32)
        half_high = half.astype(jnp.bfloat16)
        half_low = (half - half_high.astype(jnp.float32)).astype(jnp.bfloat16)
        coef = coef + lax.dot_general(
            jnp.concatenate([half_high, half_low], axis=0),
            spread_ref[:, n * wide : (n + 1) * wide],
            across,
            preferred_element_type=jnp.float32,
        )
    coef = coef[: basis_ref.shape[0]] + coef[basis_ref.shape[0] :]
    coef_ref[...] = coef[: coef_ref.shape[0]]


def profile_kernel(periods, steps, mate_from, *refs):
    own_ref, mate_ref, third_ref = refs[:3]
    plane_ref, line_ref, geos, sems = refs[-4:]
    odd = (lax.axis_index("layer") & 1) == 1
    rows = len(steps) * GEO
    copies = []
    for k, source in enumerate((own_ref, mate_ref.at[pl.ds(mate_from, rows)], third_ref)):
        copy = pltpu.make_async_copy(source, geos.at[k], sems.at[k])
        copy.start()
        copies.append(copy)
    steps_x = lax.broadcasted_iota(jnp.int32, (BX, LANES), 0).astype(jnp.float32)
    steps_y = lax.broadcasted_iota(jnp.int32, (BY, LANES), 0).astype(jnp.float32)
    grid_z = lax.broadcasted_iota(jnp.int32, (LANES, BZ), 1).astype(jnp.float32)
    lane = lax.broadcasted_iota(jnp.int32, (1, LANES), 1)
    shell = (lane % SHELLS + 1).astype(jnp.float32)
    valid = lane < 7 * SPAN
    from_own = lane < 4 * SPAN
    from_below = lane < 6 * SPAN
    lift = jnp.where(from_own, 0.0, jnp.where(from_below, -float(BZ), float(BZ))) + 0.5 * BZ

    def nearest(offset, period):
        return offset - period * jnp.floor(offset * (1.0 / period) + 0.5)

    for copy in copies:
        copy.wait()
    ahead = 1.0 - 2.0 * (lax.axis_index("col") & 1).astype(jnp.float32)
    for o, (step_row, side) in enumerate(steps):
        own, first, third = (geos[k, o * GEO : (o + 1) * GEO].astype(jnp.float32) for k in range(3))
        below = jnp.where(odd, first, third)
        above = jnp.where(odd, third, first)
        moved = jnp.where(from_below, pltpu.roll(below, 3 * SPAN, axis=1), pltpu.roll(above, 3 * SPAN, axis=1))
        geo = jnp.where(from_own, own, moved)
        extent = jnp.where(valid, geo[3:4], 1.0)
        inverse = (SHELLS / extent) * (SHELLS / extent)
        reach = jnp.where(valid, extent, -1.0)
        rate_t = inverse / (shell * shell)
        packed = jnp.concatenate(
            [0.5 * geo[2:3] + lift, reach, rate_t, inverse, jnp.zeros((4, LANES), jnp.float32)], axis=0
        )
        sub = packed.T
        d_x = nearest(steps_x - (0.5 * geo[0:1] + float(BX * step_row)), periods[0])
        d_y = nearest(steps_y - (0.5 * geo[1:2] + float(BY * side) * ahead), periods[1])
        inside_x = jnp.abs(d_x) <= reach
        inside_y = jnp.abs(d_y) <= reach
        squared_x = d_x * d_x
        squared_y = d_y * d_y
        d_z = nearest(grid_z - sub[:, 0:1], periods[2])
        inside_z = jnp.abs(d_z) <= sub[:, 1:2]
        squared_z = d_z * d_z
        for s in range(SHELLS):
            part = 1.0 / ((s + 1) * (s + 1))
            rate = inverse * part + rate_t
            along_x = jnp.where(inside_x, jnp.exp(-rate * squared_x), 0.0)
            along_y = jnp.where(inside_y, jnp.exp(-rate * squared_y), 0.0)
            for x in range(BX):
                plane_ref[o, s, x * BY : (x + 1) * BY] = (along_x[x : x + 1] * along_y).astype(plane_ref.dtype)
            rate_z = sub[:, 3:4] * part + sub[:, 2:3]
            line_ref[o, s] = jnp.where(inside_z, jnp.exp(-rate_z * squared_z), 0.0).astype(line_ref.dtype)


def merge_kernel(own_ref, mate_ref, third_ref, out_ref):
    odd = (lax.axis_index("layer") & 1) == 1
    lane = lax.broadcasted_iota(jnp.int32, out_ref.shape, 1)
    below = jnp.where(odd, mate_ref[...], third_ref[...])
    above = jnp.where(odd, third_ref[...], mate_ref[...])
    moved = jnp.where(lane < 6 * SPAN, pltpu.roll(below, 3 * SPAN, axis=1), pltpu.roll(above, 3 * SPAN, axis=1))
    out_ref[...] = jnp.where(lane < 4 * SPAN, own_ref[...], jnp.where(lane < 7 * SPAN, moved, 0.0))


def density_kernel(column_steps, *refs):
    coef_refs = refs[:column_steps]
    plane_ref, line_ref, out_ref = refs[column_steps:]
    total = jnp.zeros(out_ref.shape, jnp.float32)
    wide = SHELLS * LANES
    for o in range(plane_ref.shape[0]):
        coef = coef_refs[-o % column_steps]
        first = 8 * (o // column_steps)
        terms = [
            (plane_ref[o, s].astype(jnp.float32) * coef[first + s : first + s + 1, :]).astype(line_ref.dtype)
            for s in range(SHELLS)
        ]
        total = total + jnp.dot(
            jnp.concatenate(terms, axis=1),
            line_ref[o * wide : (o + 1) * wide],
            preferred_element_type=jnp.float32,
        )
    out_ref[...] = total


def local(sign_start, neighbors, atom_size, basis_proj, pair_extent, atom_x, atom_y, atom_z):
    n_row = lax.axis_size("row")
    n_col = lax.axis_size("col")
    n_lay = lax.axis_size("layer")
    assert n_lay == 4 and n_col >= 4 and (n_row == 2 or n_row >= 4)
    assert n_row & (n_row - 1) == 0 and n_col & (n_col - 1) == 0
    axes = (n_row, n_col, n_lay)
    atoms, slots = neighbors.shape
    size = sign_start.shape[2]
    steps = [0, 1] if n_row == 2 else [0, 1, -1]
    count = len(steps)
    others = range(1, count)
    own = sign_start[0]
    flat = own.reshape(slots * size, size)
    listings = neighbors.T
    full = slots * size
    half = full // 2
    most = half - size
    n_pick = column_targets(n_row)
    picks = n_pick * size
    part = picks + GEO

    def on_row(value, di):
        return from_offset(value, "row", steps[di])

    x_row = {di: on_row(flat, di) for di in others}
    y_row = from_layer(flat, 2)
    m_row = from_layer(flat, 1)
    picked, geo = pl.pallas_call(
        functools.partial(pick_kernel, axes),
        out_shape=(
            jax.ShapeDtypeStruct((part, size), own.dtype),
            jax.ShapeDtypeStruct((GEO, LANES), own.dtype),
        ),
        in_specs=[HBM] * 6,
        out_specs=(VMEM, VMEM),
        scratch_shapes=[
            pltpu.SMEM((slots, atoms), jnp.int32),
            pltpu.SMEM((1, slots), jnp.int32),
            pltpu.SMEM((atoms,), jnp.int32),
            pltpu.SMEM((atoms,), jnp.int32),
            pltpu.SMEM((atoms,), jnp.int32),
            pltpu.SMEM((n_pick + 1,), jnp.int32),
            pltpu.SemaphoreType.DMA((5,)),
            pltpu.SemaphoreType.DMA((n_pick,)),
        ],
        compiler_params=pltpu.CompilerParams(vmem_limit_bytes=60 << 20),
        name="pick_column_blocks",
    )(listings, pair_extent, atom_x, atom_y, atom_z, own)
    down = from_column(picked, 1)
    up = from_column(picked, 0)

    halves = pack(
        [y_row] + [x_row[di] for di in others] + [geo],
        [[(0, half, most)]] + [[(di, 0, most)] for di in others] + [[(count, 0, GEO)]],
        [],
        "pack_halves",
    )
    ends = {di: on_row(halves[0], di) for di in others}
    tops = {di: from_layer(halves[di], 2) for di in others}

    at = {}
    buffers = {}

    def note(name, value, contents):
        buffers[name] = value
        start = 0
        for what, rows in contents:
            if what is not None:
                at[what] = (name, start)
            start += rows

    def row_of(di, flip, start=0, stop=slots):
        return [(("row", slot, di, flip), size) for slot in range(start, stop)]

    halfway = slots // 2

    def side_of(kind, di, flip):
        return [((kind, di, flip), picks)]

    note("own", flat, row_of(0, 0))
    note("mate", m_row, row_of(0, 1))
    note("far", y_row, row_of(0, 2))
    note("up", up, side_of("up", 0, 0) + [(("up geo", 0, 0), GEO)])
    note("down", down, side_of("down", 0, 0) + [(("down geo", 0, 0), GEO)])
    note("geo", halves[count], [(("geo", 0, 0), GEO)])
    for di in others:
        note(("x", di), x_row[di], row_of(di, 0))
        note(("end", di), ends[di], row_of(di, 2, halfway, slots - 1))
        note(("top", di), tops[di], row_of(di, 2, 0, halfway - 1))

    corners = [("end", di) for di in others] + [("top", di) for di in others]
    names = ["down", "up", "geo", "far"] + [("x", di) for di in others]
    plans = [
        [(1, 0, picks), (0, 0, picks), (3, full - size, size), (2, 0, GEO), (1, picks, GEO), (0, picks, GEO)],
        [(1, 0, picks), (0, 0, picks)] + [(di + 3, most, size) for di in others] + [(2, 0, GEO), (1, picks, GEO), (0, picks, GEO)],
        [(2, 0, GEO), (1, picks, GEO), (0, picks, GEO)],
    ]
    two_x, two_y, geos = pack([buffers[name] for name in names], plans, [m_row], "pack_two")
    to_mate = corners + ["up", "down"]
    for di in others:
        note(("mate x", di), from_layer(x_row[di], 1), row_of(di, 1))
    note("mate far", from_layer(y_row, 1), row_of(0, 3))

    early_order = ["own", "mate", "far", "up", "down", "geo"] + [("x", di) for di in others]
    early_order += [("mate x", di) for di in others] + ["mate far"]
    early_order += corners + [("two x", di) for di in others] + ["two y", "two m"]
    late_order = [("three x", di) for di in others] + ["three y", "three m"]
    late_order += ["four"]

    contents = {}
    for di in others:
        contents["two x", di] = side_of("up", di, 0) + side_of("down", di, 0)
        contents["two x", di] += row_of(di, 2, slots - 1, slots) + [(("geo", di, 0), GEO)]
        contents["two x", di] += [(("up geo", di, 0), GEO), (("down geo", di, 0), GEO)]
    contents["two y"] = side_of("up", 0, 2) + side_of("down", 0, 2)
    contents["two y"] += sum([row_of(di, 2, halfway - 1, halfway) for di in others], []) + [(None, 3 * GEO)]
    contents["two m"] = sum([row_of(di, 3, halfway, slots - 1) for di in others], [])
    contents["two m"] += sum([row_of(di, 3, 0, halfway - 1) for di in others], [])
    contents["two m"] += side_of("up", 0, 1) + side_of("down", 0, 1)
    for di in others:
        contents["three x", di] = side_of("up", di, 2)
    contents["three y"] = sum([side_of("down", di, 2) for di in others], [])
    contents["three m"] = []
    for di in others:
        contents["three m"] += side_of("up", di, 1) + side_of("down", di, 1) + row_of(di, 3, slots - 1, slots)
    contents["three m"] += side_of("up", 0, 3) + side_of("down", 0, 3)
    contents["three m"] += sum([row_of(di, 3, halfway - 1, halfway) for di in others], []) + [(None, 3 * GEO)]
    contents["three m"] += [("geos", count * 3 * GEO)]
    contents["four"] = sum([side_of("up", di, 3) for di in others], [])
    contents["four"] += sum([side_of("down", di, 3) for di in others], [])
    lengths = {name: sum(rows for _, rows in content) for name, content in contents.items()}
    for name in early_order:
        if name in buffers:
            lengths[name] = buffers[name].shape[0]
    base = {}
    total = 0
    for name in early_order + late_order:
        base[name] = total
        total += lengths[name]
        if name == early_order[-1]:
            late_from = total
    located = dict(at)
    for name, content in contents.items():
        start = 0
        for what, rows in content:
            located[what] = (name, start)
            start += rows
    layout = [
        base[located["row", slot, di, flip][0]] + located["row", slot, di, flip][1]
        for di in range(count)
        for flip in range(n_lay)
        for slot in range(slots)
    ]
    layout += [
        base[located[kind, di, flip][0]] + located[kind, di, flip][1]
        for kind in ("up", "down")
        for di in range(count)
        for flip in range(n_lay)
    ]
    pairs = slots * (slots + 1) // 2
    entries = pairs + UNROLL + 1
    early_table, late_table, last_table, info = pl.pallas_call(
        functools.partial(prepare_kernel, axes, count, tuple(layout), late_from, base["four"]),
        out_shape=(
            jax.ShapeDtypeStruct((entries,), jnp.int32),
            jax.ShapeDtypeStruct((entries,), jnp.int32),
            jax.ShapeDtypeStruct((entries,), jnp.int32),
            jax.ShapeDtypeStruct((slots + 2,), jnp.int32),
        ),
        in_specs=[HBM, HBM, ANY],
        out_specs=(SMEM, SMEM, SMEM, SMEM),
        scratch_shapes=[
            pltpu.SMEM((slots, atoms), jnp.int32),
            pltpu.SMEM((atoms,), jnp.int32),
            pltpu.SMEM((3, slots), jnp.int32),
            pltpu.SMEM((atoms,), jnp.int32),
            pltpu.SMEM((len(layout),), jnp.int32),
            pltpu.SemaphoreType.DMA((2,)),
        ],
        compiler_params=pltpu.CompilerParams(vmem_limit_bytes=1 << 20),
        cost_estimate=pl.CostEstimate(flops=1000, bytes_accessed=1000, transcendentals=0),
        name="prepare",
    )(listings, atom_size, two_x)

    plans = [[(i, 0, picks if name in ("up", "down") else most) for i, name in enumerate(to_mate)]]
    two_m = pack([buffers[name] for name in to_mate], plans, [], "pack_two_mate", 3_000_000_000)[0]
    for di in others:
        note(("two x", di), on_row(two_x, di), contents["two x", di])
    note("two y", from_layer(two_y, 2), contents["two y"])
    early_mates = ["mate far"] + [("mate x", di) for di in others]
    note("two m", from_layer(two_m, 1), contents["two m"])

    buffers["geos"] = geos
    names = ["two y", "geos"] + [("two x", di) for di in others]
    place = {name: i for i, name in enumerate(names)}
    gather = [(place["geos"], 0, 3 * GEO)] + [(place["two x", di], 2 * picks + size, 3 * GEO) for di in others]
    xs = [place["two x", di] for di in others]
    plans = [
        [(0, 0, picks)],
        [(x, picks, picks) for x in xs],
        [(x, 0, 2 * picks + size) for x in xs] + [(0, 0, lengths["two y"])] + gather,
        gather,
    ]
    three_x, three_y, three_m, geos = pack([buffers[name] for name in names], plans, [buffers[name] for name in early_mates] + [two_m, info], "pack_three")
    for di in others:
        note(("three x", di), on_row(three_x, di), contents["three x", di])
    note("three y", from_layer(three_y, 2), contents["three y"])
    note("three m", from_layer(three_m, 1), contents["three m"])
    third_geos = from_layer(geos, 3)

    spread, own_basis = pl.pallas_call(
        functools.partial(spread_kernel, axes),
        out_shape=(
            jax.ShapeDtypeStruct((LANES, full), jnp.bfloat16),
            jax.ShapeDtypeStruct((16, size), jnp.bfloat16),
        ),
        in_specs=[HBM, VMEM, ANY],
        out_specs=(VMEM, VMEM),
        scratch_shapes=[pltpu.SMEM((slots, atoms), jnp.int32), pltpu.SemaphoreType.DMA((1,))],
        compiler_params=pltpu.CompilerParams(vmem_limit_bytes=(2 << 20) + atoms * 16384),
        cost_estimate=pl.CostEstimate(flops=1000, bytes_accessed=1000, transcendentals=0),
        name="spread_basis",
    )(listings, basis_proj.transpose(1, 0, 2).reshape(SHELLS * atoms, size), three_x)

    early_values = [buffers[name] for name in early_order]
    gram = pl.pallas_call(
        functools.partial(gram_kernel, len(early_values)),
        out_shape=jax.ShapeDtypeStruct((full, full), jnp.bfloat16),
        in_specs=[SMEM] + [VMEM] * len(early_values) + [ANY],
        out_specs=VMEM,
        scratch_shapes=[pltpu.VMEM((late_from, LANES), jnp.bfloat16)],
        compiler_params=pltpu.CompilerParams(vmem_limit_bytes=(6 << 20) + 2 * late_from * LANES * 2),
        cost_estimate=pl.CostEstimate(flops=1000, bytes_accessed=1000, transcendentals=0),
        name="gram_early",
    )(early_table, *early_values, three_x)

    thirds = [buffers["three x", di] for di in others] + [buffers["three y"]]
    four = pack(thirds, [[(i, 0, value.shape[0]) for i, value in enumerate(thirds)]], [gram, third_geos, own_basis], "pack_four")[0]
    note("four", from_layer(four, 1), contents["four"])

    column_steps = (0, 1, -1)
    tile_steps = [(dr, dc) for dr in steps for dc in column_steps]
    tiles = len(tile_steps)
    periods = (float(BX * n_row), float(BY * n_col), float(BZ * n_lay))
    plane, line = pl.pallas_call(
        functools.partial(profile_kernel, periods, tile_steps, at["geos"][1]),
        out_shape=(
            jax.ShapeDtypeStruct((tiles, SHELLS, BX * BY, LANES), jnp.bfloat16),
            jax.ShapeDtypeStruct((tiles, SHELLS, LANES, BZ), jnp.bfloat16),
        ),
        in_specs=[ANY] * 3,
        out_specs=(VMEM, VMEM),
        scratch_shapes=[
            pltpu.VMEM((3, tiles * GEO, LANES), jnp.bfloat16),
            pltpu.SemaphoreType.DMA((3,)),
        ],
        compiler_params=pltpu.CompilerParams(vmem_limit_bytes=10 << 20),
        cost_estimate=pl.CostEstimate(flops=1000, bytes_accessed=1000, transcendentals=0),
        name="profiles",
    )(geos, buffers["three m"], third_geos)

    late_values = [buffers[name] for name in late_order[:-1]]
    middle, own_kept = pl.pallas_call(
        functools.partial(middle_kernel, len(late_values)),
        out_shape=(
            jax.ShapeDtypeStruct((full, full), jnp.bfloat16),
            jax.ShapeDtypeStruct((size, full), jnp.bfloat16),
        ),
        in_specs=[SMEM, SMEM] + [VMEM] * (2 + len(late_values)) + [ANY],
        out_specs=(VMEM, VMEM),
        scratch_shapes=[pltpu.VMEM((base["four"] - late_from, LANES), jnp.bfloat16)],
        compiler_params=pltpu.CompilerParams(
            vmem_limit_bytes=(13 << 20) + 2 * (base["four"] - late_from) * LANES * 2
        ),
        cost_estimate=pl.CostEstimate(flops=1000, bytes_accessed=1000, transcendentals=0),
        name="gram_middle",
    )(late_table, info, own, gram, *late_values, four)

    late_values = [buffers["four"]]
    sign_next, coef = pl.pallas_call(
        functools.partial(step_kernel, len(late_values)),
        out_shape=(
            jax.ShapeDtypeStruct((slots, size, size), jnp.bfloat16),
            jax.ShapeDtypeStruct((8, LANES), jnp.float32),
        ),
        in_specs=[SMEM, SMEM, VMEM, VMEM, VMEM, VMEM] + [VMEM] * len(late_values),
        out_specs=(VMEM, VMEM),
        scratch_shapes=[
            pltpu.VMEM((total - base["four"], LANES), jnp.bfloat16),
            pltpu.VMEM((full, full), jnp.bfloat16),
            pltpu.VMEM((size, full), jnp.bfloat16),
        ],
        compiler_params=pltpu.CompilerParams(vmem_limit_bytes=(15 << 20) + 2 * (total - late_from) * LANES * 2),
        cost_estimate=pl.CostEstimate(flops=1_300_000_000, bytes_accessed=8_000_000, transcendentals=0),
        name="square_cube_coefficients",
    )(last_table, info, own_basis, spread, own_kept, middle, *late_values)

    mate_coef = from_layer(coef, 1)
    third_coef = from_layer(coef, 3)
    merged = pl.pallas_call(
        merge_kernel,
        out_shape=jax.ShapeDtypeStruct((8, LANES), jnp.float32),
        in_specs=[VMEM] * 3,
        out_specs=VMEM,
        compiler_params=pltpu.CompilerParams(vmem_limit_bytes=1 << 20),
        cost_estimate=pl.CostEstimate(flops=1000, bytes_accessed=1000, transcendentals=0),
        name="merge_layers",
    )(coef, mate_coef, third_coef)
    given, token = pack([sign_next.reshape(full, size)], [[(0, 0, full)], [(0, 0, GEO)]], [], "give_sign")
    parts = [merged] + [on_row(merged, di) for di in others]
    stacked = pack(parts, [[(i, 0, 8) for i in range(count)]], [token], "stack_tiles")[0]
    far_side = from_column(stacked, 1)
    received = [stacked, far_side, from_column(stacked, 0)]

    density = pl.pallas_call(
        functools.partial(density_kernel, len(column_steps)),
        out_shape=jax.ShapeDtypeStruct((BX * BY, BZ), jnp.float32),
        in_specs=[VMEM] * (len(received) + 2),
        out_specs=VMEM,
        compiler_params=pltpu.CompilerParams(vmem_limit_bytes=16 << 20),
        cost_estimate=pl.CostEstimate(flops=310_000_000, bytes_accessed=4_000_000, transcendentals=0),
        name="density",
    )(*received, plane, line.reshape(tiles * SHELLS * LANES, BZ))
    return given.reshape(1, slots, size, size), density.reshape(BX, BY, BZ)


def solution(mesh):
    rows = P(("row", "col", "layer"), None, None, None)
    in_specs = (rows, P(), P(), P(), P(("row", "col", "layer"), None), P(), P(), P())
    out_specs = (rows, P("row", "col", "layer"))
    return jax.shard_map(local, mesh=mesh, in_specs=in_specs, out_specs=out_specs, check_vma=False)
```

```python
import functools

import jax
import jax.numpy as jnp
from jax import lax
from jax.experimental import pallas as pl
from jax.experimental.pallas import tpu as pltpu
from jax.sharding import PartitionSpec as P

BX = 16
BY = 16
BZ = 128
LANES = 128
UNROLL = 4
SHELLS = 6
SPAN = 3 * SHELLS
GEO = 16
VMEM = pl.BlockSpec(memory_space=pltpu.VMEM)
SMEM = pl.BlockSpec(memory_space=pltpu.SMEM)
ANY = pl.BlockSpec(memory_space=pl.ANY)
HBM = pl.BlockSpec(memory_space=pltpu.HBM)


def from_offset(x, axis, step):
    count = lax.axis_size(axis)
    return lax.ppermute(x, axis, [((i + step) % count, i) for i in range(count)])


def from_column(x, side):
    count = lax.axis_size("col")
    step = [1 if (i + side) % 2 == 0 else -1 for i in range(count)]
    return lax.ppermute(x, "col", [((i + step[i]) % count, i) for i in range(count)])


def from_layer(x, flip):
    count = lax.axis_size("layer")
    return lax.ppermute(x, "layer", [(i ^ flip, i) for i in range(count)])


def column_targets(n_row):
    return 5 if n_row == 2 else 7


def target_place(n_row, step_row, step_lay, row):
    same = jnp.where(step_lay < 3, step_lay, -1)
    if n_row == 2:
        lead = step_lay - row
        across = jnp.where((lead >= 0) & (lead < 2), 3 + lead, -1)
    else:
        across = 3 + step_lay
    return jnp.where(step_row == 0, same, jnp.where(step_row == 1, across, -1))


class Places:
    def __init__(self, n_row, n_col, n_lay):
        self.n_row, self.n_col, self.n_lay = n_row, n_col, n_lay
        self.lay_bits = n_lay.bit_length() - 1
        self.col_bits = n_col.bit_length() - 1
        self.row = lax.axis_index("row")
        self.col = lax.axis_index("col")
        self.lay = lax.axis_index("layer")
        self.me = (((self.row << self.col_bits) + self.col) << self.lay_bits) + self.lay

    def split(self, atom):
        return (
            atom >> (self.lay_bits + self.col_bits),
            (atom >> self.lay_bits) & (self.n_col - 1),
            atom & (self.n_lay - 1),
        )


def load(sources, targets, sems):
    copies = [pltpu.make_async_copy(a, b, sems.at[i]) for i, (a, b) in enumerate(zip(sources, targets))]
    for copy in copies:
        copy.start()
    for copy in copies:
        copy.wait()


def own_ranks(at, neighbors_ref):
    seen = [jnp.int32(0)] * at.n_lay
    listed = []
    for w in range(neighbors_ref.shape[0]):
        atom = neighbors_ref[w, at.me]
        step_lay = (atom - at.lay) & (at.n_lay - 1)
        rank = jnp.int32(0)
        for k in range(at.n_lay):
            rank = jnp.where(step_lay == k, 3 * k + seen[k], rank)
            seen[k] = seen[k] + (step_lay == k).astype(jnp.int32)
        listed.append((atom, rank))
    return listed


def pick_kernel(axes, *refs):
    sign_ref, out_ref, geo_ref, neighbors_ref, extent_ref, x_ref, y_ref, z_ref, place_ref, loads, sems = refs[5:]
    at = Places(*axes)
    slots = sign_ref.shape[0]
    n_pick = place_ref.shape[0] - 1
    size = sign_ref.shape[1]
    for i in range(n_pick + 1):
        place_ref[i] = 0
    scalars = (neighbors_ref, extent_ref, x_ref, y_ref, z_ref)
    loading = [pltpu.make_async_copy(refs[i], target, loads.at[i]) for i, target in enumerate(scalars)]
    for copy in loading:
        copy.start()
    loading[0].wait()
    for w in range(slots):
        row, col, lay = at.split(neighbors_ref[w, at.me])
        place = target_place(at.n_row, (row - at.row) & (at.n_row - 1), (lay - at.lay) & (at.n_lay - 1), at.row)
        place_ref[jnp.where((col == at.col) & (place >= 0), place, n_pick)] = w
    copies = []
    for i in range(n_pick):
        copy = pltpu.make_async_copy(sign_ref.at[place_ref[i]], out_ref.at[pl.ds(i * size, size)], sems.at[i])
        copy.start()
        copies.append(copy)
    ranks = own_ranks(at, neighbors_ref)
    for copy in loading[1:]:
        copy.wait()
    sub = lax.broadcasted_iota(jnp.int32, (GEO, LANES), 0)
    lane_pair = lax.broadcasted_iota(jnp.int32, (GEO, LANES), 1) // SHELLS
    geo = jnp.zeros((GEO, LANES), jnp.int32)
    for w, (atom, rank) in enumerate(ranks):
        row, col, lay = at.split(atom)
        go_row = ((row - at.row + 1) & (at.n_row - 1)) - 1
        go_col = ((col - at.col + 1) & (at.n_col - 1)) - 1
        go_lay = jnp.minimum(((lay - at.lay + 1) & (at.n_lay - 1)) - 1, 1)
        twice_x = x_ref[at.me] + x_ref[atom] + BX * go_row
        twice_y = y_ref[at.me] + y_ref[atom] + BY * go_col
        twice_z = z_ref[at.me] + z_ref[atom] + BZ * go_lay - BZ
        extent = extent_ref[0, w]
        values = jnp.where(sub == 0, twice_x, jnp.where(sub == 1, twice_y, jnp.where(sub == 2, twice_z, extent)))
        geo = jnp.where(lane_pair == rank, values, geo)
    geo = geo.astype(jnp.float32).astype(out_ref.dtype)
    geo_ref[...] = geo
    out_ref[n_pick * size :] = geo
    for copy in copies:
        copy.wait()


def spread_kernel(axes, *refs):
    basis_ref = refs[1]
    spread_ref, own_basis_ref, neighbors_ref, loads = refs[-4:]
    at = Places(*axes)
    load(refs[:1], (neighbors_ref,), loads)
    slots, atoms = neighbors_ref.shape
    bits = atoms.bit_length() - 1

    def hot(rows, atom, first):
        sub = lax.broadcasted_iota(jnp.int32, (rows, SHELLS * atoms), 0)
        lane = lax.broadcasted_iota(jnp.int32, (rows, SHELLS * atoms), 1)
        return ((lane & (atoms - 1)) == atom) & (sub == first + (lane >> bits))

    def rows_of(chosen):
        picked = jnp.where(chosen, 1.0, 0.0).astype(jnp.bfloat16)
        return jnp.dot(picked, basis_ref[...], preferred_element_type=jnp.float32).astype(jnp.bfloat16)

    for w, (atom, rank) in enumerate(own_ranks(at, neighbors_ref)):
        spread_ref[:, w * LANES : (w + 1) * LANES] = rows_of(hot(LANES, atom, rank * SHELLS))
    own_basis_ref[...] = rows_of(hot(16, at.me, 0))


def prepare_kernel(axes, count, layout, late_from, last_from, *refs):
    early_ref, late_ref, last_ref, info_ref, neighbors_ref, size_ref, known, inverse, layout_ref, loads = refs[-10:]
    at = Places(*axes)
    load(refs[:2], (neighbors_ref, size_ref), loads)
    slots = neighbors_ref.shape[0]
    lines = count * at.n_lay
    for i, value in enumerate(layout):
        layout_ref[i] = value
    self_slot = jnp.int32(0)
    for w in range(slots):
        atom = neighbors_ref[w, at.me]
        row, col, lay = at.split(atom)
        step_row = (row - at.row) & (at.n_row - 1)
        self_slot = jnp.where(atom == at.me, w, self_slot)
        info_ref[w] = size_ref[atom]
        known[0, w] = atom
        known[1, w] = jnp.where(col == at.col, 0, jnp.where(col == (at.col ^ 1), 1, 2))
        known[2, w] = jnp.where(step_row == 0, 0, jnp.where(step_row == 1, 1, 2)) * at.n_lay + (lay ^ at.lay)
        inverse[atom] = -1
    info_ref[slots] = size_ref[at.me]
    info_ref[slots + 1] = self_slot

    def row_of_pairs(v, totals):
        early, late, last = totals
        atom = known[0, v]
        side = known[1, v]
        line = known[2, v]
        for u in range(slots):
            inverse[neighbors_ref[u, atom]] = v * 16 + u

        def from_row(totals):
            total, late, last = totals
            for w in range(slots):
                mark = inverse[known[0, w]]
                chosen = ((mark >> 4) == v) & ((known[1, w] != 0) | (v <= w))
                where = layout_ref[line * slots + (mark & 15)]
                is_late = where >= late_from
                entry = v + 16 * w
                early_ref[total + 1] = entry + 256 * where
                late_ref[late + 1] = entry + 256 * (where - late_from)
                total = total + (chosen & ~is_late).astype(jnp.int32)
                late = late + (chosen & is_late).astype(jnp.int32)
            return total, late, last

        def from_column(totals):
            early, late, last = totals
            row, _, lay = at.split(atom)
            beside = layout_ref[lines * slots + (side - 1) * lines + line]
            for w in range(slots):
                other = known[0, w]
                mark = inverse[other]
                o_row, _, o_lay = at.split(other)
                d_row = (o_row - row) & (at.n_row - 1)
                d_lay = (o_lay - lay) & (at.n_lay - 1)
                there = target_place(at.n_row, d_row, d_lay, row)
                back = target_place(at.n_row, -d_row & (at.n_row - 1), -d_lay & (at.n_lay - 1), o_row)
                chosen = ((mark >> 4) == v) & (side == known[1, w]) & (there >= 0) & ((back < 0) | (v <= w))
                where = beside + there * LANES
                is_late = where >= late_from
                is_last = where >= last_from
                entry = v + 16 * w
                early_ref[early + 1] = entry + 256 * where
                late_ref[late + 1] = entry + 256 * (where - late_from)
                last_ref[last + 1] = entry + 256 * (where - last_from)
                early = early + (chosen & ~is_late).astype(jnp.int32)
                late = late + (chosen & is_late & ~is_last).astype(jnp.int32)
                last = last + (chosen & is_last).astype(jnp.int32)
            return early, late, last

        return lax.cond(side == 0, from_row, from_column, (early, late, last))

    totals = lax.fori_loop(0, slots, row_of_pairs, (jnp.int32(0),) * 3)
    for ref, total in zip((early_ref, late_ref, last_ref), totals):
        ref[0] = (total + UNROLL - 1) // UNROLL
        for i in range(UNROLL - 1):
            ref[total + i + 1] = ref[jnp.maximum(total, 1)]


def pack_kernel(moves, inputs, *refs):
    for source, start, rows, target, place in moves:
        refs[inputs + target][place : place + rows] = refs[source][start : start + rows]


def pack(values, plans, extra, name, cost=0):
    moves, shapes = [], []
    for target, plan in enumerate(plans):
        place = 0
        for source, start, rows in plan:
            moves.append((source, start, rows, target, place))
            place += rows
        shapes.append(jax.ShapeDtypeStruct((place, LANES), values[0].dtype))
    inputs = len(values) + len(extra)
    return pl.pallas_call(
        functools.partial(pack_kernel, tuple(moves), inputs),
        out_shape=tuple(shapes),
        in_specs=[VMEM] * len(values) + [ANY] * len(extra),
        out_specs=tuple([VMEM] * len(plans)),
        compiler_params=pltpu.CompilerParams(
            vmem_limit_bytes=(1 << 20) + 256 * sum(x.shape[0] for x in list(values) + shapes)
        ),
        cost_estimate=pl.CostEstimate(flops=cost, bytes_accessed=1000, transcendentals=0),
        name=name,
    )(*values, *extra)


def fill(piece_refs, pool):
    place = 0
    for piece in piece_refs:
        rows = piece.shape[0]
        pool[place : place + rows] = piece[...]
        place += rows


def place_pairs(table_ref, pool, gram, size):
    def place(i, carry):
        for k in range(UNROLL):
            entry = table_ref[i * UNROLL + k + 1]
            p = pl.multiple_of((entry & 15) * size, size)
            q = pl.multiple_of(((entry >> 4) & 15) * size, size)
            block = pool[pl.ds(pl.multiple_of(entry >> 8, 16), size)]
            gram[pl.ds(p, size), pl.ds(q, size)] = block
            gram[pl.ds(q, size), pl.ds(p, size)] = block.T
        return carry

    lax.fori_loop(0, table_ref[0], place, 0)


def gram_kernel(pieces, *refs):
    table_ref = refs[0]
    piece_refs = refs[1 : 1 + pieces]
    gram, pool = refs[-2:]
    size = LANES
    fill(piece_refs, pool)
    for v in range(gram.shape[0] // size):
        gram[v * size : (v + 1) * size] = jnp.zeros((size, gram.shape[1]), gram.dtype)
    place_pairs(table_ref, pool, gram, size)


def middle_kernel(pieces, *refs):
    table_ref, info_ref, sign_ref, early_ref = refs[:4]
    piece_refs = refs[4 : 4 + pieces]
    gram, own, pool = refs[-3:]
    slots, size = sign_ref.shape[0], sign_ref.shape[1]
    fill(piece_refs, pool)
    for v in range(slots):
        gram[v * size : (v + 1) * size] = early_ref[v * size : (v + 1) * size]
    place_pairs(table_ref, pool, gram, size)
    rows = lax.broadcasted_iota(jnp.int32, (size, size), 0)
    lanes = lax.broadcasted_iota(jnp.int32, (size, size), 1)
    for w in range(slots):
        kept = (rows < info_ref[slots]) & (lanes < info_ref[w])
        block = jnp.where(kept, sign_ref[w].astype(jnp.float32), 0.0)
        own[:, w * size : (w + 1) * size] = block.astype(own.dtype)


def step_kernel(pieces, *refs):
    table_ref, info_ref, basis_ref, spread_ref, own, early_ref = refs[:6]
    piece_refs = refs[6 : 6 + pieces]
    next_ref, coef_ref, pool, gram, square = refs[-5:]
    slots, size = next_ref.shape[0], next_ref.shape[1]
    fill(piece_refs, pool)
    for v in range(slots):
        gram[v * size : (v + 1) * size] = early_ref[v * size : (v + 1) * size]
    own_size = info_ref[slots]
    self_slot = info_ref[slots + 1]
    place_pairs(table_ref, pool, gram, size)
    wide = 2 * size
    wide_lanes = lax.broadcasted_iota(jnp.int32, (size, wide), 1)
    wide_rows = lax.broadcasted_iota(jnp.int32, (size, wide), 0)

    def column_kept(n):
        first = info_ref[2 * n]
        second = info_ref[2 * n + 1]
        return (wide_lanes < first) | ((wide_lanes >= size) & (wide_lanes < size + second))

    for n in range(slots // 2):
        part = jnp.dot(own[...], gram[:, n * wide : (n + 1) * wide], preferred_element_type=jnp.float32)
        square[:, n * wide : (n + 1) * wide] = jnp.where(column_kept(n), part, 0.0).astype(square.dtype)
    basis = jnp.concatenate([basis_ref[...], basis_ref[...]], axis=1)
    coef = jnp.zeros((2 * basis_ref.shape[0], LANES), jnp.float32)
    across = (((1,), (1,)), ((), ()))
    for n in range(slots // 2):
        part = jnp.dot(square[...], gram[:, n * wide : (n + 1) * wide], preferred_element_type=jnp.float32)
        cube = jnp.where(column_kept(n), part, 0.0)
        full = 1.5 * own[:, n * wide : (n + 1) * wide].astype(jnp.float32) - 0.5 * cube
        next_ref[2 * n] = full[:, :size].astype(next_ref.dtype)
        next_ref[2 * n + 1] = full[:, size:].astype(next_ref.dtype)
        shift = (self_slot - 2 * n) * size
        is_self = (self_slot >= 2 * n) & (self_slot < 2 * n + 2)
        diag = (wide_lanes == wide_rows + shift) & (wide_rows < own_size) & is_self
        dmat = 0.5 * (jnp.where(diag, 1.0, 0.0) - full)
        high = dmat.astype(jnp.bfloat16)
        low = (dmat - high.astype(jnp.float32)).astype(jnp.bfloat16)
        half = jnp.dot(basis, jnp.concatenate([high, low], axis=0), preferred_element_type=jnp.float32)
        half_high = half.astype(jnp.bfloat16)
        half_low = (half - half_high.astype(jnp.float32)).astype(jnp.bfloat16)
        coef = coef + lax.dot_general(
            jnp.concatenate([half_high, half_low], axis=0),
            spread_ref[:, n * wide : (n + 1) * wide],
            across,
            preferred_element_type=jnp.float32,
        )
    coef = coef[: basis_ref.shape[0]] + coef[basis_ref.shape[0] :]
    coef_ref[...] = coef[: coef_ref.shape[0]]


def profile_kernel(periods, steps, mate_from, *refs):
    own_ref, mate_ref, third_ref = refs[:3]
    plane_ref, line_ref, geos, sems = refs[-4:]
    odd = (lax.axis_index("layer") & 1) == 1
    rows = len(steps) * GEO
    copies = []
    for k, source in enumerate((own_ref, mate_ref.at[pl.ds(mate_from, rows)], third_ref)):
        copy = pltpu.make_async_copy(source, geos.at[k], sems.at[k])
        copy.start()
        copies.append(copy)
    steps_x = lax.broadcasted_iota(jnp.int32, (BX, LANES), 0).astype(jnp.float32)
    steps_y = lax.broadcasted_iota(jnp.int32, (BY, LANES), 0).astype(jnp.float32)
    grid_z = lax.broadcasted_iota(jnp.int32, (LANES, BZ), 1).astype(jnp.float32)
    lane = lax.broadcasted_iota(jnp.int32, (1, LANES), 1)
    shell = (lane % SHELLS + 1).astype(jnp.float32)
    valid = lane < 7 * SPAN
    from_own = lane < 4 * SPAN
    from_below = lane < 6 * SPAN
    lift = jnp.where(from_own, 0.0, jnp.where(from_below, -float(BZ), float(BZ))) + 0.5 * BZ

    def nearest(offset, period):
        return offset - period * jnp.floor(offset * (1.0 / period) + 0.5)

    for copy in copies:
        copy.wait()
    ahead = 1.0 - 2.0 * (lax.axis_index("col") & 1).astype(jnp.float32)
    for o, (step_row, side) in enumerate(steps):
        own, first, third = (geos[k, o * GEO : (o + 1) * GEO].astype(jnp.float32) for k in range(3))
        below = jnp.where(odd, first, third)
        above = jnp.where(odd, third, first)
        moved = jnp.where(from_below, pltpu.roll(below, 3 * SPAN, axis=1), pltpu.roll(above, 3 * SPAN, axis=1))
        geo = jnp.where(from_own, own, moved)
        extent = jnp.where(valid, geo[3:4], 1.0)
        inverse = (SHELLS / extent) * (SHELLS / extent)
        reach = jnp.where(valid, extent, -1.0)
        rate_t = inverse / (shell * shell)
        packed = jnp.concatenate(
            [0.5 * geo[2:3] + lift, reach, rate_t, inverse, jnp.zeros((4, LANES), jnp.float32)], axis=0
        )
        sub = packed.T
        d_x = nearest(steps_x - (0.5 * geo[0:1] + float(BX * step_row)), periods[0])
        d_y = nearest(steps_y - (0.5 * geo[1:2] + float(BY * side) * ahead), periods[1])
        inside_x = jnp.abs(d_x) <= reach
        inside_y = jnp.abs(d_y) <= reach
        squared_x = d_x * d_x
        squared_y = d_y * d_y
        d_z = nearest(grid_z - sub[:, 0:1], periods[2])
        inside_z = jnp.abs(d_z) <= sub[:, 1:2]
        squared_z = d_z * d_z
        for s in range(SHELLS):
            part = 1.0 / ((s + 1) * (s + 1))
            rate = inverse * part + rate_t
            along_x = jnp.where(inside_x, jnp.exp(-rate * squared_x), 0.0)
            along_y = jnp.where(inside_y, jnp.exp(-rate * squared_y), 0.0)
            for x in range(BX):
                plane_ref[o, s, x * BY : (x + 1) * BY] = (along_x[x : x + 1] * along_y).astype(plane_ref.dtype)
            rate_z = sub[:, 3:4] * part + sub[:, 2:3]
            line_ref[o, s] = jnp.where(inside_z, jnp.exp(-rate_z * squared_z), 0.0).astype(line_ref.dtype)


def merge_kernel(own_ref, mate_ref, third_ref, out_ref):
    odd = (lax.axis_index("layer") & 1) == 1
    lane = lax.broadcasted_iota(jnp.int32, out_ref.shape, 1)
    below = jnp.where(odd, mate_ref[...], third_ref[...])
    above = jnp.where(odd, third_ref[...], mate_ref[...])
    moved = jnp.where(lane < 6 * SPAN, pltpu.roll(below, 3 * SPAN, axis=1), pltpu.roll(above, 3 * SPAN, axis=1))
    out_ref[...] = jnp.where(lane < 4 * SPAN, own_ref[...], jnp.where(lane < 7 * SPAN, moved, 0.0))


def density_kernel(column_steps, *refs):
    coef_refs = refs[:column_steps]
    plane_ref, line_ref, out_ref = refs[column_steps:]
    total = jnp.zeros(out_ref.shape, jnp.float32)
    wide = SHELLS * LANES
    for o in range(plane_ref.shape[0]):
        coef = coef_refs[o % column_steps]
        first = 8 * (o // column_steps)
        terms = [
            (plane_ref[o, s].astype(jnp.float32) * coef[first + s : first + s + 1, :]).astype(line_ref.dtype)
            for s in range(SHELLS)
        ]
        total = total + jnp.dot(
            jnp.concatenate(terms, axis=1),
            line_ref[o * wide : (o + 1) * wide],
            preferred_element_type=jnp.float32,
        )
    out_ref[...] = total


def local(sign_start, neighbors, atom_size, basis_proj, pair_extent, atom_x, atom_y, atom_z):
    n_row = lax.axis_size("row")
    n_col = lax.axis_size("col")
    n_lay = lax.axis_size("layer")
    assert n_lay == 4 and n_col >= 4 and (n_row == 2 or n_row >= 4)
    assert n_row & (n_row - 1) == 0 and n_col & (n_col - 1) == 0
    axes = (n_row, n_col, n_lay)
    atoms, slots = neighbors.shape
    size = sign_start.shape[2]
    steps = [0, 1] if n_row == 2 else [0, 1, -1]
    count = len(steps)
    others = range(1, count)
    own = sign_start[0]
    flat = own.reshape(slots * size, size)
    listings = neighbors.T
    full = slots * size
    half = full // 2
    most = half - size
    n_pick = column_targets(n_row)
    picks = n_pick * size
    part = picks + GEO

    def on_row(value, di):
        return from_offset(value, "row", steps[di])

    x_row = {di: on_row(flat, di) for di in others}
    y_row = from_layer(flat, 2)
    m_row = from_layer(flat, 1)
    picked, geo = pl.pallas_call(
        functools.partial(pick_kernel, axes),
        out_shape=(
            jax.ShapeDtypeStruct((part, size), own.dtype),
            jax.ShapeDtypeStruct((GEO, LANES), own.dtype),
        ),
        in_specs=[HBM] * 6,
        out_specs=(VMEM, VMEM),
        scratch_shapes=[
            pltpu.SMEM((slots, atoms), jnp.int32),
            pltpu.SMEM((1, slots), jnp.int32),
            pltpu.SMEM((atoms,), jnp.int32),
            pltpu.SMEM((atoms,), jnp.int32),
            pltpu.SMEM((atoms,), jnp.int32),
            pltpu.SMEM((n_pick + 1,), jnp.int32),
            pltpu.SemaphoreType.DMA((5,)),
            pltpu.SemaphoreType.DMA((n_pick,)),
        ],
        compiler_params=pltpu.CompilerParams(vmem_limit_bytes=60 << 20),
        name="pick_column_blocks",
    )(listings, pair_extent, atom_x, atom_y, atom_z, own)
    down = from_column(picked, 1)
    up = from_column(picked, 0)

    halves = pack(
        [y_row] + [x_row[di] for di in others] + [geo],
        [[(0, half, most)]] + [[(di, 0, most)] for di in others] + [[(count, 0, GEO)]],
        [],
        "pack_halves",
    )
    ends = {di: on_row(halves[0], di) for di in others}
    tops = {di: from_layer(halves[di], 2) for di in others}

    at = {}
    buffers = {}

    def note(name, value, contents):
        buffers[name] = value
        start = 0
        for what, rows in contents:
            if what is not None:
                at[what] = (name, start)
            start += rows

    def row_of(di, flip, start=0, stop=slots):
        return [(("row", slot, di, flip), size) for slot in range(start, stop)]

    halfway = slots // 2

    def side_of(kind, di, flip):
        return [((kind, di, flip), picks)]

    note("own", flat, row_of(0, 0))
    note("mate", m_row, row_of(0, 1))
    note("far", y_row, row_of(0, 2))
    note("up", up, side_of("up", 0, 0) + [(("up geo", 0, 0), GEO)])
    note("down", down, side_of("down", 0, 0) + [(("down geo", 0, 0), GEO)])
    note("geo", halves[count], [(("geo", 0, 0), GEO)])
    for di in others:
        note(("x", di), x_row[di], row_of(di, 0))
        note(("end", di), ends[di], row_of(di, 2, halfway, slots - 1))
        note(("top", di), tops[di], row_of(di, 2, 0, halfway - 1))

    corners = [("end", di) for di in others] + [("top", di) for di in others]
    names = ["down", "up", "geo", "far"] + [("x", di) for di in others]
    plans = [
        [(1, 0, picks), (0, 0, picks), (3, full - size, size), (2, 0, GEO), (1, picks, GEO), (0, picks, GEO)],
        [(1, 0, picks), (0, 0, picks)] + [(di + 3, most, size) for di in others] + [(2, 0, GEO), (1, picks, GEO), (0, picks, GEO)],
        [(2, 0, GEO), (1, picks, GEO), (0, picks, GEO)],
    ]
    two_x, two_y, geos = pack([buffers[name] for name in names], plans, [m_row], "pack_two")
    to_mate = corners + ["up", "down"]
    for di in others:
        note(("mate x", di), from_layer(x_row[di], 1), row_of(di, 1))
    note("mate far", from_layer(y_row, 1), row_of(0, 3))

    early_order = ["own", "mate", "far", "up", "down", "geo"] + [("x", di) for di in others]
    early_order += [("mate x", di) for di in others] + ["mate far"]
    early_order += corners + [("two x", di) for di in others] + ["two y", "two m"]
    late_order = [("three x", di) for di in others] + ["three y", "three m"]
    late_order += ["four"]

    contents = {}
    for di in others:
        contents["two x", di] = side_of("up", di, 0) + side_of("down", di, 0)
        contents["two x", di] += row_of(di, 2, slots - 1, slots) + [(("geo", di, 0), GEO)]
        contents["two x", di] += [(("up geo", di, 0), GEO), (("down geo", di, 0), GEO)]
    contents["two y"] = side_of("up", 0, 2) + side_of("down", 0, 2)
    contents["two y"] += sum([row_of(di, 2, halfway - 1, halfway) for di in others], []) + [(None, 3 * GEO)]
    contents["two m"] = sum([row_of(di, 3, halfway, slots - 1) for di in others], [])
    contents["two m"] += sum([row_of(di, 3, 0, halfway - 1) for di in others], [])
    contents["two m"] += side_of("up", 0, 1) + side_of("down", 0, 1)
    for di in others:
        contents["three x", di] = side_of("up", di, 2)
    contents["three y"] = sum([side_of("down", di, 2) for di in others], [])
    contents["three m"] = []
    for di in others:
        contents["three m"] += side_of("up", di, 1) + side_of("down", di, 1) + row_of(di, 3, slots - 1, slots)
    contents["three m"] += side_of("up", 0, 3) + side_of("down", 0, 3)
    contents["three m"] += sum([row_of(di, 3, halfway - 1, halfway) for di in others], []) + [(None, 3 * GEO)]
    contents["three m"] += [("geos", count * 3 * GEO)]
    contents["four"] = sum([side_of("up", di, 3) for di in others], [])
    contents["four"] += sum([side_of("down", di, 3) for di in others], [])
    lengths = {name: sum(rows for _, rows in content) for name, content in contents.items()}
    for name in early_order:
        if name in buffers:
            lengths[name] = buffers[name].shape[0]
    base = {}
    total = 0
    for name in early_order + late_order:
        base[name] = total
        total += lengths[name]
        if name == early_order[-1]:
            late_from = total
    located = dict(at)
    for name, content in contents.items():
        start = 0
        for what, rows in content:
            located[what] = (name, start)
            start += rows
    layout = [
        base[located["row", slot, di, flip][0]] + located["row", slot, di, flip][1]
        for di in range(count)
        for flip in range(n_lay)
        for slot in range(slots)
    ]
    layout += [
        base[located[kind, di, flip][0]] + located[kind, di, flip][1]
        for kind in ("up", "down")
        for di in range(count)
        for flip in range(n_lay)
    ]
    pairs = slots * (slots + 1) // 2
    entries = pairs + UNROLL + 1
    early_table, late_table, last_table, info = pl.pallas_call(
        functools.partial(prepare_kernel, axes, count, tuple(layout), late_from, base["four"]),
        out_shape=(
            jax.ShapeDtypeStruct((entries,), jnp.int32),
            jax.ShapeDtypeStruct((entries,), jnp.int32),
            jax.ShapeDtypeStruct((entries,), jnp.int32),
            jax.ShapeDtypeStruct((slots + 2,), jnp.int32),
        ),
        in_specs=[HBM, HBM, ANY],
        out_specs=(SMEM, SMEM, SMEM, SMEM),
        scratch_shapes=[
            pltpu.SMEM((slots, atoms), jnp.int32),
            pltpu.SMEM((atoms,), jnp.int32),
            pltpu.SMEM((3, slots), jnp.int32),
            pltpu.SMEM((atoms,), jnp.int32),
            pltpu.SMEM((len(layout),), jnp.int32),
            pltpu.SemaphoreType.DMA((2,)),
        ],
        compiler_params=pltpu.CompilerParams(vmem_limit_bytes=1 << 20),
        cost_estimate=pl.CostEstimate(flops=1000, bytes_accessed=1000, transcendentals=0),
        name="prepare",
    )(listings, atom_size, two_x)

    plans = [[(i, 0, picks if name in ("up", "down") else most) for i, name in enumerate(to_mate)]]
    two_m = pack([buffers[name] for name in to_mate], plans, [], "pack_two_mate", 3_000_000_000)[0]
    for di in others:
        note(("two x", di), on_row(two_x, di), contents["two x", di])
    note("two y", from_layer(two_y, 2), contents["two y"])
    early_mates = ["mate far"] + [("mate x", di) for di in others]
    note("two m", from_layer(two_m, 1), contents["two m"])

    buffers["geos"] = geos
    names = ["two y", "geos"] + [("two x", di) for di in others]
    place = {name: i for i, name in enumerate(names)}
    gather = [(place["geos"], 0, 3 * GEO)] + [(place["two x", di], 2 * picks + size, 3 * GEO) for di in others]
    xs = [place["two x", di] for di in others]
    plans = [
        [(0, 0, picks)],
        [(x, picks, picks) for x in xs],
        [(x, 0, 2 * picks + size) for x in xs] + [(0, 0, lengths["two y"])] + gather,
        gather,
    ]
    three_x, three_y, three_m, geos = pack([buffers[name] for name in names], plans, [buffers[name] for name in early_mates] + [two_m, info], "pack_three")
    for di in others:
        note(("three x", di), on_row(three_x, di), contents["three x", di])
    note("three y", from_layer(three_y, 2), contents["three y"])
    note("three m", from_layer(three_m, 1), contents["three m"])
    third_geos = from_layer(geos, 3)

    spread, own_basis = pl.pallas_call(
        functools.partial(spread_kernel, axes),
        out_shape=(
            jax.ShapeDtypeStruct((LANES, full), jnp.bfloat16),
            jax.ShapeDtypeStruct((16, size), jnp.bfloat16),
        ),
        in_specs=[HBM, VMEM, ANY],
        out_specs=(VMEM, VMEM),
        scratch_shapes=[pltpu.SMEM((slots, atoms), jnp.int32), pltpu.SemaphoreType.DMA((1,))],
        compiler_params=pltpu.CompilerParams(vmem_limit_bytes=(2 << 20) + atoms * 16384),
        cost_estimate=pl.CostEstimate(flops=1000, bytes_accessed=1000, transcendentals=0),
        name="spread_basis",
    )(listings, basis_proj.transpose(1, 0, 2).reshape(SHELLS * atoms, size), three_x)

    early_values = [buffers[name] for name in early_order]
    gram = pl.pallas_call(
        functools.partial(gram_kernel, len(early_values)),
        out_shape=jax.ShapeDtypeStruct((full, full), jnp.bfloat16),
        in_specs=[SMEM] + [VMEM] * len(early_values) + [ANY],
        out_specs=VMEM,
        scratch_shapes=[pltpu.VMEM((late_from, LANES), jnp.bfloat16)],
        compiler_params=pltpu.CompilerParams(vmem_limit_bytes=(6 << 20) + 2 * late_from * LANES * 2),
        cost_estimate=pl.CostEstimate(flops=1000, bytes_accessed=1000, transcendentals=0),
        name="gram_early",
    )(early_table, *early_values, three_x)

    thirds = [buffers["three x", di] for di in others] + [buffers["three y"]]
    four = pack(thirds, [[(i, 0, value.shape[0]) for i, value in enumerate(thirds)]], [gram, third_geos, own_basis], "pack_four")[0]
    note("four", from_layer(four, 1), contents["four"])

    column_steps = (0, 1, -1)
    tile_steps = [(dr, dc) for dr in steps for dc in column_steps]
    tiles = len(tile_steps)
    periods = (float(BX * n_row), float(BY * n_col), float(BZ * n_lay))
    plane, line = pl.pallas_call(
        functools.partial(profile_kernel, periods, tile_steps, at["geos"][1]),
        out_shape=(
            jax.ShapeDtypeStruct((tiles, SHELLS, BX * BY, LANES), jnp.bfloat16),
            jax.ShapeDtypeStruct((tiles, SHELLS, LANES, BZ), jnp.bfloat16),
        ),
        in_specs=[ANY] * 3,
        out_specs=(VMEM, VMEM),
        scratch_shapes=[
            pltpu.VMEM((3, tiles * GEO, LANES), jnp.bfloat16),
            pltpu.SemaphoreType.DMA((3,)),
        ],
        compiler_params=pltpu.CompilerParams(vmem_limit_bytes=10 << 20),
        cost_estimate=pl.CostEstimate(flops=1000, bytes_accessed=1000, transcendentals=0),
        name="profiles",
    )(geos, buffers["three m"], third_geos)

    late_values = [buffers[name] for name in late_order[:-1]]
    middle, own_kept = pl.pallas_call(
        functools.partial(middle_kernel, len(late_values)),
        out_shape=(
            jax.ShapeDtypeStruct((full, full), jnp.bfloat16),
            jax.ShapeDtypeStruct((size, full), jnp.bfloat16),
        ),
        in_specs=[SMEM, SMEM] + [VMEM] * (2 + len(late_values)) + [ANY],
        out_specs=(VMEM, VMEM),
        scratch_shapes=[pltpu.VMEM((base["four"] - late_from, LANES), jnp.bfloat16)],
        compiler_params=pltpu.CompilerParams(
            vmem_limit_bytes=(13 << 20) + 2 * (base["four"] - late_from) * LANES * 2
        ),
        cost_estimate=pl.CostEstimate(flops=1000, bytes_accessed=1000, transcendentals=0),
        name="gram_middle",
    )(late_table, info, own, gram, *late_values, four)

    late_values = [buffers["four"]]
    sign_next, coef = pl.pallas_call(
        functools.partial(step_kernel, len(late_values)),
        out_shape=(
            jax.ShapeDtypeStruct((slots, size, size), jnp.bfloat16),
            jax.ShapeDtypeStruct((8, LANES), jnp.float32),
        ),
        in_specs=[SMEM, SMEM, VMEM, VMEM, VMEM, VMEM] + [VMEM] * len(late_values),
        out_specs=(VMEM, VMEM),
        scratch_shapes=[
            pltpu.VMEM((total - base["four"], LANES), jnp.bfloat16),
            pltpu.VMEM((full, full), jnp.bfloat16),
            pltpu.VMEM((size, full), jnp.bfloat16),
        ],
        compiler_params=pltpu.CompilerParams(vmem_limit_bytes=(15 << 20) + 2 * (total - late_from) * LANES * 2),
        cost_estimate=pl.CostEstimate(flops=1_300_000_000, bytes_accessed=8_000_000, transcendentals=0),
        name="square_cube_coefficients",
    )(last_table, info, own_basis, spread, own_kept, middle, *late_values)

    mate_coef = from_layer(coef, 1)
    third_coef = from_layer(coef, 3)
    merged = pl.pallas_call(
        merge_kernel,
        out_shape=jax.ShapeDtypeStruct((8, LANES), jnp.float32),
        in_specs=[VMEM] * 3,
        out_specs=VMEM,
        compiler_params=pltpu.CompilerParams(vmem_limit_bytes=1 << 20),
        cost_estimate=pl.CostEstimate(flops=1000, bytes_accessed=1000, transcendentals=0),
        name="merge_layers",
    )(coef, mate_coef, third_coef)
    given, token = pack([sign_next.reshape(full, size)], [[(0, 0, full)], [(0, 0, GEO)]], [], "give_sign")
    parts = [merged] + [on_row(merged, di) for di in others]
    stacked = pack(parts, [[(i, 0, 8) for i in range(count)]], [token], "stack_tiles")[0]
    far_side = from_column(stacked, 1)
    received = [stacked, from_column(stacked, 0), far_side]

    density = pl.pallas_call(
        functools.partial(density_kernel, len(column_steps)),
        out_shape=jax.ShapeDtypeStruct((BX * BY, BZ), jnp.float32),
        in_specs=[VMEM] * (len(received) + 2),
        out_specs=VMEM,
        compiler_params=pltpu.CompilerParams(vmem_limit_bytes=16 << 20),
        cost_estimate=pl.CostEstimate(flops=310_000_000, bytes_accessed=4_000_000, transcendentals=0),
        name="density",
    )(*received, plane, line.reshape(tiles * SHELLS * LANES, BZ))
    return given.reshape(1, slots, size, size), density.reshape(BX, BY, BZ)


def solution(mesh):
    rows = P(("row", "col", "layer"), None, None, None)
    in_specs = (rows, P(), P(), P(), P(("row", "col", "layer"), None), P(), P(), P())
    out_specs = (rows, P("row", "col", "layer"))
    return jax.shard_map(local, mesh=mesh, in_specs=in_specs, out_specs=out_specs, check_vma=False)
```
